32 devices in a mesh: dp: 4 (over y, core), ctx: 8 (over z, x).
Axes of the slice: x: 2, y: 2, z: 4, core: 2. Of those that a mesh axis runs over, the one named last changes fastest.
Arguments:
- pixels: float32 [4, 2, 4, 5, 16384], P('dp', None, None, None, 'ctx'), may hold values from -1 to 1
- lengths: int32 [4, 2, 4], P('dp'), may hold values from 1 to 16384, 40960 in all within a row
- ctx_mask: int32 [4, 2, 4, 16384], P('dp', None, None, 'ctx'), may hold values 0 or 1
- head_w: float32 [256, 65536], P(None, 'ctx'), may hold values from -0.0034179688 to 0.0034179688
- head_mom: float32 [256, 65536], P(None, 'ctx'), may hold values from -0.0390625 to 0.0390625
- square_w: float32 [2, 256, 256], replicated
- square_mom: float32 [2, 256, 256], replicated, may hold values from -0.005859375 to 0.005859375
- small_params: float32 [15, 256], replicated, may hold values from -2 to 2, as said below
- small_mom: float32 [15, 256], replicated
- small_var: float32 [15, 256], replicated, as said below
Outputs:
- head_mom_new: float32 [256, 65536], P(None, 'ctx')
- head_new: float32 [256, 65536], P(None, 'ctx')
- head_copy: bfloat16 [256, 65536], P(None, 'ctx')
- square_mom_new: float32 [2, 256, 256], replicated
- square_new: float32 [2, 256, 256], replicated
- square_copy: bfloat16 [2, 256, 256], replicated
- small_mom_new: float32 [15, 256], replicated
- small_var_new: float32 [15, 256], replicated
- small_new: float32 [15, 256], replicated
- small_copy: bfloat16 [15, 256], replicated
- loss_value: float32 [], replicated
The draws below stay inside these ranges and needn't reach their ends.
Inputs may be any that keep to these rules, and one draw needn't show every extreme that they name: `small_params`: parameters of their usual scales; row 11 (the gain) lies near 1. `small_var`: Positive.
All inputs are finite; a program needn't handle non-finite values. No bound on the sum of `ctx_mask` on one device may be relied on, other than what follows from the above.
Results may differ from the reference program's by a relative error of at most 0.001.
The reference program's roundings to bfloat16 on the way count: a program that leaves them out, or rounds other values in their place, can miss the bound.
Values may be sent and summed in bfloat16 or wider, within the bound.
A program may use at most 320 MiB of HBM per device.

```python
import math
import jax
import jax.numpy as jnp
import numpy as np
from jax import lax

D = 256
G = 4
MB = 2
NS_STEPS = 5
STEP = 10
PIXG = 16384
LIVE_ROW = 40960
LIVE_ALL = 327680
GROUPS_ALL = 32
N_DP = 4


def row_spread():
    return jnp.array([0.45] * 5 + [0.5] * 2 + [0.0625] * 3 + [0.1, 0.1, 0.1, 0.1, 0.1], jnp.float32)


def grad_rows():
    return jnp.array([0.3] * 5 + [30.0] * 2 + [1.0] * 3 + [0.3, 0.3, 0.3, 0.3, 30.0], jnp.float32) * LIVE_ALL ** (-0.5)


def draw_small_params(key, part):
    key = jax.random.fold_in(key, 11)
    noise = jnp.clip(jax.random.normal(key, (15, D), jnp.float32), -4.0, 4.0)
    values = noise * row_spread()[:, None]
    row_ids = jnp.arange(15)[:, None]
    return jnp.where(row_ids == 11, 1.0 + values, values)


def draw_small_mom(key, part):
    key = jax.random.fold_in(key, 12)
    sign_key, size_key = jax.random.split(key)
    signs = jnp.where(jax.random.uniform(sign_key, (15, D)) < 0.5, -1.0, 1.0)
    magnitude = jnp.exp(jax.random.uniform(size_key, (15, D), jnp.float32, -0.693, 0.693))
    return signs * magnitude * 0.11 * grad_rows()[:, None]


def draw_small_var(key, part):
    key = jax.random.fold_in(key, 13)
    factor = jnp.exp(jax.random.uniform(key, (15, D), jnp.float32, -0.693, 2.079))
    scale = grad_rows()[:, None]
    return factor * scale * scale * 0.001


def draw_square_w(key, part):
    key = jax.random.fold_in(key, 14)
    noise = jnp.clip(jax.random.normal(key, (2, D, D), jnp.float32), -4.0, 4.0)
    spread = jnp.array([1.0, 0.06], jnp.float32)[:, None, None] * D ** (-0.5)
    return noise * spread


def with_ends(result, rng, low, largest):
    longest = result.shape.index(max(result.shape))
    spots = []
    for shift in (0, 1):
        where = [jax.random.randint(jax.random.fold_in(rng, axis), (), 0, length) for axis, length in enumerate(result.shape)]
        where[longest] = (where[longest] + shift) % result.shape[longest]
        spots.append(tuple(where))
    return result.at[spots[0]].set(low).at[spots[1]].set(largest)


def level_of(own_key, extent, pieces, low, largest):
    def one(dim, parts):
        heights = jax.random.uniform(jax.random.fold_in(jax.random.fold_in(own_key, 6), dim), (parts,), jnp.float32, low / len(pieces), largest / len(pieces))
        return jnp.repeat(jnp.exp(heights), extent[dim] // parts).reshape((-1,) + (1,) * (len(extent) - dim - 1))

    loudness = one(*pieces[0])
    for cut in pieces[1:]:
        loudness = loudness * one(*cut)
    return loudness


def length_profile(count, total, limit, lean):
    loads = [(1 << 20) // math.isqrt(grade ** lean) + 1 for grade in range(2, count + 1)]
    surplus, given = total - limit - (count - 1), [1] * (count - 1)
    while surplus > 0:
        free = [i for i in range(count - 1) if given[i] < limit]
        whole, left = sum([loads[i] for i in free]), surplus
        for i in free:
            extra = min(limit - given[i], max(1, left * loads[i] // whole), surplus)
            given[i] = given[i] + extra
            surplus = surplus - extra
    return np.array([limit] + given)


def uneven_parts(rng, amount, total, reach, slope):
    if amount == 2:
        one = jax.random.randint(rng, (), max(1, total - reach), min(reach, total - 1) + 1)
        return jnp.stack([one, total - one])
    sizes = jnp.asarray(length_profile(amount, total, reach, slope), jnp.int32)
    pairs = (amount - 1) // 2
    source_of, receiver = sizes[1:1 + 2 * pairs:2], sizes[2:2 + 2 * pairs:2]
    slack = jnp.minimum(source_of - 1, reach - receiver)
    passed = jax.random.randint(jax.random.fold_in(rng, 1), (pairs,), 0, 1 << 20) % (slack + 1)
    sizes = sizes.at[1:1 + 2 * pairs:2].set(source_of - passed).at[2:2 + 2 * pairs:2].set(receiver + passed)
    return sizes[jax.random.permutation(jax.random.fold_in(rng, 2), amount)]


def bell_draw(own_key, extent, width, reach, cuts=(), kind=jnp.bfloat16):
    entries = jax.random.normal(own_key, extent, jnp.float32) * width
    if len(cuts) > 0:
        entries = level_of(own_key, extent, cuts, -0.22, 0.18) * entries
    return jnp.clip(entries, min=-reach, max=reach).astype(kind)


def setup_inputs(seed: int = 0) -> dict:
    splits = jax.random.split(jax.random.key(seed), 11)
    return {
        "pixels": jnp.clip(jax.random.uniform(splits[0], (N_DP, MB, G, 5, PIXG), jnp.float32, -1.0, 1.0) * level_of(splits[0], (N_DP, MB, G, 5, PIXG), ((0, 4), (4, 8)), -0.4, 0.0), -1.0, 1.0),
        "lengths": jax.vmap(lambda own: uneven_parts(own, G, LIVE_ROW, PIXG, 2))(jax.random.split(splits[1], N_DP * MB)).reshape((N_DP, MB, G)).astype(jnp.int32),
        "ctx_mask": with_ends((jax.random.randint(splits[2], (N_DP, MB, G, PIXG), 0, 2) < 1).astype(jnp.int32), jax.random.fold_in(splits[2], 1), 0, 1),
        "head_w": bell_draw(splits[3], (D, D * D), (D * 12346) ** -0.5, 0.0034179688, ((1, 8),), jnp.float32),
        "head_mom": bell_draw(splits[4], (D, D * D), (max(LIVE_ALL * LIVE_ALL // 4000000, 4)) ** -0.5, 0.0390625, ((1, 8),), jnp.float32),
        "square_w": draw_square_w(jax.random.fold_in(splits[10], 71), 0),
        "square_mom": bell_draw(splits[6], (2, D, D), (max(LIVE_ALL * LIVE_ALL // 100000, 4)) ** -0.5, 0.005859375, (), jnp.float32),
        "small_params": draw_small_params(jax.random.fold_in(splits[10], 71), 0),
        "small_mom": draw_small_mom(jax.random.fold_in(splits[10], 71), 0),
        "small_var": draw_small_var(jax.random.fold_in(splits[10], 71), 0),
    }


exact_arithmetic_mode = lax.Precision.HIGHEST
reg_weight = 0.5
momentum_rate = 0.95
head_rate = 0.003
square_rates = (0.3, 0.02)
adam_rate = 0.05
beta_first = 0.9
beta_second = 0.999
decay_rate = 0.01
first_coef = 3.4445
second_coef = -4.775
third_coef = 2.0315

@jax.custom_vjp
def reduced_arithmetic_mode(v):
    return lax.optimization_barrier(v.astype(jnp.bfloat16)).astype(jnp.float32)

@jax.custom_vjp
def reduced_reverse_sweep(v):
    return v

def low_keep(v):
    return (reduced_arithmetic_mode(v), None)

def low_pass(kept, grad):
    return (grad,)

def back_keep(v):
    return (v, None)

def back_low(kept, grad):
    return (reduced_arithmetic_mode(grad),)
reduced_arithmetic_mode.defvjp(low_keep, low_pass)
reduced_reverse_sweep.defvjp(back_keep, back_low)

def layer_norm(values, gain_row, bias_row):
    centered = values - lax.optimization_barrier(jnp.mean(values, axis=-1, keepdims=True))
    variance = lax.optimization_barrier(jnp.mean(centered * centered, axis=-1, keepdims=True))
    return centered * lax.rsqrt(variance + 1e-05) * gain_row + bias_row

def row_loss(weights, pixels_row, lengths_row, mask_row):
    head_weight, square_weight, narrow_coefficient_table = weights
    slot_ids = jnp.arange(mask_row.shape[1], dtype=jnp.int32)
    live_slot = slot_ids[None, :] < lengths_row[:, None]
    context = jnp.where(live_slot & (mask_row == 1), 1.0, 0.0)
    query_mask = jnp.where(live_slot & (mask_row == 0), 1.0, 0.0)
    features = jnp.transpose(pixels_row, (0, 2, 1))
    first_pre = jnp.einsum('gpc,cd->gpd', features, narrow_coefficient_table[0:5], precision=exact_arithmetic_mode) + narrow_coefficient_table[10]
    normed = layer_norm(jax.nn.gelu(first_pre), narrow_coefficient_table[11], narrow_coefficient_table[12])
    second = reduced_reverse_sweep(jnp.einsum('gpd,de->gpe', reduced_arithmetic_mode(normed), reduced_arithmetic_mode(square_weight[0]), precision=exact_arithmetic_mode) + narrow_coefficient_table[13])
    encoded = jax.nn.gelu(second)
    summed = jnp.einsum('gp,gpe->ge', context, encoded, precision=exact_arithmetic_mode)
    latent = reduced_arithmetic_mode(summed / (lax.optimization_barrier(jnp.sum(context, axis=1))[:, None] + 1.0))
    generated = jnp.dot(latent, reduced_arithmetic_mode(head_weight), precision=exact_arithmetic_mode)
    gen_matrix = reduced_arithmetic_mode(generated).reshape(generated.shape[0], D, D)
    gen_bias = jnp.dot(latent, reduced_arithmetic_mode(square_weight[1]), precision=exact_arithmetic_mode)
    coord_pre = jnp.einsum('gpc,cd->gpd', features[..., 3:5], narrow_coefficient_table[5:7], precision=exact_arithmetic_mode) + narrow_coefficient_table[14]
    siren_in = reduced_arithmetic_mode(jnp.sin(30.0 * coord_pre))
    siren_pre = reduced_reverse_sweep(jnp.einsum('gpd,gde->gpe', siren_in, gen_matrix, precision=exact_arithmetic_mode) + gen_bias[:, None, :])
    periodic_model_result = reduced_arithmetic_mode(jnp.sin(30.0 * siren_pre))
    estimated_colour_values = reduced_reverse_sweep(jnp.einsum('kdg,cg->kcd', periodic_model_result, reduced_arithmetic_mode(narrow_coefficient_table[7:10]), precision=exact_arithmetic_mode))
    errors = (estimated_colour_values - pixels_row[:, 0:3]) * query_mask[:, None, :]
    return jnp.stack([jnp.sum(errors * errors), jnp.sum(generated * generated)])

def ns_update(current, gram_matrix):
    polynomial = second_coef * gram_matrix + third_coef * jnp.einsum('kij,kjl->kil', gram_matrix, gram_matrix, precision=exact_arithmetic_mode)
    return first_coef * current + jnp.einsum('kij,kjl->kil', polynomial, current, precision=exact_arithmetic_mode)

def orthogonal(matrices):
    norms = jnp.sqrt(lax.optimization_barrier(jnp.sum(matrices * matrices, axis=(1, 2), keepdims=True)))
    current = matrices / (norms + 1e-07)
    for sweep in range(NS_STEPS):
        gram_matrix = jnp.einsum('kij,klj->kil', current, current, precision=exact_arithmetic_mode)
        current = ns_update(current, gram_matrix)
    return current

def adam_update(params, grad, moment, second_moment):
    moment_new = beta_first * moment + (1.0 - beta_first) * grad
    second_new = beta_second * second_moment + (1.0 - beta_second) * grad * grad
    corrected = moment_new / (1.0 - beta_first ** STEP) / (jnp.sqrt(second_new / (1.0 - beta_second ** STEP)) + 1e-08)
    return (moment_new, second_new, params - adam_rate * (corrected + decay_rate * params))

def reference(pixels, lengths, ctx_mask, head_w, head_mom, square_w, square_mom, small_params, small_mom, small_var):
    rows_pixels = pixels.reshape((N_DP * MB, G, 5, PIXG))
    rows_lengths = lengths.reshape((N_DP * MB, G))
    rows_mask = ctx_mask.reshape((N_DP * MB, G, PIXG))

    def total_loss(weights):

        def step_fn(carry, row):
            return (carry + jax.checkpoint(row_loss)(weights, row[0], row[1], row[2]), None)
        stat_sums, unused = lax.scan(step_fn, jnp.zeros((2,), jnp.float32), (rows_pixels, rows_lengths, rows_mask))
        return (stat_sums[0] / LIVE_ALL + reg_weight * stat_sums[1] / GROUPS_ALL, stat_sums)
    loss_value, back_fn, stat_sums = jax.vjp(total_loss, (head_w, square_w, small_params), has_aux=True)
    grads, = back_fn(jnp.ones((), jnp.float32))
    grad_head, grad_square, grad_small = grads
    head_moment = momentum_rate * head_mom + grad_head
    head_dir = orthogonal(head_moment[None])[0]
    head_new = head_w - head_rate * (0.2 * D * head_dir + decay_rate * head_w)
    square_moment = momentum_rate * square_mom + grad_square
    rates = jnp.array(square_rates, jnp.float32)[:, None, None]
    square_new = square_w - rates * (0.2 * D ** 0.5 * orthogonal(square_moment) + decay_rate * square_w)
    small_moment, small_second, small_new = adam_update(small_params, grad_small, small_mom, small_var)
    return (head_moment, head_new, head_new.astype(jnp.bfloat16), square_moment, square_new, square_new.astype(jnp.bfloat16), small_moment, small_second, small_new, small_new.astype(jnp.bfloat16), loss_value)
```

```python
import functools

import jax
import jax.numpy as jnp
from jax import lax
from jax.experimental import pallas as pl
from jax.experimental.pallas import tpu as pltpu
from jax.sharding import PartitionSpec as P

NS_STEPS = 5
STEP = 10


exact_arithmetic_mode = lax.Precision.HIGHEST
reg_weight = 0.5
momentum_rate = 0.95
head_rate = 0.003
square_rates = (0.3, 0.02)
adam_rate = 0.05
beta_first = 0.9
beta_second = 0.999
decay_rate = 0.01
first_coef = 3.4445
second_coef = -4.775
third_coef = 2.0315


def layer_norm(values, gain_row, bias_row):
    centered = values - jnp.mean(values, axis=-1, keepdims=True)
    variance = jnp.mean(centered * centered, axis=-1, keepdims=True)
    return centered * lax.rsqrt(variance + 1e-05) * gain_row + bias_row


def ns_update(current, gram_matrix):
    polynomial = second_coef * gram_matrix + third_coef * jnp.einsum(
        "kij,kjl->kil", gram_matrix, gram_matrix, precision=exact_arithmetic_mode
    )
    return first_coef * current + jnp.einsum(
        "kij,kjl->kil", polynomial, current, precision=exact_arithmetic_mode
    )


def orthogonal_local(matrices):
    norms = jnp.sqrt(jnp.sum(matrices * matrices, axis=(1, 2), keepdims=True))
    current = matrices / (norms + 1e-07)
    for sweep in range(NS_STEPS):
        gram_matrix = jnp.einsum("kij,klj->kil", current, current, precision=exact_arithmetic_mode)
        current = ns_update(current, gram_matrix)
    return current


def head_orthogonal(moment):
    current = moment[None]
    total = lax.psum(jnp.sum(moment * moment), "ctx")
    current = current / (jnp.sqrt(total) + 1e-07)
    for sweep in range(NS_STEPS):
        gram_matrix = lax.psum(
            jnp.dot(current[0], current[0].T, precision=exact_arithmetic_mode), "ctx"
        )
        current = ns_update(current, gram_matrix[None])
    return current[0]


def adam_update(params, grad, moment, second_moment):
    moment_new = beta_first * moment + (1.0 - beta_first) * grad
    second_new = beta_second * second_moment + (1.0 - beta_second) * grad * grad
    corrected = (
        moment_new
        / (1.0 - beta_first**STEP)
        / (jnp.sqrt(second_new / (1.0 - beta_second**STEP)) + 1e-08)
    )
    return (moment_new, second_new, params - adam_rate * (corrected + decay_rate * params))


def encoder_forward(features, context, small_params, second_low):
    first_pre = (
        jnp.einsum("gpc,cd->gpd", features, small_params[0:5], precision=exact_arithmetic_mode)
        + small_params[10]
    )
    first_act, gelu_first = jax.vjp(jax.nn.gelu, first_pre)
    normed, norm_back = jax.vjp(layer_norm, first_act, small_params[11], small_params[12])
    normed_low = normed.astype(jnp.bfloat16)
    second = (
        jnp.einsum("gpd,de->gpe", normed_low, second_low, preferred_element_type=jnp.float32)
        + small_params[13]
    )
    encoded, gelu_second = jax.vjp(jax.nn.gelu, second)
    summed = jnp.einsum("gp,gpe->ge", context, encoded, precision=exact_arithmetic_mode)
    return (
        summed,
        jnp.sum(context, axis=1),
        (first_pre, gelu_first, norm_back, normed_low, gelu_second),
    )


def general(
    pixels,
    lengths,
    ctx_mask,
    head_w,
    head_mom,
    square_w,
    square_mom,
    small_params,
    small_mom,
    small_var,
):
    micro_count = pixels.shape[1]
    groups = pixels.shape[2]
    slot_count = pixels.shape[4]
    model_width = square_w.shape[1]
    live_all = (
        lax.axis_size("dp") * micro_count * (groups * slot_count * lax.axis_size("ctx") * 5 // 8)
    )
    groups_all = lax.axis_size("dp") * micro_count * groups
    slot_ids = lax.axis_index("ctx") * slot_count + jnp.arange(slot_count, dtype=jnp.int32)
    head_low = head_w.astype(jnp.bfloat16)
    head_back = head_low.astype(jnp.float32)
    square_low = square_w.astype(jnp.bfloat16)
    bias_head = square_low[1].astype(jnp.float32)
    final_coefficient_reduced = small_params[7:10].astype(jnp.bfloat16)
    kept = []
    sum_list = []
    count_list = []
    for micro_index in range(micro_count):
        features = jnp.transpose(pixels[0, micro_index], (0, 2, 1))
        live_slot = slot_ids[None, :] < lengths[0, micro_index][:, None]
        context = jnp.where(live_slot & (ctx_mask[0, micro_index] == 1), 1.0, 0.0).astype(
            jnp.float32
        )
        query_mask = jnp.where(live_slot & (ctx_mask[0, micro_index] == 0), 1.0, 0.0).astype(
            jnp.float32
        )
        summed, counts, saved = encoder_forward(features, context, small_params, square_low[0])
        sum_list.append(summed)
        count_list.append(counts)
        kept.append((features, context, query_mask, saved))
    totals = [
        lax.psum((sum_list[index_micro], count_list[index_micro]), "ctx")
        for index_micro in range(micro_count)
    ]
    zeros_small = jnp.zeros((model_width,), jnp.float32)
    grad_first_w = jnp.zeros((5, model_width), jnp.float32)
    grad_coord_w = jnp.zeros((2, model_width), jnp.float32)
    grad_out_w = jnp.zeros((3, model_width), jnp.float32)
    grad_vectors = [zeros_small] * 5
    grad_square = jnp.zeros_like(square_w)
    latent_rows = []
    theta_rows = []
    squared = jnp.zeros((), jnp.float32)
    regular = jnp.zeros((), jnp.float32)
    for micro_index in range(micro_count):
        features, context, query_mask, saved = kept[micro_index]
        first_pre, gelu_first, norm_back, normed_low, gelu_second = saved
        summed, counts = totals[micro_index]
        divisor = counts[:, None] + 1.0
        latent_low = (summed / divisor).astype(jnp.bfloat16)
        latent_back = latent_low.astype(jnp.float32)
        generated = jnp.dot(latent_low, head_low, preferred_element_type=jnp.float32)
        gen_parts = generated.astype(jnp.bfloat16).reshape(groups, -1, model_width)
        gen_full = lax.all_gather(gen_parts, "ctx", axis=1, tiled=True)
        gen_bias = jnp.dot(latent_low, square_low[1], preferred_element_type=jnp.float32)
        coord_pre = (
            jnp.einsum(
                "gpc,cd->gpd",
                features[..., 3:5],
                small_params[5:7],
                precision=exact_arithmetic_mode,
            )
            + small_params[14]
        )
        siren_low = jnp.sin(30.0 * coord_pre).astype(jnp.bfloat16)
        siren_pre = (
            jnp.einsum("gpd,gde->gpe", siren_low, gen_full, preferred_element_type=jnp.float32)
            + gen_bias[:, None, :]
        )
        result_reduced_form = jnp.sin(30.0 * siren_pre).astype(jnp.bfloat16)
        estimated_colour_values = jnp.einsum(
            "kdg,cg->kcd",
            result_reduced_form,
            final_coefficient_reduced,
            preferred_element_type=jnp.float32,
        )
        errors = (
            estimated_colour_values - jnp.transpose(features[..., 0:3], (0, 2, 1))
        ) * query_mask[:, None, :]
        squared = squared + jnp.sum(errors * errors)
        regular = regular + jnp.sum(generated * generated)
        prediction_gradient = (2.0 / live_all * errors).astype(jnp.bfloat16)
        grad_out_w = grad_out_w + jnp.einsum(
            "dan,dnq->aq",
            prediction_gradient,
            result_reduced_form,
            preferred_element_type=jnp.float32,
        )
        grad_out = jnp.einsum(
            "xvw,vt->xwt",
            prediction_gradient,
            final_coefficient_reduced,
            preferred_element_type=jnp.float32,
        )
        grad_inner = (grad_out * 30.0 * jnp.cos(30.0 * siren_pre)).astype(jnp.bfloat16)
        gen_part = jnp.einsum(
            "gpd,gpe->gde", siren_low, grad_inner, preferred_element_type=jnp.float32
        )
        gen_grad = lax.psum_scatter(gen_part, "ctx", scatter_dimension=1, tiled=True).reshape(
            groups, -1
        )
        gen_grad = gen_grad + 2.0 * reg_weight / groups_all * generated
        bias_part = jnp.sum(grad_inner.astype(jnp.float32), axis=1)
        grad_siren = jnp.einsum(
            "gpe,gde->gpd", grad_inner, gen_full, preferred_element_type=jnp.float32
        )
        grad_coord = grad_siren * 30.0 * jnp.cos(30.0 * coord_pre)
        grad_coord_w = grad_coord_w + jnp.einsum(
            "gpc,gpd->cd", features[..., 3:5], grad_coord, precision=exact_arithmetic_mode
        )
        grad_vectors[4] = grad_vectors[4] + jnp.sum(grad_coord, axis=(0, 1))
        latent_rows.append(latent_back)
        theta_rows.append(gen_grad)
        latent_part = jnp.dot(gen_grad, head_back.T, precision=exact_arithmetic_mode)
        latent_part, bias_full = lax.psum((latent_part, bias_part), "ctx")
        grad_square = grad_square.at[1].add(
            jnp.dot(latent_back.T, bias_part, precision=exact_arithmetic_mode)
        )
        grad_latent = latent_part + jnp.dot(bias_full, bias_head.T, precision=exact_arithmetic_mode)
        grad_encoded = context[:, :, None] * (grad_latent / divisor)[:, None, :]
        (grad_second,) = gelu_second(grad_encoded)
        second_low = grad_second.astype(jnp.bfloat16)
        grad_square = grad_square.at[0].add(
            jnp.einsum("gpd,gpe->de", normed_low, second_low, preferred_element_type=jnp.float32)
        )
        grad_vectors[3] = grad_vectors[3] + jnp.sum(second_low.astype(jnp.float32), axis=(0, 1))
        grad_normed = jnp.einsum(
            "gpe,de->gpd", second_low, square_low[0], preferred_element_type=jnp.float32
        )
        grad_act, grad_gain, grad_beta = norm_back(grad_normed)
        (grad_first,) = gelu_first(grad_act)
        grad_first_w = grad_first_w + jnp.einsum(
            "gpc,gpd->cd", features, grad_first, precision=exact_arithmetic_mode
        )
        grad_vectors[0] = grad_vectors[0] + jnp.sum(grad_first, axis=(0, 1))
        grad_vectors[1] = grad_vectors[1] + grad_gain
        grad_vectors[2] = grad_vectors[2] + grad_beta
    grad_small = jnp.concatenate(
        [
            grad_first_w,
            grad_coord_w,
            grad_out_w,
            jnp.stack(
                [
                    grad_vectors[0],
                    grad_vectors[1],
                    grad_vectors[2],
                    grad_vectors[3],
                    grad_vectors[4],
                ]
            ),
        ],
        axis=0,
    )
    grad_small, grad_square, stat_sums = lax.psum(
        (grad_small, grad_square, jnp.stack([squared, regular])), ("dp", "ctx")
    )
    latent_stack = jnp.concatenate(latent_rows, axis=0)
    theta_stack = jnp.concatenate(theta_rows, axis=0)
    grad_head = lax.psum(
        jnp.dot(latent_stack.T, theta_stack, precision=exact_arithmetic_mode), "dp"
    )
    loss_value = stat_sums[0] / live_all + reg_weight * stat_sums[1] / groups_all
    head_moment = momentum_rate * head_mom + grad_head
    head_dir = head_orthogonal(head_moment)
    head_new = head_w - head_rate * (0.2 * model_width * head_dir + decay_rate * head_w)
    square_moment = momentum_rate * square_mom + grad_square
    rates = jnp.array(square_rates, jnp.float32)[:, None, None]
    square_new = square_w - rates * (
        0.2 * model_width**0.5 * orthogonal_local(square_moment) + decay_rate * square_w
    )
    small_moment, small_second, small_new = adam_update(
        small_params, grad_small, small_mom, small_var
    )
    return (
        head_moment,
        head_new,
        head_new.astype(jnp.bfloat16),
        square_moment,
        square_new,
        square_new.astype(jnp.bfloat16),
        small_moment,
        small_second,
        small_new,
        small_new.astype(jnp.bfloat16),
        loss_value,
    )


MESH = pl.DeviceIdType.MESH
F32 = jnp.float32
BF16 = jnp.bfloat16
WIDTH = 256
TILE = 256
MIB = 1024 * 1024
TURN = 30.0 / 6.283185307179586
SIN_TERMS = (
    3.1415925800447195,
    -5.167706878925927,
    2.550031377273445,
    -0.5980451740836717,
    0.07722012888386035,
)
COS_TERMS = (
    0.9999999534666512,
    -4.934792858673131,
    4.058411914124358,
    -1.3318801609752882,
    0.21969679805650213,
)


def any_spec():
    return pl.BlockSpec(memory_space=pl.ANY)


def vmem_spec():
    return pl.BlockSpec(memory_space=pltpu.VMEM)


def smem_spec():
    return pl.BlockSpec(memory_space=pltpu.SMEM)


def dot_nn(a, b):
    return lax.dot_general(a, b, (((1,), (0,)), ((), ())), preferred_element_type=F32)


def dot_nt(a, b):
    return lax.dot_general(a, b, (((1,), (1,)), ((), ())), preferred_element_type=F32)


def full_nn(a, b):
    return lax.dot_general(
        a, b, (((1,), (0,)), ((), ())), precision=lax.Precision.HIGHEST, preferred_element_type=F32
    )


def full_nt(a, b):
    return lax.dot_general(
        a, b, (((1,), (1,)), ((), ())), precision=lax.Precision.HIGHEST, preferred_element_type=F32
    )


def split3(v):
    high = v.astype(BF16).astype(F32)
    rest = v - high
    mid = rest.astype(BF16).astype(F32)
    return high, mid, rest - mid


def greet(peers):
    barrier = pltpu.get_barrier_semaphore()
    for peer in peers:
        pl.semaphore_signal(barrier, inc=1, device_id=peer, device_id_type=MESH)
    pl.semaphore_wait(barrier, len(peers))


def ring_peers(axis, n):
    me = lax.axis_index(axis)
    return [lax.rem(me + d, n) for d in range(1, n)]


def send_all(axis, n, source, target, send_sem, recv_sem):
    copies = []
    for d, peer in enumerate(ring_peers(axis, n)):
        copy = pltpu.make_async_remote_copy(
            src_ref=source(peer),
            dst_ref=target,
            send_sem=send_sem.at[d],
            recv_sem=recv_sem.at[d],
            device_id={axis: peer},
            device_id_type=MESH,
        )
        copy.start()
        copies.append(copy)
    return copies


def column(row, width):
    return jnp.broadcast_to(row, (width, row.shape[1])).T


def gelu_parts(v):
    square = v * v
    inner = v * (0.7978845608028654 + 0.035677408136300125 * square)
    tanh = jnp.tanh(inner)
    return square, tanh


def gelu_value(v):
    square, tanh = gelu_parts(v)
    half = 0.5 * v
    return half + half * tanh


def gelu_both(v):
    square, tanh = gelu_parts(v)
    half = 0.5 * v
    value = half + half * tanh
    slope = 0.5 + 0.5 * tanh + (half - half * tanh * tanh) * (
        0.7978845608028654 + 0.10703222440890037 * square
    )
    return value, slope


def sine_pair(turns):
    frac = turns - jnp.floor(turns + 0.5)
    square = frac * frac
    s = SIN_TERMS[4]
    c = COS_TERMS[4]
    for k in (3, 2, 1, 0):
        s = s * square + SIN_TERMS[k]
        c = c * square + COS_TERMS[k]
    s = s * frac
    return (2.0 * s) * c, 30.0 - 60.0 * (s * s)


def triple_rows(block):
    high, mid, low = split3(block)
    return jnp.concatenate([high, high, mid, high, mid, low], axis=0)


def triple_weights(block):
    high, mid, low = split3(block)
    rows = jnp.concatenate([high, mid, high, low, mid, high], axis=0)
    pad = jnp.zeros((128 - rows.shape[0], rows.shape[1]), F32)
    return jnp.concatenate([rows, pad], axis=0).T.astype(BF16)


def triple_from_list(rows):
    high, mid, low = rows[0:8], rows[8:16], rows[16:24]
    pad = jnp.zeros((80, rows.shape[1]), F32)
    return jnp.concatenate([high, high, mid, high, mid, low, pad], axis=0).astype(BF16)


def weight_block(weights, bias, place):
    rows = weights.shape[0]
    parts = []
    if place > 0:
        parts.append(jnp.zeros((place, WIDTH), F32))
    parts.append(weights)
    if place + rows < 6:
        parts.append(jnp.zeros((6 - place - rows, WIDTH), F32))
    parts.append(bias)
    parts.append(jnp.zeros((1, WIDTH), F32))
    return jnp.concatenate(parts, axis=0)


def scatter_kernel(n, pix_ref, mask_ref, mom_ref, rx_ref, gram_ref, stage, buf, send_sem, recv_sem, load_sem):
    me = lax.axis_index("ctx")
    peers = ring_peers("ctx", n)
    chunk = buf.shape[2]

    def load(k):
        return pltpu.make_async_copy(mom_ref.at[:, pl.ds(k * chunk, chunk)], buf.at[k], load_sem.at[k])

    for k in range(buf.shape[0]):
        load(k).start()
    slots = pix_ref.shape[2]
    per = mask_ref.shape[1]
    for g in range(n):
        stage[g, 0:5, :] = pix_ref[g]
        stage[g, 5:6, :] = mask_ref[g // per, g % per : g % per + 1, :].astype(F32)
        stage[g, 6:7, :] = jnp.ones((1, slots), F32)
        stage[g, 7:8, :] = jnp.zeros((1, slots), F32)
    greet([{"ctx": peer} for peer in peers])
    copies = send_all("ctx", n, lambda peer: stage.at[peer], rx_ref.at[me], send_sem, recv_sem)
    rx_ref[me] = stage[me]
    total = jnp.zeros((WIDTH, WIDTH), F32)
    for k in range(buf.shape[0]):
        load(k).wait()
        block = buf[k]
        total = total + full_nt(block, block)
    gram_ref[...] = total
    for copy in copies:
        copy.wait()


def encoder_kernel(
    len_ref, rx_ref, small_ref, square_ref, z_ref, clist, qlist, count_ref,
    dest, ytile, cnt_v, cnt_s, upper, wide, zacc, sem,
):
    me = lax.axis_index("ctx")
    sources, unused, slots = rx_ref.shape
    per_source = slots // TILE
    groups = len_ref.shape[2]
    length = len_ref[0, me // groups, lax.rem(me, groups)]
    upper[...] = jnp.where(
        lax.broadcasted_iota(jnp.int32, (TILE, TILE), 0) <= lax.broadcasted_iota(jnp.int32, (TILE, TILE), 1),
        1.0,
        0.0,
    ).astype(BF16)
    place = lax.broadcasted_iota(jnp.int32, (per_source, TILE), 0) * TILE + lax.broadcasted_iota(
        jnp.int32, (per_source, TILE), 1
    )
    ones = jnp.ones((16, TILE), BF16)
    for s in range(sources):
        mask = rx_ref[s, 5:6, :]
        mask = jnp.concatenate([mask[:, k * TILE : (k + 1) * TILE] for k in range(per_source)], axis=0)
        live = place + s * slots < length
        context = jnp.where(live & (mask > 0.5), 1.0, 0.0)
        query = jnp.where(live & (mask < 0.5), 1.0, 0.0)
        both = jnp.concatenate([context, query], axis=0).astype(BF16)
        order = dot_nn(both, upper[...])
        before_c, before_q = order[0:per_source], order[per_source : 2 * per_source]
        live_c = before_c[:, TILE - 1 : TILE]
        dest[s * per_source : (s + 1) * per_source, :] = jnp.where(
            context > 0.5, before_c - 1.0, jnp.where(query > 0.5, live_c + before_q - 1.0, -1.0)
        )
        padded = jnp.concatenate([both, jnp.zeros((128 - 2 * per_source, TILE), BF16)], axis=0)
        cnt_v[s : s + 1, :] = dot_nt(ones, padded)[0:1].astype(jnp.int32)
    counts = pltpu.make_async_copy(cnt_v, cnt_s, sem)
    counts.start()
    tiles = (length + TILE - 1) // TILE
    quads = (tiles + 3) // 4
    row_ids = lax.broadcasted_iota(jnp.int32, (TILE, TILE), 0).astype(F32)

    def arrange(i, carry):
        s = i // 2
        for k in range(4):
            lane = pl.multiple_of(lax.rem(i, 2) * (4 * TILE) + k * TILE, TILE)
            rows = rx_ref[s, :, pl.ds(lane, TILE)]
            high, mid, low = split3(rows)
            stack = jnp.concatenate([high, mid, low, jnp.zeros((8, TILE), F32)], axis=0).astype(BF16)
            target = dest[pl.ds(4 * i + k, 1), :]
            chosen = jnp.where(row_ids == target, 1.0, 0.0).astype(BF16)
            ytile[4 * i + k] = dot_nt(stack, chosen)[0:24]
        return carry

    lax.fori_loop(0, quads, arrange, 0)
    counts.wait()
    empty = jnp.zeros((24, TILE), F32)
    clist[:, 0:TILE] = empty
    qlist[:, 0:TILE] = empty
    lane_ids = lax.broadcasted_iota(jnp.int32, (24, TILE), 1)

    def put(target, rows, offset, start, amount):
        shift = lax.rem(offset, TILE)
        base = pl.multiple_of(offset - shift, TILE)
        turned = pltpu.roll(rows, lax.rem(shift - start + TILE, TILE), 1)
        here = (lane_ids >= shift) & (lane_ids < shift + amount)
        there = lane_ids < shift + amount - TILE
        target[:, pl.ds(base, TILE)] += jnp.where(here, turned, 0.0)
        target[:, pl.ds(pl.multiple_of(base + TILE, TILE), TILE)] = jnp.where(there, turned, 0.0)

    def place_tile(i, carry):
        off_c, off_q = carry
        s, k = i // per_source, lax.rem(i, per_source)
        num_c, num_q = cnt_s[s, k], cnt_s[s, per_source + k]
        rows = ytile[i]
        put(clist, rows, off_c, 0, num_c)
        put(qlist, rows, off_q, num_c, num_q)
        return off_c + num_c, off_q + num_q

    num_c, num_q = lax.fori_loop(0, tiles, place_tile, (jnp.int32(0), jnp.int32(0)))
    count_ref[0] = num_c
    count_ref[1] = num_q
    small = small_ref[...]
    first = triple_weights(weight_block(small[0:5], small[10:11], 0))
    wide[0] = column(small[11:12], TILE)
    wide[1] = column(small[12:13], TILE)
    wide[2] = column(small[13:14], TILE)
    second = square_ref[0].T.astype(BF16)
    zacc[...] = jnp.zeros_like(zacc)

    def encode(t, carry):
        rows = clist[:, pl.ds(pl.multiple_of(t * TILE, TILE), TILE)]
        pre = dot_nn(first, triple_from_list(rows))
        act = gelu_value(pre)
        centered = act - jnp.sum(act, axis=0, keepdims=True) * (1.0 / WIDTH)
        variance = jnp.sum(centered * centered, axis=0, keepdims=True) * (1.0 / WIDTH)
        normed = centered * lax.rsqrt(variance + 1e-05) * wide[0] + wide[1]
        encoded = gelu_value(dot_nn(second, normed.astype(BF16)) + wide[2])
        zacc[...] += encoded * rows[6:7]
        return carry

    lax.fori_loop(0, (num_c + TILE - 1) // TILE, encode, 0)
    summed = full_nt(jnp.ones((8, TILE), F32), zacc[...])
    latent = summed / (num_c.astype(F32) + 1.0)
    z_ref[...] = latent.astype(BF16).astype(F32)


def theta_kernel(
    n, z_ref, head_ref, gram_ref, theta_ref, gen_ref, z8_ref, rows_ref, reg_ref,
    zall, head, give, turn, gram_rx, load_sem, sems,
):
    me = lax.axis_index("ctx")
    peers = ring_peers("ctx", n)
    chunk = head.shape[2]
    per = chunk // WIDTH

    def load(k):
        return pltpu.make_async_copy(head_ref.at[:, pl.ds(k * chunk, chunk)], head.at[k], load_sem.at[k])

    for k in range(head.shape[0]):
        load(k).start()
    greet([{"ctx": peer} for peer in peers])
    latents = send_all("ctx", n, lambda peer: z_ref, zall.at[me], sems.at[0], sems.at[1])
    height = WIDTH // n
    grams = send_all(
        "ctx",
        n,
        lambda peer: gram_ref.at[pl.ds(pl.multiple_of(peer * height, height), height), :],
        gram_rx.at[me],
        sems.at[2],
        sems.at[3],
    )
    zall[me] = z_ref[...]
    gram_rx[me] = gram_ref[pl.ds(pl.multiple_of(me * height, height), height), :]
    for copy in latents:
        copy.wait()
    ids = lax.broadcasted_iota(jnp.int32, (8, WIDTH), 0)
    rows = jnp.zeros((8, WIDTH), F32)
    for g in range(n):
        rows = jnp.where(ids == g, zall[g], rows)
    z8_ref[...] = rows
    left = jnp.concatenate([rows, jnp.zeros((8, WIDTH), F32)], axis=0).astype(BF16)
    regular = jnp.zeros((8, WIDTH), F32)
    for k in range(head.shape[0]):
        load(k).wait()
        part = dot_nn(left, head[k].astype(BF16))[0:8]
        for i in range(per):
            piece = part[:, i * WIDTH : (i + 1) * WIDTH]
            theta_ref[pl.ds((k * per + i) * 8, 8), :] = piece
            for half in range(2):
                turn[half, pl.ds((k * per + i) * 8, 8), :] = piece[:, half * 128 : half * 128 + 128]
            regular = regular + piece * piece
    reg_ref[...] = regular
    for g in range(n):
        for half in range(2):
            give[g, :, half * 128 : half * 128 + 128] = turn[half, pl.ds(g, height, stride=8), :].astype(BF16)
    parts = send_all(
        "ctx",
        n,
        lambda peer: give.at[peer],
        gen_ref.at[pl.ds(pl.multiple_of(me * height, height), height), :],
        sems.at[4],
        sems.at[5],
    )
    gen_ref[pl.ds(pl.multiple_of(me * height, height), height), :] = give[me]
    for copy in grams:
        copy.wait()
    total = gram_rx[0]
    for s in range(1, n):
        total = total + gram_rx[s]
    rows_ref[...] = total
    for copy in parts:
        copy.wait()


def siren_kernel(
    live_all, count_ref, q_ref, gen_ref, z_ref, small_ref, square_ref, out_ref, narrow_ref,
    gen_t, wide, sin_in, cos_in, sin_mid, back, acc_g, acc_c, acc_o, acc_b, acc_e,
):
    small = small_ref[...]
    gen_t[...] = gen_ref[...].astype(F32).T.astype(BF16)
    coord = triple_weights(weight_block(small[5:7] * TURN, small[14:15] * TURN, 3))
    latent = jnp.concatenate([z_ref[...], jnp.zeros((8, WIDTH), F32)], axis=0).astype(BF16)
    bias = dot_nn(latent, square_ref[1].astype(BF16))[0:1]
    wide[...] = column(bias * TURN, TILE)
    final = small[7:10].astype(BF16).astype(F32)
    final_rows = jnp.concatenate([final, jnp.zeros((13, WIDTH), F32)], axis=0).astype(BF16)
    final_cols = jnp.concatenate([final, jnp.zeros((125, WIDTH), F32)], axis=0).T.astype(BF16)
    for ref in (acc_g, acc_c, acc_o, acc_b, acc_e):
        ref[...] = jnp.zeros_like(ref)
    scale = 2.0 / live_all
    ones = jnp.ones((16, TILE), BF16)

    def step(t, carry):
        rows = q_ref[:, pl.ds(pl.multiple_of(t * TILE, TILE), TILE)]
        s_in, c_in = sine_pair(dot_nn(coord, triple_from_list(rows)))
        sin_in[...] = s_in.astype(BF16)
        cos_in[...] = c_in
        s_mid, c_mid = sine_pair(dot_nn(gen_t[...], sin_in[...]) * TURN + wide[...])
        sin_mid[...] = s_mid.astype(BF16)
        pred = dot_nn(final_rows, sin_mid[...])[0:8]
        ids = lax.broadcasted_iota(jnp.int32, (8, TILE), 0)
        colour = rows[0:8] + rows[8:16] + rows[16:24]
        error = jnp.where(ids < 3, (pred - colour) * rows[6:7], 0.0)
        acc_e[...] += error * error
        slope = jnp.concatenate([error * scale, jnp.zeros((8, TILE), F32)], axis=0).astype(BF16)
        acc_o[...] += dot_nt(slope, sin_mid[...])
        slope_cols = jnp.concatenate([slope, jnp.zeros((112, TILE), BF16)], axis=0)
        back[...] = (c_mid * dot_nn(final_cols, slope_cols)).astype(BF16)
        acc_g[...] += dot_nt(sin_in[...], back[...])
        acc_b[...] += dot_nt(ones, back[...])
        outer = cos_in[...] * dot_nn(gen_ref[...], back[...])
        high = outer.astype(BF16)
        low = (outer - high.astype(F32)).astype(BF16)
        left = jnp.concatenate([rows, jnp.zeros((8, TILE), F32)], axis=0).astype(BF16)
        acc_c[...] += dot_nt(left, high) + dot_nt(left, low)
        return carry

    lax.fori_loop(0, (count_ref[1] + TILE - 1) // TILE, step, 0)
    height = out_ref.shape[1] - 8
    for s in range(out_ref.shape[0]):
        out_ref[s, 0:height, :] = acc_g[s * height : (s + 1) * height, :]
        out_ref[s, height : height + 8, :] = acc_b[0:8]
    coords = acc_c[0:8] + acc_c[8:16] + acc_c[16:24]
    narrow_ref[0:2, :] = coords[3:5]
    narrow_ref[2:5, :] = acc_o[0:3]
    narrow_ref[5:6, :] = coords[6:7]
    narrow_ref[6:7, :] = jnp.broadcast_to(jnp.sum(acc_e[...]), (1, WIDTH))
    narrow_ref[7:8, :] = jnp.zeros((1, WIDTH), F32)


def latent_kernel(
    n, rows_n, groups_all, part_ref, theta_ref, head_ref, rows_ref, z8_ref,
    dz_ref, tall_ref, zd_ref, gram_ref, rx, turn, head, rxz, dz_own, load_sem, sems, dsems,
):
    me = lax.axis_index("ctx")
    r = lax.axis_index("dp")
    peers = ring_peers("ctx", n)
    rows_peers = ring_peers("dp", rows_n)
    chunk = head.shape[2]
    per = chunk // WIDTH
    height = WIDTH // n
    tall_n = height + 8

    def load(k):
        return pltpu.make_async_copy(head_ref.at[:, pl.ds(k * chunk, chunk)], head.at[k], load_sem.at[k])

    for k in range(head.shape[0]):
        load(k).start()
    greet([{"ctx": peer} for peer in peers] + [{"dp": peer} for peer in rows_peers])
    mine = pl.ds(pl.multiple_of(me * tall_n, 8), tall_n)
    parts = send_all("ctx", n, lambda peer: part_ref.at[peer], rx.at[mine, :], sems.at[0], sems.at[1])
    grams = send_all("ctx", n, lambda peer: rows_ref, gram_ref.at[me], sems.at[2], sems.at[3])
    rx[mine, :] = part_ref[me]
    gram_ref[me] = rows_ref[...]
    for copy in parts:
        copy.wait()
    own = pl.ds(pl.multiple_of(r * 8, 8), 8)
    turn[0] = rx[:, 0:128]
    turn[1] = rx[:, 128:256]

    def across(i):
        return jnp.concatenate([turn[half, pl.ds(i, 8, stride=tall_n), :] for half in range(2)], axis=1)

    for i in range(height):
        tall_ref[i, own, :] = across(i) + theta_ref[pl.ds(i * 8, 8), :] * (1.0 / groups_all)
    zd_ref[r, 0:8, :] = z8_ref[...]
    zd_ref[r, 8:16, :] = across(height)
    talls = send_all("dp", rows_n, lambda peer: tall_ref.at[:, own, :], tall_ref.at[:, own, :], dsems.at[0], dsems.at[1])
    zds = send_all("dp", rows_n, lambda peer: zd_ref.at[r], zd_ref.at[r], dsems.at[2], dsems.at[3])
    total = jnp.zeros((24, WIDTH), F32)
    for k in range(head.shape[0]):
        load(k).wait()
        block = jnp.concatenate([tall_ref[k * per + i, own, :] for i in range(per)], axis=1)
        stack = jnp.concatenate(split3(block), axis=0).astype(BF16)
        total = total + dot_nt(stack, head[k].astype(BF16))
    dz_own[...] = total[0:8] + total[8:16] + total[16:24]
    terms = send_all("ctx", n, lambda peer: dz_own, rxz.at[me], sems.at[4], sems.at[5])
    rxz[me] = dz_own[...]
    for copy in terms:
        copy.wait()
    total = rxz[0]
    for s in range(1, n):
        total = total + rxz[s]
    dz_ref[...] = total
    for copy in grams + talls + zds:
        copy.wait()


def encoder_back_kernel(
    count_ref, c_ref, small_ref, square_ref, dz_ref, part_ref, narrow_ref, reg_ref, out_ref,
    wide, acc_s, acc_f, acc_g, acc_b, rows_out,
):
    me = lax.axis_index("ctx")
    num_c = count_ref[0]
    small = small_ref[...]
    first = triple_weights(weight_block(small[0:5], small[10:11], 0))
    second = square_ref[0].astype(BF16)
    second_t = square_ref[0].T.astype(BF16)
    height = part_ref.shape[1] - 8
    bias_back = full_nt(part_ref[0, height : height + 8, :], square_ref[1].astype(BF16).astype(F32))
    latent_back = dz_ref[pl.ds(me, 1), :] + bias_back[0:1]
    wide[0] = column(small[11:12], TILE)
    wide[1] = column(small[12:13], TILE)
    wide[2] = column(small[13:14], TILE)
    wide[3] = column(latent_back / (num_c.astype(F32) + 1.0), TILE)
    for ref in (acc_s, acc_f, acc_g, acc_b):
        ref[...] = jnp.zeros_like(ref)
    ones = jnp.ones((16, TILE), BF16)

    def step(t, carry):
        rows = c_ref[:, pl.ds(pl.multiple_of(t * TILE, TILE), TILE)]
        pre = dot_nn(first, triple_from_list(rows))
        act, act_slope = gelu_both(pre)
        centered = act - jnp.sum(act, axis=0, keepdims=True) * (1.0 / WIDTH)
        variance = jnp.sum(centered * centered, axis=0, keepdims=True) * (1.0 / WIDTH)
        inverse = lax.rsqrt(variance + 1e-05)
        unit = centered * inverse
        normed = (unit * wide[0] + wide[1]).astype(BF16)
        unused, slope = gelu_both(dot_nn(second_t, normed) + wide[2])
        grad = (slope * (wide[3] * rows[6:7])).astype(BF16)
        acc_s[...] += dot_nt(normed, grad)
        acc_b[...] += dot_nt(ones, grad)
        grad_normed = dot_nn(second, grad)
        product = grad_normed * unit
        acc_g[...] += product
        grad_unit = grad_normed * wide[0]
        mean_one = jnp.sum(grad_unit, axis=0, keepdims=True) * (1.0 / WIDTH)
        mean_two = jnp.sum(product * wide[0], axis=0, keepdims=True) * (1.0 / WIDTH)
        outer = (grad_unit - mean_one - unit * mean_two) * inverse * act_slope
        high = outer.astype(BF16)
        low = (outer - high.astype(F32)).astype(BF16)
        left = jnp.concatenate([rows, jnp.zeros((8, TILE), F32)], axis=0).astype(BF16)
        acc_f[...] += dot_nt(left, high) + dot_nt(left, low)
        return carry

    lax.fori_loop(0, (num_c + TILE - 1) // TILE, step, 0)
    firsts = acc_f[0:8] + acc_f[8:16] + acc_f[16:24]
    bias_grad = acc_b[0:8]
    shift_grad = full_nt(bias_grad, second.astype(F32))
    gain_grad = full_nt(jnp.ones((8, TILE), F32), acc_g[...])
    rows_out[0:5, :] = firsts[0:5]
    rows_out[5:10, :] = narrow_ref[0:5, :]
    rows_out[10:11, :] = firsts[6:7]
    rows_out[11:12, :] = gain_grad[0:1]
    rows_out[12:13, :] = shift_grad[0:1]
    rows_out[13:14, :] = bias_grad[0:1]
    rows_out[14:15, :] = narrow_ref[5:6, :]
    lane = lax.broadcasted_iota(jnp.int32, (1, WIDTH), 1)
    regular = jnp.broadcast_to(jnp.sum(reg_ref[...]), (1, WIDTH))
    rows_out[15:16, :] = jnp.where(lane == 0, narrow_ref[6:7, :], jnp.where(lane == 1, regular, 0.0))
    n = out_ref.shape[0]
    for s in range(n):
        out_ref[s, 0:height, :] = acc_s[s * height : (s + 1) * height, :]
        out_ref[s, height : height + 2, :] = rows_out[2 * s : 2 * s + 2, :]
        out_ref[s, height + 2 : height + 8, :] = jnp.zeros((6, WIDTH), F32)


def newton(gram, steps):
    ids = lax.broadcasted_iota(jnp.int32, gram.shape, 0) == lax.broadcasted_iota(jnp.int32, gram.shape, 1)
    norm = jnp.sqrt(jnp.sum(jnp.where(ids, gram, 0.0))) + 1e-07
    inverse = 1.0 / norm
    current = gram * inverse * inverse
    product = None
    for k in range(steps):
        poly = (
            jnp.where(ids, first_coef, 0.0) + second_coef * current + third_coef * full_nn(current, current)
        )
        if k + 1 < steps:
            current = full_nn(poly, full_nn(poly, current))
        product = poly if product is None else full_nn(poly, product)
    return product * inverse


def reduce_kernel(
    n, rows_n, grad_ref, tall_ref, zd_ref, gram_ref, mom_ref, sum_ref, move_ref,
    mom, cross, rxc, rxg, rxd, fin, load_sem, sems, dsems,
):
    me = lax.axis_index("ctx")
    r = lax.axis_index("dp")
    peers = ring_peers("ctx", n)
    rows_peers = ring_peers("dp", rows_n)
    chunk = mom.shape[2]
    per = chunk // WIDTH

    def load(k):
        return pltpu.make_async_copy(mom_ref.at[:, pl.ds(k * chunk, chunk)], mom.at[k], load_sem.at[k])

    for k in range(mom.shape[0]):
        load(k).start()
    greet([{"ctx": peer} for peer in peers] + [{"dp": peer} for peer in rows_peers])
    grads = send_all("ctx", n, lambda peer: grad_ref.at[peer], rxg.at[me], sems.at[0], sems.at[1])
    rxg[me] = grad_ref[me]
    mixed = jnp.zeros((32, WIDTH), F32)
    inner = jnp.zeros((32, 32), F32)
    for k in range(mom.shape[0]):
        load(k).wait()
        for i in range(per):
            rows = tall_ref[k * per + i]
            mixed = mixed + full_nt(rows, mom[k, :, i * WIDTH : (i + 1) * WIDTH])
            inner = inner + full_nt(rows, rows)
    cross[:, 0:WIDTH] = mixed
    cross[:, WIDTH : WIDTH + 128] = jnp.concatenate([inner, jnp.zeros((32, 96), F32)], axis=1)
    terms = send_all("ctx", n, lambda peer: cross, rxc.at[me], sems.at[2], sems.at[3])
    rxc[me] = cross[...]
    for copy in grads:
        copy.wait()
    total = rxg[0]
    for s in range(1, n):
        total = total + rxg[s]
    rxd[r] = total
    across = send_all("dp", rows_n, lambda peer: rxd.at[r], rxd.at[r], dsems.at[0], dsems.at[1])
    for copy in terms:
        copy.wait()
    total = rxc[0]
    for s in range(1, n):
        total = total + rxc[s]
    latents = jnp.concatenate([zd_ref[s, 0:8, :] for s in range(rows_n)], axis=0)
    mixed = total[:, 0:WIDTH]
    inner = total[:, WIDTH : WIDTH + 32]
    weight = momentum_rate * mixed + 0.5 * full_nn(inner, latents)
    half = full_nn(latents.T, weight)
    gram = (momentum_rate * momentum_rate) * jnp.concatenate([gram_ref[s] for s in range(n)], axis=0)
    gram = gram + (half + half.T)
    for copy in across:
        copy.wait()
    total = rxd[0]
    for s in range(1, rows_n):
        total = total + rxd[s]
    fin[...] = total
    sum_ref[me] = total
    final = send_all("ctx", n, lambda peer: fin, sum_ref.at[me], sems.at[4], sems.at[5])
    move_ref[...] = newton(gram, NS_STEPS)
    for copy in final:
        copy.wait()


def square_kernel(
    live_all, groups_all, sum_ref, zd_ref, square_ref, smom_ref, small_ref, mmom_ref, mvar_ref,
    smom_out, square_out, scopy_out, mmom_out, mvar_out, small_out, mcopy_out, loss_out,
):
    n, tall_n, unused = sum_ref.shape
    height = tall_n - 8
    rows_n = zd_ref.shape[0]
    latents = jnp.concatenate([zd_ref[s, 0:8, :] for s in range(rows_n)], axis=0)
    biases = jnp.concatenate([zd_ref[s, 8:16, :] for s in range(rows_n)], axis=0)
    grads = [
        jnp.concatenate([sum_ref[s, 0:height, :] for s in range(n)], axis=0),
        full_nn(latents.T, biases),
    ]
    for k in range(2):
        moment = momentum_rate * smom_ref[k] + grads[k]
        smom_out[k] = moment
        move = full_nn(newton(full_nt(moment, moment), NS_STEPS), moment)
        old = square_ref[k]
        new = old - square_rates[k] * (0.2 * WIDTH**0.5 * move + decay_rate * old)
        square_out[k] = new
        scopy_out[k] = new.astype(BF16)
    narrow = jnp.concatenate([sum_ref[s, height : height + 2, :] for s in range(n)], axis=0)
    stats = narrow[15:16]
    lane = lax.broadcasted_iota(jnp.int32, (1, WIDTH), 1)
    weight = jnp.where(lane == 0, 1.0 / live_all, jnp.where(lane == 1, reg_weight / groups_all, 0.0))
    loss_out[...] = jnp.broadcast_to(jnp.sum(stats * weight), loss_out.shape)
    moment, second, new = adam_update(small_ref[...], narrow[0:15], mmom_ref[...], mvar_ref[...])
    mmom_out[...] = moment
    mvar_out[...] = second
    small_out[...] = new
    mcopy_out[...] = new.astype(BF16)


def head_kernel(mom_ref, head_ref, tall_ref, zd_ref, move_ref, mom_out, head_out, copy_out, left):
    @pl.when(pl.program_id(0) == 0)
    def begin():
        rows_n = zd_ref.shape[0]
        latents = jnp.concatenate([zd_ref[s, 0:8, :] for s in range(rows_n)], axis=0)
        rows = jnp.concatenate([latents] * 3 + [jnp.zeros((32, WIDTH), F32)], axis=0)
        left[...] = rows.T.astype(BF16)

    for i in range(tall_ref.shape[0]):
        lanes = slice(i * WIDTH, (i + 1) * WIDTH)
        high, mid, low = split3(tall_ref[i])
        right = jnp.concatenate([high, mid, low, jnp.zeros_like(high)], axis=0).astype(BF16)
        moment = momentum_rate * mom_ref[:, lanes] + dot_nn(left[...], right)
        mom_out[:, lanes] = moment
        move = full_nn(move_ref[...], moment)
        old = head_ref[:, lanes]
        new = old - head_rate * (0.2 * WIDTH * move + decay_rate * old)
        head_out[:, lanes] = new
        copy_out[:, lanes] = new.astype(BF16)


def shape(*dims, dtype=F32):
    return jax.ShapeDtypeStruct(dims, dtype)


def grouped(
    pixels, lengths, ctx_mask, head_w, head_mom, square_w, square_mom, small_params, small_mom, small_var
):
    micro, groups, slots = pixels.shape[1], pixels.shape[2], pixels.shape[4]
    n = lax.axis_size("ctx")
    rows_n = lax.axis_size("dp")
    columns = head_w.shape[1]
    live_all = rows_n * micro * (groups * slots * n * 5 // 8)
    groups_all = rows_n * micro * groups
    height = WIDTH // n
    chunk = 1024
    chunks = columns // chunk
    cap = slots * n + 4 * TILE
    tall_n = height + 8
    dma = pltpu.SemaphoreType.DMA
    limit = 50 * MIB

    def remote(ident):
        return pltpu.CompilerParams(collective_id=ident, has_side_effects=True, vmem_limit_bytes=limit)

    plain = pltpu.CompilerParams(vmem_limit_bytes=limit)
    received, gram_part = pl.pallas_call(
        functools.partial(scatter_kernel, n),
        out_shape=[shape(n, 8, slots), shape(WIDTH, WIDTH)],
        in_specs=[vmem_spec(), vmem_spec(), any_spec()],
        out_specs=[vmem_spec()] * 2,
        scratch_shapes=[
            pltpu.VMEM((n, 8, slots), F32),
            pltpu.VMEM((chunks, WIDTH, chunk), F32),
            dma((n - 1,)),
            dma((n - 1,)),
            dma((chunks,)),
        ],
        compiler_params=remote(1),
        name="scatter_pixels",
    )(pixels.reshape(micro * groups, 5, slots), ctx_mask[0], head_mom)
    latent, clist, qlist, counts = pl.pallas_call(
        encoder_kernel,
        out_shape=[shape(8, WIDTH), shape(24, cap), shape(24, cap), shape(2, dtype=jnp.int32)],
        in_specs=[smem_spec(), vmem_spec(), vmem_spec(), vmem_spec()],
        out_specs=[vmem_spec(), vmem_spec(), vmem_spec(), smem_spec()],
        scratch_shapes=[
            pltpu.VMEM((slots * n // TILE, TILE), F32),
            pltpu.VMEM((slots * n // TILE, 24, TILE), F32),
            pltpu.VMEM((8, 128), jnp.int32),
            pltpu.SMEM((8, 128), jnp.int32),
            pltpu.VMEM((TILE, TILE), BF16),
            pltpu.VMEM((3, WIDTH, TILE), F32),
            pltpu.VMEM((WIDTH, TILE), F32),
            dma(()),
        ],
        compiler_params=plain,
        name="encode",
    )(lengths, received, small_params, square_w)
    theta, gen, z8, gram_rows, regular = pl.pallas_call(
        functools.partial(theta_kernel, n),
        out_shape=[
            shape(WIDTH, WIDTH),
            shape(WIDTH, WIDTH, dtype=BF16),
            shape(8, WIDTH),
            shape(height, WIDTH),
            shape(8, WIDTH),
        ],
        in_specs=[vmem_spec(), any_spec(), vmem_spec()],
        out_specs=[vmem_spec()] * 5,
        scratch_shapes=[
            pltpu.VMEM((n, 8, WIDTH), F32),
            pltpu.VMEM((chunks, WIDTH, chunk), F32),
            pltpu.VMEM((n, height, WIDTH), BF16),
            pltpu.VMEM((2, WIDTH, 128), F32),
            pltpu.VMEM((n, height, WIDTH), F32),
            dma((chunks,)),
            dma((6, n - 1)),
        ],
        compiler_params=remote(2),
        name="generate",
    )(latent, head_w, gram_part)
    part, narrow = pl.pallas_call(
        functools.partial(siren_kernel, live_all),
        out_shape=[shape(n, tall_n, WIDTH), shape(8, WIDTH)],
        in_specs=[smem_spec()] + [vmem_spec()] * 5,
        out_specs=[vmem_spec()] * 2,
        scratch_shapes=[
            pltpu.VMEM((WIDTH, WIDTH), BF16),
            pltpu.VMEM((WIDTH, TILE), F32),
            pltpu.VMEM((WIDTH, TILE), BF16),
            pltpu.VMEM((WIDTH, TILE), F32),
            pltpu.VMEM((WIDTH, TILE), BF16),
            pltpu.VMEM((WIDTH, TILE), BF16),
            pltpu.VMEM((WIDTH, WIDTH), F32),
            pltpu.VMEM((32, WIDTH), F32),
            pltpu.VMEM((16, WIDTH), F32),
            pltpu.VMEM((16, WIDTH), F32),
            pltpu.VMEM((8, TILE), F32),
        ],
        compiler_params=plain,
        name="siren",
    )(counts, qlist, gen, latent, small_params, square_w)
    latent_grad, tall, latents, gram = pl.pallas_call(
        functools.partial(latent_kernel, n, rows_n, groups_all),
        out_shape=[
            shape(8, WIDTH),
            shape(height, 8 * rows_n, WIDTH),
            shape(rows_n, 16, WIDTH),
            shape(n, height, WIDTH),
        ],
        in_specs=[vmem_spec(), vmem_spec(), any_spec(), vmem_spec(), vmem_spec()],
        out_specs=[vmem_spec()] * 4,
        scratch_shapes=[
            pltpu.VMEM((n * tall_n, WIDTH), F32),
            pltpu.VMEM((2, n * tall_n, 128), F32),
            pltpu.VMEM((chunks, WIDTH, chunk), F32),
            pltpu.VMEM((n, 8, WIDTH), F32),
            pltpu.VMEM((8, WIDTH), F32),
            dma((chunks,)),
            dma((6, n - 1)),
            dma((4, rows_n - 1)),
        ],
        compiler_params=remote(3),
        name="latent_grads",
    )(part, theta, head_w, gram_rows, z8)
    grads = pl.pallas_call(
        encoder_back_kernel,
        out_shape=shape(n, tall_n, WIDTH),
        in_specs=[smem_spec()] + [vmem_spec()] * 7,
        out_specs=vmem_spec(),
        scratch_shapes=[
            pltpu.VMEM((4, WIDTH, TILE), F32),
            pltpu.VMEM((WIDTH, WIDTH), F32),
            pltpu.VMEM((32, WIDTH), F32),
            pltpu.VMEM((WIDTH, TILE), F32),
            pltpu.VMEM((16, WIDTH), F32),
            pltpu.VMEM((16, WIDTH), F32),
        ],
        compiler_params=plain,
        name="encode_back",
    )(counts, clist, small_params, square_w, latent_grad, part, narrow, regular)
    sums, move = pl.pallas_call(
        functools.partial(reduce_kernel, n, rows_n),
        out_shape=[shape(n, tall_n, WIDTH), shape(WIDTH, WIDTH)],
        in_specs=[vmem_spec()] * 4 + [any_spec()],
        out_specs=[vmem_spec()] * 2,
        scratch_shapes=[
            pltpu.VMEM((chunks, WIDTH, chunk), F32),
            pltpu.VMEM((32, WIDTH + 128), F32),
            pltpu.VMEM((n, 32, WIDTH + 128), F32),
            pltpu.VMEM((n, tall_n, WIDTH), F32),
            pltpu.VMEM((rows_n, tall_n, WIDTH), F32),
            pltpu.VMEM((tall_n, WIDTH), F32),
            dma((chunks,)),
            dma((6, n - 1)),
            dma((2, rows_n - 1)),
        ],
        compiler_params=remote(4),
        name="reduce_grads",
    )(grads, tall, latents, gram, head_mom)
    square_out = pl.pallas_call(
        functools.partial(square_kernel, live_all, groups_all),
        out_shape=[
            shape(2, WIDTH, WIDTH),
            shape(2, WIDTH, WIDTH),
            shape(2, WIDTH, WIDTH, dtype=BF16),
            shape(15, WIDTH),
            shape(15, WIDTH),
            shape(15, WIDTH),
            shape(15, WIDTH, dtype=BF16),
            shape(1, 128),
        ],
        in_specs=[vmem_spec()] * 7,
        out_specs=[vmem_spec()] * 8,
        compiler_params=plain,
        name="square_update",
    )(sums, latents, square_w, square_mom, small_params, small_mom, small_var)
    square_moment, square_new, square_copy, small_moment, small_second, small_new, small_copy, loss = square_out
    step = 2
    block = pl.BlockSpec((WIDTH, step * WIDTH), lambda i: (0, i))
    head_moment, head_new, head_copy = pl.pallas_call(
        head_kernel,
        grid=(height // step,),
        out_shape=[shape(WIDTH, columns), shape(WIDTH, columns), shape(WIDTH, columns, dtype=BF16)],
        in_specs=[
            block,
            block,
            pl.BlockSpec((step, 8 * rows_n, WIDTH), lambda i: (i, 0, 0)),
            pl.BlockSpec((rows_n, 16, WIDTH), lambda i: (0, 0, 0)),
            pl.BlockSpec((WIDTH, WIDTH), lambda i: (0, 0)),
        ],
        out_specs=[block] * 3,
        scratch_shapes=[pltpu.VMEM((WIDTH, 128), BF16)],
        compiler_params=plain,
        name="head_update",
    )(head_mom, head_w, tall, latents, move)
    return (
        head_moment,
        head_new,
        head_copy,
        square_moment,
        square_new,
        square_copy,
        small_moment,
        small_second,
        small_new,
        small_copy,
        loss[0, 0],
    )


def local(pixels, lengths, ctx_mask, head_w, *rest):
    n = lax.axis_size("ctx")
    fits = (
        pixels.shape[1] * pixels.shape[2] == n
        and n == 8
        and lax.axis_size("dp") == 4
        and pixels.shape[4] == 2048
        and head_w.shape == (WIDTH, 8192)
    )
    chosen = grouped if fits else general
    return chosen(pixels, lengths, ctx_mask, head_w, *rest)


def solution(mesh):
    placed = (
        P("dp", None, None, None, "ctx"),
        P("dp", None, None),
        P("dp", None, None, "ctx"),
        P(None, "ctx"),
        P(None, "ctx"),
        P(),
        P(),
        P(),
        P(),
        P(),
    )
    return jax.shard_map(
        local,
        mesh=mesh,
        in_specs=placed,
        out_specs=(
            P(None, "ctx"),
            P(None, "ctx"),
            P(None, "ctx"),
            P(),
            P(),
            P(),
            P(),
            P(),
            P(),
            P(),
            P(),
        ),
        check_vma=False,
    )
```

```python
import functools

import jax
import jax.numpy as jnp
from jax import lax
from jax.experimental import pallas as pl
from jax.experimental.pallas import tpu as pltpu
from jax.sharding import PartitionSpec as P

NS_STEPS = 5
STEP = 10


exact_arithmetic_mode = lax.Precision.HIGHEST
reg_weight = 0.5
momentum_rate = 0.95
head_rate = 0.003
square_rates = (0.3, 0.02)
adam_rate = 0.05
beta_first = 0.9
beta_second = 0.999
decay_rate = 0.01
first_coef = 3.4445
second_coef = -4.775
third_coef = 2.0315


def layer_norm(values, gain_row, bias_row):
    centered = values - jnp.mean(values, axis=-1, keepdims=True)
    variance = jnp.mean(centered * centered, axis=-1, keepdims=True)
    return centered * lax.rsqrt(variance + 1e-05) * gain_row + bias_row


def ns_update(current, gram_matrix):
    polynomial = second_coef * gram_matrix + third_coef * jnp.einsum(
        "kij,kjl->kil", gram_matrix, gram_matrix, precision=exact_arithmetic_mode
    )
    return first_coef * current + jnp.einsum(
        "kij,kjl->kil", polynomial, current, precision=exact_arithmetic_mode
    )


def orthogonal_local(matrices):
    norms = jnp.sqrt(jnp.sum(matrices * matrices, axis=(1, 2), keepdims=True))
    current = matrices / (norms + 1e-07)
    for sweep in range(NS_STEPS):
        gram_matrix = jnp.einsum("kij,klj->kil", current, current, precision=exact_arithmetic_mode)
        current = ns_update(current, gram_matrix)
    return current


def head_orthogonal(moment):
    current = moment[None]
    total = lax.psum(jnp.sum(moment * moment), "ctx")
    current = current / (jnp.sqrt(total) + 1e-07)
    for sweep in range(NS_STEPS):
        gram_matrix = lax.psum(
            jnp.dot(current[0], current[0].T, precision=exact_arithmetic_mode), "ctx"
        )
        current = ns_update(current, gram_matrix[None])
    return current[0]


def adam_update(params, grad, moment, second_moment):
    moment_new = beta_first * moment + (1.0 - beta_first) * grad
    second_new = beta_second * second_moment + (1.0 - beta_second) * grad * grad
    corrected = (
        moment_new
        / (1.0 - beta_first**STEP)
        / (jnp.sqrt(second_new / (1.0 - beta_second**STEP)) + 1e-08)
    )
    return (moment_new, second_new, params - adam_rate * (corrected + decay_rate * params))


def encoder_forward(features, context, small_params, second_low):
    first_pre = (
        jnp.einsum("gpc,cd->gpd", features, small_params[0:5], precision=exact_arithmetic_mode)
        + small_params[10]
    )
    first_act, gelu_first = jax.vjp(jax.nn.gelu, first_pre)
    normed, norm_back = jax.vjp(layer_norm, first_act, small_params[11], small_params[12])
    normed_low = normed.astype(jnp.bfloat16)
    second = (
        jnp.einsum("gpd,de->gpe", normed_low, second_low, preferred_element_type=jnp.float32)
        + small_params[13]
    )
    encoded, gelu_second = jax.vjp(jax.nn.gelu, second)
    summed = jnp.einsum("gp,gpe->ge", context, encoded, precision=exact_arithmetic_mode)
    return (
        summed,
        jnp.sum(context, axis=1),
        (first_pre, gelu_first, norm_back, normed_low, gelu_second),
    )


def general(
    pixels,
    lengths,
    ctx_mask,
    head_w,
    head_mom,
    square_w,
    square_mom,
    small_params,
    small_mom,
    small_var,
):
    micro_count = pixels.shape[1]
    groups = pixels.shape[2]
    slot_count = pixels.shape[4]
    model_width = square_w.shape[1]
    live_all = (
        lax.axis_size("dp") * micro_count * (groups * slot_count * lax.axis_size("ctx") * 5 // 8)
    )
    groups_all = lax.axis_size("dp") * micro_count * groups
    slot_ids = lax.axis_index("ctx") * slot_count + jnp.arange(slot_count, dtype=jnp.int32)
    head_low = head_w.astype(jnp.bfloat16)
    head_back = head_low.astype(jnp.float32)
    square_low = square_w.astype(jnp.bfloat16)
    bias_head = square_low[1].astype(jnp.float32)
    final_coefficient_reduced = small_params[7:10].astype(jnp.bfloat16)
    kept = []
    sum_list = []
    count_list = []
    for micro_index in range(micro_count):
        features = jnp.transpose(pixels[0, micro_index], (0, 2, 1))
        live_slot = slot_ids[None, :] < lengths[0, micro_index][:, None]
        context = jnp.where(live_slot & (ctx_mask[0, micro_index] == 1), 1.0, 0.0).astype(
            jnp.float32
        )
        query_mask = jnp.where(live_slot & (ctx_mask[0, micro_index] == 0), 1.0, 0.0).astype(
            jnp.float32
        )
        summed, counts, saved = encoder_forward(features, context, small_params, square_low[0])
        sum_list.append(summed)
        count_list.append(counts)
        kept.append((features, context, query_mask, saved))
    totals = [
        lax.psum((sum_list[index_micro], count_list[index_micro]), "ctx")
        for index_micro in range(micro_count)
    ]
    zeros_small = jnp.zeros((model_width,), jnp.float32)
    grad_first_w = jnp.zeros((5, model_width), jnp.float32)
    grad_coord_w = jnp.zeros((2, model_width), jnp.float32)
    grad_out_w = jnp.zeros((3, model_width), jnp.float32)
    grad_vectors = [zeros_small] * 5
    grad_square = jnp.zeros_like(square_w)
    latent_rows = []
    theta_rows = []
    squared = jnp.zeros((), jnp.float32)
    regular = jnp.zeros((), jnp.float32)
    for micro_index in range(micro_count):
        features, context, query_mask, saved = kept[micro_index]
        first_pre, gelu_first, norm_back, normed_low, gelu_second = saved
        summed, counts = totals[micro_index]
        divisor = counts[:, None] + 1.0
        latent_low = (summed / divisor).astype(jnp.bfloat16)
        latent_back = latent_low.astype(jnp.float32)
        generated = jnp.dot(latent_low, head_low, preferred_element_type=jnp.float32)
        gen_parts = generated.astype(jnp.bfloat16).reshape(groups, -1, model_width)
        gen_full = lax.all_gather(gen_parts, "ctx", axis=1, tiled=True)
        gen_bias = jnp.dot(latent_low, square_low[1], preferred_element_type=jnp.float32)
        coord_pre = (
            jnp.einsum(
                "gpc,cd->gpd",
                features[..., 3:5],
                small_params[5:7],
                precision=exact_arithmetic_mode,
            )
            + small_params[14]
        )
        siren_low = jnp.sin(30.0 * coord_pre).astype(jnp.bfloat16)
        siren_pre = (
            jnp.einsum("gpd,gde->gpe", siren_low, gen_full, preferred_element_type=jnp.float32)
            + gen_bias[:, None, :]
        )
        result_reduced_form = jnp.sin(30.0 * siren_pre).astype(jnp.bfloat16)
        estimated_colour_values = jnp.einsum(
            "kdg,cg->kcd",
            result_reduced_form,
            final_coefficient_reduced,
            preferred_element_type=jnp.float32,
        )
        errors = (
            estimated_colour_values - jnp.transpose(features[..., 0:3], (0, 2, 1))
        ) * query_mask[:, None, :]
        squared = squared + jnp.sum(errors * errors)
        regular = regular + jnp.sum(generated * generated)
        prediction_gradient = (2.0 / live_all * errors).astype(jnp.bfloat16)
        grad_out_w = grad_out_w + jnp.einsum(
            "dan,dnq->aq",
            prediction_gradient,
            result_reduced_form,
            preferred_element_type=jnp.float32,
        )
        grad_out = jnp.einsum(
            "xvw,vt->xwt",
            prediction_gradient,
            final_coefficient_reduced,
            preferred_element_type=jnp.float32,
        )
        grad_inner = (grad_out * 30.0 * jnp.cos(30.0 * siren_pre)).astype(jnp.bfloat16)
        gen_part = jnp.einsum(
            "gpd,gpe->gde", siren_low, grad_inner, preferred_element_type=jnp.float32
        )
        gen_grad = lax.psum_scatter(gen_part, "ctx", scatter_dimension=1, tiled=True).reshape(
            groups, -1
        )
        gen_grad = gen_grad + 2.0 * reg_weight / groups_all * generated
        bias_part = jnp.sum(grad_inner.astype(jnp.float32), axis=1)
        grad_siren = jnp.einsum(
            "gpe,gde->gpd", grad_inner, gen_full, preferred_element_type=jnp.float32
        )
        grad_coord = grad_siren * 30.0 * jnp.cos(30.0 * coord_pre)
        grad_coord_w = grad_coord_w + jnp.einsum(
            "gpc,gpd->cd", features[..., 3:5], grad_coord, precision=exact_arithmetic_mode
        )
        grad_vectors[4] = grad_vectors[4] + jnp.sum(grad_coord, axis=(0, 1))
        latent_rows.append(latent_back)
        theta_rows.append(gen_grad)
        latent_part = jnp.dot(gen_grad, head_back.T, precision=exact_arithmetic_mode)
        latent_part, bias_full = lax.psum((latent_part, bias_part), "ctx")
        grad_square = grad_square.at[1].add(
            jnp.dot(latent_back.T, bias_part, precision=exact_arithmetic_mode)
        )
        grad_latent = latent_part + jnp.dot(bias_full, bias_head.T, precision=exact_arithmetic_mode)
        grad_encoded = context[:, :, None] * (grad_latent / divisor)[:, None, :]
        (grad_second,) = gelu_second(grad_encoded)
        second_low = grad_second.astype(jnp.bfloat16)
        grad_square = grad_square.at[0].add(
            jnp.einsum("gpd,gpe->de", normed_low, second_low, preferred_element_type=jnp.float32)
        )
        grad_vectors[3] = grad_vectors[3] + jnp.sum(second_low.astype(jnp.float32), axis=(0, 1))
        grad_normed = jnp.einsum(
            "gpe,de->gpd", second_low, square_low[0], preferred_element_type=jnp.float32
        )
        grad_act, grad_gain, grad_beta = norm_back(grad_normed)
        (grad_first,) = gelu_first(grad_act)
        grad_first_w = grad_first_w + jnp.einsum(
            "gpc,gpd->cd", features, grad_first, precision=exact_arithmetic_mode
        )
        grad_vectors[0] = grad_vectors[0] + jnp.sum(grad_first, axis=(0, 1))
        grad_vectors[1] = grad_vectors[1] + grad_gain
        grad_vectors[2] = grad_vectors[2] + grad_beta
    grad_small = jnp.concatenate(
        [
            grad_first_w,
            grad_coord_w,
            grad_out_w,
            jnp.stack(
                [
                    grad_vectors[0],
                    grad_vectors[1],
                    grad_vectors[2],
                    grad_vectors[3],
                    grad_vectors[4],
                ]
            ),
        ],
        axis=0,
    )
    grad_small, grad_square, stat_sums = lax.psum(
        (grad_small, grad_square, jnp.stack([squared, regular])), ("dp", "ctx")
    )
    latent_stack = jnp.concatenate(latent_rows, axis=0)
    theta_stack = jnp.concatenate(theta_rows, axis=0)
    grad_head = lax.psum(
        jnp.dot(latent_stack.T, theta_stack, precision=exact_arithmetic_mode), "dp"
    )
    loss_value = stat_sums[0] / live_all + reg_weight * stat_sums[1] / groups_all
    head_moment = momentum_rate * head_mom + grad_head
    head_dir = head_orthogonal(head_moment)
    head_new = head_w - head_rate * (0.2 * model_width * head_dir + decay_rate * head_w)
    square_moment = momentum_rate * square_mom + grad_square
    rates = jnp.array(square_rates, jnp.float32)[:, None, None]
    square_new = square_w - rates * (
        0.2 * model_width**0.5 * orthogonal_local(square_moment) + decay_rate * square_w
    )
    small_moment, small_second, small_new = adam_update(
        small_params, grad_small, small_mom, small_var
    )
    return (
        head_moment,
        head_new,
        head_new.astype(jnp.bfloat16),
        square_moment,
        square_new,
        square_new.astype(jnp.bfloat16),
        small_moment,
        small_second,
        small_new,
        small_new.astype(jnp.bfloat16),
        loss_value,
    )


MESH = pl.DeviceIdType.MESH
F32 = jnp.float32
BF16 = jnp.bfloat16
WIDTH = 256
TILE = 256
MIB = 1024 * 1024
SPAN = 512
QUARTER = 64
HEAD_SHARP = 3
TURN = 30.0 / 6.283185307179586
GELU_ONE = 0.7978845608028654
GELU_CUBE = GELU_ONE * 0.044715
GELU_SCALE = GELU_CUBE ** (1.0 / 3.0)
GELU_SLOPE = GELU_ONE / GELU_SCALE
NORM_EPS = 1e-05 * (2.0 * GELU_SCALE) ** 2
SIN_TERMS = (4.442860272, -7.307432505, 3.594782484, -0.784372885)


def any_spec():
    return pl.BlockSpec(memory_space=pl.ANY)


def hbm_spec():
    return pl.BlockSpec(memory_space=pltpu.HBM)


def busy(micros):
    return pl.CostEstimate(flops=micros * 10**9, bytes_accessed=micros * 10**5, transcendentals=0)


def vmem_spec():
    return pl.BlockSpec(memory_space=pltpu.VMEM)


def smem_spec():
    return pl.BlockSpec(memory_space=pltpu.SMEM)


def turned(matrix):
    pad = jnp.zeros((matrix.shape[0], 128 - matrix.shape[1]), F32)
    return jnp.concatenate([matrix, pad], axis=1).T


def weave(order, first, second):
    for letter in order:
        next(first if letter == "A" else second, None)
    for rest in (first, second):
        for unused in rest:
            pass


def dot_nn(a, b):
    return lax.dot_general(a, b, (((1,), (0,)), ((), ())), preferred_element_type=F32)


def dot_nt(a, b):
    return lax.dot_general(a, b, (((1,), (1,)), ((), ())), preferred_element_type=F32)


def full_nn(a, b):
    return lax.dot_general(
        a, b, (((1,), (0,)), ((), ())), precision=lax.Precision.HIGHEST, preferred_element_type=F32
    )


def full_nt(a, b):
    return lax.dot_general(
        a, b, (((1,), (1,)), ((), ())), precision=lax.Precision.HIGHEST, preferred_element_type=F32
    )


def split3(v):
    high = v.astype(BF16).astype(F32)
    rest = v - high
    mid = rest.astype(BF16).astype(F32)
    return high, mid, rest - mid


def greet(peers):
    barrier = pltpu.get_barrier_semaphore()
    for peer in peers:
        pl.semaphore_signal(barrier, inc=1, device_id=peer, device_id_type=MESH)
    pl.semaphore_wait(barrier, len(peers))


def ring_peers(axis, n):
    me = lax.axis_index(axis)
    return [lax.rem(me + d, n) for d in range(1, n)]


def plan_all(axis, n, source, target, send_sem, recv_sem):
    return [
        pltpu.make_async_remote_copy(
            src_ref=source(peer),
            dst_ref=target,
            send_sem=send_sem.at[d],
            recv_sem=recv_sem.at[d],
            device_id={axis: peer},
            device_id_type=MESH,
        )
        for d, peer in enumerate(ring_peers(axis, n))
    ]


def send_all(*plan):
    copies = plan_all(*plan)
    for copy in copies:
        copy.start()
    return copies


def fenced(copies, before=None):
    @pl.when(lax.axis_index("ctx") >= 0)
    def run():
        if before is not None:
            before()
        for copy in copies:
            copy.start()

    return copies


def column(row, width):
    return jnp.broadcast_to(row, (width, row.shape[1])).T


def gelu_twice(y):
    return y + y * jnp.tanh(y * (GELU_SLOPE + y * y))


def gelu_both(y):
    square = y * y
    above = 1.0 + jnp.tanh(y * (GELU_SLOPE + square))
    value = y * above
    return value, above + (value * (2.0 - above)) * (3.0 * square + GELU_SLOPE)


def plain_twice(x):
    return x + x * jnp.tanh(x * (GELU_ONE + GELU_CUBE * (x * x)))


def plain_slope(x):
    square = GELU_CUBE * (x * x)
    above = 1.0 + jnp.tanh(x * (GELU_ONE + square))
    return above + (x * above) * (2.0 - above) * (3.0 * square + GELU_ONE)


def sine_pair(turns):
    frac = turns - jnp.round(turns)
    square = frac * frac
    s = SIN_TERMS[3] * square + SIN_TERMS[2]
    s = s * square + SIN_TERMS[1]
    s = (s * square + SIN_TERMS[0]) * frac
    cosine = 1.0 - s * s
    rest = 1.0 + cosine
    return s * (rest * lax.rsqrt(rest)), cosine


def triple_weights(block):
    high, mid, low = split3(block)
    rows = jnp.concatenate([high, mid, high, low, mid, high], axis=0)
    pad = jnp.zeros((128 - rows.shape[0], rows.shape[1]), F32)
    return jnp.concatenate([rows, pad], axis=0).T.astype(BF16)


def triple_from_list(rows):
    high, mid, low = split3(rows)
    pad = jnp.zeros((80, rows.shape[1]), F32)
    return jnp.concatenate([high, high, mid, high, mid, low, pad], axis=0).astype(BF16)


def three(matrix):
    high = matrix.astype(BF16)
    rest = matrix - high.astype(F32)
    mid = rest.astype(BF16)
    return high, mid, (rest - mid.astype(F32)).astype(BF16)


def six(left, right):
    rows = left[0].shape[0]
    first = dot_nn(jnp.concatenate(left, axis=0), right[0])
    second = dot_nn(jnp.concatenate(left[0:2], axis=0), right[1])
    third = dot_nn(left[0], right[2])
    return (first[0:rows] + second[0:rows] + third) + (
        first[rows : 2 * rows] + second[rows:] + first[2 * rows :]
    )


def few(left, right):
    rows = left[0].shape[0]
    first = dot_nn(jnp.concatenate(left[0:2], axis=0), right[0])
    return (first[0:rows] + dot_nn(left[0], right[1])) + first[rows:]


def gram_six(parts):
    high, mid, low = parts
    both = jnp.concatenate([high, mid], axis=1)
    cross = dot_nt(jnp.concatenate([high, high], axis=1), jnp.concatenate([mid, low], axis=1))
    return dot_nt(both, both) + (cross + cross.T)


def order_rows(row, per):
    return jnp.concatenate([row[:, k * TILE : (k + 1) * TILE] for k in range(per)], axis=0)


def count_tiles(rx_ref, cnt_v, code):
    sources, unused, slots = rx_ref.shape
    per = slots // TILE
    ones = jnp.ones((16, TILE), BF16)
    for s in range(sources):
        codes = order_rows(rx_ref[s, 5:6, :], per)
        parts = [jnp.where(codes == code, 1.0, 0.0), jnp.where(codes == 1.0, 1.0, 0.0)]
        pad = jnp.zeros((128 - 2 * per, TILE), F32)
        cnt_v[s : s + 1, :] = dot_nt(ones, jnp.concatenate(parts + [pad], axis=0).astype(BF16))[0:1].astype(jnp.int32)


def put(target, rows, extra, offset, start, amount):
    lane_ids = lax.broadcasted_iota(jnp.int32, (8, TILE), 1)
    shift = lax.rem(offset, TILE)
    base = pl.multiple_of(offset - shift, TILE)
    marks = [jnp.full((1, TILE), value, F32) for value in (1.0, extra)]
    moved = pltpu.roll(jnp.concatenate([rows] + marks, axis=0), lax.rem(shift - start + TILE, TILE), 1)
    here = (lane_ids >= shift) & (lane_ids < shift + amount)
    there = lane_ids < shift + amount - TILE
    target[:, pl.ds(base, TILE)] += jnp.where(here, moved, 0.0)
    target[:, pl.ds(pl.multiple_of(base + TILE, TILE), TILE)] = jnp.where(there, moved, 0.0)


def clear_tail(target, amount):
    start = pl.multiple_of((amount // TILE + 1) * TILE, TILE)
    for step in range(4 * SPAN // TILE):
        target[:, pl.ds(start + step * TILE, TILE)] = jnp.zeros((8, TILE), F32)


def weight_block(weights, bias, place):
    rows = weights.shape[0]
    parts = []
    if place > 0:
        parts.append(jnp.zeros((place, WIDTH), F32))
    parts.append(weights)
    if place + rows < 6:
        parts.append(jnp.zeros((6 - place - rows, WIDTH), F32))
    parts.append(bias)
    parts.append(jnp.zeros((1, WIDTH), F32))
    return jnp.concatenate(parts, axis=0)


def scatter_kernel(
    n, rows_n, len_hbm, pix_hbm, mask_hbm, mom_ref, rx_ref, tiles_ref, gram_ref,
    len_ref, pix_ref, mask_ref, stage, buf, own, slab_rx, upper, send_sem, recv_sem, load_sem, slab_sem, own_sem,
):
    brought = [
        pltpu.make_async_copy(source, target, own_sem.at[j])
        for j, (source, target) in enumerate(((len_hbm, len_ref), (pix_hbm, pix_ref), (mask_hbm, mask_ref)))
    ]
    for copy in brought:
        copy.start()
    me = lax.axis_index("ctx")
    peers = ring_peers("ctx", n)
    r = lax.axis_index("dp")
    span = buf.shape[1]
    load = pltpu.make_async_copy(mom_ref.at[:, pl.ds(pl.multiple_of(r * span, span), span)], buf, load_sem)
    load.start()
    slots = pix_ref.shape[4]
    per = slots // TILE
    groups = mask_ref.shape[2]
    row_ids = lax.broadcasted_iota(jnp.int32, (TILE, TILE), 0)
    upper[...] = jnp.where(row_ids <= lax.broadcasted_iota(jnp.int32, (TILE, TILE), 1), 1.0, 0.0).astype(BF16)
    row_ids = row_ids.astype(F32)
    lane_ids = lax.broadcasted_iota(jnp.int32, (TILE, TILE), 1).astype(F32)
    place = (
        lax.broadcasted_iota(jnp.int32, (per, TILE), 0) * TILE
        + lax.broadcasted_iota(jnp.int32, (per, TILE), 1)
        + me * slots
    )
    pad = jnp.zeros((2, TILE), F32)

    def arrange(b):
        for j in range(groups):
            g = b * groups + j
            mask = order_rows(mask_ref[0, b, j : j + 1, :], per)
            live = place < len_ref[0, b, j]
            context = jnp.where(live & (mask == 1), 1.0, 0.0)
            query = jnp.where(live & (mask == 0), 1.0, 0.0)
            both = jnp.concatenate([context, query], axis=0).astype(BF16)
            order = dot_nn(both, upper[...])
            before_c, before_q = order[0:per], order[per : 2 * per]
            live_c = before_c[:, TILE - 1 : TILE]
            target = jnp.where(
                context > 0.5, before_c, jnp.where(query > 0.5, live_c + before_q, 0.0)
            ) - 1.0
            code = context + 2.0 * query
            for t in range(per):
                rows = jnp.concatenate(
                    [pix_ref[0, b, c, j : j + 1, t * TILE : (t + 1) * TILE] for c in range(5)]
                    + [code[t : t + 1], pad], axis=0
                )
                high, mid, low = split3(rows)
                stack = jnp.concatenate([high, mid, low, jnp.zeros((8, TILE), F32)], axis=0).astype(BF16)
                if t % 2 == 0:
                    chosen = jnp.where(row_ids == target[t : t + 1], 1.0, 0.0).astype(BF16)
                    found = dot_nt(stack, chosen)
                else:
                    spot = column(target[t : t + 1], 128)
                    chosen = jnp.where(lane_ids == jnp.concatenate([spot, spot], axis=1), 1.0, 0.0).astype(BF16)
                    found = dot_nn(stack, chosen)
                found = found[0:8] + found[8:16] + found[16:24]
                tiles_ref[g, :, t * TILE : (t + 1) * TILE] = found
                stage[(g + t) % n, :, g * TILE : (g + 1) * TILE] = found

    copies = []
    for copy in brought:
        copy.wait()
    for b in range(mask_ref.shape[1]):
        arrange(b)
        if b == 0:
            greet([{"ctx": peer} for peer in peers] + [{"dp": peer} for peer in ring_peers("dp", rows_n)])
        lanes = pl.ds(b * groups * TILE, groups * TILE)
        copies += fenced(
            plan_all(
                "ctx",
                n,
                lambda peer: stage.at[peer, pl.ds(0, 6), lanes],
                rx_ref.at[me, pl.ds(0, 6), lanes],
                send_sem.at[b],
                recv_sem.at[b],
            )
        )
    rx_ref[me, 0:6, :] = stage[me, 0:6, :]
    quarter = gram_ref.shape[0]
    same = jnp.zeros((WIDTH, WIDTH), F32)
    cross = jnp.zeros((WIDTH, WIDTH), F32)
    load.wait()
    for i in range(buf.shape[1] // WIDTH):
        high, mid, low = three(buf[:, i * WIDTH : (i + 1) * WIDTH])
        both = jnp.concatenate([high, mid], axis=1)
        same = same + dot_nt(both, both)
        cross = cross + dot_nt(jnp.concatenate([high, high], axis=1), jnp.concatenate([mid, low], axis=1))
    own[...] = same + (cross + cross.T)
    slabs = fenced(
        plan_all(
            "dp",
            rows_n,
            lambda peer: own.at[pl.ds(pl.multiple_of(peer * quarter, quarter), quarter), :],
            slab_rx.at[r],
            slab_sem.at[0],
            slab_sem.at[1],
        )
    )
    slab_rx[r] = own[pl.ds(pl.multiple_of(r * quarter, quarter), quarter), :]
    for copy in slabs:
        copy.wait()
    total = slab_rx[0]
    for s in range(1, rows_n):
        total = total + slab_rx[s]
    gram_ref[...] = total
    for copy in copies:
        copy.wait()


def encoder_kernel(
    rx_ref, small_ref, square_ref, z_ref, clist, count_ref, cnt_v, cnt_s, wide, second, zacc, low_a, low_b, sem
):
    sources = rx_ref.shape[0]
    per = rx_ref.shape[2] // TILE
    count_tiles(rx_ref, cnt_v, 2.0)
    counts = pltpu.make_async_copy(cnt_v, cnt_s, sem)
    counts.start()
    small = small_ref[...]
    first = triple_weights(weight_block(small[0:5] * GELU_SCALE, small[10:11] * GELU_SCALE, 0))
    wide[0] = column(small[11:12], SPAN)
    wide[1] = column(small[12:13], SPAN)
    wide[2] = column(small[13:14], SPAN)
    second[...] = square_ref[0].T.astype(BF16)
    zacc[...] = jnp.zeros_like(zacc)
    clist[:, 0:TILE] = jnp.zeros((8, TILE), F32)
    counts.wait()

    def place_tile(s, offset):
        for k in range(per):
            amount = cnt_s[s, per + k]
            put(clist, rx_ref[s, 0:6, k * TILE : (k + 1) * TILE], k + 1.0, offset, 0, amount)
            offset = offset + amount
        return offset

    num_c = lax.fori_loop(0, sources, place_tile, jnp.int32(0))
    clear_tail(clist, num_c)
    count_ref[0] = num_c
    ids = lax.broadcasted_iota(jnp.int32, (16, SPAN), 0).astype(F32) + 1.0

    def window(t):
        return clist[:, pl.ds(pl.multiple_of(t * SPAN, SPAN), SPAN)]

    def begin(t, low):
        pre = dot_nn(first, triple_from_list(window(t)))
        parts = []
        total = jnp.zeros((1, SPAN), F32)
        for c in range(0, WIDTH, QUARTER):
            parts.append(gelu_twice(pre[c : c + QUARTER]))
            total = total + jnp.sum(parts[-1], axis=0, keepdims=True)
            yield
        mean = total * (1.0 / WIDTH)
        total = jnp.zeros((1, SPAN), F32)
        for c in range(len(parts)):
            parts[c] = parts[c] - mean
            total = total + jnp.sum(parts[c] * parts[c], axis=0, keepdims=True)
        inverse = lax.rsqrt(total * (1.0 / WIDTH) + NORM_EPS)
        yield
        for c in range(len(parts)):
            rows = slice(c * QUARTER, (c + 1) * QUARTER)
            low[rows, :] = (parts[c] * inverse * wide[0, rows, :] + wide[1, rows, :]).astype(BF16)
        yield

    def finish(t, low):
        pre = dot_nn(second[...], low[...])
        yield
        highs, rests = [], []
        for c in range(0, WIDTH, QUARTER):
            encoded = plain_twice(pre[c : c + QUARTER] + wide[2, c : c + QUARTER, :])
            highs.append(encoded.astype(BF16))
            rests.append((encoded - highs[-1].astype(F32)).astype(BF16))
            yield
        owner = jnp.where(ids == window(t)[7:8], 1.0, 0.0).astype(BF16)
        right = jnp.concatenate([jnp.concatenate(highs, axis=0), jnp.concatenate(rests, axis=0)], axis=1)
        zacc[...] += dot_nt(right, jnp.concatenate([owner, owner], axis=1))
        yield

    def pair(p, carry):
        weave("BAABABBABABA", begin(2 * p + 1, low_b), finish(2 * p, low_a))
        weave("BAABABBABABA", begin(2 * p + 2, low_a), finish(2 * p + 1, low_b))
        return carry

    spans = (num_c + SPAN - 1) // SPAN
    weave("", begin(0, low_a), iter(()))
    lax.fori_loop(0, spans // 2, pair, 0)

    @pl.when(lax.rem(spans, 2) == 1)
    def last():
        weave("", iter(()), finish(spans - 1, low_a))

    z_ref[:, 0:WIDTH] = turned(zacc[...])[0:8] * 0.5
    amounts = jnp.sum(cnt_v[0:sources, :].astype(F32), axis=0, keepdims=True)
    z_ref[:, WIDTH : WIDTH + 128] = jnp.broadcast_to(amounts, (8, 128))


def theta_kernel(
    n, z_ref, head_ref, tiles_ref, gram_ref, theta_ref, gen_ref, z8_ref, inv_ref, reg_ref, rx_ref, rows_ref,
    zall, head, give, turn, gram_rx, load_sem, sems,
):
    me = lax.axis_index("ctx")
    peers = ring_peers("ctx", n)
    chunk = head.shape[2]
    per = chunk // WIDTH

    def load(k):
        return pltpu.make_async_copy(head_ref.at[:, pl.ds(k * chunk, chunk)], head.at[k], load_sem.at[k])

    for k in range(head.shape[0]):
        load(k).start()
    greet([{"ctx": peer} for peer in peers])
    latents = send_all("ctx", n, lambda peer: z_ref, zall.at[me], sems.at[0], sems.at[1])
    pixels = send_all(
        "ctx",
        n,
        lambda peer: tiles_ref.at[peer, pl.ds(0, 6), :],
        rx_ref.at[me, pl.ds(0, 6), :],
        sems.at[2],
        sems.at[3],
    )
    slab = gram_ref.shape[0] // n
    grams = send_all(
        "ctx",
        n,
        lambda peer: gram_ref.at[pl.ds(pl.multiple_of(peer * slab, slab), slab), :],
        gram_rx.at[me],
        sems.at[6],
        sems.at[7],
    )
    zall[me] = z_ref[...]
    rx_ref[me, 0:6, :] = tiles_ref[me, 0:6, :]
    gram_rx[me] = gram_ref[pl.ds(pl.multiple_of(me * slab, slab), slab), :]
    for copy in latents:
        copy.wait()
    total = zall[0]
    for s in range(1, n):
        total = total + zall[s]
    lanes = lax.broadcasted_iota(jnp.int32, (8, 128), 1)
    rows = lax.broadcasted_iota(jnp.int32, (8, 128), 0)
    amounts = total[:, WIDTH : WIDTH + 128]
    counts = jnp.sum(jnp.where(lanes == rows + 8, amounts, 0.0), axis=1, keepdims=True) + 1.0
    latent = (total[:, 0:WIDTH] / counts).astype(BF16).astype(F32)
    z8_ref[...] = latent
    inv_ref[...] = jnp.broadcast_to(0.5 / counts, (8, WIDTH))
    left = jnp.concatenate([latent, jnp.zeros((8, WIDTH), F32)], axis=0).astype(BF16)
    regular = jnp.zeros((8, WIDTH), F32)
    for k in range(head.shape[0]):
        load(k).wait()
        part = dot_nn(left, head[k].astype(BF16))[0:8]
        for i in range(per):
            piece = part[:, i * WIDTH : (i + 1) * WIDTH]
            theta_ref[pl.ds((k * per + i) * 8, 8), :] = piece
            for half in range(2):
                turn[half, pl.ds((k * per + i) * 8, 8), :] = piece[:, half * 128 : half * 128 + 128]
            regular = regular + piece * piece
    reg_ref[...] = regular
    height = WIDTH // n
    for g in range(n):
        for half in range(2):
            give[g, :, half * 128 : half * 128 + 128] = turn[half, pl.ds(g, height, stride=8), :].astype(BF16)
    mine = pl.ds(pl.multiple_of(me * height, height), height)
    parts = fenced(
        plan_all("ctx", n, lambda peer: give.at[peer], gen_ref.at[mine, :], sems.at[4], sems.at[5])
    )
    gen_ref[mine, :] = give[me]
    for copy in grams:
        copy.wait()
    total = gram_rx[0]
    for s in range(1, n):
        total = total + gram_rx[s]
    rows_ref[...] = total
    for copy in pixels + parts:
        copy.wait()


def siren_kernel(
    live_all, len_ref, rx_ref, gen_ref, z_ref, small_ref, square_ref, out_ref, bias_ref, narrow_ref,
    q_ref, cnt_v, cnt_s, inner, shift, sa, sb, ca, cb, ma, mb, na, nb, acc_g, acc_c, acc_o, acc_e, sem,
):
    sin_in, cos_in, sin_mid, cos_mid = (sa, sb), (ca, cb), (ma, mb), (na, nb)
    me = lax.axis_index("ctx")
    per = rx_ref.shape[2] // TILE
    groups = len_ref.shape[2]
    length = len_ref[0, me // groups, lax.rem(me, groups)]
    count_tiles(rx_ref, cnt_v, 2.0)
    counts = pltpu.make_async_copy(cnt_v, cnt_s, sem)
    counts.start()
    small = small_ref[...]
    coord = triple_weights(weight_block(small[5:7] * TURN, small[14:15] * TURN, 3))
    latent = jnp.broadcast_to(z_ref[pl.ds(me, 1), :], (16, WIDTH)).astype(BF16)
    bias = dot_nn(latent, square_ref[1].astype(BF16))[0:1]
    inner[...] = gen_ref[...].astype(F32).T.astype(BF16)
    shift[...] = column(bias * TURN, SPAN)
    final = small[7:10].astype(BF16).astype(F32)
    final_rows = jnp.concatenate([final, jnp.zeros((13, WIDTH), F32)], axis=0).astype(BF16)
    large = final * 30.0
    high = large.astype(BF16).astype(F32)
    gap = jnp.zeros((5, WIDTH), F32)
    final_cols = jnp.concatenate([high, gap, large - high, jnp.zeros((117, WIDTH), F32)], axis=0).T.astype(BF16)
    for ref in (acc_g, acc_c, acc_o, acc_e):
        ref[...] = jnp.zeros_like(ref)
    scale = 2.0 / live_all
    ones = jnp.ones((16, SPAN), BF16)
    q_ref[:, 0:TILE] = jnp.zeros((8, TILE), F32)
    counts.wait()

    def place_tile(s, offset):
        for k in range(per):
            amount = cnt_s[s, k]
            put(q_ref, rx_ref[s, 0:6, k * TILE : (k + 1) * TILE], 0.0, offset, cnt_s[s, per + k], amount)
            offset = offset + amount
        return offset

    num_q = lax.fori_loop(0, (length + per * TILE - 1) // (per * TILE), place_tile, jnp.int32(0))
    clear_tail(q_ref, num_q)
    ids = lax.broadcasted_iota(jnp.int32, (8, SPAN), 0)

    def window(t):
        return q_ref[:, pl.ds(pl.multiple_of(t * SPAN, SPAN), SPAN)]

    def ahead(t, k):
        turns = dot_nn(coord, triple_from_list(window(t)))
        for c in range(0, WIDTH, QUARTER):
            s_in, c_in = sine_pair(turns[c : c + QUARTER])
            sin_in[k][c : c + QUARTER, :] = s_in.astype(BF16)
            cos_in[k][c : c + QUARTER, :] = c_in
            yield
        turns = dot_nn(inner[...], sin_in[k][...])
        yield
        for c in range(0, WIDTH, QUARTER):
            s_mid, c_mid = sine_pair(turns[c : c + QUARTER] * TURN + shift[c : c + QUARTER, :])
            sin_mid[k][c : c + QUARTER, :] = s_mid.astype(BF16)
            cos_mid[k][c : c + QUARTER, :] = c_mid
            yield

    def back_part(t, k):
        rows = window(t)
        pred = dot_nn(final_rows, sin_mid[k][...])[0:8]
        error = jnp.where(ids < 3, (pred - rows) * rows[6:7], 0.0)
        acc_e[...] += error * error
        slope = (error * scale).astype(BF16).astype(F32)
        slope = jnp.concatenate([slope, slope], axis=0).astype(BF16)
        yield
        acc_o[...] += dot_nt(sin_mid[k][...], slope)
        slope_cols = jnp.concatenate([slope, jnp.zeros((112, SPAN), BF16)], axis=0)
        back = (cos_mid[k][...] * dot_nn(final_cols, slope_cols)).astype(BF16)
        yield
        acc_g[...] += dot_nt(jnp.concatenate([sin_in[k][...], ones], axis=0), back)
        yield
        grads = dot_nn(gen_ref[...], back)
        yield
        outer = cos_in[k][...] * grads
        high = outer.astype(BF16)
        low = (outer - high.astype(F32)).astype(BF16)
        yield
        left = jnp.concatenate(split3(rows) + (jnp.zeros((8, SPAN), F32),), axis=0).astype(BF16)
        acc_c[...] += dot_nt(jnp.concatenate([high, low], axis=1), jnp.concatenate([left, left], axis=1))
        yield

    def pair(p, carry):
        weave("BABABABAABABAA", ahead(2 * p + 1, 1), back_part(2 * p, 0))
        weave("BABABABAABABAA", ahead(2 * p + 2, 0), back_part(2 * p + 1, 1))
        return carry

    spans = (num_q + SPAN - 1) // SPAN
    weave("", ahead(0, 0), iter(()))
    lax.fori_loop(0, spans // 2, pair, 0)

    @pl.when(lax.rem(spans, 2) == 1)
    def last():
        weave("", iter(()), back_part(spans - 1, 0))

    out_ref[...] = acc_g[0:WIDTH, :]
    bias_ref[...] = acc_g[WIDTH : WIDTH + 8, :]
    coords = turned(acc_c[...])
    coords = (coords[0:8] + coords[8:16] + coords[16:24]) * 30.0
    narrow_ref[0:2, :] = coords[3:5]
    narrow_ref[2:5, :] = turned(acc_o[...])[0:3]
    narrow_ref[5:6, :] = coords[6:7]
    narrow_ref[6:7, :] = jnp.broadcast_to(jnp.sum(acc_e[...]), (1, WIDTH))
    narrow_ref[7:8, :] = jnp.zeros((1, WIDTH), F32)


def latent_kernel(
    n, rows_n, groups_all, part_ref, bias_ref, theta_ref, head_ref, mom_ref, z8_ref, rows_ref,
    dz_ref, tall_ref, cross_ref, gram_ref,
    rx, rxb, turn, head, mom, low_head, low_mom, rxz, dz_own, lefts, mixed, rxs, load_sem, mom_sem, sems, dsems,
):
    me = lax.axis_index("ctx")
    r = lax.axis_index("dp")
    peers = ring_peers("ctx", n)
    rows_peers = ring_peers("dp", rows_n)
    chunk = head.shape[2]
    per = chunk // WIDTH
    height = WIDTH // n

    def load(k):
        return pltpu.make_async_copy(head_ref.at[:, pl.ds(k * chunk, chunk)], head.at[k], load_sem.at[k])

    def load_mom(k):
        return pltpu.make_async_copy(mom_ref.at[:, pl.ds(k * chunk, chunk)], mom.at[k], mom_sem.at[k])

    for k in range(head.shape[0]):
        load(k).start()
    for k in range(head.shape[0]):
        load_mom(k).start()
    greet([{"ctx": peer} for peer in peers] + [{"dp": peer} for peer in rows_peers])
    mine = pl.ds(pl.multiple_of(me * height, 8), height)
    parts = send_all(
        "ctx",
        n,
        lambda peer: part_ref.at[pl.ds(pl.multiple_of(peer * height, 8), height), :],
        rx.at[mine, :],
        sems.at[0],
        sems.at[1],
    )
    biases = send_all(
        "ctx", n, lambda peer: bias_ref.at[pl.ds(0, 1), :], rxb.at[me, pl.ds(0, 1), :], sems.at[6], sems.at[7]
    )
    grams = send_all("ctx", n, lambda peer: rows_ref, rxs.at[me], sems.at[4], sems.at[5])
    rx[mine, :] = part_ref[mine, :]
    rxb[me, 0:1, :] = bias_ref[0:1, :]
    rxs[me] = rows_ref[...]
    for k in range(head.shape[0]):
        load(k).wait()
        for i in range(per):
            low_head[k * per + i] = head[k, :, i * WIDTH : (i + 1) * WIDTH].astype(BF16)
    for copy in grams:
        copy.wait()
    gram_ref[r] = rxs[...]
    slabs = send_all("dp", rows_n, lambda peer: gram_ref.at[r], gram_ref.at[r], dsems.at[0], dsems.at[1])
    for k in range(head.shape[0]):
        load_mom(k).wait()
        for i in range(per):
            for j, part in enumerate(three(mom[k, :, i * WIDTH : (i + 1) * WIDTH])):
                low_mom[k * per + i, pl.ds(j * WIDTH, WIDTH), :] = part
    for copy in biases + parts:
        copy.wait()
    turn[0] = rx[:, 0:128]
    turn[1] = rx[:, 128:256]

    def across(i):
        return jnp.concatenate([turn[half, pl.ds(i, 8, stride=height), :] for half in range(2)], axis=1)

    blank = jnp.zeros((8, WIDTH), F32)
    for i in range(height):
        rows = across(i) + theta_ref[pl.ds(i * 8, 8), :] * (1.0 / groups_all)
        tall_ref[i] = rows
        lefts[i] = jnp.concatenate(split3(rows) + (blank,), axis=0).astype(BF16)
    tall_ref[height] = z8_ref[...]
    tall_ref[height + 1] = jnp.concatenate([rxb[s, 0:1, :] for s in range(n)], axis=0)
    totals = [jnp.zeros((32, WIDTH), F32)] * 2
    for i in range(height):
        totals[i % 2] = totals[i % 2] + dot_nt(lefts[i], low_head[i])
    total = totals[0] + totals[1]
    dz_own[...] = total[0:8] + total[8:16] + total[16:24]
    terms = fenced(plan_all("ctx", n, lambda peer: dz_own, rxz.at[me], sems.at[2], sems.at[3]))
    rxz[me] = dz_own[...]
    mixed[...] = jnp.zeros_like(mixed)

    def mix(i, carry):
        for k in range(4):
            mixed[k % 2] += dot_nt(low_mom[4 * i + k], lefts[4 * i + k])
        return carry

    lax.fori_loop(0, height // 4, mix, 0)
    total = mixed[0] + mixed[1]
    total = turned(total[0:WIDTH] + total[WIDTH : 2 * WIDTH] + total[2 * WIDTH :])
    cross_ref[...] = total[0:8] + total[8:16] + total[16:24]
    for copy in terms:
        copy.wait()
    total = rxz[0]
    for s in range(1, n):
        total = total + rxz[s]
    dz_ref[...] = total
    for copy in slabs:
        copy.wait()


def encoder_back_kernel(
    count_ref, c_ref, small_ref, square_ref, dz_ref, inv_ref, tall_ref, narrow_ref, reg_ref, out_ref, thin_ref,
    wide, second, spread, ua, ub, ka, kb, na, nb, ga, gb, acc_s, acc_f, acc_g, rows_out,
):
    unit, chain, normed, grad = (ua, ub), (ka, kb), (na, nb), (ga, gb)
    num_c = count_ref[0]
    small = small_ref[...]
    first = triple_weights(weight_block(small[0:5] * GELU_SCALE, small[10:11] * GELU_SCALE, 0))
    plain = square_ref[0].astype(BF16)
    low = plain.astype(F32)
    second[...] = low.T.astype(BF16)
    height = tall_ref.shape[0] - 2
    bias_back = full_nt(tall_ref[height + 1], square_ref[1].astype(BF16).astype(F32))
    latent_back = (dz_ref[...] + bias_back) * inv_ref[...]
    wide[0] = column(small[11:12], SPAN)
    wide[1] = column(small[12:13], SPAN)
    latent_cols = jnp.concatenate(split3(latent_back) + (jnp.zeros((104, WIDTH), F32),), axis=0).T.astype(BF16)
    wide[2] = column(small[13:14], SPAN)
    centre = split3(full_nn(jnp.broadcast_to(small[11:12], (8, WIDTH)), low) * (1.0 / WIDTH))
    rows = jnp.concatenate([part[0:1] for part in centre] + [jnp.zeros((13, WIDTH), F32)], axis=0)
    spread[...] = jnp.concatenate([plain, rows.astype(BF16)], axis=0)
    for ref in (acc_s, acc_f, acc_g):
        ref[...] = jnp.zeros_like(ref)
    ones = jnp.ones((16, SPAN), BF16)
    ids = lax.broadcasted_iota(jnp.int32, (8, SPAN), 0).astype(F32) + 1.0
    blank = jnp.zeros((104, SPAN), F32)

    def window(t):
        return c_ref[:, pl.ds(pl.multiple_of(t * SPAN, SPAN), SPAN)]

    def ahead(t, k):
        pre = dot_nn(first, triple_from_list(window(t)))
        parts, slopes = [], []
        total = jnp.zeros((1, SPAN), F32)
        for c in range(0, WIDTH, QUARTER):
            value, slope = gelu_both(pre[c : c + QUARTER])
            parts.append(value)
            slopes.append(slope)
            total = total + jnp.sum(value, axis=0, keepdims=True)
            yield
        mean = total * (1.0 / WIDTH)
        total = jnp.zeros((1, SPAN), F32)
        for c in range(len(parts)):
            parts[c] = parts[c] - mean
            total = total + jnp.sum(parts[c] * parts[c], axis=0, keepdims=True)
        inverse = lax.rsqrt(total * (1.0 / WIDTH) + NORM_EPS)
        yield
        scale = inverse * GELU_SCALE
        for c in range(len(parts)):
            rows = slice(c * QUARTER, (c + 1) * QUARTER)
            value = parts[c] * inverse
            unit[k][rows, :] = value
            normed[k][rows, :] = (value * wide[0, rows, :] + wide[1, rows, :]).astype(BF16)
            chain[k][rows, :] = slopes[c] * scale
        yield
        owner = jnp.where(ids == window(t)[7:8], 1.0, 0.0)
        owner = jnp.concatenate([owner, owner, owner, blank], axis=0).astype(BF16)
        pre = dot_nn(second[...], normed[k][...])
        outer = dot_nn(latent_cols, owner)
        yield
        for c in range(0, WIDTH, QUARTER):
            rows = slice(c, c + QUARTER)
            grad[k][rows, :] = (plain_slope(pre[rows] + wide[2, rows, :]) * outer[rows]).astype(BF16)
            yield

    def back_part(t, k):
        slopes = dot_nn(spread[...], grad[k][...])
        yield
        acc_s[...] += dot_nt(jnp.concatenate([normed[k][...], ones], axis=0), grad[k][...])
        yield
        means = jnp.sum(slopes[WIDTH : WIDTH + 8], axis=0, keepdims=True)
        total = jnp.zeros((1, SPAN), F32)
        parts = []
        for c in range(0, WIDTH, QUARTER):
            rows = slice(c, c + QUARTER)
            parts.append(slopes[rows] * wide[0, rows, :] - means)
            acc_g[rows, :] += slopes[rows] * unit[k][rows, :]
            total = total + jnp.sum(parts[-1] * unit[k][rows, :], axis=0, keepdims=True)
        mean = total * (1.0 / WIDTH)
        yield
        highs, rests = [], []
        for c in range(len(parts)):
            rows = slice(c * QUARTER, (c + 1) * QUARTER)
            outer = (parts[c] - unit[k][rows, :] * mean) * chain[k][rows, :]
            highs.append(outer.astype(BF16))
            rests.append((outer - highs[-1].astype(F32)).astype(BF16))
        yield
        left = jnp.concatenate(split3(window(t)) + (jnp.zeros((8, SPAN), F32),), axis=0).astype(BF16)
        right = jnp.concatenate([jnp.concatenate(highs, axis=0), jnp.concatenate(rests, axis=0)], axis=1)
        acc_f[...] += dot_nt(right, jnp.concatenate([left, left], axis=1))
        yield

    def pair(p, carry):
        weave("ABABAAAABABABAA", ahead(2 * p + 1, 1), back_part(2 * p, 0))
        weave("ABABAAAABABABAA", ahead(2 * p + 2, 0), back_part(2 * p + 1, 1))
        return carry

    spans = (num_c + SPAN - 1) // SPAN
    weave("", ahead(0, 0), iter(()))
    lax.fori_loop(0, spans // 2, pair, 0)

    @pl.when(lax.rem(spans, 2) == 1)
    def last():
        weave("", iter(()), back_part(spans - 1, 0))

    firsts = turned(acc_f[...])
    firsts = firsts[0:8] + firsts[8:16] + firsts[16:24]
    bias_grad = acc_s[WIDTH : WIDTH + 8]
    shift_grad = full_nt(bias_grad, low)
    gain_grad = full_nt(jnp.ones((8, SPAN), F32), acc_g[...])
    rows_out[0:5, :] = firsts[0:5]
    rows_out[5:10, :] = narrow_ref[0:5, :]
    rows_out[10:11, :] = firsts[6:7]
    rows_out[11:12, :] = gain_grad[0:1]
    rows_out[12:13, :] = shift_grad[0:1]
    rows_out[13:14, :] = bias_grad[0:1]
    rows_out[14:15, :] = narrow_ref[5:6, :]
    lane = lax.broadcasted_iota(jnp.int32, (1, WIDTH), 1)
    regular = jnp.broadcast_to(jnp.sum(reg_ref[...]), (1, WIDTH))
    rows_out[15:16, :] = jnp.where(lane == 0, narrow_ref[6:7, :], jnp.where(lane == 1, regular, 0.0))
    for q in range(32):
        out_ref[q // 16, q % 16] = acc_s[8 * q : 8 * q + 8, :]
        lanes = slice((q % 2) * 128, (q % 2) * 128 + 128)
        thin_ref[q // 16, q % 16, 0:1, :] = rows_out[q // 2 : q // 2 + 1, lanes]


def newton(gram, sharp):
    ids = lax.broadcasted_iota(jnp.int32, (WIDTH, WIDTH), 0) == lax.broadcasted_iota(jnp.int32, (WIDTH, WIDTH), 1)
    scale = 1.0 / (jnp.sqrt(jnp.sum(jnp.where(ids, gram, 0.0))) + 1e-07)
    sides = (slice(0, WIDTH // 2), slice(WIDTH // 2, WIDTH))
    state = [gram[side] * (scale * scale) for side in sides]
    unit = [jnp.where(ids[side], first_coef, 0.0) for side in sides]

    def joined(halves):
        return [jnp.concatenate(pair, axis=0) for pair in zip(*halves)]

    product = None
    for k in range(NS_STEPS):
        times = six if k < sharp else few
        parts = [three(one) for one in state]
        whole = joined(parts)
        square = [few(part, whole) for part in parts]
        yield None
        poly = [unit[j] + second_coef * state[j] + third_coef * square[j] for j in range(2)]
        left = [three(one) for one in poly]
        if k + 1 < NS_STEPS:
            half = [times(one, whole) for one in left]
            yield None
        if k == 0:
            product = poly
        else:
            right = joined([three(one) for one in product])
            product = [times(one, right) for one in left]
        if k + 1 < NS_STEPS:
            yield None
            outer = joined(left)
            state = [times(three(one), outer) for one in half]
            yield None
    yield jnp.concatenate([one * scale for one in product], axis=0)


def drain(chain):
    result = None
    for result in chain:
        pass
    return result


def square_rows(sum_ref):
    return jnp.concatenate([sum_ref[q // 16, q % 16] for q in range(32)], axis=0)


def small_rows(sum_ref):
    halves = [sum_ref[q // 16, q % 16, 0:1, :] for q in range(32)]
    return jnp.concatenate(
        [jnp.concatenate([halves[2 * k], halves[2 * k + 1]], axis=1) for k in range(16)], axis=0
    )


def reduce_kernel(
    n, rows_n, grad_ref, thin_ref, own_ref, far_ref, cross_ref, gram_ref, smom_ref,
    sum_ref, thin_sum, tall_ref, move_ref,
    rxh, half_sum, rxq, fin, rxh_thin, half_thin, rxq_thin, fin_thin, mixed, rxm, rxc, rxx, sems, dsems, csems, qsems,
):
    me = lax.axis_index("ctx")
    r = lax.axis_index("dp")
    chips = (rows_n // 2) * n
    par = lax.rem(r, 2)
    chip = (r // 2) * n + me
    far = lax.rem(r + rows_n // 2, rows_n)
    near = r + 1 - 2 * par
    cross_near = lax.rem(near + rows_n // 2, rows_n)
    own_rows = pl.ds(pl.multiple_of(r * 8, 8), 8)
    far_rows = pl.ds(pl.multiple_of(far * 8, 8), 8)
    for i in range(own_ref.shape[0]):
        tall_ref[i, own_rows, :] = own_ref[i]
        tall_ref[i, far_rows, :] = far_ref[i]
    others = [lax.rem(chip + d, chips) for d in range(1, chips)]
    places = [{"dp": 2 * (other // n) + par, "ctx": lax.rem(other, n)} for other in others]
    greet(places + [{"dp": near}, {"dp": cross_near}])

    def near_copy(source, target, j):
        return pltpu.make_async_remote_copy(
            src_ref=source,
            dst_ref=target,
            send_sem=csems.at[0, j],
            recv_sem=csems.at[1, j],
            device_id={"dp": near},
            device_id_type=MESH,
        )

    def chip_copies(source, target, k):
        return [
            copy for pair in zip(*(chip_plan(*plan, k + 2 * j) for j, plan in enumerate(zip(source, target)))) for copy in pair
        ]

    def chip_plan(source, target, k):
        return [
            pltpu.make_async_remote_copy(
                src_ref=source(other),
                dst_ref=target,
                send_sem=qsems.at[2 * k, d],
                recv_sem=qsems.at[2 * k + 1, d],
                device_id=place,
                device_id_type=MESH,
            )
            for d, (other, place) in enumerate(zip(others, places))
        ]

    top = pl.ds(0, 1)
    halves = [
        near_copy(grad_ref.at[1 - par], rxh, 0),
        near_copy(thin_ref.at[1 - par, :, top, :], rxh_thin.at[:, top, :], 4),
    ]
    for copy in halves:
        copy.start()
    blocks = [
        near_copy(tall_ref.at[:, rows, :], tall_ref.at[:, rows, :], j + 1)
        for j, rows in enumerate((own_rows, far_rows))
    ]
    for copy in blocks:
        copy.start()
    crosses = send_all("ctx", n, lambda peer: cross_ref, rxx.at[me], sems.at[0], sems.at[1])
    rxx[me] = cross_ref[...]

    def first_sum():
        for copy in halves:
            copy.wait()
        half_sum[...] = grad_ref[par] + rxh[...]
        half_thin[:, 0:1, :] = thin_ref[par, :, 0:1, :] + rxh_thin[:, 0:1, :]
        rxq[chip] = half_sum[chip]
        rxq_thin[chip, 0:1, :] = half_thin[chip, 0:1, :]

    scattered = fenced(
        chip_copies(
            (lambda other: half_sum.at[other], lambda other: half_thin.at[other, top, :]),
            (rxq.at[chip], rxq_thin.at[chip, top, :]),
            0,
        ),
        first_sum,
    )
    for copy in blocks:
        copy.wait()
    height = own_ref.shape[0] - 2
    inners = [jnp.zeros((96, 96), F32)] * 2
    for i in range(height):
        stack = jnp.concatenate(split3(tall_ref[i]), axis=0).astype(BF16)
        inners[i % 2] = inners[i % 2] + dot_nt(stack, stack)
    inner = inners[0] + inners[1]
    inner = inner[0:32] + inner[32:64] + inner[64:96]
    inner = inner[:, 0:32] + inner[:, 32:64] + inner[:, 64:96]
    mixed[...] = jnp.concatenate([inner, jnp.zeros((32, 96), F32)], axis=1)
    rxm[me] = mixed[...]
    terms = fenced(plan_all("ctx", n, lambda peer: mixed, rxm.at[me], sems.at[2], sems.at[3]))
    latents = tall_ref[height]
    bias_moment = momentum_rate * smom_ref[1] + full_nn(latents.T, tall_ref[height + 1])
    side = newton(gram_six(three(bias_moment)), NS_STEPS)

    def advance(count):
        for step in range(count):
            next(side)

    advance(3)

    def share():
        for copy in crosses:
            copy.wait()
        total = rxx[0]
        for s in range(1, n):
            total = total + rxx[s]
        rxc[r] = total

    shared = fenced(plan_all("dp", rows_n, lambda peer: rxc.at[r], rxc.at[r], dsems.at[0], dsems.at[1]), share)
    advance(8)

    def second_sum():
        for copy in scattered:
            copy.wait()
        total = rxq[0]
        thin = rxq_thin[0, 0:1, :]
        for s in range(1, chips):
            total = total + rxq[s]
            thin = thin + rxq_thin[s, 0:1, :]
        fin[...] = total
        fin_thin[0:1, :] = thin
        sum_ref[par, chip] = total
        thin_sum[par, chip, 0:1, :] = thin

    gathered = fenced(
        chip_copies(
            (lambda other: fin, lambda other: fin_thin.at[top, :]),
            (sum_ref.at[par, chip], thin_sum.at[par, chip, top, :]),
            1,
        ),
        second_sum,
    )
    advance(3)
    for copy in terms:
        copy.wait()
    total = rxm[0]
    for s in range(1, n):
        total = total + rxm[s]
    inner = total[:, 0:32]
    for copy in shared:
        copy.wait()
    cross = jnp.concatenate([rxc[s] for s in range(rows_n)], axis=0)
    weight = momentum_rate * cross + 0.5 * full_nn(inner, latents)
    half = full_nn(latents.T, weight)
    slabs = [gram_ref[s, t] for s in range(rows_n) for t in range(n)]
    gram = (momentum_rate * momentum_rate) * jnp.concatenate(slabs, axis=0) + (half + half.T)
    advance(3)
    move_ref[2] = next(side)
    side = newton(gram, HEAD_SHARP)
    advance(12)

    def all_here():
        for copy in gathered:
            copy.wait()

    last = fenced(
        [
            near_copy(sum_ref.at[par], sum_ref.at[par], 3),
            near_copy(thin_sum.at[par, :, top, :], thin_sum.at[par, :, top, :], 5),
        ],
        all_here,
    )
    advance(5)
    move_ref[0] = next(side)
    for copy in last:
        copy.wait()
    moment = momentum_rate * smom_ref[0] + square_rows(sum_ref)
    move_ref[1] = drain(newton(gram_six(three(moment)), NS_STEPS))


def update_kernel(
    live_all, groups_all, mom_ref, head_ref, tall_ref, move_ref, sum_ref, thin_ref, square_ref, smom_ref,
    small_ref, mmom_ref, mvar_ref,
    mom_out, head_out, copy_out, smom_out, square_out, scopy_out, mmom_out, mvar_out, small_out, mcopy_out,
    loss_out, mom, head, low_copy, left, wide, middle, store_sem,
):
    chunks, unused, chunk = mom.shape
    per = chunk // WIDTH

    def stores(k):
        lanes = pl.ds(pl.multiple_of(k * chunk, chunk), chunk)
        return [
            pltpu.make_async_copy(source.at[k], target.at[:, lanes], store_sem.at[j, k])
            for j, (source, target) in enumerate(((mom, mom_out), (head, head_out), (low_copy, copy_out)))
        ]

    height = tall_ref.shape[0] - 2
    latents = tall_ref[height]
    rows = jnp.concatenate([latents] * 3 + [jnp.zeros((32, WIDTH), F32)], axis=0)
    left[...] = rows.T.astype(BF16)
    ids = lax.broadcasted_iota(jnp.int32, (WIDTH, WIDTH), 0) == lax.broadcasted_iota(jnp.int32, (WIDTH, WIDTH), 1)
    move = move_ref[0] * (-head_rate * 0.2 * WIDTH)
    centre = jnp.sum(jnp.where(ids, move, 0.0)) * (1.0 / WIDTH)
    middle[0] = centre
    wide[...] = jnp.concatenate(three(jnp.where(ids, move - centre, move))[0:2], axis=0)
    grads = [square_rows(sum_ref), full_nn(latents.T, tall_ref[height + 1])]
    for k in range(2):
        moment = momentum_rate * smom_ref[k] + grads[k]
        smom_out[k] = moment
        move = six(three(move_ref[k + 1]), three(moment))
        old = square_ref[k]
        new = old - square_rates[k] * (0.2 * WIDTH**0.5 * move + decay_rate * old)
        square_out[k] = new
        scopy_out[k] = new.astype(BF16)
    narrow = small_rows(thin_ref)
    stats = narrow[15:16]
    lane = lax.broadcasted_iota(jnp.int32, (1, WIDTH), 1)
    weight = jnp.where(lane == 0, 1.0 / live_all, jnp.where(lane == 1, reg_weight / groups_all, 0.0))
    loss_out[...] = jnp.broadcast_to(jnp.sum(stats * weight), loss_out.shape)
    moment, second, new = adam_update(small_ref[...], narrow[0:15], mmom_ref[...], mvar_ref[...])
    mmom_out[...] = moment
    mvar_out[...] = second
    small_out[...] = new
    mcopy_out[...] = new.astype(BF16)
    keep = 1.0 - head_rate * decay_rate

    def advance(k, carry):
        centre = middle[0]

        def begin_tile(i):
            lanes = slice(i * WIDTH, (i + 1) * WIDTH)
            high, mid, low = three(tall_ref[k * per + i])
            right = jnp.concatenate([high, mid, low, jnp.zeros_like(high)], axis=0)
            wide_lanes = pl.ds(pl.multiple_of(k * chunk + i * WIDTH, WIDTH), WIDTH)
            moment = momentum_rate * mom_ref[:, wide_lanes] + dot_nn(left[...], right)
            mom[k, :, lanes] = moment
            high = moment.astype(BF16)
            mid = (moment - high.astype(F32)).astype(BF16)
            return keep * head_ref[:, wide_lanes] + centre * moment, high, mid

        def finish_tile(i):
            lanes = slice(i * WIDTH, (i + 1) * WIDTH)
            base, high, mid = ready[i]
            first = dot_nn(wide[...], high)
            new = (first[0:WIDTH] + dot_nn(wide[0:WIDTH, :], mid)) + (first[WIDTH:] + base)
            head[k, :, lanes] = new
            low_copy[k, :, lanes] = new.astype(BF16)

        ready = [begin_tile(0), begin_tile(1)]
        for i in range(per):
            if i + 2 < per:
                ready.append(begin_tile(i + 2))
            finish_tile(i)
        for copy in stores(k):
            copy.start()
        return carry

    lax.fori_loop(0, chunks, advance, 0)
    for k in range(chunks):
        for copy in stores(k):
            copy.wait()


def shape(*dims, dtype=F32):
    return jax.ShapeDtypeStruct(dims, dtype)


def dma_sems(*dims):
    return pltpu.SemaphoreType.DMA(dims)


def remote_params(ident, room=50):
    return pltpu.CompilerParams(collective_id=ident, has_side_effects=True, vmem_limit_bytes=room * MIB)


def plain_params(room=16):
    return pltpu.CompilerParams(vmem_limit_bytes=room * MIB)


CHUNK = 1024


def call_scatter(n, rows_n, lengths, pixels, ctx_mask, head_mom):
    micro, groups, slots = pixels.shape[1], pixels.shape[2], pixels.shape[4]
    return pl.pallas_call(
        functools.partial(scatter_kernel, n, rows_n),
        out_shape=[shape(n, 8, slots), shape(n, 8, slots), shape(WIDTH // rows_n, WIDTH)],
        in_specs=[hbm_spec()] * 4,
        out_specs=[vmem_spec()] * 3,
        scratch_shapes=[
            pltpu.SMEM(lengths.shape, jnp.int32),
            pltpu.VMEM((1, micro, 5, groups, slots), F32),
            pltpu.VMEM(ctx_mask.shape, jnp.int32),
            pltpu.VMEM((n, 8, slots), F32),
            pltpu.VMEM((WIDTH, head_mom.shape[1] // rows_n), F32),
            pltpu.VMEM((WIDTH, WIDTH), F32),
            pltpu.VMEM((rows_n, WIDTH // rows_n, WIDTH), F32),
            pltpu.VMEM((TILE, TILE), BF16),
            dma_sems(micro, n - 1),
            dma_sems(micro, n - 1),
            dma_sems(),
            dma_sems(2, rows_n - 1),
            dma_sems(3),
        ],
        compiler_params=remote_params(1, 50),
        name="scatter_pixels",
        cost_estimate=busy(14),
    )(lengths, jnp.transpose(pixels, (0, 1, 3, 2, 4)), ctx_mask, head_mom)


def call_encode(received, small_params, square_w):
    cap = received.shape[0] * received.shape[2] + 5 * SPAN
    return pl.pallas_call(
        encoder_kernel,
        out_shape=[shape(8, WIDTH + 128), shape(8, cap), shape(1, dtype=jnp.int32)],
        in_specs=[vmem_spec()] * 3,
        out_specs=[vmem_spec(), vmem_spec(), smem_spec()],
        scratch_shapes=[
            pltpu.VMEM((8, 128), jnp.int32),
            pltpu.SMEM((8, 128), jnp.int32),
            pltpu.VMEM((3, WIDTH, SPAN), F32),
            pltpu.VMEM((WIDTH, WIDTH), BF16),
            pltpu.VMEM((WIDTH, 16), F32),
            pltpu.VMEM((WIDTH, SPAN), BF16),
            pltpu.VMEM((WIDTH, SPAN), BF16),
            dma_sems(),
        ],
        compiler_params=plain_params(),
        name="encode",
        cost_estimate=busy(10),
    )(received, small_params, square_w)


def call_generate(n, latent, head_w, tiles, gram_part):
    height = WIDTH // n
    chunks = head_w.shape[1] // CHUNK
    slab = gram_part.shape[0] // n
    return pl.pallas_call(
        functools.partial(theta_kernel, n),
        out_shape=[
            shape(WIDTH, WIDTH),
            shape(WIDTH, WIDTH, dtype=BF16),
            shape(8, WIDTH),
            shape(8, WIDTH),
            shape(8, WIDTH),
            shape(*tiles.shape),
            shape(slab, WIDTH),
        ],
        in_specs=[vmem_spec(), any_spec(), vmem_spec(), vmem_spec()],
        out_specs=[vmem_spec()] * 7,
        scratch_shapes=[
            pltpu.VMEM((n, 8, WIDTH + 128), F32),
            pltpu.VMEM((chunks, WIDTH, CHUNK), F32),
            pltpu.VMEM((n, height, WIDTH), BF16),
            pltpu.VMEM((2, WIDTH, 128), F32),
            pltpu.VMEM((n, slab, WIDTH), F32),
            dma_sems(chunks),
            dma_sems(8, n - 1),
        ],
        compiler_params=remote_params(2),
        name="generate",
        cost_estimate=busy(17),
    )(latent, head_w, tiles, gram_part)


def call_siren(n, live_all, lengths, received, gen, latent, small_params, square_w):
    cap = received.shape[0] * received.shape[2] + 5 * SPAN
    return pl.pallas_call(
        functools.partial(siren_kernel, live_all),
        out_shape=[shape(WIDTH, WIDTH), shape(8, WIDTH), shape(8, WIDTH)],
        in_specs=[smem_spec()] + [vmem_spec()] * 5,
        out_specs=[vmem_spec()] * 3,
        scratch_shapes=[
            pltpu.VMEM((8, cap), F32),
            pltpu.VMEM((8, 128), jnp.int32),
            pltpu.SMEM((8, 128), jnp.int32),
            pltpu.VMEM((WIDTH, WIDTH), BF16),
            pltpu.VMEM((WIDTH, SPAN), F32),
            pltpu.VMEM((WIDTH, SPAN), BF16),
            pltpu.VMEM((WIDTH, SPAN), BF16),
            pltpu.VMEM((WIDTH, SPAN), F32),
            pltpu.VMEM((WIDTH, SPAN), F32),
            pltpu.VMEM((WIDTH, SPAN), BF16),
            pltpu.VMEM((WIDTH, SPAN), BF16),
            pltpu.VMEM((WIDTH, SPAN), F32),
            pltpu.VMEM((WIDTH, SPAN), F32),
            pltpu.VMEM((WIDTH + 16, WIDTH), F32),
            pltpu.VMEM((WIDTH, 32), F32),
            pltpu.VMEM((WIDTH, 16), F32),
            pltpu.VMEM((8, SPAN), F32),
            dma_sems(),
        ],
        compiler_params=plain_params(),
        name="siren",
        cost_estimate=busy(16),
    )(lengths, received, gen, latent, small_params, square_w)


def call_latent(n, rows_n, groups_all, part, bias, theta, head_w, head_mom, z8, gram_rows):
    height = WIDTH // n
    chunks = head_w.shape[1] // CHUNK
    slab = gram_rows.shape[0]
    return pl.pallas_call(
        functools.partial(latent_kernel, n, rows_n, groups_all),
        out_shape=[
            shape(8, WIDTH),
            shape(height + 2, 8, WIDTH),
            shape(8, WIDTH),
            shape(rows_n, n, slab, WIDTH),
        ],
        in_specs=[vmem_spec()] * 3 + [any_spec()] * 2 + [vmem_spec()] * 2,
        out_specs=[vmem_spec()] * 4,
        scratch_shapes=[
            pltpu.VMEM((WIDTH, WIDTH), F32),
            pltpu.VMEM((n, 8, WIDTH), F32),
            pltpu.VMEM((2, WIDTH, 128), F32),
            pltpu.VMEM((chunks, WIDTH, CHUNK), F32),
            pltpu.VMEM((chunks, WIDTH, CHUNK), F32),
            pltpu.VMEM((height, WIDTH, WIDTH), BF16),
            pltpu.VMEM((height, 3 * WIDTH, WIDTH), BF16),
            pltpu.VMEM((n, 8, WIDTH), F32),
            pltpu.VMEM((8, WIDTH), F32),
            pltpu.VMEM((height, 32, WIDTH), BF16),
            pltpu.VMEM((2, 3 * WIDTH, 32), F32),
            pltpu.VMEM((n, slab, WIDTH), F32),
            dma_sems(chunks),
            dma_sems(chunks),
            dma_sems(8, n - 1),
            dma_sems(2, rows_n - 1),
        ],
        compiler_params=remote_params(3),
        name="latent_grads",
        cost_estimate=busy(18),
    )(part, bias, theta, head_w, head_mom, z8, gram_rows)


def call_back(counts, clist, small_params, square_w, latent_grad, inverse, tall, narrow, regular):
    return pl.pallas_call(
        encoder_back_kernel,
        out_shape=[shape(2, 16, 8, WIDTH), shape(2, 16, 8, 128)],
        in_specs=[smem_spec()] + [vmem_spec()] * 8,
        out_specs=[vmem_spec()] * 2,
        scratch_shapes=[
            pltpu.VMEM((3, WIDTH, SPAN), F32),
            pltpu.VMEM((WIDTH, WIDTH), BF16),
            pltpu.VMEM((WIDTH + 16, WIDTH), BF16),
            pltpu.VMEM((WIDTH, SPAN), F32),
            pltpu.VMEM((WIDTH, SPAN), F32),
            pltpu.VMEM((WIDTH, SPAN), F32),
            pltpu.VMEM((WIDTH, SPAN), F32),
            pltpu.VMEM((WIDTH, SPAN), BF16),
            pltpu.VMEM((WIDTH, SPAN), BF16),
            pltpu.VMEM((WIDTH, SPAN), BF16),
            pltpu.VMEM((WIDTH, SPAN), BF16),
            pltpu.VMEM((WIDTH + 16, WIDTH), F32),
            pltpu.VMEM((WIDTH, 32), F32),
            pltpu.VMEM((WIDTH, SPAN), F32),
            pltpu.VMEM((16, WIDTH), F32),
        ],
        compiler_params=plain_params(),
        name="encode_back",
        cost_estimate=busy(16),
    )(counts, clist, small_params, square_w, latent_grad, inverse, tall, narrow, regular)


def call_reduce(n, rows_n, grads, thin, own, far, cross, gram, square_mom):
    chips = (rows_n // 2) * n
    return pl.pallas_call(
        functools.partial(reduce_kernel, n, rows_n),
        out_shape=[
            shape(*grads.shape),
            shape(*thin.shape),
            shape(own.shape[0], 8 * rows_n, WIDTH),
            shape(3, WIDTH, WIDTH),
        ],
        in_specs=[vmem_spec()] * 7,
        out_specs=[vmem_spec()] * 4,
        scratch_shapes=[
            pltpu.VMEM((chips, 8, WIDTH), F32),
            pltpu.VMEM((chips, 8, WIDTH), F32),
            pltpu.VMEM((chips, 8, WIDTH), F32),
            pltpu.VMEM((8, WIDTH), F32),
            pltpu.VMEM((chips, 8, 128), F32),
            pltpu.VMEM((chips, 8, 128), F32),
            pltpu.VMEM((chips, 8, 128), F32),
            pltpu.VMEM((8, 128), F32),
            pltpu.VMEM((32, 128), F32),
            pltpu.VMEM((n, 32, 128), F32),
            pltpu.VMEM((rows_n, 8, WIDTH), F32),
            pltpu.VMEM((n, 8, WIDTH), F32),
            dma_sems(4, n - 1),
            dma_sems(2, rows_n - 1),
            dma_sems(2, 6),
            dma_sems(8, chips - 1),
        ],
        compiler_params=remote_params(4, 16),
        name="reduce_grads",
        cost_estimate=busy(24),
    )(grads, thin, own, far, cross, gram, square_mom)


def call_update(
    live_all, groups_all, head_mom, head_w, tall, move, sums, thin_sums, square_w, square_mom, small_params,
    small_mom, small_var,
):
    columns = head_w.shape[1]
    chunks = columns // CHUNK
    small_copy = shape(15, WIDTH, dtype=BF16)
    square_copy = shape(2, WIDTH, WIDTH, dtype=BF16)
    loss = shape(1, 128)
    others = [square_mom, square_w, square_copy, small_mom, small_var, small_params, small_copy, loss]
    return pl.pallas_call(
        functools.partial(update_kernel, live_all, groups_all),
        out_shape=[shape(WIDTH, columns), shape(WIDTH, columns), shape(WIDTH, columns, dtype=BF16)]
        + [shape(*one.shape, dtype=one.dtype) for one in others],
        in_specs=[vmem_spec()] * 11,
        out_specs=[any_spec()] * 3 + [vmem_spec()] * 8,
        scratch_shapes=[
            pltpu.VMEM((chunks, WIDTH, CHUNK), F32),
            pltpu.VMEM((chunks, WIDTH, CHUNK), F32),
            pltpu.VMEM((chunks, WIDTH, CHUNK), BF16),
            pltpu.VMEM((WIDTH, 128), BF16),
            pltpu.VMEM((2 * WIDTH, WIDTH), BF16),
            pltpu.SMEM((1,), F32),
            dma_sems(3, chunks),
        ],
        compiler_params=plain_params(26),
        name="update_all",
        cost_estimate=busy(12),
    )(
        head_mom, head_w, tall, move, sums, thin_sums, square_w, square_mom, small_params, small_mom, small_var
    )


def grouped(
    pixels, lengths, ctx_mask, head_w, head_mom, square_w, square_mom, small_params, small_mom, small_var
):
    micro, groups, slots = pixels.shape[1], pixels.shape[2], pixels.shape[4]
    n = lax.axis_size("ctx")
    rows_n = lax.axis_size("dp")
    live_all = rows_n * micro * (groups * slots * n * 5 // 8)
    groups_all = rows_n * micro * groups
    received, tiles, gram_part = call_scatter(n, rows_n, lengths, pixels, ctx_mask, head_mom)
    latent, clist, counts = call_encode(received, small_params, square_w)
    theta, gen, z8, inverse, regular, group_rows, gram_rows = call_generate(
        n, latent, head_w, tiles, gram_part
    )
    part, bias, narrow = call_siren(n, live_all, lengths, group_rows, gen, z8, small_params, square_w)
    latent_grad, own, cross, gram = call_latent(
        n, rows_n, groups_all, part, bias, theta, head_w, head_mom, z8, gram_rows
    )
    far = lax.ppermute(own, "dp", [(r, (r + rows_n // 2) % rows_n) for r in range(rows_n)])
    grads, thin = call_back(
        counts, clist, small_params, square_w, latent_grad, inverse, own, narrow, regular
    )
    sums, thin_sums, tall, move = call_reduce(n, rows_n, grads, thin, own, far, cross, gram, square_mom)
    updated = call_update(
        live_all, groups_all, head_mom, head_w, tall, move, sums, thin_sums, square_w, square_mom, small_params,
        small_mom, small_var,
    )
    (
        head_moment,
        head_new,
        head_copy,
        square_moment,
        square_new,
        square_copy,
        small_moment,
        small_second,
        small_new,
        small_copy,
        loss,
    ) = updated
    return (
        head_moment,
        head_new,
        head_copy,
        square_moment,
        square_new,
        square_copy,
        small_moment,
        small_second,
        small_new,
        small_copy,
        loss[0, 0],
    )


def local(pixels, lengths, ctx_mask, head_w, *rest):
    n = lax.axis_size("ctx")
    fits = (
        pixels.shape[1] * pixels.shape[2] == n
        and n == 8
        and lax.axis_size("dp") == 4
        and pixels.shape[4] == 2048
        and head_w.shape == (WIDTH, 8192)
    )
    chosen = grouped if fits else general
    return chosen(pixels, lengths, ctx_mask, head_w, *rest)


def solution(mesh):
    placed = (
        P("dp", None, None, None, "ctx"),
        P("dp", None, None),
        P("dp", None, None, "ctx"),
        P(None, "ctx"),
        P(None, "ctx"),
        P(),
        P(),
        P(),
        P(),
        P(),
    )
    return jax.shard_map(
        local,
        mesh=mesh,
        in_specs=placed,
        out_specs=(
            P(None, "ctx"),
            P(None, "ctx"),
            P(None, "ctx"),
            P(),
            P(),
            P(),
            P(),
            P(),
            P(),
            P(),
            P(),
        ),
        check_vma=False,
    )
```

```python
import functools

import jax
import jax.numpy as jnp
from jax import lax
from jax.experimental import pallas as pl
from jax.experimental.pallas import tpu as pltpu
from jax.sharding import PartitionSpec as P

NS_STEPS = 5
STEP = 10


exact_arithmetic_mode = lax.Precision.HIGHEST
reg_weight = 0.5
momentum_rate = 0.95
head_rate = 0.003
square_rates = (0.3, 0.02)
adam_rate = 0.05
beta_first = 0.9
beta_second = 0.999
decay_rate = 0.01
first_coef = 3.4445
second_coef = -4.775
third_coef = 2.0315


def layer_norm(values, gain_row, bias_row):
    centered = values - jnp.mean(values, axis=-1, keepdims=True)
    variance = jnp.mean(centered * centered, axis=-1, keepdims=True)
    return centered * lax.rsqrt(variance + 1e-05) * gain_row + bias_row


def ns_update(current, gram_matrix):
    polynomial = second_coef * gram_matrix + third_coef * jnp.einsum(
        "kij,kjl->kil", gram_matrix, gram_matrix, precision=exact_arithmetic_mode
    )
    return first_coef * current + jnp.einsum(
        "kij,kjl->kil", polynomial, current, precision=exact_arithmetic_mode
    )


def orthogonal_local(matrices):
    norms = jnp.sqrt(jnp.sum(matrices * matrices, axis=(1, 2), keepdims=True))
    current = matrices / (norms + 1e-07)
    for sweep in range(NS_STEPS):
        gram_matrix = jnp.einsum("kij,klj->kil", current, current, precision=exact_arithmetic_mode)
        current = ns_update(current, gram_matrix)
    return current


def head_orthogonal(moment):
    current = moment[None]
    total = lax.psum(jnp.sum(moment * moment), "ctx")
    current = current / (jnp.sqrt(total) + 1e-07)
    for sweep in range(NS_STEPS):
        gram_matrix = lax.psum(
            jnp.dot(current[0], current[0].T, precision=exact_arithmetic_mode), "ctx"
        )
        current = ns_update(current, gram_matrix[None])
    return current[0]


def adam_update(params, grad, moment, second_moment):
    moment_new = beta_first * moment + (1.0 - beta_first) * grad
    second_new = beta_second * second_moment + (1.0 - beta_second) * grad * grad
    corrected = (
        moment_new
        / (1.0 - beta_first**STEP)
        / (jnp.sqrt(second_new / (1.0 - beta_second**STEP)) + 1e-08)
    )
    return (moment_new, second_new, params - adam_rate * (corrected + decay_rate * params))


def encoder_forward(features, context, small_params, second_low):
    first_pre = (
        jnp.einsum("gpc,cd->gpd", features, small_params[0:5], precision=exact_arithmetic_mode)
        + small_params[10]
    )
    first_act, gelu_first = jax.vjp(jax.nn.gelu, first_pre)
    normed, norm_back = jax.vjp(layer_norm, first_act, small_params[11], small_params[12])
    normed_low = normed.astype(jnp.bfloat16)
    second = (
        jnp.einsum("gpd,de->gpe", normed_low, second_low, preferred_element_type=jnp.float32)
        + small_params[13]
    )
    encoded, gelu_second = jax.vjp(jax.nn.gelu, second)
    summed = jnp.einsum("gp,gpe->ge", context, encoded, precision=exact_arithmetic_mode)
    return (
        summed,
        jnp.sum(context, axis=1),
        (first_pre, gelu_first, norm_back, normed_low, gelu_second),
    )


def general(
    pixels,
    lengths,
    ctx_mask,
    head_w,
    head_mom,
    square_w,
    square_mom,
    small_params,
    small_mom,
    small_var,
):
    micro_count = pixels.shape[1]
    groups = pixels.shape[2]
    slot_count = pixels.shape[4]
    model_width = square_w.shape[1]
    live_all = (
        lax.axis_size("dp") * micro_count * (groups * slot_count * lax.axis_size("ctx") * 5 // 8)
    )
    groups_all = lax.axis_size("dp") * micro_count * groups
    slot_ids = lax.axis_index("ctx") * slot_count + jnp.arange(slot_count, dtype=jnp.int32)
    head_low = head_w.astype(jnp.bfloat16)
    head_back = head_low.astype(jnp.float32)
    square_low = square_w.astype(jnp.bfloat16)
    bias_head = square_low[1].astype(jnp.float32)
    final_coefficient_reduced = small_params[7:10].astype(jnp.bfloat16)
    kept = []
    sum_list = []
    count_list = []
    for micro_index in range(micro_count):
        features = jnp.transpose(pixels[0, micro_index], (0, 2, 1))
        live_slot = slot_ids[None, :] < lengths[0, micro_index][:, None]
        context = jnp.where(live_slot & (ctx_mask[0, micro_index] == 1), 1.0, 0.0).astype(
            jnp.float32
        )
        query_mask = jnp.where(live_slot & (ctx_mask[0, micro_index] == 0), 1.0, 0.0).astype(
            jnp.float32
        )
        summed, counts, saved = encoder_forward(features, context, small_params, square_low[0])
        sum_list.append(summed)
        count_list.append(counts)
        kept.append((features, context, query_mask, saved))
    totals = [
        lax.psum((sum_list[index_micro], count_list[index_micro]), "ctx")
        for index_micro in range(micro_count)
    ]
    zeros_small = jnp.zeros((model_width,), jnp.float32)
    grad_first_w = jnp.zeros((5, model_width), jnp.float32)
    grad_coord_w = jnp.zeros((2, model_width), jnp.float32)
    grad_out_w = jnp.zeros((3, model_width), jnp.float32)
    grad_vectors = [zeros_small] * 5
    grad_square = jnp.zeros_like(square_w)
    latent_rows = []
    theta_rows = []
    squared = jnp.zeros((), jnp.float32)
    regular = jnp.zeros((), jnp.float32)
    for micro_index in range(micro_count):
        features, context, query_mask, saved = kept[micro_index]
        first_pre, gelu_first, norm_back, normed_low, gelu_second = saved
        summed, counts = totals[micro_index]
        divisor = counts[:, None] + 1.0
        latent_low = (summed / divisor).astype(jnp.bfloat16)
        latent_back = latent_low.astype(jnp.float32)
        generated = jnp.dot(latent_low, head_low, preferred_element_type=jnp.float32)
        gen_parts = generated.astype(jnp.bfloat16).reshape(groups, -1, model_width)
        gen_full = lax.all_gather(gen_parts, "ctx", axis=1, tiled=True)
        gen_bias = jnp.dot(latent_low, square_low[1], preferred_element_type=jnp.float32)
        coord_pre = (
            jnp.einsum(
                "gpc,cd->gpd",
                features[..., 3:5],
                small_params[5:7],
                precision=exact_arithmetic_mode,
            )
            + small_params[14]
        )
        siren_low = jnp.sin(30.0 * coord_pre).astype(jnp.bfloat16)
        siren_pre = (
            jnp.einsum("gpd,gde->gpe", siren_low, gen_full, preferred_element_type=jnp.float32)
            + gen_bias[:, None, :]
        )
        result_reduced_form = jnp.sin(30.0 * siren_pre).astype(jnp.bfloat16)
        estimated_colour_values = jnp.einsum(
            "kdg,cg->kcd",
            result_reduced_form,
            final_coefficient_reduced,
            preferred_element_type=jnp.float32,
        )
        errors = (
            estimated_colour_values - jnp.transpose(features[..., 0:3], (0, 2, 1))
        ) * query_mask[:, None, :]
        squared = squared + jnp.sum(errors * errors)
        regular = regular + jnp.sum(generated * generated)
        prediction_gradient = (2.0 / live_all * errors).astype(jnp.bfloat16)
        grad_out_w = grad_out_w + jnp.einsum(
            "dan,dnq->aq",
            prediction_gradient,
            result_reduced_form,
            preferred_element_type=jnp.float32,
        )
        grad_out = jnp.einsum(
            "xvw,vt->xwt",
            prediction_gradient,
            final_coefficient_reduced,
            preferred_element_type=jnp.float32,
        )
        grad_inner = (grad_out * 30.0 * jnp.cos(30.0 * siren_pre)).astype(jnp.bfloat16)
        gen_part = jnp.einsum(
            "gpd,gpe->gde", siren_low, grad_inner, preferred_element_type=jnp.float32
        )
        gen_grad = lax.psum_scatter(gen_part, "ctx", scatter_dimension=1, tiled=True).reshape(
            groups, -1
        )
        gen_grad = gen_grad + 2.0 * reg_weight / groups_all * generated
        bias_part = jnp.sum(grad_inner.astype(jnp.float32), axis=1)
        grad_siren = jnp.einsum(
            "gpe,gde->gpd", grad_inner, gen_full, preferred_element_type=jnp.float32
        )
        grad_coord = grad_siren * 30.0 * jnp.cos(30.0 * coord_pre)
        grad_coord_w = grad_coord_w + jnp.einsum(
            "gpc,gpd->cd", features[..., 3:5], grad_coord, precision=exact_arithmetic_mode
        )
        grad_vectors[4] = grad_vectors[4] + jnp.sum(grad_coord, axis=(0, 1))
        latent_rows.append(latent_back)
        theta_rows.append(gen_grad)
        latent_part = jnp.dot(gen_grad, head_back.T, precision=exact_arithmetic_mode)
        latent_part, bias_full = lax.psum((latent_part, bias_part), "ctx")
        grad_square = grad_square.at[1].add(
            jnp.dot(latent_back.T, bias_part, precision=exact_arithmetic_mode)
        )
        grad_latent = latent_part + jnp.dot(bias_full, bias_head.T, precision=exact_arithmetic_mode)
        grad_encoded = context[:, :, None] * (grad_latent / divisor)[:, None, :]
        (grad_second,) = gelu_second(grad_encoded)
        second_low = grad_second.astype(jnp.bfloat16)
        grad_square = grad_square.at[0].add(
            jnp.einsum("gpd,gpe->de", normed_low, second_low, preferred_element_type=jnp.float32)
        )
        grad_vectors[3] = grad_vectors[3] + jnp.sum(second_low.astype(jnp.float32), axis=(0, 1))
        grad_normed = jnp.einsum(
            "gpe,de->gpd", second_low, square_low[0], preferred_element_type=jnp.float32
        )
        grad_act, grad_gain, grad_beta = norm_back(grad_normed)
        (grad_first,) = gelu_first(grad_act)
        grad_first_w = grad_first_w + jnp.einsum(
            "gpc,gpd->cd", features, grad_first, precision=exact_arithmetic_mode
        )
        grad_vectors[0] = grad_vectors[0] + jnp.sum(grad_first, axis=(0, 1))
        grad_vectors[1] = grad_vectors[1] + grad_gain
        grad_vectors[2] = grad_vectors[2] + grad_beta
    grad_small = jnp.concatenate(
        [
            grad_first_w,
            grad_coord_w,
            grad_out_w,
            jnp.stack(
                [
                    grad_vectors[0],
                    grad_vectors[1],
                    grad_vectors[2],
                    grad_vectors[3],
                    grad_vectors[4],
                ]
            ),
        ],
        axis=0,
    )
    grad_small, grad_square, stat_sums = lax.psum(
        (grad_small, grad_square, jnp.stack([squared, regular])), ("dp", "ctx")
    )
    latent_stack = jnp.concatenate(latent_rows, axis=0)
    theta_stack = jnp.concatenate(theta_rows, axis=0)
    grad_head = lax.psum(
        jnp.dot(latent_stack.T, theta_stack, precision=exact_arithmetic_mode), "dp"
    )
    loss_value = stat_sums[0] / live_all + reg_weight * stat_sums[1] / groups_all
    head_moment = momentum_rate * head_mom + grad_head
    head_dir = head_orthogonal(head_moment)
    head_new = head_w - head_rate * (0.2 * model_width * head_dir + decay_rate * head_w)
    square_moment = momentum_rate * square_mom + grad_square
    rates = jnp.array(square_rates, jnp.float32)[:, None, None]
    square_new = square_w - rates * (
        0.2 * model_width**0.5 * orthogonal_local(square_moment) + decay_rate * square_w
    )
    small_moment, small_second, small_new = adam_update(
        small_params, grad_small, small_mom, small_var
    )
    return (
        head_moment,
        head_new,
        head_new.astype(jnp.bfloat16),
        square_moment,
        square_new,
        square_new.astype(jnp.bfloat16),
        small_moment,
        small_second,
        small_new,
        small_new.astype(jnp.bfloat16),
        loss_value,
    )


MESH = pl.DeviceIdType.MESH
F32 = jnp.float32
BF16 = jnp.bfloat16
WIDTH = 256
TILE = 256
MIB = 1024 * 1024
SPAN = 768
QUARTER = 64
HALF = 128
HEAD_SHARP = 3
TURN = 30.0 / 6.283185307179586
GELU_ONE = 0.7978845608028654
GELU_CUBE = GELU_ONE * 0.044715
GELU_SCALE = GELU_CUBE ** (1.0 / 3.0)
GELU_SLOPE = GELU_ONE / GELU_SCALE
NORM_EPS = 1e-05 * (2.0 * GELU_SCALE) ** 2
SIN_TERMS = (4.442860272, -7.307432505, 3.594782484, -0.784372885)


def any_spec():
    return pl.BlockSpec(memory_space=pl.ANY)


def hbm_spec():
    return pl.BlockSpec(memory_space=pltpu.HBM)


def busy(micros):
    return pl.CostEstimate(flops=micros * 10**9, bytes_accessed=micros * 10**5, transcendentals=0)


def vmem_spec():
    return pl.BlockSpec(memory_space=pltpu.VMEM)


def smem_spec():
    return pl.BlockSpec(memory_space=pltpu.SMEM)


def turned(matrix):
    pad = jnp.zeros((matrix.shape[0], 128 - matrix.shape[1]), F32)
    return jnp.concatenate([matrix, pad], axis=1).T


def weave(order, first, second):
    for letter in order:
        next(first if letter == "A" else second, None)
    for rest in (first, second):
        for unused in rest:
            pass


def dot_nn(a, b):
    return lax.dot_general(a, b, (((1,), (0,)), ((), ())), preferred_element_type=F32)


def dot_nt(a, b):
    return lax.dot_general(a, b, (((1,), (1,)), ((), ())), preferred_element_type=F32)


def full_nn(a, b):
    return lax.dot_general(
        a, b, (((1,), (0,)), ((), ())), precision=lax.Precision.HIGHEST, preferred_element_type=F32
    )


def full_nt(a, b):
    return lax.dot_general(
        a, b, (((1,), (1,)), ((), ())), precision=lax.Precision.HIGHEST, preferred_element_type=F32
    )


def split3(v):
    high = v.astype(BF16).astype(F32)
    rest = v - high
    mid = rest.astype(BF16).astype(F32)
    return high, mid, rest - mid


def hail(peers):
    barrier = pltpu.get_barrier_semaphore()
    for peer in peers:
        pl.semaphore_signal(barrier, inc=1, device_id=peer, device_id_type=MESH)
    return len(peers)


def meet(count):
    pl.semaphore_wait(pltpu.get_barrier_semaphore(), count)


def greet(peers):
    meet(hail(peers))


def ring_peers(axis, n):
    me = lax.axis_index(axis)
    return [lax.rem(me + d, n) for d in range(1, n)]


def plan_all(axis, n, source, target, send_sem, recv_sem):
    return [
        pltpu.make_async_remote_copy(
            src_ref=source(peer),
            dst_ref=target,
            send_sem=send_sem.at[d],
            recv_sem=recv_sem.at[d],
            device_id={axis: peer},
            device_id_type=MESH,
        )
        for d, peer in enumerate(ring_peers(axis, n))
    ]


def send_all(*plan):
    copies = plan_all(*plan)
    for copy in copies:
        copy.start()
    return copies


def fenced(copies, before=None):
    @pl.when(lax.axis_index("ctx") >= 0)
    def run():
        if before is not None:
            before()
        for copy in copies:
            copy.start()

    return copies


def column(row, width):
    return jnp.broadcast_to(row, (width, row.shape[1])).T


def gelu_twice(y):
    return y + y * jnp.tanh(y * (GELU_SLOPE + y * y))


def gelu_both(y):
    square = y * y
    above = 1.0 + jnp.tanh(y * (GELU_SLOPE + square))
    value = y * above
    return value, above + (value * (2.0 - above)) * (3.0 * square + GELU_SLOPE)


def plain_twice(x):
    return x + x * jnp.tanh(x * (GELU_ONE + GELU_CUBE * (x * x)))


def plain_slope(x):
    square = GELU_CUBE * (x * x)
    above = 1.0 + jnp.tanh(x * (GELU_ONE + square))
    return above + (x * above) * (2.0 - above) * (3.0 * square + GELU_ONE)


def sine_pair(turns):
    frac = turns - jnp.round(turns)
    square = frac * frac
    s = SIN_TERMS[3] * square + SIN_TERMS[2]
    s = s * square + SIN_TERMS[1]
    s = (s * square + SIN_TERMS[0]) * frac
    cosine = 1.0 - s * s
    rest = 1.0 + cosine
    return s * (rest * lax.rsqrt(rest)), cosine


def triple_weights(block):
    high, mid, low = split3(block)
    rows = jnp.concatenate([high, mid, high, low, mid, high], axis=0)
    pad = jnp.zeros((128 - rows.shape[0], rows.shape[1]), F32)
    return jnp.concatenate([rows, pad], axis=0).T.astype(BF16)[:, 0:48]


def triple_from_list(rows):
    high, mid, low = split3(rows)
    return jnp.concatenate([high, high, mid, high, mid, low], axis=0).astype(BF16)


def three(matrix):
    high = matrix.astype(BF16)
    rest = matrix - high.astype(F32)
    mid = rest.astype(BF16)
    return high, mid, (rest - mid.astype(F32)).astype(BF16)


def six(left, right):
    rows = left[0].shape[0]
    first = dot_nn(jnp.concatenate(left, axis=0), right[0])
    second = dot_nn(jnp.concatenate(left[0:2], axis=0), right[1])
    third = dot_nn(left[0], right[2])
    return (first[0:rows] + second[0:rows] + third) + (
        first[rows : 2 * rows] + second[rows:] + first[2 * rows :]
    )


def few(left, right):
    rows = left[0].shape[0]
    first = dot_nn(jnp.concatenate(left[0:2], axis=0), right[0])
    return (first[0:rows] + dot_nn(left[0], right[1])) + first[rows:]


def gram_six(parts):
    high, mid, low = parts
    both = jnp.concatenate([high, mid], axis=1)
    cross = dot_nt(jnp.concatenate([high, high], axis=1), jnp.concatenate([mid, low], axis=1))
    return dot_nt(both, both) + (cross + cross.T)


def order_rows(row, per):
    return jnp.concatenate([row[:, k * TILE : (k + 1) * TILE] for k in range(per)], axis=0)


def bring_counts(seen_ref, cnt_v, cnt_s, sem):
    for s in range(seen_ref.shape[0]):
        cnt_v[s : s + 1, :] = seen_ref[s, 0:1, :].astype(jnp.int32)
    counts = pltpu.make_async_copy(cnt_v, cnt_s, sem)
    counts.start()
    return counts


def put(target, rows, extra, offset, start, amount):
    lane_ids = lax.broadcasted_iota(jnp.int32, (8, TILE), 1)
    shift = lax.rem(offset, TILE)
    base = pl.multiple_of(offset - shift, TILE)
    marks = [jnp.full((1, TILE), value, F32) for value in (0.0, 1.0, extra)]
    moved = pltpu.roll(jnp.concatenate([rows] + marks, axis=0), lax.rem(shift - start + TILE, TILE), 1)
    here = (lane_ids >= shift) & (lane_ids < shift + amount)
    there = lane_ids < shift + amount - TILE
    target[:, pl.ds(base, TILE)] += jnp.where(here, moved, 0.0)
    target[:, pl.ds(pl.multiple_of(base + TILE, TILE), TILE)] = jnp.where(there, moved, 0.0)


def clear_tail(target, amount):
    start = pl.multiple_of((amount // TILE + 1) * TILE, TILE)
    for step in range(4 * SPAN // TILE):
        target[:, pl.ds(start + step * TILE, TILE)] = jnp.zeros((8, TILE), F32)


def weight_block(weights, bias, place):
    rows = weights.shape[0]
    parts = []
    if place > 0:
        parts.append(jnp.zeros((place, WIDTH), F32))
    parts.append(weights)
    if place + rows < 6:
        parts.append(jnp.zeros((6 - place - rows, WIDTH), F32))
    parts.append(bias)
    parts.append(jnp.zeros((1, WIDTH), F32))
    return jnp.concatenate(parts, axis=0)


def scatter_kernel(
    n, rows_n, len_hbm, pix_hbm, mask_hbm, mom_ref, rx_ref, seen_ref, tiles_ref, share_ref, gram_ref,
    len_ref, pix_ref, mask_ref, stage, stage_n, buf, own, slab_rx, upper,
    send_sem, recv_sem, load_sem, slab_sem, own_sem, tell_sem,
):
    brought = [
        pltpu.make_async_copy(source, target, own_sem.at[j])
        for j, (source, target) in enumerate(((len_hbm, len_ref), (pix_hbm, pix_ref), (mask_hbm, mask_ref)))
    ]
    for copy in brought:
        copy.start()
    me = lax.axis_index("ctx")
    peers = ring_peers("ctx", n)
    r = lax.axis_index("dp")
    span = buf.shape[1]
    load = pltpu.make_async_copy(mom_ref.at[:, pl.ds(pl.multiple_of(r * span, span), span)], buf, load_sem)
    load.start()
    count = hail([{"ctx": peer} for peer in peers] + [{"dp": peer} for peer in ring_peers("dp", rows_n)])
    slots = pix_ref.shape[4]
    per = slots // TILE
    groups = mask_ref.shape[2]
    row_ids = lax.broadcasted_iota(jnp.int32, (TILE, TILE), 0)
    upper[...] = jnp.where(row_ids <= lax.broadcasted_iota(jnp.int32, (TILE, TILE), 1), 1.0, 0.0).astype(BF16)
    row_ids = row_ids.astype(F32)
    lane_ids = lax.broadcasted_iota(jnp.int32, (TILE, TILE), 1).astype(F32)
    place = (
        lax.broadcasted_iota(jnp.int32, (per, TILE), 0) * TILE
        + lax.broadcasted_iota(jnp.int32, (per, TILE), 1)
        + me * slots
    )
    pad = jnp.zeros((3, TILE), F32)
    ones = jnp.ones((16, TILE), BF16)
    blank = jnp.zeros((128 - 2 * per, TILE), BF16)
    wide_ids = lax.broadcasted_iota(jnp.int32, (per, 128), 1)
    told = [jnp.zeros((per, 128), F32)]

    def arrange(b):
        for j in range(groups):
            g = b * groups + j
            mask = order_rows(mask_ref[0, b, j : j + 1, :], per)
            live = place < len_ref[0, b, j]
            context = jnp.where(live & (mask == 1), 1.0, 0.0)
            query = jnp.where(live & (mask == 0), 1.0, 0.0)
            both = jnp.concatenate([context, query], axis=0).astype(BF16)
            order = dot_nn(both, upper[...])
            before_c, before_q = order[0:per], order[per : 2 * per]
            live_c = before_c[:, TILE - 1 : TILE]
            target = jnp.where(
                context > 0.5, before_c, jnp.where(query > 0.5, live_c + before_q, 0.0)
            ) - 1.0
            amounts = dot_nt(ones, jnp.concatenate([both, blank], axis=0))[0:1]
            share_ref[g, 0:1, :] = amounts
            moved = jnp.concatenate([live_c[per - g % n :], live_c[0 : per - g % n]], axis=0) if g % n else live_c
            told[0] = jnp.where(wide_ids == g, moved, told[0])
            for t in range(per):
                rows = jnp.concatenate(
                    [pix_ref[0, b, c, j : j + 1, t * TILE : (t + 1) * TILE] for c in range(5)]
                    + [pad], axis=0
                )
                high, mid, low = split3(rows)
                stack = jnp.concatenate([high, mid, low, jnp.zeros((8, TILE), F32)], axis=0).astype(BF16)
                if t % 2 == 0:
                    chosen = jnp.where(row_ids == target[t : t + 1], 1.0, 0.0).astype(BF16)
                    found = dot_nt(stack, chosen)
                else:
                    spot = column(target[t : t + 1], 128)
                    chosen = jnp.where(lane_ids == jnp.concatenate([spot, spot], axis=1), 1.0, 0.0).astype(BF16)
                    found = dot_nn(stack, chosen)
                found = found[0:8] + found[8:16] + found[16:24]
                tiles_ref[g, :, t * TILE : (t + 1) * TILE] = found
                stage[(g + t) % n, :, g * TILE : (g + 1) * TILE] = found

    copies = []
    for copy in brought:
        copy.wait()
    for b in range(mask_ref.shape[1]):
        arrange(b)
        if b == 0:
            meet(count)
        lanes = pl.ds(b * groups * TILE, groups * TILE)
        copies += fenced(
            plan_all(
                "ctx",
                n,
                lambda peer: stage.at[peer, pl.ds(0, 5), lanes],
                rx_ref.at[me, pl.ds(0, 5), lanes],
                send_sem.at[b],
                recv_sem.at[b],
            )
        )
    for p in range(n):
        stage_n[p, 0:1, :] = told[0][p : p + 1]
    top = pl.ds(0, 1)
    copies += fenced(
        plan_all("ctx", n, lambda peer: stage_n.at[peer, top, :], seen_ref.at[me, top, :], tell_sem.at[0], tell_sem.at[1])
    )
    rx_ref[me, 0:5, :] = stage[me, 0:5, :]
    seen_ref[me, 0:1, :] = stage_n[me, 0:1, :]
    quarter = gram_ref.shape[0]
    same = jnp.zeros((WIDTH, WIDTH), F32)
    cross = jnp.zeros((WIDTH, WIDTH), F32)
    load.wait()
    for i in range(buf.shape[1] // WIDTH):
        high, mid, low = three(buf[:, i * WIDTH : (i + 1) * WIDTH])
        both = jnp.concatenate([high, mid], axis=1)
        same = same + dot_nt(both, both)
        cross = cross + dot_nt(jnp.concatenate([high, high], axis=1), jnp.concatenate([mid, low], axis=1))
    own[...] = same + (cross + cross.T)
    slabs = fenced(
        plan_all(
            "dp",
            rows_n,
            lambda peer: own.at[pl.ds(pl.multiple_of(peer * quarter, quarter), quarter), :],
            slab_rx.at[r],
            slab_sem.at[0],
            slab_sem.at[1],
        )
    )
    slab_rx[r] = own[pl.ds(pl.multiple_of(r * quarter, quarter), quarter), :]
    for copy in slabs:
        copy.wait()
    total = slab_rx[0]
    for s in range(1, rows_n):
        total = total + slab_rx[s]
    gram_ref[...] = total
    for copy in copies:
        copy.wait()


def encoder_kernel(
    rx_ref, seen_ref, small_ref, square_ref, z_ref, amount_ref, clist, count_ref, cnt_v, cnt_s, wide, second, zacc, low_a, low_b, sem
):
    sources = rx_ref.shape[0]
    per = rx_ref.shape[2] // TILE
    counts = bring_counts(seen_ref, cnt_v, cnt_s, sem)
    small = small_ref[...]
    first = triple_weights(weight_block(small[0:5] * GELU_SCALE, small[10:11] * GELU_SCALE, 0))
    wide[0] = column(small[11:12], SPAN)
    wide[1] = column(small[12:13], SPAN)
    wide[2] = column(small[13:14], SPAN)
    second[...] = square_ref[0].T.astype(BF16)
    zacc[...] = jnp.zeros_like(zacc)
    clist[:, 0:TILE] = jnp.zeros((8, TILE), F32)
    counts.wait()

    def place_tile(s, offset):
        for k in range(per):
            amount = cnt_s[s, k]
            put(clist, rx_ref[s, 0:5, k * TILE : (k + 1) * TILE], k + 1.0, offset, 0, amount)
            offset = offset + amount
        return offset

    num_c = lax.fori_loop(0, sources, place_tile, jnp.int32(0))
    clear_tail(clist, num_c)
    count_ref[0] = num_c
    ids = lax.broadcasted_iota(jnp.int32, (16, SPAN), 0).astype(F32) + 1.0

    def window(t):
        return clist[:, pl.ds(pl.multiple_of(t * SPAN, SPAN), SPAN)]

    def begin(t, low):
        pre = dot_nn(first, triple_from_list(window(t)))
        parts = []
        total = jnp.zeros((1, SPAN), F32)
        for c in range(0, WIDTH, HALF):
            parts.append(gelu_twice(pre[c : c + HALF]))
            total = total + jnp.sum(parts[-1], axis=0, keepdims=True)
            yield
        mean = total * (1.0 / WIDTH)
        total = jnp.zeros((1, SPAN), F32)
        for c in range(len(parts)):
            parts[c] = parts[c] - mean
            total = total + jnp.sum(parts[c] * parts[c], axis=0, keepdims=True)
        inverse = lax.rsqrt(total * (1.0 / WIDTH) + NORM_EPS)
        yield
        for c in range(len(parts)):
            rows = slice(c * HALF, (c + 1) * HALF)
            low[rows, :] = (parts[c] * inverse * wide[0, rows, :] + wide[1, rows, :]).astype(BF16)
        yield

    def finish(t, low):
        pre = dot_nn(second[...], low[...])
        yield
        highs, rests = [], []
        for c in range(0, WIDTH, HALF):
            encoded = plain_twice(pre[c : c + HALF] + wide[2, c : c + HALF, :])
            highs.append(encoded.astype(BF16))
            rests.append((encoded - highs[-1].astype(F32)).astype(BF16))
            yield
        owner = jnp.where(ids == window(t)[7:8], 1.0, 0.0).astype(BF16)
        right = jnp.concatenate([jnp.concatenate(highs, axis=0), jnp.concatenate(rests, axis=0)], axis=1)
        zacc[...] += dot_nt(right, jnp.concatenate([owner, owner], axis=1))
        yield

    def pair(p, carry):
        weave("BAABABBABABA", begin(2 * p + 1, low_b), finish(2 * p, low_a))
        weave("BAABABBABABA", begin(2 * p + 2, low_a), finish(2 * p + 1, low_b))
        return carry

    spans = (num_c + SPAN - 1) // SPAN
    weave("", begin(0, low_a), iter(()))
    lax.fori_loop(0, spans // 2, pair, 0)

    @pl.when(lax.rem(spans, 2) == 1)
    def last():
        weave("", iter(()), finish(spans - 1, low_a))

    z_ref[...] = turned(zacc[...])[0:8] * 0.5
    total = seen_ref[0, 0:1, :]
    for s in range(1, sources):
        total = total + seen_ref[s, 0:1, :]
    amount_ref[...] = jnp.broadcast_to(total, (8, 128))


def theta_kernel(
    n, z_ref, amount_ref, head_ref, tiles_ref, share_ref, theta_ref, gen_ref, z8_ref, inv_ref, reg_ref,
    rx_ref, seen_ref, zall, nall, head, give, turn, load_sem, sems,
):
    me = lax.axis_index("ctx")
    peers = ring_peers("ctx", n)
    chunk = head.shape[2]
    per = chunk // WIDTH

    def load(k):
        return pltpu.make_async_copy(head_ref.at[:, pl.ds(k * chunk, chunk)], head.at[k], load_sem.at[k])

    for k in range(head.shape[0]):
        load(k).start()
    greet([{"ctx": peer} for peer in peers])
    top = pl.ds(0, 1)
    latents = send_all("ctx", n, lambda peer: z_ref, zall.at[me], sems.at[0], sems.at[1])
    latents += send_all(
        "ctx", n, lambda peer: amount_ref.at[top, :], nall.at[me, top, :], sems.at[6], sems.at[7]
    )
    pixels = send_all(
        "ctx",
        n,
        lambda peer: tiles_ref.at[peer, pl.ds(0, 5), :],
        rx_ref.at[me, pl.ds(0, 5), :],
        sems.at[2],
        sems.at[3],
    )
    pixels += send_all(
        "ctx", n, lambda peer: share_ref.at[peer, top, :], seen_ref.at[me, top, :], sems.at[8], sems.at[9]
    )
    zall[me] = z_ref[...]
    nall[me, 0:1, :] = amount_ref[0:1, :]
    rx_ref[me, 0:5, :] = tiles_ref[me, 0:5, :]
    seen_ref[me, 0:1, :] = share_ref[me, 0:1, :]
    for copy in latents:
        copy.wait()
    total = zall[0]
    amounts = nall[0, 0:1, :]
    for s in range(1, n):
        total = total + zall[s]
        amounts = amounts + nall[s, 0:1, :]
    lanes = lax.broadcasted_iota(jnp.int32, (8, 128), 1)
    rows = lax.broadcasted_iota(jnp.int32, (8, 128), 0)
    counts = jnp.sum(jnp.where(lanes == rows, amounts, 0.0), axis=1, keepdims=True) + 1.0
    latent = (total / counts).astype(BF16).astype(F32)
    z8_ref[...] = latent
    inv_ref[...] = jnp.broadcast_to(0.5 / counts, (8, WIDTH))
    left = jnp.concatenate([latent, jnp.zeros((8, WIDTH), F32)], axis=0).astype(BF16)
    regular = jnp.zeros((8, WIDTH), F32)
    for k in range(head.shape[0]):
        load(k).wait()
        part = dot_nn(left, head[k].astype(BF16))[0:8]
        for i in range(per):
            piece = part[:, i * WIDTH : (i + 1) * WIDTH]
            theta_ref[pl.ds((k * per + i) * 8, 8), :] = piece
            for half in range(2):
                turn[half, pl.ds((k * per + i) * 8, 8), :] = piece[:, half * 128 : half * 128 + 128]
            regular = regular + piece * piece
    reg_ref[...] = regular
    height = WIDTH // n
    for g in range(n):
        for half in range(2):
            give[g, :, half * 128 : half * 128 + 128] = turn[half, pl.ds(g, height, stride=8), :].astype(BF16)
    mine = pl.ds(pl.multiple_of(me * height, height), height)
    parts = fenced(
        plan_all("ctx", n, lambda peer: give.at[peer], gen_ref.at[mine, :], sems.at[4], sems.at[5])
    )
    gen_ref[mine, :] = give[me]
    for copy in pixels + parts:
        copy.wait()


def siren_kernel(
    live_all, len_ref, rx_ref, seen_ref, gen_ref, z_ref, small_ref, square_ref, out_ref, bias_ref, narrow_ref,
    q_ref, cnt_v, cnt_s, inner, shift, sa, sb, ca, cb, ma, mb, na, nb, acc_g, acc_c, acc_o, acc_e, sem,
):
    sin_in, cos_in, sin_mid, cos_mid = (sa, sb), (ca, cb), (ma, mb), (na, nb)
    me = lax.axis_index("ctx")
    per = rx_ref.shape[2] // TILE
    groups = len_ref.shape[2]
    length = len_ref[0, me // groups, lax.rem(me, groups)]
    counts = bring_counts(seen_ref, cnt_v, cnt_s, sem)
    small = small_ref[...]
    coord = triple_weights(weight_block(small[5:7] * TURN, small[14:15] * TURN, 3))
    latent = jnp.broadcast_to(z_ref[pl.ds(me, 1), :], (16, WIDTH)).astype(BF16)
    bias = dot_nn(latent, square_ref[1].astype(BF16))[0:1]
    inner[...] = gen_ref[...].astype(F32).T.astype(BF16)
    shift[...] = column(bias * TURN, SPAN)
    final = small[7:10].astype(BF16).astype(F32)
    final_rows = jnp.concatenate([final, jnp.zeros((13, WIDTH), F32)], axis=0).astype(BF16)
    large = final * 30.0
    high = large.astype(BF16).astype(F32)
    gap = jnp.zeros((5, WIDTH), F32)
    final_cols = jnp.concatenate([high, gap, large - high, jnp.zeros((117, WIDTH), F32)], axis=0).T.astype(BF16)[:, 0:16]
    for ref in (acc_g, acc_c, acc_o, acc_e):
        ref[...] = jnp.zeros_like(ref)
    scale = 2.0 / live_all
    ones = jnp.ones((16, SPAN), BF16)
    q_ref[:, 0:TILE] = jnp.zeros((8, TILE), F32)
    counts.wait()

    def place_tile(s, offset):
        for k in range(per):
            amount = cnt_s[s, per + k]
            put(q_ref, rx_ref[s, 0:5, k * TILE : (k + 1) * TILE], 0.0, offset, cnt_s[s, k], amount)
            offset = offset + amount
        return offset

    num_q = lax.fori_loop(0, (length + per * TILE - 1) // (per * TILE), place_tile, jnp.int32(0))
    clear_tail(q_ref, num_q)
    ids = lax.broadcasted_iota(jnp.int32, (8, SPAN), 0)

    def window(t):
        return q_ref[:, pl.ds(pl.multiple_of(t * SPAN, SPAN), SPAN)]

    def ahead(t, k):
        turns = dot_nn(coord, triple_from_list(window(t)))
        for c in range(0, WIDTH, WIDTH):
            s_in, c_in = sine_pair(turns[c : c + WIDTH])
            sin_in[k][c : c + WIDTH, :] = s_in.astype(BF16)
            cos_in[k][c : c + WIDTH, :] = c_in
            yield
        turns = dot_nn(inner[...], sin_in[k][...])
        yield
        for c in range(0, WIDTH, WIDTH):
            s_mid, c_mid = sine_pair(turns[c : c + WIDTH] * TURN + shift[c : c + WIDTH, :])
            sin_mid[k][c : c + WIDTH, :] = s_mid.astype(BF16)
            cos_mid[k][c : c + WIDTH, :] = c_mid
            yield

    def back_part(t, k):
        rows = window(t)
        pred = dot_nn(final_rows, sin_mid[k][...])[0:8]
        error = jnp.where(ids < 3, (pred - rows) * rows[6:7], 0.0)
        acc_e[...] += error * error
        slope = (error * scale).astype(BF16).astype(F32)
        slope = jnp.concatenate([slope, slope], axis=0).astype(BF16)
        yield
        acc_o[...] += dot_nt(sin_mid[k][...], slope)
        back = (cos_mid[k][...] * dot_nn(final_cols, slope)).astype(BF16)
        yield
        grads = dot_nn(gen_ref[...], back)
        yield
        outer = cos_in[k][...] * grads
        high = outer.astype(BF16)
        low = (outer - high.astype(F32)).astype(BF16)
        yield
        acc_g[...] += dot_nt(jnp.concatenate([sin_in[k][...], ones], axis=0), back)
        yield
        left = jnp.concatenate(split3(rows) + (jnp.zeros((8, SPAN), F32),), axis=0).astype(BF16)
        acc_c[...] += dot_nt(jnp.concatenate([high, low], axis=1), jnp.concatenate([left, left], axis=1))
        yield

    def pair(p, carry):
        weave("BABABABAABABAA", ahead(2 * p + 1, 1), back_part(2 * p, 0))
        weave("BABABABAABABAA", ahead(2 * p + 2, 0), back_part(2 * p + 1, 1))
        return carry

    spans = (num_q + SPAN - 1) // SPAN
    weave("", ahead(0, 0), iter(()))
    lax.fori_loop(0, spans // 2, pair, 0)

    @pl.when(lax.rem(spans, 2) == 1)
    def last():
        weave("", iter(()), back_part(spans - 1, 0))

    out_ref[...] = acc_g[0:WIDTH, :]
    bias_ref[...] = acc_g[WIDTH : WIDTH + 8, :]
    coords = turned(acc_c[...])
    coords = (coords[0:8] + coords[8:16] + coords[16:24]) * 30.0
    narrow_ref[0:2, :] = coords[3:5]
    narrow_ref[2:5, :] = turned(acc_o[...])[0:3]
    narrow_ref[5:6, :] = coords[6:7]
    narrow_ref[6:7, :] = jnp.broadcast_to(jnp.sum(acc_e[...]), (1, WIDTH))
    narrow_ref[7:8, :] = jnp.zeros((1, WIDTH), F32)


def latent_kernel(
    n, groups_all, part_ref, bias_ref, theta_ref, head_ref, mom_ref, z8_ref, gram_ref,
    dz_ref, tall_ref, cross_ref,
    rx, rxb, turn, head, mom, low_head, low_mom, rxz, dz_own, lefts, rxs, slab_sum, load_sem, mom_sem, sems,
):
    me = lax.axis_index("ctx")
    peers = ring_peers("ctx", n)
    chunk = head.shape[2]
    per = chunk // WIDTH
    height = WIDTH // n

    def load(k):
        return pltpu.make_async_copy(head_ref.at[:, pl.ds(k * chunk, chunk)], head.at[k], load_sem.at[k])

    def load_mom(k):
        return pltpu.make_async_copy(mom_ref.at[:, pl.ds(k * chunk, chunk)], mom.at[k], mom_sem.at[k])

    for k in range(head.shape[0]):
        load(k).start()
    for k in range(head.shape[0]):
        load_mom(k).start()
    greet([{"ctx": peer} for peer in peers])
    mine = pl.ds(pl.multiple_of(me * height, 8), height)
    parts = send_all(
        "ctx",
        n,
        lambda peer: part_ref.at[pl.ds(pl.multiple_of(peer * height, 8), height), :],
        rx.at[mine, :],
        sems.at[0],
        sems.at[1],
    )
    biases = send_all(
        "ctx", n, lambda peer: bias_ref.at[pl.ds(0, 1), :], rxb.at[me, pl.ds(0, 1), :], sems.at[6], sems.at[7]
    )
    slab = gram_ref.shape[0] // n
    grams = send_all(
        "ctx",
        n,
        lambda peer: gram_ref.at[pl.ds(pl.multiple_of(peer * slab, slab), slab), :],
        rxs.at[me],
        sems.at[4],
        sems.at[5],
    )
    rx[mine, :] = part_ref[mine, :]
    rxb[me, 0:1, :] = bias_ref[0:1, :]
    rxs[me] = gram_ref[pl.ds(pl.multiple_of(me * slab, slab), slab), :]
    for k in range(head.shape[0]):
        load(k).wait()
        for i in range(per):
            low_head[k * per + i] = head[k, :, i * WIDTH : (i + 1) * WIDTH].astype(BF16)
    for k in range(head.shape[0]):
        load_mom(k).wait()
        for i in range(per):
            for j, part in enumerate(three(mom[k, :, i * WIDTH : (i + 1) * WIDTH].T)):
                low_mom[j, k * per + i] = part

    def slab_total():
        for copy in grams:
            copy.wait()
        total = rxs[0]
        for s in range(1, n):
            total = total + rxs[s]
        slab_sum[...] = total
        tall_ref[height + 2 + me] = total

    slabs = fenced(
        plan_all("ctx", n, lambda peer: slab_sum, tall_ref.at[height + 2 + me], sems.at[8], sems.at[9]), slab_total
    )
    for copy in biases + parts:
        copy.wait()
    turn[0] = rx[:, 0:128]
    turn[1] = rx[:, 128:256]

    def across(i):
        return jnp.concatenate([turn[half, pl.ds(i, 8, stride=height), :] for half in range(2)], axis=1)

    blank = jnp.zeros((8, WIDTH), F32)
    for i in range(height):
        rows = across(i) + theta_ref[pl.ds(i * 8, 8), :] * (1.0 / groups_all)
        tall_ref[i] = rows
        lefts[i] = jnp.concatenate(split3(rows) + (blank,), axis=0).astype(BF16)
    tall_ref[height] = z8_ref[...]
    tall_ref[height + 1] = jnp.concatenate([rxb[s, 0:1, :] for s in range(n)], axis=0)
    totals = [jnp.zeros((32, WIDTH), F32)] * 2
    for i in range(height):
        totals[i % 2] = totals[i % 2] + dot_nt(lefts[i], low_head[i])
    total = totals[0] + totals[1]
    dz_own[...] = total[0:8] + total[8:16] + total[16:24]
    terms = fenced(plan_all("ctx", n, lambda peer: dz_own, rxz.at[me], sems.at[2], sems.at[3]))
    rxz[me] = dz_own[...]

    def mix(i, carry):
        totals = list(carry)
        for k in range(4):
            for j in range(3):
                totals[k % 2] = totals[k % 2] + dot_nn(lefts[4 * i + k], low_mom[j, 4 * i + k])
        return tuple(totals)

    empty = jnp.zeros((32, WIDTH), F32)
    totals = lax.fori_loop(0, height // 4, mix, (empty, empty))
    total = totals[0] + totals[1]
    cross_ref[...] = total[0:8] + total[8:16] + total[16:24]
    for copy in terms:
        copy.wait()
    total = rxz[0]
    for s in range(1, n):
        total = total + rxz[s]
    dz_ref[...] = total
    for copy in slabs:
        copy.wait()


def encoder_back_kernel(
    count_ref, c_ref, small_ref, square_ref, dz_ref, inv_ref, tall_ref, narrow_ref, reg_ref, out_ref, thin_ref,
    wide, second, spread, ua, ub, ka, kb, na, nb, ga, gb, acc_s, acc_f, acc_g, rows_out,
):
    unit, chain, normed, grad = (ua, ub), (ka, kb), (na, nb), (ga, gb)
    num_c = count_ref[0]
    small = small_ref[...]
    first = triple_weights(weight_block(small[0:5] * GELU_SCALE, small[10:11] * GELU_SCALE, 0))
    plain = square_ref[0].astype(BF16)
    low = plain.astype(F32)
    second[...] = low.T.astype(BF16)
    height = tall_ref.shape[0] - 10
    bias_back = full_nt(tall_ref[height + 1], square_ref[1].astype(BF16).astype(F32))
    latent_back = (dz_ref[...] + bias_back) * inv_ref[...]
    wide[0] = column(small[11:12], SPAN)
    wide[1] = column(small[12:13], SPAN)
    latent_cols = jnp.concatenate(split3(latent_back) + (jnp.zeros((104, WIDTH), F32),), axis=0).T.astype(BF16)[:, 0:32]
    wide[2] = column(small[13:14], SPAN)
    centre = split3(full_nn(jnp.broadcast_to(small[11:12], (8, WIDTH)), low) * (1.0 / WIDTH))
    rows = jnp.concatenate([part[0:1] for part in centre] + [jnp.zeros((13, WIDTH), F32)], axis=0)
    spread[...] = jnp.concatenate([plain, rows.astype(BF16)], axis=0)
    for ref in (acc_s, acc_f, acc_g):
        ref[...] = jnp.zeros_like(ref)
    ones = jnp.ones((16, SPAN), BF16)
    ids = lax.broadcasted_iota(jnp.int32, (8, SPAN), 0).astype(F32) + 1.0
    blank = jnp.zeros((8, SPAN), F32)

    def window(t):
        return c_ref[:, pl.ds(pl.multiple_of(t * SPAN, SPAN), SPAN)]

    def ahead(t, k):
        pre = dot_nn(first, triple_from_list(window(t)))
        parts, slopes = [], []
        total = jnp.zeros((1, SPAN), F32)
        for c in range(0, WIDTH, QUARTER):
            value, slope = gelu_both(pre[c : c + QUARTER])
            parts.append(value)
            slopes.append(slope)
            total = total + jnp.sum(value, axis=0, keepdims=True)
            yield
        mean = total * (1.0 / WIDTH)
        total = jnp.zeros((1, SPAN), F32)
        for c in range(len(parts)):
            parts[c] = parts[c] - mean
            total = total + jnp.sum(parts[c] * parts[c], axis=0, keepdims=True)
        inverse = lax.rsqrt(total * (1.0 / WIDTH) + NORM_EPS)
        yield
        scale = inverse * GELU_SCALE
        for c in range(len(parts)):
            rows = slice(c * QUARTER, (c + 1) * QUARTER)
            value = parts[c] * inverse
            unit[k][rows, :] = value
            normed[k][rows, :] = (value * wide[0, rows, :] + wide[1, rows, :]).astype(BF16)
            chain[k][rows, :] = slopes[c] * scale
        yield
        owner = jnp.where(ids == window(t)[7:8], 1.0, 0.0)
        owner = jnp.concatenate([owner, owner, owner, blank], axis=0).astype(BF16)
        pre = dot_nn(second[...], normed[k][...])
        outer = dot_nn(latent_cols, owner)
        yield
        for c in range(0, WIDTH, QUARTER):
            rows = slice(c, c + QUARTER)
            grad[k][rows, :] = (plain_slope(pre[rows] + wide[2, rows, :]) * outer[rows]).astype(BF16)
            yield

    def back_part(t, k):
        slopes = dot_nn(spread[...], grad[k][...])
        yield
        acc_s[...] += dot_nt(jnp.concatenate([normed[k][...], ones], axis=0), grad[k][...])
        yield
        means = jnp.sum(slopes[WIDTH : WIDTH + 8], axis=0, keepdims=True)
        total = jnp.zeros((1, SPAN), F32)
        parts = []
        for c in range(0, WIDTH, QUARTER):
            rows = slice(c, c + QUARTER)
            parts.append(slopes[rows] * wide[0, rows, :] - means)
            acc_g[rows, :] += slopes[rows] * unit[k][rows, :]
            total = total + jnp.sum(parts[-1] * unit[k][rows, :], axis=0, keepdims=True)
        mean = total * (1.0 / WIDTH)
        yield
        highs, rests = [], []
        for c in range(len(parts)):
            rows = slice(c * QUARTER, (c + 1) * QUARTER)
            outer = (parts[c] - unit[k][rows, :] * mean) * chain[k][rows, :]
            highs.append(outer.astype(BF16))
            rests.append((outer - highs[-1].astype(F32)).astype(BF16))
        yield
        left = jnp.concatenate(split3(window(t)) + (jnp.zeros((8, SPAN), F32),), axis=0).astype(BF16)
        right = jnp.concatenate([jnp.concatenate(highs, axis=0), jnp.concatenate(rests, axis=0)], axis=1)
        acc_f[...] += dot_nt(right, jnp.concatenate([left, left], axis=1))
        yield

    def pair(p, carry):
        weave("ABABAAAABABABAA", ahead(2 * p + 1, 1), back_part(2 * p, 0))
        weave("ABABAAAABABABAA", ahead(2 * p + 2, 0), back_part(2 * p + 1, 1))
        return carry

    spans = (num_c + SPAN - 1) // SPAN
    weave("", ahead(0, 0), iter(()))
    lax.fori_loop(0, spans // 2, pair, 0)

    @pl.when(lax.rem(spans, 2) == 1)
    def last():
        weave("", iter(()), back_part(spans - 1, 0))

    firsts = turned(acc_f[...])
    firsts = firsts[0:8] + firsts[8:16] + firsts[16:24]
    bias_grad = acc_s[WIDTH : WIDTH + 8]
    shift_grad = full_nt(bias_grad, low)
    gain_grad = full_nt(jnp.ones((8, SPAN), F32), acc_g[...])
    rows_out[0:5, :] = firsts[0:5]
    rows_out[5:10, :] = narrow_ref[0:5, :]
    rows_out[10:11, :] = firsts[6:7]
    rows_out[11:12, :] = gain_grad[0:1]
    rows_out[12:13, :] = shift_grad[0:1]
    rows_out[13:14, :] = bias_grad[0:1]
    rows_out[14:15, :] = narrow_ref[5:6, :]
    lane = lax.broadcasted_iota(jnp.int32, (1, WIDTH), 1)
    regular = jnp.broadcast_to(jnp.sum(reg_ref[...]), (1, WIDTH))
    rows_out[15:16, :] = jnp.where(lane == 0, narrow_ref[6:7, :], jnp.where(lane == 1, regular, 0.0))
    for q in range(32):
        out_ref[q // 16, q % 16] = acc_s[8 * q : 8 * q + 8, :]
        lanes = slice((q % 2) * 128, (q % 2) * 128 + 128)
        thin_ref[q // 16, q % 16, 0:1, :] = rows_out[q // 2 : q // 2 + 1, lanes]


def newton(gram, sharp):
    ids = lax.broadcasted_iota(jnp.int32, (WIDTH, WIDTH), 0) == lax.broadcasted_iota(jnp.int32, (WIDTH, WIDTH), 1)
    scale = 1.0 / (jnp.sqrt(jnp.sum(jnp.where(ids, gram, 0.0))) + 1e-07)
    sides = (slice(0, WIDTH // 2), slice(WIDTH // 2, WIDTH))
    state = [gram[side] * (scale * scale) for side in sides]
    unit = [jnp.where(ids[side], first_coef, 0.0) for side in sides]

    def joined(halves):
        return [jnp.concatenate(pair, axis=0) for pair in zip(*halves)]

    product = None
    for k in range(NS_STEPS):
        times = six if k < sharp else few
        parts = [three(one) for one in state]
        whole = joined(parts)
        square = [few(part, whole) for part in parts]
        yield None
        poly = [unit[j] + second_coef * state[j] + third_coef * square[j] for j in range(2)]
        left = [three(one) for one in poly]
        if k + 1 < NS_STEPS:
            half = [times(one, whole) for one in left]
            yield None
        if k == 0:
            product = poly
        else:
            right = joined([three(one) for one in product])
            product = [times(one, right) for one in left]
        if k + 1 < NS_STEPS:
            yield None
            outer = joined(left)
            state = [times(three(one), outer) for one in half]
            yield None
    yield jnp.concatenate([one * scale for one in product], axis=0)


def drain(chain):
    result = None
    for result in chain:
        pass
    return result


def square_rows(sum_ref):
    return jnp.concatenate([sum_ref[q // 16, q % 16] for q in range(32)], axis=0)


def small_rows(sum_ref):
    halves = [sum_ref[q // 16, q % 16, 0:1, :] for q in range(32)]
    return jnp.concatenate(
        [jnp.concatenate([halves[2 * k], halves[2 * k + 1]], axis=1) for k in range(16)], axis=0
    )


def reduce_kernel(
    n, rows_n, grad_ref, thin_ref, own_ref, far_ref, cross_ref, smom_ref,
    sum_ref, thin_sum, tall_ref, move_ref,
    rxh, half_sum, rxq, fin, rxh_thin, half_thin, rxq_thin, fin_thin, mixed, rxm, rxc, rxx, sems, dsems, csems, qsems,
):
    me = lax.axis_index("ctx")
    r = lax.axis_index("dp")
    chips = (rows_n // 2) * n
    par = lax.rem(r, 2)
    chip = (r // 2) * n + me
    far = lax.rem(r + rows_n // 2, rows_n)
    near = r + 1 - 2 * par
    diag = lax.rem(near + rows_n // 2, rows_n)
    places_here = [pl.ds(pl.multiple_of(place * 8, 8), 8) for place in (r, far)]
    others = [lax.rem(chip + d, chips) for d in range(1, chips)]
    places = [{"dp": 2 * (other // n) + par, "ctx": lax.rem(other, n)} for other in others]
    count = hail(places + [{"dp": near}, {"dp": diag}])
    for i in range(own_ref.shape[0]):
        for rows, ref in zip(places_here, (own_ref, far_ref)):
            tall_ref[i, rows, :] = ref[i]
    height = own_ref.shape[0] - 10

    def advance(count):
        for step in range(count):
            next(side)

    def near_copy(source, target, j):
        return pltpu.make_async_remote_copy(
            src_ref=source,
            dst_ref=target,
            send_sem=csems.at[0, j],
            recv_sem=csems.at[1, j],
            device_id={"dp": near},
            device_id_type=MESH,
        )

    def chip_copies(source, target, k):
        return [
            copy for pair in zip(*(chip_plan(*plan, k + 2 * j) for j, plan in enumerate(zip(source, target)))) for copy in pair
        ]

    def chip_plan(source, target, k):
        return [
            pltpu.make_async_remote_copy(
                src_ref=source(other),
                dst_ref=target,
                send_sem=qsems.at[2 * k, d],
                recv_sem=qsems.at[2 * k + 1, d],
                device_id=place,
                device_id_type=MESH,
            )
            for d, (other, place) in enumerate(zip(others, places))
        ]

    top = pl.ds(0, 1)
    halves = [
        near_copy(grad_ref.at[1 - par], rxh, 0),
        near_copy(thin_ref.at[1 - par, :, top, :], rxh_thin.at[:, top, :], 4),
    ]
    crosses = plan_all("ctx", n, lambda peer: cross_ref, rxx.at[me], sems.at[0], sems.at[1])
    terms = plan_all("ctx", n, lambda peer: mixed, rxm.at[me], sems.at[2], sems.at[3])
    blocks = [
        near_copy(tall_ref.at[:, rows, :], tall_ref.at[:, rows, :], j + 1) for j, rows in enumerate(places_here)
    ]
    fenced(halves + blocks + crosses, lambda: meet(count))
    rxx[me] = cross_ref[...]

    def first_sum():
        for copy in halves:
            copy.wait()
        half_sum[...] = grad_ref[par] + rxh[...]
        half_thin[:, 0:1, :] = thin_ref[par, :, 0:1, :] + rxh_thin[:, 0:1, :]
        rxq[chip] = half_sum[chip]
        rxq_thin[chip, 0:1, :] = half_thin[chip, 0:1, :]

    scattered = fenced(
        chip_copies(
            (lambda other: half_sum.at[other], lambda other: half_thin.at[other, top, :]),
            (rxq.at[chip], rxq_thin.at[chip, top, :]),
            0,
        ),
        first_sum,
    )
    for copy in blocks:
        copy.wait()
    inners = [jnp.zeros((96, 96), F32)] * 2
    for i in range(height):
        stack = jnp.concatenate(split3(tall_ref[i]), axis=0).astype(BF16)
        inners[i % 2] = inners[i % 2] + dot_nt(stack, stack)
    inner = inners[0] + inners[1]
    inner = inner[0:32] + inner[32:64] + inner[64:96]
    inner = inner[:, 0:32] + inner[:, 32:64] + inner[:, 64:96]
    mixed[...] = jnp.concatenate([inner, jnp.zeros((32, 96), F32)], axis=1)
    rxm[me] = mixed[...]
    fenced(terms)
    latents = tall_ref[height]
    bias_moment = momentum_rate * smom_ref[1] + full_nn(latents.T, tall_ref[height + 1])
    side = newton(gram_six(three(bias_moment)), NS_STEPS)
    advance(4)

    def share():
        for copy in crosses:
            copy.wait()
        total = rxx[0]
        for s in range(1, n):
            total = total + rxx[s]
        rxc[r] = total

    shared = fenced(
        plan_all("dp", rows_n, lambda peer: rxc.at[r], rxc.at[r], dsems.at[0], dsems.at[1]), share
    )
    advance(7)

    def second_sum():
        for copy in scattered:
            copy.wait()
        total = rxq[0]
        thin = rxq_thin[0, 0:1, :]
        for s in range(1, chips):
            total = total + rxq[s]
            thin = thin + rxq_thin[s, 0:1, :]
        fin[...] = total
        fin_thin[0:1, :] = thin
        sum_ref[par, chip] = total
        thin_sum[par, chip, 0:1, :] = thin

    gathered = fenced(
        chip_copies(
            (lambda other: fin, lambda other: fin_thin.at[top, :]),
            (sum_ref.at[par, chip], thin_sum.at[par, chip, top, :]),
            1,
        ),
        second_sum,
    )
    advance(6)
    move_ref[1] = next(side)
    for copy in terms:
        copy.wait()
    total = rxm[0]
    for s in range(1, n):
        total = total + rxm[s]
    inner = total[:, 0:32]
    for copy in shared:
        copy.wait()
    cross = jnp.concatenate([rxc[s] for s in range(rows_n)], axis=0)
    weight = momentum_rate * cross + 0.5 * full_nn(inner, latents)
    half = full_nn(latents.T, weight)
    slabs = [tall_ref[height + 2 + t, 8 * s : 8 * s + 8, :] for s in range(rows_n) for t in range(n)]
    gram = (momentum_rate * momentum_rate) * jnp.concatenate(slabs, axis=0) + (half + half.T)
    side = newton(gram, HEAD_SHARP)
    advance(11)

    def all_here():
        for copy in gathered:
            copy.wait()

    last = fenced(
        [
            near_copy(sum_ref.at[par], sum_ref.at[par], 3),
            near_copy(thin_sum.at[par, :, top, :], thin_sum.at[par, :, top, :], 5),
        ],
        all_here,
    )
    advance(6)
    move_ref[0] = next(side)
    for copy in last:
        copy.wait()


def update_kernel(
    live_all, groups_all, mom_ref, head_ref, tall_ref, move_ref, sum_ref, thin_ref, square_ref, smom_ref,
    small_ref, mmom_ref, mvar_ref,
    mom_out, head_out, copy_out, smom_out, square_out, scopy_out, mmom_out, mvar_out, small_out, mcopy_out,
    loss_out, mom, head, low_copy, left, wide, store_sem,
):
    ring, unused, chunk = mom.shape
    chunks = mom_ref.shape[1] // chunk
    per = chunk // WIDTH

    def stores(k):
        lanes = pl.ds(k * chunk, chunk)
        return [
            pltpu.make_async_copy(source.at[k % ring], target.at[:, lanes], store_sem.at[j, k % ring])
            for j, (source, target) in enumerate(((mom, mom_out), (head, head_out), (low_copy, copy_out)))
        ]

    height = tall_ref.shape[0] - 10
    latents = tall_ref[height]
    rows = jnp.concatenate([latents] * 3 + [jnp.zeros((32, WIDTH), F32)], axis=0)
    left[...] = rows.T.astype(BF16)
    ids = lax.broadcasted_iota(jnp.int32, (WIDTH, WIDTH), 0) == lax.broadcasted_iota(jnp.int32, (WIDTH, WIDTH), 1)
    move = move_ref[0] * (-head_rate * 0.2 * WIDTH)
    centre = jnp.sum(jnp.where(ids, move, 0.0)) * (1.0 / WIDTH)
    wide[...] = jnp.concatenate(three(jnp.where(ids, move - centre, move))[0:2], axis=0)
    narrow = small_rows(thin_ref)
    stats = narrow[15:16]
    lane = lax.broadcasted_iota(jnp.int32, (1, WIDTH), 1)
    weight = jnp.where(lane == 0, 1.0 / live_all, jnp.where(lane == 1, reg_weight / groups_all, 0.0))
    loss_out[...] = jnp.broadcast_to(jnp.sum(stats * weight), loss_out.shape)
    moment, second, new = adam_update(small_ref[...], narrow[0:15], mmom_ref[...], mvar_ref[...])
    mmom_out[...] = moment
    mvar_out[...] = second
    small_out[...] = new
    mcopy_out[...] = new.astype(BF16)
    keep = 1.0 - head_rate * decay_rate

    grads = [square_rows(sum_ref), full_nn(latents.T, tall_ref[height + 1])]
    moments = [momentum_rate * smom_ref[k] + grads[k] for k in range(2)]
    side = newton(gram_six(three(moments[0])), NS_STEPS)
    for k in range(chunks):
        slot = k % ring
        if k >= ring:
            for copy in stores(k - ring):
                copy.wait()

        def begin_tile(i):
            lanes = slice(i * WIDTH, (i + 1) * WIDTH)
            wide_lanes = slice(k * chunk + i * WIDTH, k * chunk + (i + 1) * WIDTH)
            high, mid, low = three(tall_ref[k * per + i])
            right = jnp.concatenate([high, mid, low, jnp.zeros_like(high)], axis=0)
            moment = momentum_rate * mom_ref[:, wide_lanes] + dot_nn(left[...], right)
            mom[slot, :, lanes] = moment
            high = moment.astype(BF16)
            mid = (moment - high.astype(F32)).astype(BF16)
            return keep * head_ref[:, wide_lanes] + centre * moment, high, mid

        def finish_tile(i):
            lanes = slice(i * WIDTH, (i + 1) * WIDTH)
            base, high, mid = ready[i]
            first = dot_nn(wide[...], high)
            new = (first[0:WIDTH] + dot_nn(wide[0:WIDTH, :], mid)) + (first[WIDTH:] + base)
            head[slot, :, lanes] = new
            low_copy[slot, :, lanes] = new.astype(BF16)

        ready = [begin_tile(0), begin_tile(1)]
        for i in range(per):
            if i + 2 < per:
                ready.append(begin_tile(i + 2))
            finish_tile(i)
            if i < 3:
                next(side, None) if k * 3 + i < 17 else None
        for copy in stores(k):
            copy.start()
    for k, move in enumerate((drain(side), move_ref[1])):
        smom_out[k] = moments[k]
        old = square_ref[k]
        change = 0.2 * WIDTH**0.5 * six(three(move), three(moments[k])) + decay_rate * old
        new = old - square_rates[k] * change
        square_out[k] = new
        scopy_out[k] = new.astype(BF16)
    for k in range(chunks - ring, chunks):
        for copy in stores(k):
            copy.wait()


def shape(*dims, dtype=F32):
    return jax.ShapeDtypeStruct(dims, dtype)


def dma_sems(*dims):
    return pltpu.SemaphoreType.DMA(dims)


def remote_params(ident, room=50):
    return pltpu.CompilerParams(collective_id=ident, has_side_effects=True, vmem_limit_bytes=room * MIB)


def plain_params(room=16):
    return pltpu.CompilerParams(vmem_limit_bytes=room * MIB)


CHUNK = 1024
RING = 4


def call_scatter(n, rows_n, lengths, pixels, ctx_mask, head_mom):
    micro, groups, slots = pixels.shape[1], pixels.shape[2], pixels.shape[4]
    return pl.pallas_call(
        functools.partial(scatter_kernel, n, rows_n),
        out_shape=[
            shape(n, 8, slots),
            shape(n, 8, 128),
            shape(n, 8, slots),
            shape(n, 8, 128),
            shape(WIDTH // rows_n, WIDTH),
        ],
        in_specs=[hbm_spec()] * 4,
        out_specs=[vmem_spec()] * 5,
        scratch_shapes=[
            pltpu.SMEM(lengths.shape, jnp.int32),
            pltpu.VMEM((1, micro, 5, groups, slots), F32),
            pltpu.VMEM(ctx_mask.shape, jnp.int32),
            pltpu.VMEM((n, 8, slots), F32),
            pltpu.VMEM((n, 8, 128), F32),
            pltpu.VMEM((WIDTH, head_mom.shape[1] // rows_n), F32),
            pltpu.VMEM((WIDTH, WIDTH), F32),
            pltpu.VMEM((rows_n, WIDTH // rows_n, WIDTH), F32),
            pltpu.VMEM((TILE, TILE), BF16),
            dma_sems(micro, n - 1),
            dma_sems(micro, n - 1),
            dma_sems(),
            dma_sems(2, rows_n - 1),
            dma_sems(3),
            dma_sems(2, n - 1),
        ],
        compiler_params=remote_params(1, 50),
        name="scatter_pixels",
        cost_estimate=busy(14),
    )(lengths, jnp.transpose(pixels, (0, 1, 3, 2, 4)), ctx_mask, head_mom)


def call_encode(received, seen, small_params, square_w):
    cap = received.shape[0] * received.shape[2] + 5 * SPAN
    return pl.pallas_call(
        encoder_kernel,
        out_shape=[shape(8, WIDTH), shape(8, 128), shape(8, cap), shape(1, dtype=jnp.int32)],
        in_specs=[vmem_spec()] * 4,
        out_specs=[vmem_spec()] * 3 + [smem_spec()],
        scratch_shapes=[
            pltpu.VMEM((8, 128), jnp.int32),
            pltpu.SMEM((8, 128), jnp.int32),
            pltpu.VMEM((3, WIDTH, SPAN), F32),
            pltpu.VMEM((WIDTH, WIDTH), BF16),
            pltpu.VMEM((WIDTH, 16), F32),
            pltpu.VMEM((WIDTH, SPAN), BF16),
            pltpu.VMEM((WIDTH, SPAN), BF16),
            dma_sems(),
        ],
        compiler_params=plain_params(),
        name="encode",
        cost_estimate=busy(10),
    )(received, seen, small_params, square_w)


def call_generate(n, latent, amount, head_w, tiles, share):
    height = WIDTH // n
    chunks = head_w.shape[1] // CHUNK
    return pl.pallas_call(
        functools.partial(theta_kernel, n),
        out_shape=[
            shape(WIDTH, WIDTH),
            shape(WIDTH, WIDTH, dtype=BF16),
            shape(8, WIDTH),
            shape(8, WIDTH),
            shape(8, WIDTH),
            shape(*tiles.shape),
            shape(*share.shape),
        ],
        in_specs=[vmem_spec()] * 2 + [any_spec()] + [vmem_spec()] * 2,
        out_specs=[vmem_spec()] * 7,
        scratch_shapes=[
            pltpu.VMEM((n, 8, WIDTH), F32),
            pltpu.VMEM((n, 8, 128), F32),
            pltpu.VMEM((chunks, WIDTH, CHUNK), F32),
            pltpu.VMEM((n, height, WIDTH), BF16),
            pltpu.VMEM((2, WIDTH, 128), F32),
            dma_sems(chunks),
            dma_sems(10, n - 1),
        ],
        compiler_params=remote_params(2),
        name="generate",
        cost_estimate=busy(17),
    )(latent, amount, head_w, tiles, share)


def call_siren(n, live_all, lengths, received, seen, gen, latent, small_params, square_w):
    cap = received.shape[0] * received.shape[2] + 5 * SPAN
    return pl.pallas_call(
        functools.partial(siren_kernel, live_all),
        out_shape=[shape(WIDTH, WIDTH), shape(8, WIDTH), shape(8, WIDTH)],
        in_specs=[smem_spec()] + [vmem_spec()] * 6,
        out_specs=[vmem_spec()] * 3,
        scratch_shapes=[
            pltpu.VMEM((8, cap), F32),
            pltpu.VMEM((8, 128), jnp.int32),
            pltpu.SMEM((8, 128), jnp.int32),
            pltpu.VMEM((WIDTH, WIDTH), BF16),
            pltpu.VMEM((WIDTH, SPAN), F32),
            pltpu.VMEM((WIDTH, SPAN), BF16),
            pltpu.VMEM((WIDTH, SPAN), BF16),
            pltpu.VMEM((WIDTH, SPAN), F32),
            pltpu.VMEM((WIDTH, SPAN), F32),
            pltpu.VMEM((WIDTH, SPAN), BF16),
            pltpu.VMEM((WIDTH, SPAN), BF16),
            pltpu.VMEM((WIDTH, SPAN), F32),
            pltpu.VMEM((WIDTH, SPAN), F32),
            pltpu.VMEM((WIDTH + 16, WIDTH), F32),
            pltpu.VMEM((WIDTH, 32), F32),
            pltpu.VMEM((WIDTH, 16), F32),
            pltpu.VMEM((8, SPAN), F32),
            dma_sems(),
        ],
        compiler_params=plain_params(),
        name="siren",
        cost_estimate=busy(16),
    )(lengths, received, seen, gen, latent, small_params, square_w)


def call_latent(n, groups_all, part, bias, theta, head_w, head_mom, z8, gram_part):
    height = WIDTH // n
    chunks = head_w.shape[1] // CHUNK
    slab = gram_part.shape[0] // n
    return pl.pallas_call(
        functools.partial(latent_kernel, n, groups_all),
        out_shape=[
            shape(8, WIDTH),
            shape(height + 2 + n, 8, WIDTH),
            shape(8, WIDTH),
        ],
        in_specs=[vmem_spec()] * 3 + [any_spec()] * 2 + [vmem_spec()] * 2,
        out_specs=[vmem_spec()] * 3,
        scratch_shapes=[
            pltpu.VMEM((WIDTH, WIDTH), F32),
            pltpu.VMEM((n, 8, WIDTH), F32),
            pltpu.VMEM((2, WIDTH, 128), F32),
            pltpu.VMEM((chunks, WIDTH, CHUNK), F32),
            pltpu.VMEM((chunks, WIDTH, CHUNK), F32),
            pltpu.VMEM((height, WIDTH, WIDTH), BF16),
            pltpu.VMEM((3, height, WIDTH, WIDTH), BF16),
            pltpu.VMEM((n, 8, WIDTH), F32),
            pltpu.VMEM((8, WIDTH), F32),
            pltpu.VMEM((height, 32, WIDTH), BF16),
            pltpu.VMEM((n, slab, WIDTH), F32),
            pltpu.VMEM((slab, WIDTH), F32),
            dma_sems(chunks),
            dma_sems(chunks),
            dma_sems(10, n - 1),
        ],
        compiler_params=remote_params(3),
        name="latent_grads",
        cost_estimate=busy(18),
    )(part, bias, theta, head_w, head_mom, z8, gram_part)


def call_back(counts, clist, small_params, square_w, latent_grad, inverse, tall, narrow, regular):
    return pl.pallas_call(
        encoder_back_kernel,
        out_shape=[shape(2, 16, 8, WIDTH), shape(2, 16, 8, 128)],
        in_specs=[smem_spec()] + [vmem_spec()] * 8,
        out_specs=[vmem_spec()] * 2,
        scratch_shapes=[
            pltpu.VMEM((3, WIDTH, SPAN), F32),
            pltpu.VMEM((WIDTH, WIDTH), BF16),
            pltpu.VMEM((WIDTH + 16, WIDTH), BF16),
            pltpu.VMEM((WIDTH, SPAN), F32),
            pltpu.VMEM((WIDTH, SPAN), F32),
            pltpu.VMEM((WIDTH, SPAN), F32),
            pltpu.VMEM((WIDTH, SPAN), F32),
            pltpu.VMEM((WIDTH, SPAN), BF16),
            pltpu.VMEM((WIDTH, SPAN), BF16),
            pltpu.VMEM((WIDTH, SPAN), BF16),
            pltpu.VMEM((WIDTH, SPAN), BF16),
            pltpu.VMEM((WIDTH + 16, WIDTH), F32),
            pltpu.VMEM((WIDTH, 32), F32),
            pltpu.VMEM((WIDTH, SPAN), F32),
            pltpu.VMEM((16, WIDTH), F32),
        ],
        compiler_params=plain_params(),
        name="encode_back",
        cost_estimate=busy(16),
    )(counts, clist, small_params, square_w, latent_grad, inverse, tall, narrow, regular)


def call_reduce(n, rows_n, grads, thin, own, far, cross, square_mom):
    chips = (rows_n // 2) * n
    return pl.pallas_call(
        functools.partial(reduce_kernel, n, rows_n),
        out_shape=[
            shape(*grads.shape),
            shape(*thin.shape),
            shape(own.shape[0], 8 * rows_n, WIDTH),
            shape(2, WIDTH, WIDTH),
        ],
        in_specs=[vmem_spec()] * 6,
        out_specs=[vmem_spec()] * 4,
        scratch_shapes=[
            pltpu.VMEM((chips, 8, WIDTH), F32),
            pltpu.VMEM((chips, 8, WIDTH), F32),
            pltpu.VMEM((chips, 8, WIDTH), F32),
            pltpu.VMEM((8, WIDTH), F32),
            pltpu.VMEM((chips, 8, 128), F32),
            pltpu.VMEM((chips, 8, 128), F32),
            pltpu.VMEM((chips, 8, 128), F32),
            pltpu.VMEM((8, 128), F32),
            pltpu.VMEM((32, 128), F32),
            pltpu.VMEM((n, 32, 128), F32),
            pltpu.VMEM((rows_n, 8, WIDTH), F32),
            pltpu.VMEM((n, 8, WIDTH), F32),
            dma_sems(4, n - 1),
            dma_sems(2, rows_n - 1),
            dma_sems(2, 6),
            dma_sems(8, chips - 1),
        ],
        compiler_params=remote_params(4, 16),
        name="reduce_grads",
        cost_estimate=busy(24),
    )(grads, thin, own, far, cross, square_mom)


def call_update(
    live_all, groups_all, head_mom, head_w, tall, move, sums, thin_sums, square_w, square_mom, small_params,
    small_mom, small_var,
):
    columns = head_w.shape[1]
    small_copy = shape(15, WIDTH, dtype=BF16)
    square_copy = shape(2, WIDTH, WIDTH, dtype=BF16)
    loss = shape(1, 128)
    others = [square_mom, square_w, square_copy, small_mom, small_var, small_params, small_copy, loss]
    return pl.pallas_call(
        functools.partial(update_kernel, live_all, groups_all),
        out_shape=[shape(WIDTH, columns), shape(WIDTH, columns), shape(WIDTH, columns, dtype=BF16)]
        + [shape(*one.shape, dtype=one.dtype) for one in others],
        in_specs=[vmem_spec()] * 11,
        out_specs=[any_spec()] * 3 + [vmem_spec()] * 8,
        scratch_shapes=[
            pltpu.VMEM((RING, WIDTH, CHUNK), F32),
            pltpu.VMEM((RING, WIDTH, CHUNK), F32),
            pltpu.VMEM((RING, WIDTH, CHUNK), BF16),
            pltpu.VMEM((WIDTH, 128), BF16),
            pltpu.VMEM((2 * WIDTH, WIDTH), BF16),
            dma_sems(3, RING),
        ],
        compiler_params=plain_params(30),
        name="update_all",
        cost_estimate=busy(12),
    )(
        head_mom, head_w, tall, move, sums, thin_sums, square_w, square_mom, small_params, small_mom, small_var
    )


def grouped(
    pixels, lengths, ctx_mask, head_w, head_mom, square_w, square_mom, small_params, small_mom, small_var
):
    micro, groups, slots = pixels.shape[1], pixels.shape[2], pixels.shape[4]
    n = lax.axis_size("ctx")
    rows_n = lax.axis_size("dp")
    live_all = rows_n * micro * (groups * slots * n * 5 // 8)
    groups_all = rows_n * micro * groups
    received, seen, tiles, share, gram_part = call_scatter(n, rows_n, lengths, pixels, ctx_mask, head_mom)
    latent, amount, clist, counts = call_encode(received, seen, small_params, square_w)
    theta, gen, z8, inverse, regular, group_rows, group_seen = call_generate(
        n, latent, amount, head_w, tiles, share
    )
    part, bias, narrow = call_siren(
        n, live_all, lengths, group_rows, group_seen, gen, z8, small_params, square_w
    )
    latent_grad, own, cross = call_latent(
        n, groups_all, part, bias, theta, head_w, head_mom, z8, gram_part
    )
    far = lax.ppermute(own, "dp", [(r, (r + rows_n // 2) % rows_n) for r in range(rows_n)])
    grads, thin = call_back(
        counts, clist, small_params, square_w, latent_grad, inverse, own, narrow, regular
    )
    sums, thin_sums, tall, move = call_reduce(n, rows_n, grads, thin, own, far, cross, square_mom)
    updated = call_update(
        live_all, groups_all, head_mom, head_w, tall, move, sums, thin_sums, square_w, square_mom, small_params,
        small_mom, small_var,
    )
    (
        head_moment,
        head_new,
        head_copy,
        square_moment,
        square_new,
        square_copy,
        small_moment,
        small_second,
        small_new,
        small_copy,
        loss,
    ) = updated
    return (
        head_moment,
        head_new,
        head_copy,
        square_moment,
        square_new,
        square_copy,
        small_moment,
        small_second,
        small_new,
        small_copy,
        loss[0, 0],
    )


def local(pixels, lengths, ctx_mask, head_w, *rest):
    n = lax.axis_size("ctx")
    fits = (
        pixels.shape[1] * pixels.shape[2] == n
        and n == 8
        and lax.axis_size("dp") == 4
        and pixels.shape[4] == 2048
        and head_w.shape == (WIDTH, 8192)
    )
    chosen = grouped if fits else general
    return chosen(pixels, lengths, ctx_mask, head_w, *rest)


def solution(mesh):
    placed = (
        P("dp", None, None, None, "ctx"),
        P("dp", None, None),
        P("dp", None, None, "ctx"),
        P(None, "ctx"),
        P(None, "ctx"),
        P(),
        P(),
        P(),
        P(),
        P(),
    )
    return jax.shard_map(
        local,
        mesh=mesh,
        in_specs=placed,
        out_specs=(
            P(None, "ctx"),
            P(None, "ctx"),
            P(None, "ctx"),
            P(),
            P(),
            P(),
            P(),
            P(),
            P(),
            P(),
            P(),
        ),
        check_vma=False,
    )
```

```python
import functools

import jax
import jax.numpy as jnp
from jax import lax
from jax.experimental import pallas as pl
from jax.experimental.pallas import tpu as pltpu
from jax.sharding import PartitionSpec as P

NS_STEPS = 5
STEP = 10


exact_arithmetic_mode = lax.Precision.HIGHEST
reg_weight = 0.5
momentum_rate = 0.95
head_rate = 0.003
square_rates = (0.3, 0.02)
adam_rate = 0.05
beta_first = 0.9
beta_second = 0.999
decay_rate = 0.01
first_coef = 3.4445
second_coef = -4.775
third_coef = 2.0315


def layer_norm(values, gain_row, bias_row):
    centered = values - jnp.mean(values, axis=-1, keepdims=True)
    variance = jnp.mean(centered * centered, axis=-1, keepdims=True)
    return centered * lax.rsqrt(variance + 1e-05) * gain_row + bias_row


def ns_update(current, gram_matrix):
    polynomial = second_coef * gram_matrix + third_coef * jnp.einsum(
        "kij,kjl->kil", gram_matrix, gram_matrix, precision=exact_arithmetic_mode
    )
    return first_coef * current + jnp.einsum(
        "kij,kjl->kil", polynomial, current, precision=exact_arithmetic_mode
    )


def orthogonal_local(matrices):
    norms = jnp.sqrt(jnp.sum(matrices * matrices, axis=(1, 2), keepdims=True))
    current = matrices / (norms + 1e-07)
    for sweep in range(NS_STEPS):
        gram_matrix = jnp.einsum("kij,klj->kil", current, current, precision=exact_arithmetic_mode)
        current = ns_update(current, gram_matrix)
    return current


def head_orthogonal(moment):
    current = moment[None]
    total = lax.psum(jnp.sum(moment * moment), "ctx")
    current = current / (jnp.sqrt(total) + 1e-07)
    for sweep in range(NS_STEPS):
        gram_matrix = lax.psum(
            jnp.dot(current[0], current[0].T, precision=exact_arithmetic_mode), "ctx"
        )
        current = ns_update(current, gram_matrix[None])
    return current[0]


def adam_update(params, grad, moment, second_moment):
    moment_new = beta_first * moment + (1.0 - beta_first) * grad
    second_new = beta_second * second_moment + (1.0 - beta_second) * grad * grad
    corrected = (
        moment_new
        / (1.0 - beta_first**STEP)
        / (jnp.sqrt(second_new / (1.0 - beta_second**STEP)) + 1e-08)
    )
    return (moment_new, second_new, params - adam_rate * (corrected + decay_rate * params))


def encoder_forward(features, context, small_params, second_low):
    first_pre = (
        jnp.einsum("gpc,cd->gpd", features, small_params[0:5], precision=exact_arithmetic_mode)
        + small_params[10]
    )
    first_act, gelu_first = jax.vjp(jax.nn.gelu, first_pre)
    normed, norm_back = jax.vjp(layer_norm, first_act, small_params[11], small_params[12])
    normed_low = normed.astype(jnp.bfloat16)
    second = (
        jnp.einsum("gpd,de->gpe", normed_low, second_low, preferred_element_type=jnp.float32)
        + small_params[13]
    )
    encoded, gelu_second = jax.vjp(jax.nn.gelu, second)
    summed = jnp.einsum("gp,gpe->ge", context, encoded, precision=exact_arithmetic_mode)
    return (
        summed,
        jnp.sum(context, axis=1),
        (first_pre, gelu_first, norm_back, normed_low, gelu_second),
    )


def general(
    pixels,
    lengths,
    ctx_mask,
    head_w,
    head_mom,
    square_w,
    square_mom,
    small_params,
    small_mom,
    small_var,
):
    micro_count = pixels.shape[1]
    groups = pixels.shape[2]
    slot_count = pixels.shape[4]
    model_width = square_w.shape[1]
    live_all = (
        lax.axis_size("dp") * micro_count * (groups * slot_count * lax.axis_size("ctx") * 5 // 8)
    )
    groups_all = lax.axis_size("dp") * micro_count * groups
    slot_ids = lax.axis_index("ctx") * slot_count + jnp.arange(slot_count, dtype=jnp.int32)
    head_low = head_w.astype(jnp.bfloat16)
    head_back = head_low.astype(jnp.float32)
    square_low = square_w.astype(jnp.bfloat16)
    bias_head = square_low[1].astype(jnp.float32)
    final_coefficient_reduced = small_params[7:10].astype(jnp.bfloat16)
    kept = []
    sum_list = []
    count_list = []
    for micro_index in range(micro_count):
        features = jnp.transpose(pixels[0, micro_index], (0, 2, 1))
        live_slot = slot_ids[None, :] < lengths[0, micro_index][:, None]
        context = jnp.where(live_slot & (ctx_mask[0, micro_index] == 1), 1.0, 0.0).astype(
            jnp.float32
        )
        query_mask = jnp.where(live_slot & (ctx_mask[0, micro_index] == 0), 1.0, 0.0).astype(
            jnp.float32
        )
        summed, counts, saved = encoder_forward(features, context, small_params, square_low[0])
        sum_list.append(summed)
        count_list.append(counts)
        kept.append((features, context, query_mask, saved))
    totals = [
        lax.psum((sum_list[index_micro], count_list[index_micro]), "ctx")
        for index_micro in range(micro_count)
    ]
    zeros_small = jnp.zeros((model_width,), jnp.float32)
    grad_first_w = jnp.zeros((5, model_width), jnp.float32)
    grad_coord_w = jnp.zeros((2, model_width), jnp.float32)
    grad_out_w = jnp.zeros((3, model_width), jnp.float32)
    grad_vectors = [zeros_small] * 5
    grad_square = jnp.zeros_like(square_w)
    latent_rows = []
    theta_rows = []
    squared = jnp.zeros((), jnp.float32)
    regular = jnp.zeros((), jnp.float32)
    for micro_index in range(micro_count):
        features, context, query_mask, saved = kept[micro_index]
        first_pre, gelu_first, norm_back, normed_low, gelu_second = saved
        summed, counts = totals[micro_index]
        divisor = counts[:, None] + 1.0
        latent_low = (summed / divisor).astype(jnp.bfloat16)
        latent_back = latent_low.astype(jnp.float32)
        generated = jnp.dot(latent_low, head_low, preferred_element_type=jnp.float32)
        gen_parts = generated.astype(jnp.bfloat16).reshape(groups, -1, model_width)
        gen_full = lax.all_gather(gen_parts, "ctx", axis=1, tiled=True)
        gen_bias = jnp.dot(latent_low, square_low[1], preferred_element_type=jnp.float32)
        coord_pre = (
            jnp.einsum(
                "gpc,cd->gpd",
                features[..., 3:5],
                small_params[5:7],
                precision=exact_arithmetic_mode,
            )
            + small_params[14]
        )
        siren_low = jnp.sin(30.0 * coord_pre).astype(jnp.bfloat16)
        siren_pre = (
            jnp.einsum("gpd,gde->gpe", siren_low, gen_full, preferred_element_type=jnp.float32)
            + gen_bias[:, None, :]
        )
        result_reduced_form = jnp.sin(30.0 * siren_pre).astype(jnp.bfloat16)
        estimated_colour_values = jnp.einsum(
            "kdg,cg->kcd",
            result_reduced_form,
            final_coefficient_reduced,
            preferred_element_type=jnp.float32,
        )
        errors = (
            estimated_colour_values - jnp.transpose(features[..., 0:3], (0, 2, 1))
        ) * query_mask[:, None, :]
        squared = squared + jnp.sum(errors * errors)
        regular = regular + jnp.sum(generated * generated)
        prediction_gradient = (2.0 / live_all * errors).astype(jnp.bfloat16)
        grad_out_w = grad_out_w + jnp.einsum(
            "dan,dnq->aq",
            prediction_gradient,
            result_reduced_form,
            preferred_element_type=jnp.float32,
        )
        grad_out = jnp.einsum(
            "xvw,vt->xwt",
            prediction_gradient,
            final_coefficient_reduced,
            preferred_element_type=jnp.float32,
        )
        grad_inner = (grad_out * 30.0 * jnp.cos(30.0 * siren_pre)).astype(jnp.bfloat16)
        gen_part = jnp.einsum(
            "gpd,gpe->gde", siren_low, grad_inner, preferred_element_type=jnp.float32
        )
        gen_grad = lax.psum_scatter(gen_part, "ctx", scatter_dimension=1, tiled=True).reshape(
            groups, -1
        )
        gen_grad = gen_grad + 2.0 * reg_weight / groups_all * generated
        bias_part = jnp.sum(grad_inner.astype(jnp.float32), axis=1)
        grad_siren = jnp.einsum(
            "gpe,gde->gpd", grad_inner, gen_full, preferred_element_type=jnp.float32
        )
        grad_coord = grad_siren * 30.0 * jnp.cos(30.0 * coord_pre)
        grad_coord_w = grad_coord_w + jnp.einsum(
            "gpc,gpd->cd", features[..., 3:5], grad_coord, precision=exact_arithmetic_mode
        )
        grad_vectors[4] = grad_vectors[4] + jnp.sum(grad_coord, axis=(0, 1))
        latent_rows.append(latent_back)
        theta_rows.append(gen_grad)
        latent_part = jnp.dot(gen_grad, head_back.T, precision=exact_arithmetic_mode)
        latent_part, bias_full = lax.psum((latent_part, bias_part), "ctx")
        grad_square = grad_square.at[1].add(
            jnp.dot(latent_back.T, bias_part, precision=exact_arithmetic_mode)
        )
        grad_latent = latent_part + jnp.dot(bias_full, bias_head.T, precision=exact_arithmetic_mode)
        grad_encoded = context[:, :, None] * (grad_latent / divisor)[:, None, :]
        (grad_second,) = gelu_second(grad_encoded)
        second_low = grad_second.astype(jnp.bfloat16)
        grad_square = grad_square.at[0].add(
            jnp.einsum("gpd,gpe->de", normed_low, second_low, preferred_element_type=jnp.float32)
        )
        grad_vectors[3] = grad_vectors[3] + jnp.sum(second_low.astype(jnp.float32), axis=(0, 1))
        grad_normed = jnp.einsum(
            "gpe,de->gpd", second_low, square_low[0], preferred_element_type=jnp.float32
        )
        grad_act, grad_gain, grad_beta = norm_back(grad_normed)
        (grad_first,) = gelu_first(grad_act)
        grad_first_w = grad_first_w + jnp.einsum(
            "gpc,gpd->cd", features, grad_first, precision=exact_arithmetic_mode
        )
        grad_vectors[0] = grad_vectors[0] + jnp.sum(grad_first, axis=(0, 1))
        grad_vectors[1] = grad_vectors[1] + grad_gain
        grad_vectors[2] = grad_vectors[2] + grad_beta
    grad_small = jnp.concatenate(
        [
            grad_first_w,
            grad_coord_w,
            grad_out_w,
            jnp.stack(
                [
                    grad_vectors[0],
                    grad_vectors[1],
                    grad_vectors[2],
                    grad_vectors[3],
                    grad_vectors[4],
                ]
            ),
        ],
        axis=0,
    )
    grad_small, grad_square, stat_sums = lax.psum(
        (grad_small, grad_square, jnp.stack([squared, regular])), ("dp", "ctx")
    )
    latent_stack = jnp.concatenate(latent_rows, axis=0)
    theta_stack = jnp.concatenate(theta_rows, axis=0)
    grad_head = lax.psum(
        jnp.dot(latent_stack.T, theta_stack, precision=exact_arithmetic_mode), "dp"
    )
    loss_value = stat_sums[0] / live_all + reg_weight * stat_sums[1] / groups_all
    head_moment = momentum_rate * head_mom + grad_head
    head_dir = head_orthogonal(head_moment)
    head_new = head_w - head_rate * (0.2 * model_width * head_dir + decay_rate * head_w)
    square_moment = momentum_rate * square_mom + grad_square
    rates = jnp.array(square_rates, jnp.float32)[:, None, None]
    square_new = square_w - rates * (
        0.2 * model_width**0.5 * orthogonal_local(square_moment) + decay_rate * square_w
    )
    small_moment, small_second, small_new = adam_update(
        small_params, grad_small, small_mom, small_var
    )
    return (
        head_moment,
        head_new,
        head_new.astype(jnp.bfloat16),
        square_moment,
        square_new,
        square_new.astype(jnp.bfloat16),
        small_moment,
        small_second,
        small_new,
        small_new.astype(jnp.bfloat16),
        loss_value,
    )


MESH = pl.DeviceIdType.MESH
F32 = jnp.float32
BF16 = jnp.bfloat16
WIDTH = 256
TILE = 256
MIB = 1024 * 1024
SPAN = 768
QUARTER = 64
HALF = 128
HEAD_SHARP = 3
TURN = 30.0 / 6.283185307179586
GELU_ONE = 0.7978845608028654
GELU_CUBE = GELU_ONE * 0.044715
GELU_SCALE = GELU_CUBE ** (1.0 / 3.0)
GELU_SLOPE = GELU_ONE / GELU_SCALE
NORM_EPS = 1e-05 * (2.0 * GELU_SCALE) ** 2
SIN_TERMS = (4.442860272, -7.307432505, 3.594782484, -0.784372885)


def any_spec():
    return pl.BlockSpec(memory_space=pl.ANY)


def hbm_spec():
    return pl.BlockSpec(memory_space=pltpu.HBM)


def busy(micros):
    return pl.CostEstimate(flops=micros * 10**9, bytes_accessed=micros * 10**5, transcendentals=0)


def vmem_spec():
    return pl.BlockSpec(memory_space=pltpu.VMEM)


def smem_spec():
    return pl.BlockSpec(memory_space=pltpu.SMEM)


def turned(matrix):
    pad = jnp.zeros((matrix.shape[0], 128 - matrix.shape[1]), F32)
    return jnp.concatenate([matrix, pad], axis=1).T


def weave(order, first, second):
    for letter in order:
        next(first if letter == "A" else second, None)
    for rest in (first, second):
        for unused in rest:
            pass


def dot_nn(a, b):
    return lax.dot_general(a, b, (((1,), (0,)), ((), ())), preferred_element_type=F32)


def dot_nt(a, b):
    return lax.dot_general(a, b, (((1,), (1,)), ((), ())), preferred_element_type=F32)


def full_nn(a, b):
    return lax.dot_general(
        a, b, (((1,), (0,)), ((), ())), precision=lax.Precision.HIGHEST, preferred_element_type=F32
    )


def full_nt(a, b):
    return lax.dot_general(
        a, b, (((1,), (1,)), ((), ())), precision=lax.Precision.HIGHEST, preferred_element_type=F32
    )


def split3(v):
    high = v.astype(BF16).astype(F32)
    rest = v - high
    mid = rest.astype(BF16).astype(F32)
    return high, mid, rest - mid


def hail(peers):
    barrier = pltpu.get_barrier_semaphore()
    for peer in peers:
        pl.semaphore_signal(barrier, inc=1, device_id=peer, device_id_type=MESH)
    return len(peers)


def meet(count):
    pl.semaphore_wait(pltpu.get_barrier_semaphore(), count)


def greet(peers):
    meet(hail(peers))


def ring_peers(axis, n):
    me = lax.axis_index(axis)
    return [lax.rem(me + d, n) for d in range(1, n)]


def plan_all(axis, n, source, target, send_sem, recv_sem):
    return [
        pltpu.make_async_remote_copy(
            src_ref=source(peer),
            dst_ref=target,
            send_sem=send_sem.at[d],
            recv_sem=recv_sem.at[d],
            device_id={axis: peer},
            device_id_type=MESH,
        )
        for d, peer in enumerate(ring_peers(axis, n))
    ]


def send_all(*plan):
    copies = plan_all(*plan)
    for copy in copies:
        copy.start()
    return copies


def fenced(copies, before=None):
    @pl.when(lax.axis_index("ctx") >= 0)
    def run():
        if before is not None:
            before()
        for copy in copies:
            copy.start()

    return copies


def column(row, width):
    return jnp.broadcast_to(row, (width, row.shape[1])).T


def gelu_twice(y):
    return y + y * jnp.tanh(y * (GELU_SLOPE + y * y))


def gelu_both(y):
    square = y * y
    above = 1.0 + jnp.tanh(y * (GELU_SLOPE + square))
    value = y * above
    return value, above + (value * (2.0 - above)) * (3.0 * square + GELU_SLOPE)


def plain_twice(x):
    return x + x * jnp.tanh(x * (GELU_ONE + GELU_CUBE * (x * x)))


def plain_slope(x):
    square = GELU_CUBE * (x * x)
    above = 1.0 + jnp.tanh(x * (GELU_ONE + square))
    return above + (x * above) * (2.0 - above) * (3.0 * square + GELU_ONE)


def sine_pair(turns):
    frac = turns - jnp.round(turns)
    square = frac * frac
    s = SIN_TERMS[3] * square + SIN_TERMS[2]
    s = s * square + SIN_TERMS[1]
    s = (s * square + SIN_TERMS[0]) * frac
    cosine = 1.0 - s * s
    rest = 1.0 + cosine
    return s * (rest * lax.rsqrt(rest)), cosine


def triple_weights(block):
    high, mid, low = split3(block)
    rows = jnp.concatenate([high, mid, high, low, mid, high], axis=0)
    pad = jnp.zeros((128 - rows.shape[0], rows.shape[1]), F32)
    return jnp.concatenate([rows, pad], axis=0).T.astype(BF16)[:, 0:48]


def triple_from_list(rows):
    high, mid, low = split3(rows)
    return jnp.concatenate([high, high, mid, high, mid, low], axis=0).astype(BF16)


def three(matrix):
    high = matrix.astype(BF16)
    rest = matrix - high.astype(F32)
    mid = rest.astype(BF16)
    return high, mid, (rest - mid.astype(F32)).astype(BF16)


def six(left, right):
    rows = left[0].shape[0]
    first = dot_nn(jnp.concatenate(left, axis=0), right[0])
    second = dot_nn(jnp.concatenate(left[0:2], axis=0), right[1])
    third = dot_nn(left[0], right[2])
    return (first[0:rows] + second[0:rows] + third) + (
        first[rows : 2 * rows] + second[rows:] + first[2 * rows :]
    )


def few(left, right):
    rows = left[0].shape[0]
    first = dot_nn(jnp.concatenate(left[0:2], axis=0), right[0])
    return (first[0:rows] + dot_nn(left[0], right[1])) + first[rows:]


def gram_six(parts):
    high, mid, low = parts
    both = jnp.concatenate([high, mid], axis=1)
    cross = dot_nt(jnp.concatenate([high, high], axis=1), jnp.concatenate([mid, low], axis=1))
    return dot_nt(both, both) + (cross + cross.T)


def order_rows(row, per):
    return jnp.concatenate([row[:, k * TILE : (k + 1) * TILE] for k in range(per)], axis=0)


def bring_counts(seen_ref, cnt_v, cnt_s, sem):
    for s in range(seen_ref.shape[0]):
        cnt_v[s : s + 1, :] = seen_ref[s, 0:1, :].astype(jnp.int32)
    counts = pltpu.make_async_copy(cnt_v, cnt_s, sem)
    counts.start()
    return counts


def put(target, rows, extra, offset, start, amount):
    lane_ids = lax.broadcasted_iota(jnp.int32, (8, TILE), 1)
    shift = lax.rem(offset, TILE)
    base = pl.multiple_of(offset - shift, TILE)
    marks = [jnp.full((1, TILE), value, F32) for value in (0.0, 1.0, extra)]
    moved = pltpu.roll(jnp.concatenate([rows] + marks, axis=0), lax.rem(shift - start + TILE, TILE), 1)
    here = (lane_ids >= shift) & (lane_ids < shift + amount)
    there = lane_ids < shift + amount - TILE
    target[:, pl.ds(base, TILE)] += jnp.where(here, moved, 0.0)
    target[:, pl.ds(pl.multiple_of(base + TILE, TILE), TILE)] = jnp.where(there, moved, 0.0)


def clear_tail(target, amount):
    start = pl.multiple_of((amount // TILE + 1) * TILE, TILE)
    for step in range(4 * SPAN // TILE):
        target[:, pl.ds(start + step * TILE, TILE)] = jnp.zeros((8, TILE), F32)


def weight_block(weights, bias, place):
    rows = weights.shape[0]
    parts = []
    if place > 0:
        parts.append(jnp.zeros((place, WIDTH), F32))
    parts.append(weights)
    if place + rows < 6:
        parts.append(jnp.zeros((6 - place - rows, WIDTH), F32))
    parts.append(bias)
    parts.append(jnp.zeros((1, WIDTH), F32))
    return jnp.concatenate(parts, axis=0)


def scatter_kernel(
    n, rows_n, len_hbm, pix_hbm, mask_hbm, mom_ref, rx_ref, seen_ref, tiles_ref, share_ref, gram_ref,
    len_ref, pix_ref, mask_ref, stage, stage_n, told, buf, own, slab_rx, upper,
    send_sem, recv_sem, load_sem, slab_sem, own_sem, tell_sem,
):
    brought = [
        pltpu.make_async_copy(source, target, own_sem.at[j])
        for j, (source, target) in enumerate(((len_hbm, len_ref), (pix_hbm, pix_ref), (mask_hbm, mask_ref)))
    ]
    for copy in brought:
        copy.start()
    me = lax.axis_index("ctx")
    peers = ring_peers("ctx", n)
    r = lax.axis_index("dp")
    span = buf.shape[1]
    load = pltpu.make_async_copy(mom_ref.at[:, pl.ds(pl.multiple_of(r * span, span), span)], buf, load_sem)
    load.start()
    count = hail([{"ctx": peer} for peer in peers] + [{"dp": peer} for peer in ring_peers("dp", rows_n)])
    slots = pix_ref.shape[4]
    per = slots // TILE
    groups = mask_ref.shape[2]
    row_ids = lax.broadcasted_iota(jnp.int32, (TILE, TILE), 0)
    upper[...] = jnp.where(row_ids <= lax.broadcasted_iota(jnp.int32, (TILE, TILE), 1), 1.0, 0.0).astype(BF16)
    row_ids = row_ids.astype(F32)
    lane_ids = lax.broadcasted_iota(jnp.int32, (TILE, TILE), 1).astype(F32)
    place = (
        lax.broadcasted_iota(jnp.int32, (per, TILE), 0) * TILE
        + lax.broadcasted_iota(jnp.int32, (per, TILE), 1)
        + me * slots
    )
    pad = jnp.zeros((3, TILE), F32)
    ones = jnp.ones((16, TILE), BF16)
    blank = jnp.zeros((128 - 2 * per, TILE), BF16)
    wide_ids = lax.broadcasted_iota(jnp.int32, (per, 128), 1)
    told[...] = jnp.zeros_like(told)

    def arrange(b):
        def one(j, carry):
            g = b * groups + j
            mask = order_rows(mask_ref[0, b, pl.ds(j, 1), :], per)
            live = place < len_ref[0, b, j]
            context = jnp.where(live & (mask == 1), 1.0, 0.0)
            query = jnp.where(live & (mask == 0), 1.0, 0.0)
            both = jnp.concatenate([context, query], axis=0).astype(BF16)
            order = dot_nn(both, upper[...])
            before_c, before_q = order[0:per], order[per : 2 * per]
            live_c = before_c[:, TILE - 1 : TILE]
            target = jnp.where(
                context > 0.5, before_c, jnp.where(query > 0.5, live_c + before_q, 0.0)
            ) - 1.0
            amounts = dot_nt(ones, jnp.concatenate([both, blank], axis=0))[0:1]
            share_ref[g, 0:1, :] = amounts
            for t in range(per):
                place_t = pl.ds(lax.rem(g + t, n), 1)
                told[place_t, :] = jnp.where(wide_ids[0:1] == g, live_c[t : t + 1], told[place_t, :])
            for t in range(per):
                rows = jnp.concatenate(
                    [pix_ref[0, b, c, pl.ds(j, 1), t * TILE : (t + 1) * TILE] for c in range(5)]
                    + [pad], axis=0
                )
                high, mid, low = split3(rows)
                stack = jnp.concatenate([high, mid, low, jnp.zeros((8, TILE), F32)], axis=0).astype(BF16)
                if t % 2 == 0:
                    chosen = jnp.where(row_ids == target[t : t + 1], 1.0, 0.0).astype(BF16)
                    found = dot_nt(stack, chosen)
                else:
                    spot = column(target[t : t + 1], 128)
                    chosen = jnp.where(lane_ids == jnp.concatenate([spot, spot], axis=1), 1.0, 0.0).astype(BF16)
                    found = dot_nn(stack, chosen)
                found = found[0:8] + found[8:16] + found[16:24]
                tiles_ref[g, :, t * TILE : (t + 1) * TILE] = found
                stage[lax.rem(g + t, n), :, pl.ds(pl.multiple_of(g * TILE, TILE), TILE)] = found
            return carry

        lax.fori_loop(0, groups, one, 0)

    copies = []
    for copy in brought:
        copy.wait()
    for b in range(mask_ref.shape[1]):
        arrange(b)
        if b == 0:
            meet(count)
        lanes = pl.ds(b * groups * TILE, groups * TILE)
        copies += fenced(
            plan_all(
                "ctx",
                n,
                lambda peer: stage.at[peer, pl.ds(0, 5), lanes],
                rx_ref.at[me, pl.ds(0, 5), lanes],
                send_sem.at[b],
                recv_sem.at[b],
            )
        )
    for p in range(n):
        stage_n[p, 0:1, :] = told[p : p + 1, :]
    top = pl.ds(0, 1)
    copies += fenced(
        plan_all("ctx", n, lambda peer: stage_n.at[peer, top, :], seen_ref.at[me, top, :], tell_sem.at[0], tell_sem.at[1])
    )
    rx_ref[me, 0:5, :] = stage[me, 0:5, :]
    seen_ref[me, 0:1, :] = stage_n[me, 0:1, :]
    quarter = gram_ref.shape[0]
    same = jnp.zeros((WIDTH, WIDTH), F32)
    cross = jnp.zeros((WIDTH, WIDTH), F32)
    load.wait()
    for i in range(buf.shape[1] // WIDTH):
        high, mid, low = three(buf[:, i * WIDTH : (i + 1) * WIDTH])
        both = jnp.concatenate([high, mid], axis=1)
        same = same + dot_nt(both, both)
        cross = cross + dot_nt(jnp.concatenate([high, high], axis=1), jnp.concatenate([mid, low], axis=1))
    own[...] = same + (cross + cross.T)
    slabs = fenced(
        plan_all(
            "dp",
            rows_n,
            lambda peer: own.at[pl.ds(pl.multiple_of(peer * quarter, quarter), quarter), :],
            slab_rx.at[r],
            slab_sem.at[0],
            slab_sem.at[1],
        )
    )
    slab_rx[r] = own[pl.ds(pl.multiple_of(r * quarter, quarter), quarter), :]
    for copy in slabs:
        copy.wait()
    total = slab_rx[0]
    for s in range(1, rows_n):
        total = total + slab_rx[s]
    gram_ref[...] = total
    for copy in copies:
        copy.wait()


def encoder_kernel(
    rx_ref, seen_ref, small_ref, square_ref, z_ref, amount_ref, clist, count_ref, cnt_v, cnt_s, wide, second, zacc, low_a, low_b, sem
):
    sources = rx_ref.shape[0]
    per = rx_ref.shape[2] // TILE
    counts = bring_counts(seen_ref, cnt_v, cnt_s, sem)
    small = small_ref[...]
    first = triple_weights(weight_block(small[0:5] * GELU_SCALE, small[10:11] * GELU_SCALE, 0))
    wide[0] = column(small[11:12], SPAN)
    wide[1] = column(small[12:13], SPAN)
    wide[2] = column(small[13:14], SPAN)
    second[...] = square_ref[0].T.astype(BF16)
    zacc[...] = jnp.zeros_like(zacc)
    clist[:, 0:TILE] = jnp.zeros((8, TILE), F32)
    counts.wait()

    def place_tile(s, offset):
        for k in range(per):
            amount = cnt_s[s, k]
            put(clist, rx_ref[s, 0:5, k * TILE : (k + 1) * TILE], k + 1.0, offset, 0, amount)
            offset = offset + amount
        return offset

    num_c = lax.fori_loop(0, sources, place_tile, jnp.int32(0))
    clear_tail(clist, num_c)
    count_ref[0] = num_c
    ids = lax.broadcasted_iota(jnp.int32, (16, SPAN), 0).astype(F32) + 1.0

    def window(t):
        return clist[:, pl.ds(pl.multiple_of(t * SPAN, SPAN), SPAN)]

    def begin(t, low):
        pre = dot_nn(first, triple_from_list(window(t)))
        parts = []
        total = jnp.zeros((1, SPAN), F32)
        for c in range(0, WIDTH, HALF):
            parts.append(gelu_twice(pre[c : c + HALF]))
            total = total + jnp.sum(parts[-1], axis=0, keepdims=True)
            yield
        mean = total * (1.0 / WIDTH)
        total = jnp.zeros((1, SPAN), F32)
        for c in range(len(parts)):
            parts[c] = parts[c] - mean
            total = total + jnp.sum(parts[c] * parts[c], axis=0, keepdims=True)
        inverse = lax.rsqrt(total * (1.0 / WIDTH) + NORM_EPS)
        yield
        for c in range(len(parts)):
            rows = slice(c * HALF, (c + 1) * HALF)
            low[rows, :] = (parts[c] * inverse * wide[0, rows, :] + wide[1, rows, :]).astype(BF16)
        yield

    def finish(t, low):
        pre = dot_nn(second[...], low[...])
        yield
        highs, rests = [], []
        for c in range(0, WIDTH, HALF):
            encoded = plain_twice(pre[c : c + HALF] + wide[2, c : c + HALF, :])
            highs.append(encoded.astype(BF16))
            rests.append((encoded - highs[-1].astype(F32)).astype(BF16))
            yield
        owner = jnp.where(ids == window(t)[7:8], 1.0, 0.0).astype(BF16)
        right = jnp.concatenate([jnp.concatenate(highs, axis=0), jnp.concatenate(rests, axis=0)], axis=1)
        zacc[...] += dot_nt(right, jnp.concatenate([owner, owner], axis=1))
        yield

    def pair(p, carry):
        weave("BAABABBABABA", begin(2 * p + 1, low_b), finish(2 * p, low_a))
        weave("BAABABBABABA", begin(2 * p + 2, low_a), finish(2 * p + 1, low_b))
        return carry

    spans = (num_c + SPAN - 1) // SPAN
    weave("", begin(0, low_a), iter(()))
    lax.fori_loop(0, spans // 2, pair, 0)

    @pl.when(lax.rem(spans, 2) == 1)
    def last():
        weave("", iter(()), finish(spans - 1, low_a))

    z_ref[...] = turned(zacc[...])[0:8] * 0.5
    total = seen_ref[0, 0:1, :]
    for s in range(1, sources):
        total = total + seen_ref[s, 0:1, :]
    amount_ref[...] = jnp.broadcast_to(total, (8, 128))


def theta_kernel(
    n, z_ref, amount_ref, head_ref, tiles_ref, share_ref, theta_ref, gen_ref, z8_ref, inv_ref, reg_ref,
    rx_ref, seen_ref, zall, nall, head, give, turn, load_sem, sems,
):
    me = lax.axis_index("ctx")
    peers = ring_peers("ctx", n)
    chunk = head.shape[2]
    per = chunk // WIDTH

    def load(k):
        return pltpu.make_async_copy(head_ref.at[:, pl.ds(k * chunk, chunk)], head.at[k], load_sem.at[k])

    for k in range(head.shape[0]):
        load(k).start()
    greet([{"ctx": peer} for peer in peers])
    top = pl.ds(0, 1)
    latents = send_all("ctx", n, lambda peer: z_ref, zall.at[me], sems.at[0], sems.at[1])
    latents += send_all(
        "ctx", n, lambda peer: amount_ref.at[top, :], nall.at[me, top, :], sems.at[6], sems.at[7]
    )
    pixels = send_all(
        "ctx",
        n,
        lambda peer: tiles_ref.at[peer, pl.ds(0, 5), :],
        rx_ref.at[me, pl.ds(0, 5), :],
        sems.at[2],
        sems.at[3],
    )
    pixels += send_all(
        "ctx", n, lambda peer: share_ref.at[peer, top, :], seen_ref.at[me, top, :], sems.at[8], sems.at[9]
    )
    zall[me] = z_ref[...]
    nall[me, 0:1, :] = amount_ref[0:1, :]
    rx_ref[me, 0:5, :] = tiles_ref[me, 0:5, :]
    seen_ref[me, 0:1, :] = share_ref[me, 0:1, :]
    for copy in latents:
        copy.wait()
    total = zall[0]
    amounts = nall[0, 0:1, :]
    for s in range(1, n):
        total = total + zall[s]
        amounts = amounts + nall[s, 0:1, :]
    lanes = lax.broadcasted_iota(jnp.int32, (8, 128), 1)
    rows = lax.broadcasted_iota(jnp.int32, (8, 128), 0)
    counts = jnp.sum(jnp.where(lanes == rows, amounts, 0.0), axis=1, keepdims=True) + 1.0
    latent = (total / counts).astype(BF16).astype(F32)
    z8_ref[...] = latent
    inv_ref[...] = jnp.broadcast_to(0.5 / counts, (8, WIDTH))
    left = jnp.concatenate([latent, jnp.zeros((8, WIDTH), F32)], axis=0).astype(BF16)
    regular = jnp.zeros((8, WIDTH), F32)
    for k in range(head.shape[0]):
        load(k).wait()
        part = dot_nn(left, head[k].astype(BF16))[0:8]
        for i in range(per):
            piece = part[:, i * WIDTH : (i + 1) * WIDTH]
            theta_ref[pl.ds((k * per + i) * 8, 8), :] = piece
            for half in range(2):
                turn[half, pl.ds((k * per + i) * 8, 8), :] = piece[:, half * 128 : half * 128 + 128]
            regular = regular + piece * piece
    reg_ref[...] = regular
    height = WIDTH // n
    for g in range(n):
        for half in range(2):
            give[g, :, half * 128 : half * 128 + 128] = turn[half, pl.ds(g, height, stride=8), :].astype(BF16)
    mine = pl.ds(pl.multiple_of(me * height, height), height)
    parts = fenced(
        plan_all("ctx", n, lambda peer: give.at[peer], gen_ref.at[mine, :], sems.at[4], sems.at[5])
    )
    gen_ref[mine, :] = give[me]
    for copy in pixels + parts:
        copy.wait()


def siren_kernel(
    live_all, len_ref, rx_ref, seen_ref, gen_ref, z_ref, small_ref, square_ref, out_ref, bias_ref, narrow_ref,
    q_ref, cnt_v, cnt_s, inner, shift, sa, sb, ca, cb, ma, mb, na, nb, acc_g, acc_c, acc_o, acc_e, sem,
):
    sin_in, cos_in, sin_mid, cos_mid = (sa, sb), (ca, cb), (ma, mb), (na, nb)
    me = lax.axis_index("ctx")
    per = rx_ref.shape[2] // TILE
    groups = len_ref.shape[2]
    length = len_ref[0, me // groups, lax.rem(me, groups)]
    counts = bring_counts(seen_ref, cnt_v, cnt_s, sem)
    small = small_ref[...]
    coord = triple_weights(weight_block(small[5:7] * TURN, small[14:15] * TURN, 3))
    latent = jnp.broadcast_to(z_ref[pl.ds(me, 1), :], (16, WIDTH)).astype(BF16)
    bias = dot_nn(latent, square_ref[1].astype(BF16))[0:1]
    inner[...] = gen_ref[...].astype(F32).T.astype(BF16)
    shift[...] = column(bias * TURN, SPAN)
    final = small[7:10].astype(BF16).astype(F32)
    final_rows = jnp.concatenate([final, jnp.zeros((13, WIDTH), F32)], axis=0).astype(BF16)
    large = final * 30.0
    high = large.astype(BF16).astype(F32)
    gap = jnp.zeros((5, WIDTH), F32)
    final_cols = jnp.concatenate([high, gap, large - high, jnp.zeros((117, WIDTH), F32)], axis=0).T.astype(BF16)[:, 0:16]
    for ref in (acc_g, acc_c, acc_o, acc_e):
        ref[...] = jnp.zeros_like(ref)
    scale = 2.0 / live_all
    ones = jnp.ones((16, SPAN), BF16)
    q_ref[:, 0:TILE] = jnp.zeros((8, TILE), F32)
    counts.wait()

    def place_tile(s, offset):
        for k in range(per):
            amount = cnt_s[s, per + k]
            put(q_ref, rx_ref[s, 0:5, k * TILE : (k + 1) * TILE], 0.0, offset, cnt_s[s, k], amount)
            offset = offset + amount
        return offset

    num_q = lax.fori_loop(0, (length + per * TILE - 1) // (per * TILE), place_tile, jnp.int32(0))
    clear_tail(q_ref, num_q)
    ids = lax.broadcasted_iota(jnp.int32, (8, SPAN), 0)

    def window(t):
        return q_ref[:, pl.ds(pl.multiple_of(t * SPAN, SPAN), SPAN)]

    def ahead(t, k):
        turns = dot_nn(coord, triple_from_list(window(t)))
        for c in range(0, WIDTH, WIDTH):
            s_in, c_in = sine_pair(turns[c : c + WIDTH])
            sin_in[k][c : c + WIDTH, :] = s_in.astype(BF16)
            cos_in[k][c : c + WIDTH, :] = c_in
            yield
        turns = dot_nn(inner[...], sin_in[k][...])
        yield
        for c in range(0, WIDTH, WIDTH):
            s_mid, c_mid = sine_pair(turns[c : c + WIDTH] * TURN + shift[c : c + WIDTH, :])
            sin_mid[k][c : c + WIDTH, :] = s_mid.astype(BF16)
            cos_mid[k][c : c + WIDTH, :] = c_mid
            yield

    def back_part(t, k):
        rows = window(t)
        pred = dot_nn(final_rows, sin_mid[k][...])[0:8]
        error = jnp.where(ids < 3, (pred - rows) * rows[6:7], 0.0)
        acc_e[...] += error * error
        slope = (error * scale).astype(BF16).astype(F32)
        slope = jnp.concatenate([slope, slope], axis=0).astype(BF16)
        yield
        acc_o[...] += dot_nt(sin_mid[k][...], slope)
        back = (cos_mid[k][...] * dot_nn(final_cols, slope)).astype(BF16)
        yield
        grads = dot_nn(gen_ref[...], back)
        yield
        outer = cos_in[k][...] * grads
        high = outer.astype(BF16)
        low = (outer - high.astype(F32)).astype(BF16)
        yield
        acc_g[...] += dot_nt(jnp.concatenate([sin_in[k][...], ones], axis=0), back)
        yield
        left = jnp.concatenate(split3(rows) + (jnp.zeros((8, SPAN), F32),), axis=0).astype(BF16)
        acc_c[...] += dot_nt(jnp.concatenate([high, low], axis=1), jnp.concatenate([left, left], axis=1))
        yield

    def pair(p, carry):
        weave("BABABABAABABAA", ahead(2 * p + 1, 1), back_part(2 * p, 0))
        weave("BABABABAABABAA", ahead(2 * p + 2, 0), back_part(2 * p + 1, 1))
        return carry

    spans = (num_q + SPAN - 1) // SPAN
    weave("", ahead(0, 0), iter(()))
    lax.fori_loop(0, spans // 2, pair, 0)

    @pl.when(lax.rem(spans, 2) == 1)
    def last():
        weave("", iter(()), back_part(spans - 1, 0))

    out_ref[...] = acc_g[0:WIDTH, :]
    bias_ref[...] = acc_g[WIDTH : WIDTH + 8, :]
    coords = turned(acc_c[...])
    coords = (coords[0:8] + coords[8:16] + coords[16:24]) * 30.0
    narrow_ref[0:2, :] = coords[3:5]
    narrow_ref[2:5, :] = turned(acc_o[...])[0:3]
    narrow_ref[5:6, :] = coords[6:7]
    narrow_ref[6:7, :] = jnp.broadcast_to(jnp.sum(acc_e[...]), (1, WIDTH))
    narrow_ref[7:8, :] = jnp.zeros((1, WIDTH), F32)


def latent_kernel(
    n, groups_all, part_ref, bias_ref, theta_ref, head_ref, mom_ref, z8_ref, gram_ref,
    dz_ref, tall_ref, cross_ref,
    rx, rxb, turn, head, mom, low_head, low_mom, rxz, dz_own, lefts, rxs, slab_sum, load_sem, mom_sem, sems,
):
    me = lax.axis_index("ctx")
    peers = ring_peers("ctx", n)
    chunk = head.shape[2]
    per = chunk // WIDTH
    height = WIDTH // n

    def load(k):
        return pltpu.make_async_copy(head_ref.at[:, pl.ds(k * chunk, chunk)], head.at[k], load_sem.at[k])

    def load_mom(k):
        return pltpu.make_async_copy(mom_ref.at[:, pl.ds(k * chunk, chunk)], mom.at[k], mom_sem.at[k])

    for k in range(head.shape[0]):
        load(k).start()
    for k in range(head.shape[0]):
        load_mom(k).start()
    greet([{"ctx": peer} for peer in peers])
    mine = pl.ds(pl.multiple_of(me * height, 8), height)
    parts = send_all(
        "ctx",
        n,
        lambda peer: part_ref.at[pl.ds(pl.multiple_of(peer * height, 8), height), :],
        rx.at[mine, :],
        sems.at[0],
        sems.at[1],
    )
    biases = send_all(
        "ctx", n, lambda peer: bias_ref.at[pl.ds(0, 1), :], rxb.at[me, pl.ds(0, 1), :], sems.at[6], sems.at[7]
    )
    slab = gram_ref.shape[0] // n
    grams = send_all(
        "ctx",
        n,
        lambda peer: gram_ref.at[pl.ds(pl.multiple_of(peer * slab, slab), slab), :],
        rxs.at[me],
        sems.at[4],
        sems.at[5],
    )
    rx[mine, :] = part_ref[mine, :]
    rxb[me, 0:1, :] = bias_ref[0:1, :]
    rxs[me] = gram_ref[pl.ds(pl.multiple_of(me * slab, slab), slab), :]

    def split_head(k, carry):
        load(k).wait()
        for i in range(per):
            low_head[k * per + i] = head[k, :, i * WIDTH : (i + 1) * WIDTH].astype(BF16)
        return carry

    lax.fori_loop(0, head.shape[0], split_head, 0)

    def split_mom(k, carry):
        load_mom(k).wait()
        for i in range(per):
            for j, part in enumerate(three(mom[k, :, i * WIDTH : (i + 1) * WIDTH].T)):
                low_mom[j, k * per + i] = part
        return carry

    lax.fori_loop(0, head.shape[0], split_mom, 0)

    def slab_total():
        for copy in grams:
            copy.wait()
        total = rxs[0]
        for s in range(1, n):
            total = total + rxs[s]
        slab_sum[...] = total
        tall_ref[height + 2 + me] = total

    slabs = fenced(
        plan_all("ctx", n, lambda peer: slab_sum, tall_ref.at[height + 2 + me], sems.at[8], sems.at[9]), slab_total
    )
    for copy in biases + parts:
        copy.wait()
    turn[0] = rx[:, 0:128]
    turn[1] = rx[:, 128:256]

    def across(i):
        return jnp.concatenate([turn[half, pl.ds(i, 8, stride=height), :] for half in range(2)], axis=1)

    blank = jnp.zeros((8, WIDTH), F32)
    for i in range(height):
        rows = across(i) + theta_ref[pl.ds(i * 8, 8), :] * (1.0 / groups_all)
        tall_ref[i] = rows
        lefts[i] = jnp.concatenate(split3(rows) + (blank,), axis=0).astype(BF16)
    tall_ref[height] = z8_ref[...]
    tall_ref[height + 1] = jnp.concatenate([rxb[s, 0:1, :] for s in range(n)], axis=0)
    totals = [jnp.zeros((32, WIDTH), F32)] * 2
    for i in range(height):
        totals[i % 2] = totals[i % 2] + dot_nt(lefts[i], low_head[i])
    total = totals[0] + totals[1]
    dz_own[...] = total[0:8] + total[8:16] + total[16:24]
    terms = fenced(plan_all("ctx", n, lambda peer: dz_own, rxz.at[me], sems.at[2], sems.at[3]))
    rxz[me] = dz_own[...]

    def mix(i, carry):
        totals = list(carry)
        for k in range(4):
            for j in range(3):
                totals[k % 2] = totals[k % 2] + dot_nn(lefts[4 * i + k], low_mom[j, 4 * i + k])
        return tuple(totals)

    empty = jnp.zeros((32, WIDTH), F32)
    totals = lax.fori_loop(0, height // 4, mix, (empty, empty))
    total = totals[0] + totals[1]
    cross_ref[...] = total[0:8] + total[8:16] + total[16:24]
    for copy in terms:
        copy.wait()
    total = rxz[0]
    for s in range(1, n):
        total = total + rxz[s]
    dz_ref[...] = total
    for copy in slabs:
        copy.wait()


def encoder_back_kernel(
    count_ref, c_ref, small_ref, square_ref, dz_ref, inv_ref, tall_ref, narrow_ref, reg_ref, out_ref, thin_ref,
    wide, second, spread, ua, ub, ka, kb, na, nb, ga, gb, acc_s, acc_f, acc_g, rows_out,
):
    unit, chain, normed, grad = (ua, ub), (ka, kb), (na, nb), (ga, gb)
    num_c = count_ref[0]
    small = small_ref[...]
    first = triple_weights(weight_block(small[0:5] * GELU_SCALE, small[10:11] * GELU_SCALE, 0))
    plain = square_ref[0].astype(BF16)
    low = plain.astype(F32)
    second[...] = low.T.astype(BF16)
    height = tall_ref.shape[0] - 10
    bias_back = full_nt(tall_ref[height + 1], square_ref[1].astype(BF16).astype(F32))
    latent_back = (dz_ref[...] + bias_back) * inv_ref[...]
    wide[0] = column(small[11:12], SPAN)
    wide[1] = column(small[12:13], SPAN)
    latent_cols = jnp.concatenate(split3(latent_back) + (jnp.zeros((104, WIDTH), F32),), axis=0).T.astype(BF16)[:, 0:32]
    wide[2] = column(small[13:14], SPAN)
    centre = split3(full_nn(jnp.broadcast_to(small[11:12], (8, WIDTH)), low) * (1.0 / WIDTH))
    rows = jnp.concatenate([part[0:1] for part in centre] + [jnp.zeros((13, WIDTH), F32)], axis=0)
    spread[...] = jnp.concatenate([plain, rows.astype(BF16)], axis=0)
    for ref in (acc_s, acc_f, acc_g):
        ref[...] = jnp.zeros_like(ref)
    ones = jnp.ones((16, SPAN), BF16)
    ids = lax.broadcasted_iota(jnp.int32, (8, SPAN), 0).astype(F32) + 1.0
    blank = jnp.zeros((8, SPAN), F32)

    def window(t):
        return c_ref[:, pl.ds(pl.multiple_of(t * SPAN, SPAN), SPAN)]

    def ahead(t, k):
        pre = dot_nn(first, triple_from_list(window(t)))
        parts, slopes = [], []
        total = jnp.zeros((1, SPAN), F32)
        for c in range(0, WIDTH, QUARTER):
            value, slope = gelu_both(pre[c : c + QUARTER])
            parts.append(value)
            slopes.append(slope)
            total = total + jnp.sum(value, axis=0, keepdims=True)
            yield
        mean = total * (1.0 / WIDTH)
        total = jnp.zeros((1, SPAN), F32)
        for c in range(len(parts)):
            parts[c] = parts[c] - mean
            total = total + jnp.sum(parts[c] * parts[c], axis=0, keepdims=True)
        inverse = lax.rsqrt(total * (1.0 / WIDTH) + NORM_EPS)
        yield
        scale = inverse * GELU_SCALE
        for c in range(len(parts)):
            rows = slice(c * QUARTER, (c + 1) * QUARTER)
            value = parts[c] * inverse
            unit[k][rows, :] = value
            normed[k][rows, :] = (value * wide[0, rows, :] + wide[1, rows, :]).astype(BF16)
            chain[k][rows, :] = slopes[c] * scale
        yield
        owner = jnp.where(ids == window(t)[7:8], 1.0, 0.0)
        owner = jnp.concatenate([owner, owner, owner, blank], axis=0).astype(BF16)
        pre = dot_nn(second[...], normed[k][...])
        outer = dot_nn(latent_cols, owner)
        yield
        for c in range(0, WIDTH, QUARTER):
            rows = slice(c, c + QUARTER)
            grad[k][rows, :] = (plain_slope(pre[rows] + wide[2, rows, :]) * outer[rows]).astype(BF16)
            yield

    def back_part(t, k):
        slopes = dot_nn(spread[...], grad[k][...])
        yield
        acc_s[...] += dot_nt(jnp.concatenate([normed[k][...], ones], axis=0), grad[k][...])
        yield
        means = jnp.sum(slopes[WIDTH : WIDTH + 8], axis=0, keepdims=True)
        total = jnp.zeros((1, SPAN), F32)
        parts = []
        for c in range(0, WIDTH, QUARTER):
            rows = slice(c, c + QUARTER)
            parts.append(slopes[rows] * wide[0, rows, :] - means)
            acc_g[rows, :] += slopes[rows] * unit[k][rows, :]
            total = total + jnp.sum(parts[-1] * unit[k][rows, :], axis=0, keepdims=True)
        mean = total * (1.0 / WIDTH)
        yield
        highs, rests = [], []
        for c in range(len(parts)):
            rows = slice(c * QUARTER, (c + 1) * QUARTER)
            outer = (parts[c] - unit[k][rows, :] * mean) * chain[k][rows, :]
            highs.append(outer.astype(BF16))
            rests.append((outer - highs[-1].astype(F32)).astype(BF16))
        yield
        left = jnp.concatenate(split3(window(t)) + (jnp.zeros((8, SPAN), F32),), axis=0).astype(BF16)
        right = jnp.concatenate([jnp.concatenate(highs, axis=0), jnp.concatenate(rests, axis=0)], axis=1)
        acc_f[...] += dot_nt(right, jnp.concatenate([left, left], axis=1))
        yield

    def pair(p, carry):
        weave("ABABAAAABABABAA", ahead(2 * p + 1, 1), back_part(2 * p, 0))
        weave("ABABAAAABABABAA", ahead(2 * p + 2, 0), back_part(2 * p + 1, 1))
        return carry

    spans = (num_c + SPAN - 1) // SPAN
    weave("", ahead(0, 0), iter(()))
    lax.fori_loop(0, spans // 2, pair, 0)

    @pl.when(lax.rem(spans, 2) == 1)
    def last():
        weave("", iter(()), back_part(spans - 1, 0))

    firsts = turned(acc_f[...])
    firsts = firsts[0:8] + firsts[8:16] + firsts[16:24]
    bias_grad = acc_s[WIDTH : WIDTH + 8]
    shift_grad = full_nt(bias_grad, low)
    gain_grad = full_nt(jnp.ones((8, SPAN), F32), acc_g[...])
    rows_out[0:5, :] = firsts[0:5]
    rows_out[5:10, :] = narrow_ref[0:5, :]
    rows_out[10:11, :] = firsts[6:7]
    rows_out[11:12, :] = gain_grad[0:1]
    rows_out[12:13, :] = shift_grad[0:1]
    rows_out[13:14, :] = bias_grad[0:1]
    rows_out[14:15, :] = narrow_ref[5:6, :]
    lane = lax.broadcasted_iota(jnp.int32, (1, WIDTH), 1)
    regular = jnp.broadcast_to(jnp.sum(reg_ref[...]), (1, WIDTH))
    rows_out[15:16, :] = jnp.where(lane == 0, narrow_ref[6:7, :], jnp.where(lane == 1, regular, 0.0))
    for q in range(32):
        out_ref[q // 16, q % 16] = acc_s[8 * q : 8 * q + 8, :]
        lanes = slice((q % 2) * 128, (q % 2) * 128 + 128)
        thin_ref[q // 16, q % 16, 0:1, :] = rows_out[q // 2 : q // 2 + 1, lanes]


def newton(gram, sharp):
    ids = lax.broadcasted_iota(jnp.int32, (WIDTH, WIDTH), 0) == lax.broadcasted_iota(jnp.int32, (WIDTH, WIDTH), 1)
    scale = 1.0 / (jnp.sqrt(jnp.sum(jnp.where(ids, gram, 0.0))) + 1e-07)
    sides = (slice(0, WIDTH // 2), slice(WIDTH // 2, WIDTH))
    state = [gram[side] * (scale * scale) for side in sides]
    unit = [jnp.where(ids[side], first_coef, 0.0) for side in sides]

    def joined(halves):
        return [jnp.concatenate(pair, axis=0) for pair in zip(*halves)]

    product = None
    for k in range(NS_STEPS):
        times = six if k < sharp else few
        parts = [three(one) for one in state]
        whole = joined(parts)
        square = [few(part, whole) for part in parts]
        yield None
        poly = [unit[j] + second_coef * state[j] + third_coef * square[j] for j in range(2)]
        left = [three(one) for one in poly]
        if k + 1 < NS_STEPS:
            half = [times(one, whole) for one in left]
            yield None
        if k == 0:
            product = poly
        else:
            right = joined([three(one) for one in product])
            product = [times(one, right) for one in left]
        if k + 1 < NS_STEPS:
            yield None
            outer = joined(left)
            state = [times(three(one), outer) for one in half]
            yield None
    yield jnp.concatenate([one * scale for one in product], axis=0)


def newton_step(state_ref, product_ref):
    ids = lax.broadcasted_iota(jnp.int32, (WIDTH, WIDTH), 0) == lax.broadcasted_iota(jnp.int32, (WIDTH, WIDTH), 1)
    sides = (slice(0, WIDTH // 2), slice(WIDTH // 2, WIDTH))
    state = [state_ref[side, :] for side in sides]
    parts = [three(one) for one in state]
    whole = three(state_ref[...])
    square = [few(part, whole) for part in parts]
    yield None
    left = [
        three(jnp.where(ids[side], first_coef, 0.0) + second_coef * state[j] + third_coef * square[j])
        for j, side in enumerate(sides)
    ]
    half = [six(one, whole) for one in left]
    yield None
    right = three(product_ref[...])
    for one, side in zip(left, sides):
        product_ref[side, :] = six(one, right)
    yield None
    outer = [jnp.concatenate(pair, axis=0) for pair in zip(*left)]
    for one, side in zip(half, sides):
        state_ref[side, :] = six(three(one), outer)
    yield None


def square_rows(sum_ref):
    return jnp.concatenate([sum_ref[q // 16, q % 16] for q in range(32)], axis=0)


def small_rows(sum_ref):
    halves = [sum_ref[q // 16, q % 16, 0:1, :] for q in range(32)]
    return jnp.concatenate(
        [jnp.concatenate([halves[2 * k], halves[2 * k + 1]], axis=1) for k in range(16)], axis=0
    )


def reduce_kernel(
    n, rows_n, grad_ref, thin_ref, own_ref, far_ref, cross_ref, smom_ref,
    sum_ref, thin_sum, tall_ref, move_ref,
    rxh, half_sum, rxq, fin, rxh_thin, half_thin, rxq_thin, fin_thin, mixed, rxm, rxc, rxx, sems, dsems, csems, qsems,
):
    me = lax.axis_index("ctx")
    r = lax.axis_index("dp")
    chips = (rows_n // 2) * n
    par = lax.rem(r, 2)
    chip = (r // 2) * n + me
    far = lax.rem(r + rows_n // 2, rows_n)
    near = r + 1 - 2 * par
    diag = lax.rem(near + rows_n // 2, rows_n)
    places_here = [pl.ds(pl.multiple_of(place * 8, 8), 8) for place in (r, far)]
    others = [lax.rem(chip + d, chips) for d in range(1, chips)]
    places = [{"dp": 2 * (other // n) + par, "ctx": lax.rem(other, n)} for other in others]
    count = hail(places + [{"dp": near}, {"dp": diag}])
    for i in range(own_ref.shape[0]):
        for rows, ref in zip(places_here, (own_ref, far_ref)):
            tall_ref[i, rows, :] = ref[i]
    height = own_ref.shape[0] - 10

    def advance(count):
        for step in range(count):
            next(side)

    def near_copy(source, target, j):
        return pltpu.make_async_remote_copy(
            src_ref=source,
            dst_ref=target,
            send_sem=csems.at[0, j],
            recv_sem=csems.at[1, j],
            device_id={"dp": near},
            device_id_type=MESH,
        )

    def chip_copies(source, target, k):
        return [
            copy for pair in zip(*(chip_plan(*plan, k + 2 * j) for j, plan in enumerate(zip(source, target)))) for copy in pair
        ]

    def chip_plan(source, target, k):
        return [
            pltpu.make_async_remote_copy(
                src_ref=source(other),
                dst_ref=target,
                send_sem=qsems.at[2 * k, d],
                recv_sem=qsems.at[2 * k + 1, d],
                device_id=place,
                device_id_type=MESH,
            )
            for d, (other, place) in enumerate(zip(others, places))
        ]

    top = pl.ds(0, 1)
    halves = [
        near_copy(grad_ref.at[1 - par], rxh, 0),
        near_copy(thin_ref.at[1 - par, :, top, :], rxh_thin.at[:, top, :], 4),
    ]
    crosses = plan_all("ctx", n, lambda peer: cross_ref, rxx.at[me], sems.at[0], sems.at[1])
    terms = plan_all("ctx", n, lambda peer: mixed, rxm.at[me], sems.at[2], sems.at[3])
    blocks = [
        near_copy(tall_ref.at[:, rows, :], tall_ref.at[:, rows, :], j + 1) for j, rows in enumerate(places_here)
    ]
    fenced(halves + blocks + crosses, lambda: meet(count))
    rxx[me] = cross_ref[...]

    def first_sum():
        for copy in halves:
            copy.wait()
        half_sum[...] = grad_ref[par] + rxh[...]
        half_thin[:, 0:1, :] = thin_ref[par, :, 0:1, :] + rxh_thin[:, 0:1, :]
        rxq[chip] = half_sum[chip]
        rxq_thin[chip, 0:1, :] = half_thin[chip, 0:1, :]

    scattered = fenced(
        chip_copies(
            (lambda other: half_sum.at[other], lambda other: half_thin.at[other, top, :]),
            (rxq.at[chip], rxq_thin.at[chip, top, :]),
            0,
        ),
        first_sum,
    )
    for copy in blocks:
        copy.wait()
    inners = [jnp.zeros((96, 96), F32)] * 2
    for i in range(height):
        stack = jnp.concatenate(split3(tall_ref[i]), axis=0).astype(BF16)
        inners[i % 2] = inners[i % 2] + dot_nt(stack, stack)
    inner = inners[0] + inners[1]
    inner = inner[0:32] + inner[32:64] + inner[64:96]
    inner = inner[:, 0:32] + inner[:, 32:64] + inner[:, 64:96]
    mixed[...] = jnp.concatenate([inner, jnp.zeros((32, 96), F32)], axis=1)
    rxm[me] = mixed[...]
    fenced(terms)
    latents = tall_ref[height]
    bias_moment = momentum_rate * smom_ref[1] + full_nn(latents.T, tall_ref[height + 1])
    side = newton(gram_six(three(bias_moment)), NS_STEPS)
    advance(4)

    def share():
        for copy in crosses:
            copy.wait()
        total = rxx[0]
        for s in range(1, n):
            total = total + rxx[s]
        rxc[r] = total

    shared = fenced(
        plan_all("dp", rows_n, lambda peer: rxc.at[r], rxc.at[r], dsems.at[0], dsems.at[1]), share
    )
    advance(7)

    def second_sum():
        for copy in scattered:
            copy.wait()
        total = rxq[0]
        thin = rxq_thin[0, 0:1, :]
        for s in range(1, chips):
            total = total + rxq[s]
            thin = thin + rxq_thin[s, 0:1, :]
        fin[...] = total
        fin_thin[0:1, :] = thin
        sum_ref[par, chip] = total
        thin_sum[par, chip, 0:1, :] = thin

    gathered = fenced(
        chip_copies(
            (lambda other: fin, lambda other: fin_thin.at[top, :]),
            (sum_ref.at[par, chip], thin_sum.at[par, chip, top, :]),
            1,
        ),
        second_sum,
    )
    advance(6)
    move_ref[1] = next(side)
    for copy in terms:
        copy.wait()
    total = rxm[0]
    for s in range(1, n):
        total = total + rxm[s]
    inner = total[:, 0:32]
    for copy in shared:
        copy.wait()
    cross = jnp.concatenate([rxc[s] for s in range(rows_n)], axis=0)
    weight = momentum_rate * cross + 0.5 * full_nn(inner, latents)
    half = full_nn(latents.T, weight)
    slabs = [tall_ref[height + 2 + t, 8 * s : 8 * s + 8, :] for s in range(rows_n) for t in range(n)]
    gram = (momentum_rate * momentum_rate) * jnp.concatenate(slabs, axis=0) + (half + half.T)
    side = newton(gram, HEAD_SHARP)
    advance(11)

    def all_here():
        for copy in gathered:
            copy.wait()

    last = fenced(
        [
            near_copy(sum_ref.at[par], sum_ref.at[par], 3),
            near_copy(thin_sum.at[par, :, top, :], thin_sum.at[par, :, top, :], 5),
        ],
        all_here,
    )
    advance(6)
    move_ref[0] = next(side)
    for copy in last:
        copy.wait()


def update_kernel(
    live_all, groups_all, mom_ref, head_ref, tall_ref, move_ref, sum_ref, thin_ref, square_ref, smom_ref,
    small_ref, mmom_ref, mvar_ref,
    mom_out, head_out, copy_out, smom_out, square_out, scopy_out, mmom_out, mvar_out, small_out, mcopy_out,
    loss_out, mom, head, low_copy, left, wide, state, product, middle, store_sem,
):
    ring, unused, chunk = mom.shape
    chunks = mom_ref.shape[1] // chunk
    per = chunk // WIDTH

    def stores(k):
        lanes = pl.ds(pl.multiple_of(k * chunk, chunk), chunk)
        return [
            pltpu.make_async_copy(source.at[lax.rem(k, ring)], target.at[:, lanes], store_sem.at[j, lax.rem(k, ring)])
            for j, (source, target) in enumerate(((mom, mom_out), (head, head_out), (low_copy, copy_out)))
        ]

    height = tall_ref.shape[0] - 10
    latents = tall_ref[height]
    rows = jnp.concatenate([latents] * 3 + [jnp.zeros((32, WIDTH), F32)], axis=0)
    left[...] = rows.T.astype(BF16)
    ids = lax.broadcasted_iota(jnp.int32, (WIDTH, WIDTH), 0) == lax.broadcasted_iota(jnp.int32, (WIDTH, WIDTH), 1)
    move = move_ref[0] * (-head_rate * 0.2 * WIDTH)
    centre = jnp.sum(jnp.where(ids, move, 0.0)) * (1.0 / WIDTH)
    middle[0] = centre
    wide[...] = jnp.concatenate(three(jnp.where(ids, move - centre, move))[0:2], axis=0)
    narrow = small_rows(thin_ref)
    stats = narrow[15:16]
    lane = lax.broadcasted_iota(jnp.int32, (1, WIDTH), 1)
    weight = jnp.where(lane == 0, 1.0 / live_all, jnp.where(lane == 1, reg_weight / groups_all, 0.0))
    loss_out[...] = jnp.broadcast_to(jnp.sum(stats * weight), loss_out.shape)
    moment, second, new = adam_update(small_ref[...], narrow[0:15], mmom_ref[...], mvar_ref[...])
    mmom_out[...] = moment
    mvar_out[...] = second
    small_out[...] = new
    mcopy_out[...] = new.astype(BF16)
    keep = 1.0 - head_rate * decay_rate


    grads = [square_rows(sum_ref), full_nn(latents.T, tall_ref[height + 1])]
    for k in range(2):
        smom_out[k] = momentum_rate * smom_ref[k] + grads[k]
    gram = gram_six(three(smom_out[0]))
    scale = 1.0 / (jnp.sqrt(jnp.sum(jnp.where(ids, gram, 0.0))) + 1e-07)
    middle[1] = scale
    state[...] = gram * (scale * scale)
    product[...] = jnp.where(ids, 1.0, 0.0)

    def advance(k, step):
        slot = lax.rem(k, ring)

        @pl.when(k >= ring)
        def drained():
            for copy in stores(k - ring):
                copy.wait()

        def begin_tile(i):
            lanes = slice(i * WIDTH, (i + 1) * WIDTH)
            wide_lanes = pl.ds(pl.multiple_of(k * chunk + i * WIDTH, WIDTH), WIDTH)
            high, mid, low = three(tall_ref[k * per + i])
            right = jnp.concatenate([high, mid, low, jnp.zeros_like(high)], axis=0)
            moment = momentum_rate * mom_ref[:, wide_lanes] + dot_nn(left[...], right)
            mom[slot, :, lanes] = moment
            high = moment.astype(BF16)
            mid = (moment - high.astype(F32)).astype(BF16)
            return keep * head_ref[:, wide_lanes] + middle[0] * moment, high, mid

        def finish_tile(i):
            lanes = slice(i * WIDTH, (i + 1) * WIDTH)
            base, high, mid = ready[i]
            first = dot_nn(wide[...], high)
            new = (first[0:WIDTH] + dot_nn(wide[0:WIDTH, :], mid)) + (first[WIDTH:] + base)
            head[slot, :, lanes] = new
            low_copy[slot, :, lanes] = new.astype(BF16)

        ready = [begin_tile(0), begin_tile(1)]
        for i in range(per):
            if i + 2 < per:
                ready.append(begin_tile(i + 2))
            finish_tile(i)
            next(step, None)
        for copy in stores(k):
            copy.start()

    def both(k, carry):
        advance(k, newton_step(state, product))
        return carry

    def alone(k, carry):
        advance(k, iter(()))
        return carry

    lax.fori_loop(0, NS_STEPS, both, 0)
    lax.fori_loop(NS_STEPS, chunks, alone, 0)
    for k, move in enumerate((product[...] * middle[1], move_ref[1])):
        old = square_ref[k]
        change = 0.2 * WIDTH**0.5 * six(three(move), three(smom_out[k])) + decay_rate * old
        new = old - square_rates[k] * change
        square_out[k] = new
        scopy_out[k] = new.astype(BF16)
    for k in range(chunks - ring, chunks):
        for copy in stores(k):
            copy.wait()


def shape(*dims, dtype=F32):
    return jax.ShapeDtypeStruct(dims, dtype)


def dma_sems(*dims):
    return pltpu.SemaphoreType.DMA(dims)


def remote_params(ident, room=50):
    return pltpu.CompilerParams(collective_id=ident, has_side_effects=True, vmem_limit_bytes=room * MIB)


def plain_params(room=16):
    return pltpu.CompilerParams(vmem_limit_bytes=room * MIB)


CHUNK = 1024
RING = 4


def call_scatter(n, rows_n, lengths, pixels, ctx_mask, head_mom):
    micro, groups, slots = pixels.shape[1], pixels.shape[2], pixels.shape[4]
    return pl.pallas_call(
        functools.partial(scatter_kernel, n, rows_n),
        out_shape=[
            shape(n, 8, slots),
            shape(n, 8, 128),
            shape(n, 8, slots),
            shape(n, 8, 128),
            shape(WIDTH // rows_n, WIDTH),
        ],
        in_specs=[hbm_spec()] * 4,
        out_specs=[vmem_spec()] * 5,
        scratch_shapes=[
            pltpu.SMEM(lengths.shape, jnp.int32),
            pltpu.VMEM((1, micro, 5, groups, slots), F32),
            pltpu.VMEM(ctx_mask.shape, jnp.int32),
            pltpu.VMEM((n, 8, slots), F32),
            pltpu.VMEM((n, 8, 128), F32),
            pltpu.VMEM((n, 128), F32),
            pltpu.VMEM((WIDTH, head_mom.shape[1] // rows_n), F32),
            pltpu.VMEM((WIDTH, WIDTH), F32),
            pltpu.VMEM((rows_n, WIDTH // rows_n, WIDTH), F32),
            pltpu.VMEM((TILE, TILE), BF16),
            dma_sems(micro, n - 1),
            dma_sems(micro, n - 1),
            dma_sems(),
            dma_sems(2, rows_n - 1),
            dma_sems(3),
            dma_sems(2, n - 1),
        ],
        compiler_params=remote_params(1, 50),
        name="scatter_pixels",
        cost_estimate=busy(14),
    )(lengths, jnp.transpose(pixels, (0, 1, 3, 2, 4)), ctx_mask, head_mom)


def call_encode(received, seen, small_params, square_w):
    cap = received.shape[0] * received.shape[2] + 5 * SPAN
    return pl.pallas_call(
        encoder_kernel,
        out_shape=[shape(8, WIDTH), shape(8, 128), shape(8, cap), shape(1, dtype=jnp.int32)],
        in_specs=[vmem_spec()] * 4,
        out_specs=[vmem_spec()] * 3 + [smem_spec()],
        scratch_shapes=[
            pltpu.VMEM((8, 128), jnp.int32),
            pltpu.SMEM((8, 128), jnp.int32),
            pltpu.VMEM((3, WIDTH, SPAN), F32),
            pltpu.VMEM((WIDTH, WIDTH), BF16),
            pltpu.VMEM((WIDTH, 16), F32),
            pltpu.VMEM((WIDTH, SPAN), BF16),
            pltpu.VMEM((WIDTH, SPAN), BF16),
            dma_sems(),
        ],
        compiler_params=plain_params(),
        name="encode",
        cost_estimate=busy(10),
    )(received, seen, small_params, square_w)


def call_generate(n, latent, amount, head_w, tiles, share):
    height = WIDTH // n
    chunks = head_w.shape[1] // CHUNK
    return pl.pallas_call(
        functools.partial(theta_kernel, n),
        out_shape=[
            shape(WIDTH, WIDTH),
            shape(WIDTH, WIDTH, dtype=BF16),
            shape(8, WIDTH),
            shape(8, WIDTH),
            shape(8, WIDTH),
            shape(*tiles.shape),
            shape(*share.shape),
        ],
        in_specs=[vmem_spec()] * 2 + [any_spec()] + [vmem_spec()] * 2,
        out_specs=[vmem_spec()] * 7,
        scratch_shapes=[
            pltpu.VMEM((n, 8, WIDTH), F32),
            pltpu.VMEM((n, 8, 128), F32),
            pltpu.VMEM((chunks, WIDTH, CHUNK), F32),
            pltpu.VMEM((n, height, WIDTH), BF16),
            pltpu.VMEM((2, WIDTH, 128), F32),
            dma_sems(chunks),
            dma_sems(10, n - 1),
        ],
        compiler_params=remote_params(2),
        name="generate",
        cost_estimate=busy(17),
    )(latent, amount, head_w, tiles, share)


def call_siren(n, live_all, lengths, received, seen, gen, latent, small_params, square_w):
    cap = received.shape[0] * received.shape[2] + 5 * SPAN
    return pl.pallas_call(
        functools.partial(siren_kernel, live_all),
        out_shape=[shape(WIDTH, WIDTH), shape(8, WIDTH), shape(8, WIDTH)],
        in_specs=[smem_spec()] + [vmem_spec()] * 6,
        out_specs=[vmem_spec()] * 3,
        scratch_shapes=[
            pltpu.VMEM((8, cap), F32),
            pltpu.VMEM((8, 128), jnp.int32),
            pltpu.SMEM((8, 128), jnp.int32),
            pltpu.VMEM((WIDTH, WIDTH), BF16),
            pltpu.VMEM((WIDTH, SPAN), F32),
            pltpu.VMEM((WIDTH, SPAN), BF16),
            pltpu.VMEM((WIDTH, SPAN), BF16),
            pltpu.VMEM((WIDTH, SPAN), F32),
            pltpu.VMEM((WIDTH, SPAN), F32),
            pltpu.VMEM((WIDTH, SPAN), BF16),
            pltpu.VMEM((WIDTH, SPAN), BF16),
            pltpu.VMEM((WIDTH, SPAN), F32),
            pltpu.VMEM((WIDTH, SPAN), F32),
            pltpu.VMEM((WIDTH + 16, WIDTH), F32),
            pltpu.VMEM((WIDTH, 32), F32),
            pltpu.VMEM((WIDTH, 16), F32),
            pltpu.VMEM((8, SPAN), F32),
            dma_sems(),
        ],
        compiler_params=plain_params(),
        name="siren",
        cost_estimate=busy(16),
    )(lengths, received, seen, gen, latent, small_params, square_w)


def call_latent(n, groups_all, part, bias, theta, head_w, head_mom, z8, gram_part):
    height = WIDTH // n
    chunks = head_w.shape[1] // CHUNK
    slab = gram_part.shape[0] // n
    return pl.pallas_call(
        functools.partial(latent_kernel, n, groups_all),
        out_shape=[
            shape(8, WIDTH),
            shape(height + 2 + n, 8, WIDTH),
            shape(8, WIDTH),
        ],
        in_specs=[vmem_spec()] * 3 + [any_spec()] * 2 + [vmem_spec()] * 2,
        out_specs=[vmem_spec()] * 3,
        scratch_shapes=[
            pltpu.VMEM((WIDTH, WIDTH), F32),
            pltpu.VMEM((n, 8, WIDTH), F32),
            pltpu.VMEM((2, WIDTH, 128), F32),
            pltpu.VMEM((chunks, WIDTH, CHUNK), F32),
            pltpu.VMEM((chunks, WIDTH, CHUNK), F32),
            pltpu.VMEM((height, WIDTH, WIDTH), BF16),
            pltpu.VMEM((3, height, WIDTH, WIDTH), BF16),
            pltpu.VMEM((n, 8, WIDTH), F32),
            pltpu.VMEM((8, WIDTH), F32),
            pltpu.VMEM((height, 32, WIDTH), BF16),
            pltpu.VMEM((n, slab, WIDTH), F32),
            pltpu.VMEM((slab, WIDTH), F32),
            dma_sems(chunks),
            dma_sems(chunks),
            dma_sems(10, n - 1),
        ],
        compiler_params=remote_params(3),
        name="latent_grads",
        cost_estimate=busy(18),
    )(part, bias, theta, head_w, head_mom, z8, gram_part)


def call_back(counts, clist, small_params, square_w, latent_grad, inverse, tall, narrow, regular):
    return pl.pallas_call(
        encoder_back_kernel,
        out_shape=[shape(2, 16, 8, WIDTH), shape(2, 16, 8, 128)],
        in_specs=[smem_spec()] + [vmem_spec()] * 8,
        out_specs=[vmem_spec()] * 2,
        scratch_shapes=[
            pltpu.VMEM((3, WIDTH, SPAN), F32),
            pltpu.VMEM((WIDTH, WIDTH), BF16),
            pltpu.VMEM((WIDTH + 16, WIDTH), BF16),
            pltpu.VMEM((WIDTH, SPAN), F32),
            pltpu.VMEM((WIDTH, SPAN), F32),
            pltpu.VMEM((WIDTH, SPAN), F32),
            pltpu.VMEM((WIDTH, SPAN), F32),
            pltpu.VMEM((WIDTH, SPAN), BF16),
            pltpu.VMEM((WIDTH, SPAN), BF16),
            pltpu.VMEM((WIDTH, SPAN), BF16),
            pltpu.VMEM((WIDTH, SPAN), BF16),
            pltpu.VMEM((WIDTH + 16, WIDTH), F32),
            pltpu.VMEM((WIDTH, 32), F32),
            pltpu.VMEM((WIDTH, SPAN), F32),
            pltpu.VMEM((16, WIDTH), F32),
        ],
        compiler_params=plain_params(),
        name="encode_back",
        cost_estimate=busy(16),
    )(counts, clist, small_params, square_w, latent_grad, inverse, tall, narrow, regular)


def call_reduce(n, rows_n, grads, thin, own, far, cross, square_mom):
    chips = (rows_n // 2) * n
    return pl.pallas_call(
        functools.partial(reduce_kernel, n, rows_n),
        out_shape=[
            shape(*grads.shape),
            shape(*thin.shape),
            shape(own.shape[0], 8 * rows_n, WIDTH),
            shape(2, WIDTH, WIDTH),
        ],
        in_specs=[vmem_spec()] * 6,
        out_specs=[vmem_spec()] * 4,
        scratch_shapes=[
            pltpu.VMEM((chips, 8, WIDTH), F32),
            pltpu.VMEM((chips, 8, WIDTH), F32),
            pltpu.VMEM((chips, 8, WIDTH), F32),
            pltpu.VMEM((8, WIDTH), F32),
            pltpu.VMEM((chips, 8, 128), F32),
            pltpu.VMEM((chips, 8, 128), F32),
            pltpu.VMEM((chips, 8, 128), F32),
            pltpu.VMEM((8, 128), F32),
            pltpu.VMEM((32, 128), F32),
            pltpu.VMEM((n, 32, 128), F32),
            pltpu.VMEM((rows_n, 8, WIDTH), F32),
            pltpu.VMEM((n, 8, WIDTH), F32),
            dma_sems(4, n - 1),
            dma_sems(2, rows_n - 1),
            dma_sems(2, 6),
            dma_sems(8, chips - 1),
        ],
        compiler_params=remote_params(4, 16),
        name="reduce_grads",
        cost_estimate=busy(24),
    )(grads, thin, own, far, cross, square_mom)


def call_update(
    live_all, groups_all, head_mom, head_w, tall, move, sums, thin_sums, square_w, square_mom, small_params,
    small_mom, small_var,
):
    columns = head_w.shape[1]
    small_copy = shape(15, WIDTH, dtype=BF16)
    square_copy = shape(2, WIDTH, WIDTH, dtype=BF16)
    loss = shape(1, 128)
    others = [square_mom, square_w, square_copy, small_mom, small_var, small_params, small_copy, loss]
    return pl.pallas_call(
        functools.partial(update_kernel, live_all, groups_all),
        out_shape=[shape(WIDTH, columns), shape(WIDTH, columns), shape(WIDTH, columns, dtype=BF16)]
        + [shape(*one.shape, dtype=one.dtype) for one in others],
        in_specs=[vmem_spec()] * 11,
        out_specs=[any_spec()] * 3 + [vmem_spec()] * 8,
        scratch_shapes=[
            pltpu.VMEM((RING, WIDTH, CHUNK), F32),
            pltpu.VMEM((RING, WIDTH, CHUNK), F32),
            pltpu.VMEM((RING, WIDTH, CHUNK), BF16),
            pltpu.VMEM((WIDTH, 128), BF16),
            pltpu.VMEM((2 * WIDTH, WIDTH), BF16),
            pltpu.VMEM((WIDTH, WIDTH), F32),
            pltpu.VMEM((WIDTH, WIDTH), F32),
            pltpu.SMEM((2,), F32),
            dma_sems(3, RING),
        ],
        compiler_params=plain_params(30),
        name="update_all",
        cost_estimate=busy(12),
    )(
        head_mom, head_w, tall, move, sums, thin_sums, square_w, square_mom, small_params, small_mom, small_var
    )


def grouped(
    pixels, lengths, ctx_mask, head_w, head_mom, square_w, square_mom, small_params, small_mom, small_var
):
    micro, groups, slots = pixels.shape[1], pixels.shape[2], pixels.shape[4]
    n = lax.axis_size("ctx")
    rows_n = lax.axis_size("dp")
    live_all = rows_n * micro * (groups * slots * n * 5 // 8)
    groups_all = rows_n * micro * groups
    received, seen, tiles, share, gram_part = call_scatter(n, rows_n, lengths, pixels, ctx_mask, head_mom)
    latent, amount, clist, counts = call_encode(received, seen, small_params, square_w)
    theta, gen, z8, inverse, regular, group_rows, group_seen = call_generate(
        n, latent, amount, head_w, tiles, share
    )
    part, bias, narrow = call_siren(
        n, live_all, lengths, group_rows, group_seen, gen, z8, small_params, square_w
    )
    latent_grad, own, cross = call_latent(
        n, groups_all, part, bias, theta, head_w, head_mom, z8, gram_part
    )
    far = lax.ppermute(own, "dp", [(r, (r + rows_n // 2) % rows_n) for r in range(rows_n)])
    grads, thin = call_back(
        counts, clist, small_params, square_w, latent_grad, inverse, own, narrow, regular
    )
    sums, thin_sums, tall, move = call_reduce(n, rows_n, grads, thin, own, far, cross, square_mom)
    updated = call_update(
        live_all, groups_all, head_mom, head_w, tall, move, sums, thin_sums, square_w, square_mom, small_params,
        small_mom, small_var,
    )
    (
        head_moment,
        head_new,
        head_copy,
        square_moment,
        square_new,
        square_copy,
        small_moment,
        small_second,
        small_new,
        small_copy,
        loss,
    ) = updated
    return (
        head_moment,
        head_new,
        head_copy,
        square_moment,
        square_new,
        square_copy,
        small_moment,
        small_second,
        small_new,
        small_copy,
        loss[0, 0],
    )


def local(pixels, lengths, ctx_mask, head_w, *rest):
    n = lax.axis_size("ctx")
    fits = (
        pixels.shape[1] * pixels.shape[2] == n
        and n == 8
        and lax.axis_size("dp") == 4
        and pixels.shape[4] == 2048
        and head_w.shape == (WIDTH, 8192)
    )
    chosen = grouped if fits else general
    return chosen(pixels, lengths, ctx_mask, head_w, *rest)


def solution(mesh):
    placed = (
        P("dp", None, None, None, "ctx"),
        P("dp", None, None),
        P("dp", None, None, "ctx"),
        P(None, "ctx"),
        P(None, "ctx"),
        P(),
        P(),
        P(),
        P(),
        P(),
    )
    return jax.shard_map(
        local,
        mesh=mesh,
        in_specs=placed,
        out_specs=(
            P(None, "ctx"),
            P(None, "ctx"),
            P(None, "ctx"),
            P(),
            P(),
            P(),
            P(),
            P(),
            P(),
            P(),
            P(),
        ),
        check_vma=False,
    )
```

```python
import functools

import jax
import jax.numpy as jnp
from jax import lax
from jax.experimental import pallas as pl
from jax.experimental.pallas import tpu as pltpu
from jax.sharding import PartitionSpec as P

NS_STEPS = 5
STEP = 10


exact_arithmetic_mode = lax.Precision.HIGHEST
reg_weight = 0.5
momentum_rate = 0.95
head_rate = 0.003
square_rates = (0.3, 0.02)
adam_rate = 0.05
beta_first = 0.9
beta_second = 0.999
decay_rate = 0.01
first_coef = 3.4445
second_coef = -4.775
third_coef = 2.0315


def layer_norm(values, gain_row, bias_row):
    centered = values - jnp.mean(values, axis=-1, keepdims=True)
    variance = jnp.mean(centered * centered, axis=-1, keepdims=True)
    return centered * lax.rsqrt(variance + 1e-05) * gain_row + bias_row


def ns_update(current, gram_matrix):
    polynomial = second_coef * gram_matrix + third_coef * jnp.einsum(
        "kij,kjl->kil", gram_matrix, gram_matrix, precision=exact_arithmetic_mode
    )
    return first_coef * current + jnp.einsum(
        "kij,kjl->kil", polynomial, current, precision=exact_arithmetic_mode
    )


def orthogonal_local(matrices):
    norms = jnp.sqrt(jnp.sum(matrices * matrices, axis=(1, 2), keepdims=True))
    current = matrices / (norms + 1e-07)
    for sweep in range(NS_STEPS):
        gram_matrix = jnp.einsum("kij,klj->kil", current, current, precision=exact_arithmetic_mode)
        current = ns_update(current, gram_matrix)
    return current


def head_orthogonal(moment):
    current = moment[None]
    total = lax.psum(jnp.sum(moment * moment), "ctx")
    current = current / (jnp.sqrt(total) + 1e-07)
    for sweep in range(NS_STEPS):
        gram_matrix = lax.psum(
            jnp.dot(current[0], current[0].T, precision=exact_arithmetic_mode), "ctx"
        )
        current = ns_update(current, gram_matrix[None])
    return current[0]


def adam_update(params, grad, moment, second_moment):
    moment_new = beta_first * moment + (1.0 - beta_first) * grad
    second_new = beta_second * second_moment + (1.0 - beta_second) * grad * grad
    corrected = (
        moment_new
        / (1.0 - beta_first**STEP)
        / (jnp.sqrt(second_new / (1.0 - beta_second**STEP)) + 1e-08)
    )
    return (moment_new, second_new, params - adam_rate * (corrected + decay_rate * params))


def encoder_forward(features, context, small_params, second_low):
    first_pre = (
        jnp.einsum("gpc,cd->gpd", features, small_params[0:5], precision=exact_arithmetic_mode)
        + small_params[10]
    )
    first_act, gelu_first = jax.vjp(jax.nn.gelu, first_pre)
    normed, norm_back = jax.vjp(layer_norm, first_act, small_params[11], small_params[12])
    normed_low = normed.astype(jnp.bfloat16)
    second = (
        jnp.einsum("gpd,de->gpe", normed_low, second_low, preferred_element_type=jnp.float32)
        + small_params[13]
    )
    encoded, gelu_second = jax.vjp(jax.nn.gelu, second)
    summed = jnp.einsum("gp,gpe->ge", context, encoded, precision=exact_arithmetic_mode)
    return (
        summed,
        jnp.sum(context, axis=1),
        (first_pre, gelu_first, norm_back, normed_low, gelu_second),
    )


def general(
    pixels,
    lengths,
    ctx_mask,
    head_w,
    head_mom,
    square_w,
    square_mom,
    small_params,
    small_mom,
    small_var,
):
    micro_count = pixels.shape[1]
    groups = pixels.shape[2]
    slot_count = pixels.shape[4]
    model_width = square_w.shape[1]
    live_all = (
        lax.axis_size("dp") * micro_count * (groups * slot_count * lax.axis_size("ctx") * 5 // 8)
    )
    groups_all = lax.axis_size("dp") * micro_count * groups
    slot_ids = lax.axis_index("ctx") * slot_count + jnp.arange(slot_count, dtype=jnp.int32)
    head_low = head_w.astype(jnp.bfloat16)
    head_back = head_low.astype(jnp.float32)
    square_low = square_w.astype(jnp.bfloat16)
    bias_head = square_low[1].astype(jnp.float32)
    final_coefficient_reduced = small_params[7:10].astype(jnp.bfloat16)
    kept = []
    sum_list = []
    count_list = []
    for micro_index in range(micro_count):
        features = jnp.transpose(pixels[0, micro_index], (0, 2, 1))
        live_slot = slot_ids[None, :] < lengths[0, micro_index][:, None]
        context = jnp.where(live_slot & (ctx_mask[0, micro_index] == 1), 1.0, 0.0).astype(
            jnp.float32
        )
        query_mask = jnp.where(live_slot & (ctx_mask[0, micro_index] == 0), 1.0, 0.0).astype(
            jnp.float32
        )
        summed, counts, saved = encoder_forward(features, context, small_params, square_low[0])
        sum_list.append(summed)
        count_list.append(counts)
        kept.append((features, context, query_mask, saved))
    totals = [
        lax.psum((sum_list[index_micro], count_list[index_micro]), "ctx")
        for index_micro in range(micro_count)
    ]
    zeros_small = jnp.zeros((model_width,), jnp.float32)
    grad_first_w = jnp.zeros((5, model_width), jnp.float32)
    grad_coord_w = jnp.zeros((2, model_width), jnp.float32)
    grad_out_w = jnp.zeros((3, model_width), jnp.float32)
    grad_vectors = [zeros_small] * 5
    grad_square = jnp.zeros_like(square_w)
    latent_rows = []
    theta_rows = []
    squared = jnp.zeros((), jnp.float32)
    regular = jnp.zeros((), jnp.float32)
    for micro_index in range(micro_count):
        features, context, query_mask, saved = kept[micro_index]
        first_pre, gelu_first, norm_back, normed_low, gelu_second = saved
        summed, counts = totals[micro_index]
        divisor = counts[:, None] + 1.0
        latent_low = (summed / divisor).astype(jnp.bfloat16)
        latent_back = latent_low.astype(jnp.float32)
        generated = jnp.dot(latent_low, head_low, preferred_element_type=jnp.float32)
        gen_parts = generated.astype(jnp.bfloat16).reshape(groups, -1, model_width)
        gen_full = lax.all_gather(gen_parts, "ctx", axis=1, tiled=True)
        gen_bias = jnp.dot(latent_low, square_low[1], preferred_element_type=jnp.float32)
        coord_pre = (
            jnp.einsum(
                "gpc,cd->gpd",
                features[..., 3:5],
                small_params[5:7],
                precision=exact_arithmetic_mode,
            )
            + small_params[14]
        )
        siren_low = jnp.sin(30.0 * coord_pre).astype(jnp.bfloat16)
        siren_pre = (
            jnp.einsum("gpd,gde->gpe", siren_low, gen_full, preferred_element_type=jnp.float32)
            + gen_bias[:, None, :]
        )
        result_reduced_form = jnp.sin(30.0 * siren_pre).astype(jnp.bfloat16)
        estimated_colour_values = jnp.einsum(
            "kdg,cg->kcd",
            result_reduced_form,
            final_coefficient_reduced,
            preferred_element_type=jnp.float32,
        )
        errors = (
            estimated_colour_values - jnp.transpose(features[..., 0:3], (0, 2, 1))
        ) * query_mask[:, None, :]
        squared = squared + jnp.sum(errors * errors)
        regular = regular + jnp.sum(generated * generated)
        prediction_gradient = (2.0 / live_all * errors).astype(jnp.bfloat16)
        grad_out_w = grad_out_w + jnp.einsum(
            "dan,dnq->aq",
            prediction_gradient,
            result_reduced_form,
            preferred_element_type=jnp.float32,
        )
        grad_out = jnp.einsum(
            "xvw,vt->xwt",
            prediction_gradient,
            final_coefficient_reduced,
            preferred_element_type=jnp.float32,
        )
        grad_inner = (grad_out * 30.0 * jnp.cos(30.0 * siren_pre)).astype(jnp.bfloat16)
        gen_part = jnp.einsum(
            "gpd,gpe->gde", siren_low, grad_inner, preferred_element_type=jnp.float32
        )
        gen_grad = lax.psum_scatter(gen_part, "ctx", scatter_dimension=1, tiled=True).reshape(
            groups, -1
        )
        gen_grad = gen_grad + 2.0 * reg_weight / groups_all * generated
        bias_part = jnp.sum(grad_inner.astype(jnp.float32), axis=1)
        grad_siren = jnp.einsum(
            "gpe,gde->gpd", grad_inner, gen_full, preferred_element_type=jnp.float32
        )
        grad_coord = grad_siren * 30.0 * jnp.cos(30.0 * coord_pre)
        grad_coord_w = grad_coord_w + jnp.einsum(
            "gpc,gpd->cd", features[..., 3:5], grad_coord, precision=exact_arithmetic_mode
        )
        grad_vectors[4] = grad_vectors[4] + jnp.sum(grad_coord, axis=(0, 1))
        latent_rows.append(latent_back)
        theta_rows.append(gen_grad)
        latent_part = jnp.dot(gen_grad, head_back.T, precision=exact_arithmetic_mode)
        latent_part, bias_full = lax.psum((latent_part, bias_part), "ctx")
        grad_square = grad_square.at[1].add(
            jnp.dot(latent_back.T, bias_part, precision=exact_arithmetic_mode)
        )
        grad_latent = latent_part + jnp.dot(bias_full, bias_head.T, precision=exact_arithmetic_mode)
        grad_encoded = context[:, :, None] * (grad_latent / divisor)[:, None, :]
        (grad_second,) = gelu_second(grad_encoded)
        second_low = grad_second.astype(jnp.bfloat16)
        grad_square = grad_square.at[0].add(
            jnp.einsum("gpd,gpe->de", normed_low, second_low, preferred_element_type=jnp.float32)
        )
        grad_vectors[3] = grad_vectors[3] + jnp.sum(second_low.astype(jnp.float32), axis=(0, 1))
        grad_normed = jnp.einsum(
            "gpe,de->gpd", second_low, square_low[0], preferred_element_type=jnp.float32
        )
        grad_act, grad_gain, grad_beta = norm_back(grad_normed)
        (grad_first,) = gelu_first(grad_act)
        grad_first_w = grad_first_w + jnp.einsum(
            "gpc,gpd->cd", features, grad_first, precision=exact_arithmetic_mode
        )
        grad_vectors[0] = grad_vectors[0] + jnp.sum(grad_first, axis=(0, 1))
        grad_vectors[1] = grad_vectors[1] + grad_gain
        grad_vectors[2] = grad_vectors[2] + grad_beta
    grad_small = jnp.concatenate(
        [
            grad_first_w,
            grad_coord_w,
            grad_out_w,
            jnp.stack(
                [
                    grad_vectors[0],
                    grad_vectors[1],
                    grad_vectors[2],
                    grad_vectors[3],
                    grad_vectors[4],
                ]
            ),
        ],
        axis=0,
    )
    grad_small, grad_square, stat_sums = lax.psum(
        (grad_small, grad_square, jnp.stack([squared, regular])), ("dp", "ctx")
    )
    latent_stack = jnp.concatenate(latent_rows, axis=0)
    theta_stack = jnp.concatenate(theta_rows, axis=0)
    grad_head = lax.psum(
        jnp.dot(latent_stack.T, theta_stack, precision=exact_arithmetic_mode), "dp"
    )
    loss_value = stat_sums[0] / live_all + reg_weight * stat_sums[1] / groups_all
    head_moment = momentum_rate * head_mom + grad_head
    head_dir = head_orthogonal(head_moment)
    head_new = head_w - head_rate * (0.2 * model_width * head_dir + decay_rate * head_w)
    square_moment = momentum_rate * square_mom + grad_square
    rates = jnp.array(square_rates, jnp.float32)[:, None, None]
    square_new = square_w - rates * (
        0.2 * model_width**0.5 * orthogonal_local(square_moment) + decay_rate * square_w
    )
    small_moment, small_second, small_new = adam_update(
        small_params, grad_small, small_mom, small_var
    )
    return (
        head_moment,
        head_new,
        head_new.astype(jnp.bfloat16),
        square_moment,
        square_new,
        square_new.astype(jnp.bfloat16),
        small_moment,
        small_second,
        small_new,
        small_new.astype(jnp.bfloat16),
        loss_value,
    )


MESH = pl.DeviceIdType.MESH
F32 = jnp.float32
BF16 = jnp.bfloat16
WIDTH = 256
TILE = 256
MIB = 1024 * 1024
SPAN = 768
QUARTER = 64
HALF = 128
TURN = 30.0 / 6.283185307179586
GELU_ONE = 0.7978845608028654
GELU_CUBE = GELU_ONE * 0.044715
GELU_SCALE = GELU_CUBE ** (1.0 / 3.0)
GELU_SLOPE = GELU_ONE / GELU_SCALE
NORM_EPS = 1e-05 * (2.0 * GELU_SCALE) ** 2
SIN_TERMS = (4.442860272, -7.307432505, 3.594782484, -0.784372885)


def any_spec():
    return pl.BlockSpec(memory_space=pl.ANY)


def hbm_spec():
    return pl.BlockSpec(memory_space=pltpu.HBM)


def busy(micros):
    return pl.CostEstimate(flops=micros * 10**9, bytes_accessed=micros * 10**5, transcendentals=0)


def vmem_spec():
    return pl.BlockSpec(memory_space=pltpu.VMEM)


def smem_spec():
    return pl.BlockSpec(memory_space=pltpu.SMEM)


def turned(matrix):
    pad = jnp.zeros((matrix.shape[0], 128 - matrix.shape[1]), F32)
    return jnp.concatenate([matrix, pad], axis=1).T


def weave(order, first, second):
    for letter in order:
        next(first if letter == "A" else second, None)
    for rest in (first, second):
        for unused in rest:
            pass


def dot_nn(a, b):
    return lax.dot_general(a, b, (((1,), (0,)), ((), ())), preferred_element_type=F32)


def dot_nt(a, b):
    return lax.dot_general(a, b, (((1,), (1,)), ((), ())), preferred_element_type=F32)


def full_nn(a, b):
    return lax.dot_general(
        a, b, (((1,), (0,)), ((), ())), precision=lax.Precision.HIGHEST, preferred_element_type=F32
    )


def full_nt(a, b):
    return lax.dot_general(
        a, b, (((1,), (1,)), ((), ())), precision=lax.Precision.HIGHEST, preferred_element_type=F32
    )


def split3(v):
    high = v.astype(BF16).astype(F32)
    rest = v - high
    mid = rest.astype(BF16).astype(F32)
    return high, mid, rest - mid


def hail(peers):
    barrier = pltpu.get_barrier_semaphore()
    for peer in peers:
        pl.semaphore_signal(barrier, inc=1, device_id=peer, device_id_type=MESH)
    return len(peers)


def meet(count):
    pl.semaphore_wait(pltpu.get_barrier_semaphore(), count)


def greet(peers):
    meet(hail(peers))


def ring_peers(axis, n):
    me = lax.axis_index(axis)
    return [lax.rem(me + d, n) for d in range(1, n)]


def plan_all(axis, n, source, target, send_sem, recv_sem):
    return [
        pltpu.make_async_remote_copy(
            src_ref=source(peer),
            dst_ref=target,
            send_sem=send_sem.at[d],
            recv_sem=recv_sem.at[d],
            device_id={axis: peer},
            device_id_type=MESH,
        )
        for d, peer in enumerate(ring_peers(axis, n))
    ]


def send_all(*plan):
    copies = plan_all(*plan)
    for copy in copies:
        copy.start()
    return copies


def fenced(copies, before=None):
    @pl.when(lax.axis_index("ctx") >= 0)
    def run():
        if before is not None:
            before()
        for copy in copies:
            copy.start()

    return copies


def column(row, width):
    return jnp.broadcast_to(row, (width, row.shape[1])).T


def gelu_twice(y):
    return y + y * jnp.tanh(y * (GELU_SLOPE + y * y))


def gelu_both(y):
    square = y * y
    above = 1.0 + jnp.tanh(y * (GELU_SLOPE + square))
    value = y * above
    return value, above + (value * (2.0 - above)) * (3.0 * square + GELU_SLOPE)


def plain_twice(x):
    return x + x * jnp.tanh(x * (GELU_ONE + GELU_CUBE * (x * x)))


def plain_slope(x):
    square = GELU_CUBE * (x * x)
    above = 1.0 + jnp.tanh(x * (GELU_ONE + square))
    return above + (x * above) * (2.0 - above) * (3.0 * square + GELU_ONE)


def sine_pair(turns):
    frac = turns - jnp.round(turns)
    square = frac * frac
    s = SIN_TERMS[3] * square + SIN_TERMS[2]
    s = s * square + SIN_TERMS[1]
    s = (s * square + SIN_TERMS[0]) * frac
    cosine = 1.0 - s * s
    rest = 1.0 + cosine
    return s * (rest * lax.rsqrt(rest)), cosine


def triple_weights(block):
    high, mid, low = split3(block)
    rows = jnp.concatenate([high, mid, high, low, mid, high], axis=0)
    pad = jnp.zeros((128 - rows.shape[0], rows.shape[1]), F32)
    return jnp.concatenate([rows, pad], axis=0).T.astype(BF16)[:, 0:48]


def triple_from_list(rows):
    high, mid, low = split3(rows)
    return jnp.concatenate([high, high, mid, high, mid, low], axis=0).astype(BF16)


def three(matrix):
    high = matrix.astype(BF16)
    rest = matrix - high.astype(F32)
    mid = rest.astype(BF16)
    return high, mid, (rest - mid.astype(F32)).astype(BF16)


def six(left, right):
    rows = left[0].shape[0]
    first = dot_nn(jnp.concatenate(left, axis=0), right[0])
    second = dot_nn(jnp.concatenate(left[0:2], axis=0), right[1])
    third = dot_nn(left[0], right[2])
    return (first[0:rows] + second[0:rows] + third) + (
        first[rows : 2 * rows] + second[rows:] + first[2 * rows :]
    )


def few(left, right):
    rows = left[0].shape[0]
    first = dot_nn(jnp.concatenate(left[0:2], axis=0), right[0])
    return (first[0:rows] + dot_nn(left[0], right[1])) + first[rows:]


def gram_six(parts):
    high, mid, low = parts
    both = jnp.concatenate([high, mid], axis=1)
    cross = dot_nt(jnp.concatenate([high, high], axis=1), jnp.concatenate([mid, low], axis=1))
    return dot_nt(both, both) + (cross + cross.T)


def order_rows(row, per):
    return jnp.concatenate([row[:, k * TILE : (k + 1) * TILE] for k in range(per)], axis=0)


def bring_counts(seen_ref, cnt_v, cnt_s, sem):
    for s in range(seen_ref.shape[0]):
        cnt_v[s : s + 1, :] = seen_ref[s, 0:1, :].astype(jnp.int32)
    counts = pltpu.make_async_copy(cnt_v, cnt_s, sem)
    counts.start()
    return counts


def put(target, rows, extra, offset, start, amount):
    lane_ids = lax.broadcasted_iota(jnp.int32, (8, TILE), 1)
    shift = lax.rem(offset, TILE)
    base = pl.multiple_of(offset - shift, TILE)
    marks = [jnp.full((1, TILE), value, F32) for value in (0.0, 1.0, extra)]
    moved = pltpu.roll(jnp.concatenate([rows] + marks, axis=0), lax.rem(shift - start + TILE, TILE), 1)
    here = (lane_ids >= shift) & (lane_ids < shift + amount)
    there = lane_ids < shift + amount - TILE
    target[:, pl.ds(base, TILE)] += jnp.where(here, moved, 0.0)
    target[:, pl.ds(pl.multiple_of(base + TILE, TILE), TILE)] = jnp.where(there, moved, 0.0)


def clear_tail(target, amount):
    start = pl.multiple_of((amount // TILE + 1) * TILE, TILE)
    for step in range(4 * SPAN // TILE):
        target[:, pl.ds(start + step * TILE, TILE)] = jnp.zeros((8, TILE), F32)


def weight_block(weights, bias, place):
    rows = weights.shape[0]
    parts = []
    if place > 0:
        parts.append(jnp.zeros((place, WIDTH), F32))
    parts.append(weights)
    if place + rows < 6:
        parts.append(jnp.zeros((6 - place - rows, WIDTH), F32))
    parts.append(bias)
    parts.append(jnp.zeros((1, WIDTH), F32))
    return jnp.concatenate(parts, axis=0)


def scatter_kernel(
    n, rows_n, len_hbm, pix_hbm, mask_hbm, mom_ref, rx_ref, seen_ref, tiles_ref, share_ref, gram_ref,
    len_ref, pix_ref, mask_ref, stage, stage_n, told, buf, own, slab_rx, upper,
    send_sem, recv_sem, load_sem, slab_sem, own_sem, tell_sem,
):
    brought = [
        pltpu.make_async_copy(source, target, own_sem.at[j])
        for j, (source, target) in enumerate(((len_hbm, len_ref), (pix_hbm, pix_ref), (mask_hbm, mask_ref)))
    ]
    for copy in brought:
        copy.start()
    me = lax.axis_index("ctx")
    peers = ring_peers("ctx", n)
    r = lax.axis_index("dp")
    span = buf.shape[1]
    load = pltpu.make_async_copy(mom_ref.at[:, pl.ds(pl.multiple_of(r * span, span), span)], buf, load_sem)
    load.start()
    count = hail([{"ctx": peer} for peer in peers] + [{"dp": peer} for peer in ring_peers("dp", rows_n)])
    slots = pix_ref.shape[4]
    per = slots // TILE
    groups = mask_ref.shape[2]
    row_ids = lax.broadcasted_iota(jnp.int32, (TILE, TILE), 0)
    upper[...] = jnp.where(row_ids <= lax.broadcasted_iota(jnp.int32, (TILE, TILE), 1), 1.0, 0.0).astype(BF16)
    row_ids = row_ids.astype(F32)
    lane_ids = lax.broadcasted_iota(jnp.int32, (TILE, TILE), 1).astype(F32)
    place = (
        lax.broadcasted_iota(jnp.int32, (per, TILE), 0) * TILE
        + lax.broadcasted_iota(jnp.int32, (per, TILE), 1)
        + me * slots
    )
    pad = jnp.zeros((3, TILE), F32)
    ones = jnp.ones((16, TILE), BF16)
    blank = jnp.zeros((128 - 2 * per, TILE), BF16)
    wide_ids = lax.broadcasted_iota(jnp.int32, (per, 128), 1)
    told[...] = jnp.zeros_like(told)

    def arrange(b):
        def one(j, carry):
            g = b * groups + j
            mask = order_rows(mask_ref[0, b, pl.ds(j, 1), :], per)
            live = place < len_ref[0, b, j]
            context = jnp.where(live & (mask == 1), 1.0, 0.0)
            query = jnp.where(live & (mask == 0), 1.0, 0.0)
            both = jnp.concatenate([context, query], axis=0).astype(BF16)
            order = dot_nn(both, upper[...])
            before_c, before_q = order[0:per], order[per : 2 * per]
            live_c = before_c[:, TILE - 1 : TILE]
            target = jnp.where(
                context > 0.5, before_c, jnp.where(query > 0.5, live_c + before_q, 0.0)
            ) - 1.0
            amounts = dot_nt(ones, jnp.concatenate([both, blank], axis=0))[0:1]
            share_ref[g, 0:1, :] = amounts
            for t in range(per):
                place_t = pl.ds(lax.rem(g + t, n), 1)
                told[place_t, :] = jnp.where(wide_ids[0:1] == g, live_c[t : t + 1], told[place_t, :])
            for t in range(per):
                rows = jnp.concatenate(
                    [pix_ref[0, b, c, pl.ds(j, 1), t * TILE : (t + 1) * TILE] for c in range(5)]
                    + [pad], axis=0
                )
                high, mid, low = split3(rows)
                stack = jnp.concatenate([high, mid, low, jnp.zeros((8, TILE), F32)], axis=0).astype(BF16)
                if t % 2 == 0:
                    chosen = jnp.where(row_ids == target[t : t + 1], 1.0, 0.0).astype(BF16)
                    found = dot_nt(stack, chosen)
                else:
                    spot = column(target[t : t + 1], 128)
                    chosen = jnp.where(lane_ids == jnp.concatenate([spot, spot], axis=1), 1.0, 0.0).astype(BF16)
                    found = dot_nn(stack, chosen)
                found = found[0:8] + found[8:16] + found[16:24]
                tiles_ref[g, :, t * TILE : (t + 1) * TILE] = found
                stage[lax.rem(g + t, n), :, pl.ds(pl.multiple_of(g * TILE, TILE), TILE)] = found
            return carry

        lax.fori_loop(0, groups, one, 0)

    copies = []
    for copy in brought:
        copy.wait()
    for b in range(mask_ref.shape[1]):
        arrange(b)
        if b == 0:
            meet(count)
        lanes = pl.ds(b * groups * TILE, groups * TILE)
        copies += fenced(
            plan_all(
                "ctx",
                n,
                lambda peer: stage.at[peer, pl.ds(0, 5), lanes],
                rx_ref.at[me, pl.ds(0, 5), lanes],
                send_sem.at[b],
                recv_sem.at[b],
            )
        )
    for p in range(n):
        stage_n[p, 0:1, :] = told[p : p + 1, :]
    top = pl.ds(0, 1)
    copies += fenced(
        plan_all("ctx", n, lambda peer: stage_n.at[peer, top, :], seen_ref.at[me, top, :], tell_sem.at[0], tell_sem.at[1])
    )
    rx_ref[me, 0:5, :] = stage[me, 0:5, :]
    seen_ref[me, 0:1, :] = stage_n[me, 0:1, :]
    quarter = gram_ref.shape[0]
    same = jnp.zeros((WIDTH, WIDTH), F32)
    cross = jnp.zeros((WIDTH, WIDTH), F32)
    load.wait()
    for i in range(buf.shape[1] // WIDTH):
        high, mid, low = three(buf[:, i * WIDTH : (i + 1) * WIDTH])
        both = jnp.concatenate([high, mid], axis=1)
        same = same + dot_nt(both, both)
        cross = cross + dot_nt(jnp.concatenate([high, high], axis=1), jnp.concatenate([mid, low], axis=1))
    own[...] = same + (cross + cross.T)
    slabs = fenced(
        plan_all(
            "dp",
            rows_n,
            lambda peer: own.at[pl.ds(pl.multiple_of(peer * quarter, quarter), quarter), :],
            slab_rx.at[r],
            slab_sem.at[0],
            slab_sem.at[1],
        )
    )
    slab_rx[r] = own[pl.ds(pl.multiple_of(r * quarter, quarter), quarter), :]
    for copy in slabs:
        copy.wait()
    total = slab_rx[0]
    for s in range(1, rows_n):
        total = total + slab_rx[s]
    gram_ref[...] = total
    for copy in copies:
        copy.wait()


def encoder_kernel(
    rx_ref, seen_ref, small_ref, square_ref, z_ref, amount_ref, clist, stats_ref, count_ref, cnt_v, cnt_s, wide, second, zacc, low_a, low_b, sem
):
    sources = rx_ref.shape[0]
    per = rx_ref.shape[2] // TILE
    counts = bring_counts(seen_ref, cnt_v, cnt_s, sem)
    small = small_ref[...]
    first = triple_weights(weight_block(small[0:5] * GELU_SCALE, small[10:11] * GELU_SCALE, 0))
    wide[0] = column(small[11:12], SPAN)
    wide[1] = column(small[12:13], SPAN)
    wide[2] = column(small[13:14], SPAN)
    second[...] = square_ref[0].T.astype(BF16)
    zacc[...] = jnp.zeros_like(zacc)
    clist[:, 0:TILE] = jnp.zeros((8, TILE), F32)
    counts.wait()

    def place_tile(s, offset):
        for k in range(per):
            amount = cnt_s[s, k]
            put(clist, rx_ref[s, 0:5, k * TILE : (k + 1) * TILE], k + 1.0, offset, 0, amount)
            offset = offset + amount
        return offset

    num_c = lax.fori_loop(0, sources, place_tile, jnp.int32(0))
    clear_tail(clist, num_c)
    count_ref[0] = num_c
    ids = lax.broadcasted_iota(jnp.int32, (16, SPAN), 0).astype(F32) + 1.0

    def window(t):
        return clist[:, pl.ds(pl.multiple_of(t * SPAN, SPAN), SPAN)]

    def begin(t, low):
        pre = dot_nn(first, triple_from_list(window(t)))
        parts = []
        total = jnp.zeros((1, SPAN), F32)
        for c in range(0, WIDTH, HALF):
            parts.append(gelu_twice(pre[c : c + HALF]))
            total = total + jnp.sum(parts[-1], axis=0, keepdims=True)
            yield
        mean = total * (1.0 / WIDTH)
        total = jnp.zeros((1, SPAN), F32)
        for c in range(len(parts)):
            parts[c] = parts[c] - mean
            total = total + jnp.sum(parts[c] * parts[c], axis=0, keepdims=True)
        inverse = lax.rsqrt(total * (1.0 / WIDTH) + NORM_EPS)
        stats_ref[0:1, pl.ds(pl.multiple_of(t * SPAN, SPAN), SPAN)] = mean
        stats_ref[1:2, pl.ds(pl.multiple_of(t * SPAN, SPAN), SPAN)] = inverse
        yield
        for c in range(len(parts)):
            rows = slice(c * HALF, (c + 1) * HALF)
            low[rows, :] = (parts[c] * inverse * wide[0, rows, :] + wide[1, rows, :]).astype(BF16)
        yield

    def finish(t, low):
        pre = dot_nn(second[...], low[...])
        yield
        highs, rests = [], []
        for c in range(0, WIDTH, HALF):
            encoded = plain_twice(pre[c : c + HALF] + wide[2, c : c + HALF, :])
            highs.append(encoded.astype(BF16))
            rests.append((encoded - highs[-1].astype(F32)).astype(BF16))
            yield
        owner = jnp.where(ids == window(t)[7:8], 1.0, 0.0).astype(BF16)
        right = jnp.concatenate([jnp.concatenate(highs, axis=0), jnp.concatenate(rests, axis=0)], axis=1)
        zacc[...] += dot_nt(right, jnp.concatenate([owner, owner], axis=1))
        yield

    def pair(p, carry):
        weave("BAABABBABABA", begin(2 * p + 1, low_b), finish(2 * p, low_a))
        weave("BAABABBABABA", begin(2 * p + 2, low_a), finish(2 * p + 1, low_b))
        return carry

    spans = (num_c + SPAN - 1) // SPAN
    weave("", begin(0, low_a), iter(()))
    lax.fori_loop(0, spans // 2, pair, 0)

    @pl.when(lax.rem(spans, 2) == 1)
    def last():
        weave("", iter(()), finish(spans - 1, low_a))

    z_ref[...] = turned(zacc[...])[0:8] * 0.5
    total = seen_ref[0, 0:1, :]
    for s in range(1, sources):
        total = total + seen_ref[s, 0:1, :]
    amount_ref[...] = jnp.broadcast_to(total, (8, 128))


def theta_kernel(
    n, z_ref, amount_ref, head_ref, tiles_ref, share_ref, theta_ref, gen_ref, z8_ref, inv_ref, reg_ref,
    rx_ref, seen_ref, zall, nall, head, give, turn, load_sem, sems,
):
    me = lax.axis_index("ctx")
    peers = ring_peers("ctx", n)
    chunk = head.shape[2]
    per = chunk // WIDTH

    def load(k):
        return pltpu.make_async_copy(head_ref.at[:, pl.ds(k * chunk, chunk)], head.at[k], load_sem.at[k])

    for k in range(head.shape[0]):
        load(k).start()
    greet([{"ctx": peer} for peer in peers])
    top = pl.ds(0, 1)
    latents = send_all("ctx", n, lambda peer: z_ref, zall.at[me], sems.at[0], sems.at[1])
    latents += send_all(
        "ctx", n, lambda peer: amount_ref.at[top, :], nall.at[me, top, :], sems.at[6], sems.at[7]
    )
    pixels = send_all(
        "ctx",
        n,
        lambda peer: tiles_ref.at[peer, pl.ds(0, 5), :],
        rx_ref.at[me, pl.ds(0, 5), :],
        sems.at[2],
        sems.at[3],
    )
    pixels += send_all(
        "ctx", n, lambda peer: share_ref.at[peer, top, :], seen_ref.at[me, top, :], sems.at[8], sems.at[9]
    )
    zall[me] = z_ref[...]
    nall[me, 0:1, :] = amount_ref[0:1, :]
    rx_ref[me, 0:5, :] = tiles_ref[me, 0:5, :]
    seen_ref[me, 0:1, :] = share_ref[me, 0:1, :]
    for copy in latents:
        copy.wait()
    total = zall[0]
    amounts = nall[0, 0:1, :]
    for s in range(1, n):
        total = total + zall[s]
        amounts = amounts + nall[s, 0:1, :]
    lanes = lax.broadcasted_iota(jnp.int32, (8, 128), 1)
    rows = lax.broadcasted_iota(jnp.int32, (8, 128), 0)
    counts = jnp.sum(jnp.where(lanes == rows, amounts, 0.0), axis=1, keepdims=True) + 1.0
    latent = (total / counts).astype(BF16).astype(F32)
    z8_ref[...] = latent
    inv_ref[...] = jnp.broadcast_to(0.5 / counts, (8, WIDTH))
    left = jnp.concatenate([latent, jnp.zeros((8, WIDTH), F32)], axis=0).astype(BF16)
    regular = jnp.zeros((8, WIDTH), F32)
    for k in range(head.shape[0]):
        load(k).wait()
        part = dot_nn(left, head[k].astype(BF16))[0:8]
        for i in range(per):
            piece = part[:, i * WIDTH : (i + 1) * WIDTH]
            theta_ref[pl.ds((k * per + i) * 8, 8), :] = piece
            for half in range(2):
                turn[half, pl.ds((k * per + i) * 8, 8), :] = piece[:, half * 128 : half * 128 + 128]
            regular = regular + piece * piece
    reg_ref[...] = regular
    height = WIDTH // n
    for g in range(n):
        for half in range(2):
            give[g, :, half * 128 : half * 128 + 128] = turn[half, pl.ds(g, height, stride=8), :].astype(BF16)
    mine = pl.ds(pl.multiple_of(me * height, height), height)
    parts = fenced(
        plan_all("ctx", n, lambda peer: give.at[peer], gen_ref.at[mine, :], sems.at[4], sems.at[5])
    )
    gen_ref[mine, :] = give[me]
    for copy in pixels + parts:
        copy.wait()


def siren_kernel(
    live_all, len_ref, rx_ref, seen_ref, gen_ref, z_ref, small_ref, square_ref, out_ref, bias_ref, narrow_ref,
    q_ref, cnt_v, cnt_s, inner, shift, sa, sb, ca, cb, ma, mb, na, nb, acc_g, acc_c, acc_o, acc_e, sem,
):
    sin_in, cos_in, sin_mid, cos_mid = (sa, sb), (ca, cb), (ma, mb), (na, nb)
    me = lax.axis_index("ctx")
    per = rx_ref.shape[2] // TILE
    groups = len_ref.shape[2]
    length = len_ref[0, me // groups, lax.rem(me, groups)]
    counts = bring_counts(seen_ref, cnt_v, cnt_s, sem)
    small = small_ref[...]
    coord = triple_weights(weight_block(small[5:7] * TURN, small[14:15] * TURN, 3))
    latent = jnp.broadcast_to(z_ref[pl.ds(me, 1), :], (16, WIDTH)).astype(BF16)
    bias = dot_nn(latent, square_ref[1].astype(BF16))[0:1]
    inner[...] = gen_ref[...].astype(F32).T.astype(BF16)
    shift[...] = column(bias * TURN, SPAN)
    final = small[7:10].astype(BF16).astype(F32)
    final_rows = jnp.concatenate([final, jnp.zeros((13, WIDTH), F32)], axis=0).astype(BF16)
    large = final * 30.0
    high = large.astype(BF16).astype(F32)
    gap = jnp.zeros((5, WIDTH), F32)
    final_cols = jnp.concatenate([high, gap, large - high, jnp.zeros((117, WIDTH), F32)], axis=0).T.astype(BF16)[:, 0:16]
    for ref in (acc_g, acc_c, acc_o, acc_e):
        ref[...] = jnp.zeros_like(ref)
    scale = 2.0 / live_all
    ones = jnp.ones((16, SPAN), BF16)
    q_ref[:, 0:TILE] = jnp.zeros((8, TILE), F32)
    counts.wait()

    def place_tile(s, offset):
        for k in range(per):
            amount = cnt_s[s, per + k]
            put(q_ref, rx_ref[s, 0:5, k * TILE : (k + 1) * TILE], 0.0, offset, cnt_s[s, k], amount)
            offset = offset + amount
        return offset

    num_q = lax.fori_loop(0, (length + per * TILE - 1) // (per * TILE), place_tile, jnp.int32(0))
    clear_tail(q_ref, num_q)
    ids = lax.broadcasted_iota(jnp.int32, (8, SPAN), 0)

    def window(t):
        return q_ref[:, pl.ds(pl.multiple_of(t * SPAN, SPAN), SPAN)]

    def ahead(t, k):
        turns = dot_nn(coord, triple_from_list(window(t)))
        for c in range(0, WIDTH, WIDTH):
            s_in, c_in = sine_pair(turns[c : c + WIDTH])
            sin_in[k][c : c + WIDTH, :] = s_in.astype(BF16)
            cos_in[k][c : c + WIDTH, :] = c_in
            yield
        turns = dot_nn(inner[...], sin_in[k][...])
        yield
        for c in range(0, WIDTH, WIDTH):
            s_mid, c_mid = sine_pair(turns[c : c + WIDTH] * TURN + shift[c : c + WIDTH, :])
            sin_mid[k][c : c + WIDTH, :] = s_mid.astype(BF16)
            cos_mid[k][c : c + WIDTH, :] = c_mid
            yield

    def back_part(t, k):
        rows = window(t)
        pred = dot_nn(final_rows, sin_mid[k][...])[0:8]
        error = jnp.where(ids < 3, (pred - rows) * rows[6:7], 0.0)
        acc_e[...] += error * error
        slope = (error * scale).astype(BF16).astype(F32)
        slope = jnp.concatenate([slope, slope], axis=0).astype(BF16)
        yield
        acc_o[...] += dot_nt(sin_mid[k][...], slope)
        back = (cos_mid[k][...] * dot_nn(final_cols, slope)).astype(BF16)
        yield
        grads = dot_nn(gen_ref[...], back)
        yield
        outer = cos_in[k][...] * grads
        high = outer.astype(BF16)
        low = (outer - high.astype(F32)).astype(BF16)
        yield
        acc_g[...] += dot_nt(jnp.concatenate([sin_in[k][...], ones], axis=0), back)
        yield
        left = jnp.concatenate(split3(rows) + (jnp.zeros((8, SPAN), F32),), axis=0).astype(BF16)
        acc_c[...] += dot_nt(jnp.concatenate([high, low], axis=1), jnp.concatenate([left, left], axis=1))
        yield

    def pair(p, carry):
        weave("BABABABAABABAA", ahead(2 * p + 1, 1), back_part(2 * p, 0))
        weave("BABABABAABABAA", ahead(2 * p + 2, 0), back_part(2 * p + 1, 1))
        return carry

    spans = (num_q + SPAN - 1) // SPAN
    weave("", ahead(0, 0), iter(()))
    lax.fori_loop(0, spans // 2, pair, 0)

    @pl.when(lax.rem(spans, 2) == 1)
    def last():
        weave("", iter(()), back_part(spans - 1, 0))

    out_ref[...] = acc_g[0:WIDTH, :]
    bias_ref[...] = acc_g[WIDTH : WIDTH + 8, :]
    coords = turned(acc_c[...])
    coords = (coords[0:8] + coords[8:16] + coords[16:24]) * 30.0
    narrow_ref[0:2, :] = coords[3:5]
    narrow_ref[2:5, :] = turned(acc_o[...])[0:3]
    narrow_ref[5:6, :] = coords[6:7]
    narrow_ref[6:7, :] = jnp.broadcast_to(jnp.sum(acc_e[...]), (1, WIDTH))
    narrow_ref[7:8, :] = jnp.zeros((1, WIDTH), F32)


def latent_kernel(
    n, groups_all, part_ref, bias_ref, theta_ref, head_ref, mom_ref, z8_ref, gram_ref,
    dz_ref, tall_ref, cross_ref,
    rx, rxb, turn, head, mom, low_head, low_mom, rxz, dz_own, lefts, rxs, slab_sum, load_sem, mom_sem, sems,
):
    me = lax.axis_index("ctx")
    peers = ring_peers("ctx", n)
    chunk = head.shape[2]
    per = chunk // WIDTH
    height = WIDTH // n

    def load(k):
        return pltpu.make_async_copy(head_ref.at[:, pl.ds(k * chunk, chunk)], head.at[k], load_sem.at[k])

    def load_mom(k):
        return pltpu.make_async_copy(mom_ref.at[:, pl.ds(k * chunk, chunk)], mom.at[k], mom_sem.at[k])

    for k in range(head.shape[0]):
        load(k).start()
    for k in range(head.shape[0]):
        load_mom(k).start()
    greet([{"ctx": peer} for peer in peers])
    mine = pl.ds(pl.multiple_of(me * height, 8), height)
    parts = send_all(
        "ctx",
        n,
        lambda peer: part_ref.at[pl.ds(pl.multiple_of(peer * height, 8), height), :],
        rx.at[mine, :],
        sems.at[0],
        sems.at[1],
    )
    biases = send_all(
        "ctx", n, lambda peer: bias_ref.at[pl.ds(0, 1), :], rxb.at[me, pl.ds(0, 1), :], sems.at[6], sems.at[7]
    )
    slab = gram_ref.shape[0] // n
    grams = send_all(
        "ctx",
        n,
        lambda peer: gram_ref.at[pl.ds(pl.multiple_of(peer * slab, slab), slab), :],
        rxs.at[me],
        sems.at[4],
        sems.at[5],
    )
    rx[mine, :] = part_ref[mine, :]
    rxb[me, 0:1, :] = bias_ref[0:1, :]
    rxs[me] = gram_ref[pl.ds(pl.multiple_of(me * slab, slab), slab), :]

    def split_head(k, carry):
        load(k).wait()
        for i in range(per):
            low_head[k * per + i] = head[k, :, i * WIDTH : (i + 1) * WIDTH].astype(BF16)
        return carry

    lax.fori_loop(0, head.shape[0], split_head, 0)

    def split_mom(k, carry):
        load_mom(k).wait()
        for i in range(per):
            for j, part in enumerate(three(mom[k, :, i * WIDTH : (i + 1) * WIDTH].T)):
                low_mom[j, k * per + i] = part
        return carry

    lax.fori_loop(0, head.shape[0], split_mom, 0)

    def slab_total():
        for copy in grams:
            copy.wait()
        total = rxs[0]
        for s in range(1, n):
            total = total + rxs[s]
        slab_sum[...] = total
        tall_ref[height + 2 + me] = total

    slabs = fenced(
        plan_all("ctx", n, lambda peer: slab_sum, tall_ref.at[height + 2 + me], sems.at[8], sems.at[9]), slab_total
    )
    for copy in biases + parts:
        copy.wait()
    turn[0] = rx[:, 0:128]
    turn[1] = rx[:, 128:256]

    def across(i):
        return jnp.concatenate([turn[half, pl.ds(i, 8, stride=height), :] for half in range(2)], axis=1)

    blank = jnp.zeros((8, WIDTH), F32)
    for i in range(height):
        rows = across(i) + theta_ref[pl.ds(i * 8, 8), :] * (1.0 / groups_all)
        tall_ref[i] = rows
        lefts[i] = jnp.concatenate(split3(rows) + (blank,), axis=0).astype(BF16)
    tall_ref[height] = z8_ref[...]
    tall_ref[height + 1] = jnp.concatenate([rxb[s, 0:1, :] for s in range(n)], axis=0)
    totals = [jnp.zeros((32, WIDTH), F32)] * 2
    for i in range(height):
        totals[i % 2] = totals[i % 2] + dot_nt(lefts[i], low_head[i])
    total = totals[0] + totals[1]
    dz_own[...] = total[0:8] + total[8:16] + total[16:24]
    terms = fenced(plan_all("ctx", n, lambda peer: dz_own, rxz.at[me], sems.at[2], sems.at[3]))
    rxz[me] = dz_own[...]

    def mix(i, carry):
        totals = list(carry)
        for k in range(4):
            for j in range(3):
                totals[k % 2] = totals[k % 2] + dot_nn(lefts[4 * i + k], low_mom[j, 4 * i + k])
        return tuple(totals)

    empty = jnp.zeros((32, WIDTH), F32)
    totals = lax.fori_loop(0, height // 4, mix, (empty, empty))
    total = totals[0] + totals[1]
    cross_ref[...] = total[0:8] + total[8:16] + total[16:24]
    for copy in terms:
        copy.wait()
    total = rxz[0]
    for s in range(1, n):
        total = total + rxz[s]
    dz_ref[...] = total
    for copy in slabs:
        copy.wait()


def encoder_back_kernel(
    count_ref, c_ref, stats_ref, small_ref, square_ref, dz_ref, inv_ref, tall_ref, narrow_ref, reg_ref, out_ref, thin_ref,
    wide, second, spread, ua, ub, ka, kb, na, nb, ga, gb, acc_s, acc_f, acc_g, rows_out,
):
    unit, chain, normed, grad = (ua, ub), (ka, kb), (na, nb), (ga, gb)
    num_c = count_ref[0]
    small = small_ref[...]
    first = triple_weights(weight_block(small[0:5] * GELU_SCALE, small[10:11] * GELU_SCALE, 0))
    plain = square_ref[0].astype(BF16)
    low = plain.astype(F32)
    second[...] = low.T.astype(BF16)
    height = tall_ref.shape[0] - 10
    bias_back = full_nt(tall_ref[height + 1], square_ref[1].astype(BF16).astype(F32))
    latent_back = (dz_ref[...] + bias_back) * inv_ref[...]
    wide[0] = column(small[11:12], SPAN)
    wide[1] = column(small[12:13], SPAN)
    latent_cols = jnp.concatenate(split3(latent_back) + (jnp.zeros((104, WIDTH), F32),), axis=0).T.astype(BF16)[:, 0:32]
    wide[2] = column(small[13:14], SPAN)
    centre = split3(full_nn(jnp.broadcast_to(small[11:12], (8, WIDTH)), low) * (1.0 / WIDTH))
    rows = jnp.concatenate([part[0:1] for part in centre] + [jnp.zeros((13, WIDTH), F32)], axis=0)
    spread[...] = jnp.concatenate([plain, rows.astype(BF16)], axis=0)
    for ref in (acc_s, acc_f, acc_g):
        ref[...] = jnp.zeros_like(ref)
    ones = jnp.ones((16, SPAN), BF16)
    ids = lax.broadcasted_iota(jnp.int32, (8, SPAN), 0).astype(F32) + 1.0
    blank = jnp.zeros((8, SPAN), F32)

    def window(t):
        return c_ref[:, pl.ds(pl.multiple_of(t * SPAN, SPAN), SPAN)]

    def ahead(t, k):
        pre = dot_nn(first, triple_from_list(window(t)))
        stats = stats_ref[0:2, pl.ds(pl.multiple_of(t * SPAN, SPAN), SPAN)]
        mean, inverse = stats[0:1], stats[1:2]
        parts, slopes = [], []
        for c in range(0, WIDTH, QUARTER):
            value, slope = gelu_both(pre[c : c + QUARTER])
            parts.append((value - mean) * inverse)
            slopes.append(slope)
            yield
        scale = inverse * GELU_SCALE
        for c in range(len(parts)):
            rows = slice(c * QUARTER, (c + 1) * QUARTER)
            value = parts[c]
            unit[k][rows, :] = value
            normed[k][rows, :] = (value * wide[0, rows, :] + wide[1, rows, :]).astype(BF16)
            chain[k][rows, :] = slopes[c] * scale
        yield
        owner = jnp.where(ids == window(t)[7:8], 1.0, 0.0)
        owner = jnp.concatenate([owner, owner, owner, blank], axis=0).astype(BF16)
        pre = dot_nn(second[...], normed[k][...])
        outer = dot_nn(latent_cols, owner)
        yield
        for c in range(0, WIDTH, QUARTER):
            rows = slice(c, c + QUARTER)
            grad[k][rows, :] = (plain_slope(pre[rows] + wide[2, rows, :]) * outer[rows]).astype(BF16)
            yield

    def back_part(t, k):
        slopes = dot_nn(spread[...], grad[k][...])
        yield
        acc_s[...] += dot_nt(jnp.concatenate([normed[k][...], ones], axis=0), grad[k][...])
        yield
        means = jnp.sum(slopes[WIDTH : WIDTH + 8], axis=0, keepdims=True)
        total = jnp.zeros((1, SPAN), F32)
        parts = []
        for c in range(0, WIDTH, QUARTER):
            rows = slice(c, c + QUARTER)
            parts.append(slopes[rows] * wide[0, rows, :] - means)
            acc_g[rows, :] += slopes[rows] * unit[k][rows, :]
            total = total + jnp.sum(parts[-1] * unit[k][rows, :], axis=0, keepdims=True)
        mean = total * (1.0 / WIDTH)
        yield
        highs, rests = [], []
        for c in range(len(parts)):
            rows = slice(c * QUARTER, (c + 1) * QUARTER)
            outer = (parts[c] - unit[k][rows, :] * mean) * chain[k][rows, :]
            highs.append(outer.astype(BF16))
            rests.append((outer - highs[-1].astype(F32)).astype(BF16))
        yield
        left = jnp.concatenate(split3(window(t)) + (jnp.zeros((8, SPAN), F32),), axis=0).astype(BF16)
        right = jnp.concatenate([jnp.concatenate(highs, axis=0), jnp.concatenate(rests, axis=0)], axis=1)
        acc_f[...] += dot_nt(right, jnp.concatenate([left, left], axis=1))
        yield

    def pair(p, carry):
        weave("ABABAAAABABABAA", ahead(2 * p + 1, 1), back_part(2 * p, 0))
        weave("ABABAAAABABABAA", ahead(2 * p + 2, 0), back_part(2 * p + 1, 1))
        return carry

    spans = (num_c + SPAN - 1) // SPAN
    weave("", ahead(0, 0), iter(()))
    lax.fori_loop(0, spans // 2, pair, 0)

    @pl.when(lax.rem(spans, 2) == 1)
    def last():
        weave("", iter(()), back_part(spans - 1, 0))

    firsts = turned(acc_f[...])
    firsts = firsts[0:8] + firsts[8:16] + firsts[16:24]
    bias_grad = acc_s[WIDTH : WIDTH + 8]
    shift_grad = full_nt(bias_grad, low)
    gain_grad = full_nt(jnp.ones((8, SPAN), F32), acc_g[...])
    rows_out[0:5, :] = firsts[0:5]
    rows_out[5:10, :] = narrow_ref[0:5, :]
    rows_out[10:11, :] = firsts[6:7]
    rows_out[11:12, :] = gain_grad[0:1]
    rows_out[12:13, :] = shift_grad[0:1]
    rows_out[13:14, :] = bias_grad[0:1]
    rows_out[14:15, :] = narrow_ref[5:6, :]
    lane = lax.broadcasted_iota(jnp.int32, (1, WIDTH), 1)
    regular = jnp.broadcast_to(jnp.sum(reg_ref[...]), (1, WIDTH))
    rows_out[15:16, :] = jnp.where(lane == 0, narrow_ref[6:7, :], jnp.where(lane == 1, regular, 0.0))
    for q in range(32):
        out_ref[q // 16, q % 16] = acc_s[8 * q : 8 * q + 8, :]
        lanes = slice((q % 2) * 128, (q % 2) * 128 + 128)
        thin_ref[q // 16, q % 16, 0:1, :] = rows_out[q // 2 : q // 2 + 1, lanes]


def newton(gram, sharp):
    ids = lax.broadcasted_iota(jnp.int32, (WIDTH, WIDTH), 0) == lax.broadcasted_iota(jnp.int32, (WIDTH, WIDTH), 1)
    scale = 1.0 / (jnp.sqrt(jnp.sum(jnp.where(ids, gram, 0.0))) + 1e-07)
    sides = (slice(0, WIDTH // 2), slice(WIDTH // 2, WIDTH))
    state = [gram[side] * (scale * scale) for side in sides]
    unit = [jnp.where(ids[side], first_coef, 0.0) for side in sides]

    def joined(halves):
        return [jnp.concatenate(pair, axis=0) for pair in zip(*halves)]

    product = None
    for k in range(NS_STEPS):
        times = six if k < sharp else few
        parts = [three(one) for one in state]
        whole = joined(parts)
        square = [few(part, whole) for part in parts]
        yield None
        poly = [unit[j] + second_coef * state[j] + third_coef * square[j] for j in range(2)]
        left = [three(one) for one in poly]
        if k + 1 < NS_STEPS:
            half = [times(one, whole) for one in left]
            yield None
        if k == 0:
            product = poly
        else:
            right = joined([three(one) for one in product])
            product = [times(one, right) for one in left]
        if k + 1 < NS_STEPS:
            yield None
            outer = joined(left)
            state = [times(three(one), outer) for one in half]
            yield None
    yield jnp.concatenate([one * scale for one in product], axis=0)


def drain(chain):
    result = None
    for result in chain:
        pass
    return result


def newton_begin(gram, state_ref, product_ref):
    ids = lax.broadcasted_iota(jnp.int32, (WIDTH, WIDTH), 0) == lax.broadcasted_iota(jnp.int32, (WIDTH, WIDTH), 1)
    scale = 1.0 / (jnp.sqrt(jnp.sum(jnp.where(ids, gram, 0.0))) + 1e-07)
    state_ref[...] = gram * (scale * scale)
    product_ref[...] = jnp.where(ids, 1.0, 0.0)
    return scale


def newton_step(state_ref, product_ref):
    ids = lax.broadcasted_iota(jnp.int32, (WIDTH, WIDTH), 0) == lax.broadcasted_iota(jnp.int32, (WIDTH, WIDTH), 1)
    sides = (slice(0, WIDTH // 2), slice(WIDTH // 2, WIDTH))
    state = [state_ref[side, :] for side in sides]
    parts = [three(one) for one in state]
    whole = [jnp.concatenate(pair, axis=0) for pair in zip(*parts)]
    square = [few(part, whole) for part in parts]
    left = [
        three(jnp.where(ids[side], first_coef, 0.0) + second_coef * state[j] + third_coef * square[j])
        for j, side in enumerate(sides)
    ]
    half = [six(one, whole) for one in left]
    right = three(product_ref[...])
    for one, side in zip(left, sides):
        product_ref[side, :] = six(one, right)
    outer = [jnp.concatenate(pair, axis=0) for pair in zip(*left)]
    for one, side in zip(half, sides):
        state_ref[side, :] = six(three(one), outer)


def square_rows(sum_ref):
    return jnp.concatenate([sum_ref[q // 16, q % 16] for q in range(32)], axis=0)


def small_rows(sum_ref):
    halves = [sum_ref[q // 16, q % 16, 0:1, :] for q in range(32)]
    return jnp.concatenate(
        [jnp.concatenate([halves[2 * k], halves[2 * k + 1]], axis=1) for k in range(16)], axis=0
    )


def reduce_kernel(
    n, rows_n, grad_ref, thin_ref, own_ref, far_ref, cross_ref, smom_ref,
    sum_ref, thin_sum, tall_ref, move_ref,
    rxh, half_sum, rxq, fin, rxh_thin, half_thin, rxq_thin, fin_thin, mixed, rxm, rxc, rxx, state, product, scales, sems, dsems, csems, qsems,
):
    me = lax.axis_index("ctx")
    r = lax.axis_index("dp")
    chips = (rows_n // 2) * n
    par = lax.rem(r, 2)
    chip = (r // 2) * n + me
    far = lax.rem(r + rows_n // 2, rows_n)
    near = r + 1 - 2 * par
    diag = lax.rem(near + rows_n // 2, rows_n)
    places_here = [pl.ds(pl.multiple_of(place * 8, 8), 8) for place in (r, far)]
    others = [lax.rem(chip + d, chips) for d in range(1, chips)]
    places = [{"dp": 2 * (other // n) + par, "ctx": lax.rem(other, n)} for other in others]
    count = hail(places + [{"dp": near}, {"dp": diag}])
    for i in range(own_ref.shape[0]):
        for rows, ref in zip(places_here, (own_ref, far_ref)):
            tall_ref[i, rows, :] = ref[i]
    height = own_ref.shape[0] - 10

    def near_copy(source, target, j):
        return pltpu.make_async_remote_copy(
            src_ref=source,
            dst_ref=target,
            send_sem=csems.at[0, j],
            recv_sem=csems.at[1, j],
            device_id={"dp": near},
            device_id_type=MESH,
        )

    def chip_copies(source, target, k):
        return [
            copy for pair in zip(*(chip_plan(*plan, k + 2 * j) for j, plan in enumerate(zip(source, target)))) for copy in pair
        ]

    def chip_plan(source, target, k):
        return [
            pltpu.make_async_remote_copy(
                src_ref=source(other),
                dst_ref=target,
                send_sem=qsems.at[2 * k, d],
                recv_sem=qsems.at[2 * k + 1, d],
                device_id=place,
                device_id_type=MESH,
            )
            for d, (other, place) in enumerate(zip(others, places))
        ]

    top = pl.ds(0, 1)
    halves = [
        near_copy(grad_ref.at[1 - par], rxh, 0),
        near_copy(thin_ref.at[1 - par, :, top, :], rxh_thin.at[:, top, :], 4),
    ]
    crosses = plan_all("ctx", n, lambda peer: cross_ref, rxx.at[me], sems.at[0], sems.at[1])
    terms = plan_all("ctx", n, lambda peer: mixed, rxm.at[me], sems.at[2], sems.at[3])
    blocks = [
        near_copy(tall_ref.at[:, rows, :], tall_ref.at[:, rows, :], j + 1) for j, rows in enumerate(places_here)
    ]
    fenced(halves + blocks + crosses, lambda: meet(count))
    rxx[me] = cross_ref[...]

    def first_sum():
        for copy in halves:
            copy.wait()
        half_sum[...] = grad_ref[par] + rxh[...]
        half_thin[:, 0:1, :] = thin_ref[par, :, 0:1, :] + rxh_thin[:, 0:1, :]
        rxq[chip] = half_sum[chip]
        rxq_thin[chip, 0:1, :] = half_thin[chip, 0:1, :]

    scattered = fenced(
        chip_copies(
            (lambda other: half_sum.at[other], lambda other: half_thin.at[other, top, :]),
            (rxq.at[chip], rxq_thin.at[chip, top, :]),
            0,
        ),
        first_sum,
    )
    for copy in blocks:
        copy.wait()
    inners = [jnp.zeros((96, 96), F32)] * 2
    for i in range(height):
        stack = jnp.concatenate(split3(tall_ref[i]), axis=0).astype(BF16)
        inners[i % 2] = inners[i % 2] + dot_nt(stack, stack)
    inner = inners[0] + inners[1]
    inner = inner[0:32] + inner[32:64] + inner[64:96]
    inner = inner[:, 0:32] + inner[:, 32:64] + inner[:, 64:96]
    mixed[...] = jnp.concatenate([inner, jnp.zeros((32, 96), F32)], axis=1)
    rxm[me] = mixed[...]
    fenced(terms)
    latents = tall_ref[height]
    bias_moment = momentum_rate * smom_ref[1] + full_nn(latents.T, tall_ref[height + 1])
    scales[0] = newton_begin(gram_six(three(bias_moment)), state, product)

    def share():
        for copy in crosses:
            copy.wait()
        total = rxx[0]
        for s in range(1, n):
            total = total + rxx[s]
        rxc[r] = total

    def second_sum():
        for copy in scattered:
            copy.wait()
        total = rxq[0]
        thin = rxq_thin[0, 0:1, :]
        for s in range(1, chips):
            total = total + rxq[s]
            thin = thin + rxq_thin[s, 0:1, :]
        fin[...] = total
        fin_thin[0:1, :] = thin
        sum_ref[par, chip] = total
        thin_sum[par, chip, 0:1, :] = thin

    def change_chain():
        move_ref[1] = product[...] * scales[0]
        for copy in terms:
            copy.wait()
        total = rxm[0]
        for s in range(1, n):
            total = total + rxm[s]
        inner = total[:, 0:32]
        for copy in shared:
            copy.wait()
        latents = tall_ref[height]
        cross = jnp.concatenate([rxc[s] for s in range(rows_n)], axis=0)
        weight = momentum_rate * cross + 0.5 * full_nn(inner, latents)
        half = full_nn(latents.T, weight)
        slabs = [tall_ref[height + 2 + t, 8 * s : 8 * s + 8, :] for s in range(rows_n) for t in range(n)]
        gram = (momentum_rate * momentum_rate) * jnp.concatenate(slabs, axis=0) + (half + half.T)
        scales[0] = newton_begin(gram, state, product)

    def all_here():
        for copy in gathered:
            copy.wait()

    shared = plan_all("dp", rows_n, lambda peer: rxc.at[r], rxc.at[r], dsems.at[0], dsems.at[1])
    gathered = chip_copies(
        (lambda other: fin, lambda other: fin_thin.at[top, :]),
        (sum_ref.at[par, chip], thin_sum.at[par, chip, top, :]),
        1,
    )
    last = [
        near_copy(sum_ref.at[par], sum_ref.at[par], 3),
        near_copy(thin_sum.at[par, :, top, :], thin_sum.at[par, :, top, :], 5),
    ]
    events = ((1, share, shared), (3, second_sum, gathered), (5, change_chain, []), (8, all_here, last))

    def iterate(i, carry):
        for place, before, copies in events:

            @pl.when(i == place)
            def run():
                before()
                for copy in copies:
                    copy.start()

        newton_step(state, product)
        return carry

    lax.fori_loop(0, 2 * NS_STEPS, iterate, 0)
    move_ref[0] = product[...] * scales[0]
    for copy in last:
        copy.wait()


def update_kernel(
    live_all, groups_all, mom_ref, head_ref, tall_ref, move_ref, sum_ref, thin_ref, square_ref, smom_ref,
    small_ref, mmom_ref, mvar_ref,
    mom_out, head_out, copy_out, smom_out, square_out, scopy_out, mmom_out, mvar_out, small_out, mcopy_out,
    loss_out, mom, head, low_copy, left, wide, store_sem,
):
    ring, unused, chunk = mom.shape
    chunks = mom_ref.shape[1] // chunk
    per = chunk // WIDTH

    def stores(k):
        lanes = pl.ds(k * chunk, chunk)
        return [
            pltpu.make_async_copy(source.at[k % ring], target.at[:, lanes], store_sem.at[j, k % ring])
            for j, (source, target) in enumerate(((mom, mom_out), (head, head_out), (low_copy, copy_out)))
        ]

    height = tall_ref.shape[0] - 10
    latents = tall_ref[height]
    rows = jnp.concatenate([latents] * 3 + [jnp.zeros((32, WIDTH), F32)], axis=0)
    left[...] = rows.T.astype(BF16)
    ids = lax.broadcasted_iota(jnp.int32, (WIDTH, WIDTH), 0) == lax.broadcasted_iota(jnp.int32, (WIDTH, WIDTH), 1)
    move = move_ref[0] * (-head_rate * 0.2 * WIDTH)
    centre = jnp.sum(jnp.where(ids, move, 0.0)) * (1.0 / WIDTH)
    wide[...] = jnp.concatenate(three(jnp.where(ids, move - centre, move))[0:2], axis=0)
    narrow = small_rows(thin_ref)
    stats = narrow[15:16]
    lane = lax.broadcasted_iota(jnp.int32, (1, WIDTH), 1)
    weight = jnp.where(lane == 0, 1.0 / live_all, jnp.where(lane == 1, reg_weight / groups_all, 0.0))
    loss_out[...] = jnp.broadcast_to(jnp.sum(stats * weight), loss_out.shape)
    moment, second, new = adam_update(small_ref[...], narrow[0:15], mmom_ref[...], mvar_ref[...])
    mmom_out[...] = moment
    mvar_out[...] = second
    small_out[...] = new
    mcopy_out[...] = new.astype(BF16)
    keep = 1.0 - head_rate * decay_rate

    grads = [square_rows(sum_ref), full_nn(latents.T, tall_ref[height + 1])]
    moments = [momentum_rate * smom_ref[k] + grads[k] for k in range(2)]
    side = newton(gram_six(three(moments[0])), NS_STEPS)
    for k in range(chunks):
        slot = k % ring
        if k >= ring:
            for copy in stores(k - ring):
                copy.wait()

        def begin_tile(i):
            lanes = slice(i * WIDTH, (i + 1) * WIDTH)
            wide_lanes = slice(k * chunk + i * WIDTH, k * chunk + (i + 1) * WIDTH)
            high, mid, low = three(tall_ref[k * per + i])
            right = jnp.concatenate([high, mid, low, jnp.zeros_like(high)], axis=0)
            moment = momentum_rate * mom_ref[:, wide_lanes] + dot_nn(left[...], right)
            mom[slot, :, lanes] = moment
            high = moment.astype(BF16)
            mid = (moment - high.astype(F32)).astype(BF16)
            return keep * head_ref[:, wide_lanes] + centre * moment, high, mid

        def finish_tile(i):
            lanes = slice(i * WIDTH, (i + 1) * WIDTH)
            base, high, mid = ready[i]
            first = dot_nn(wide[...], high)
            new = (first[0:WIDTH] + dot_nn(wide[0:WIDTH, :], mid)) + (first[WIDTH:] + base)
            head[slot, :, lanes] = new
            low_copy[slot, :, lanes] = new.astype(BF16)

        ready = [begin_tile(0), begin_tile(1)]
        for i in range(per):
            if i + 2 < per:
                ready.append(begin_tile(i + 2))
            finish_tile(i)
            if i < 3:
                next(side, None) if k * 3 + i < 17 else None
        for copy in stores(k):
            copy.start()
    for k, move in enumerate((drain(side), move_ref[1])):
        smom_out[k] = moments[k]
        old = square_ref[k]
        change = 0.2 * WIDTH**0.5 * six(three(move), three(moments[k])) + decay_rate * old
        new = old - square_rates[k] * change
        square_out[k] = new
        scopy_out[k] = new.astype(BF16)
    for k in range(chunks - ring, chunks):
        for copy in stores(k):
            copy.wait()


def shape(*dims, dtype=F32):
    return jax.ShapeDtypeStruct(dims, dtype)


def dma_sems(*dims):
    return pltpu.SemaphoreType.DMA(dims)


def remote_params(ident, room=50):
    return pltpu.CompilerParams(collective_id=ident, has_side_effects=True, vmem_limit_bytes=room * MIB)


def plain_params(room=16):
    return pltpu.CompilerParams(vmem_limit_bytes=room * MIB)


CHUNK = 1024
RING = 4


def call_scatter(n, rows_n, lengths, pixels, ctx_mask, head_mom):
    micro, groups, slots = pixels.shape[1], pixels.shape[2], pixels.shape[4]
    return pl.pallas_call(
        functools.partial(scatter_kernel, n, rows_n),
        out_shape=[
            shape(n, 8, slots),
            shape(n, 8, 128),
            shape(n, 8, slots),
            shape(n, 8, 128),
            shape(WIDTH // rows_n, WIDTH),
        ],
        in_specs=[hbm_spec()] * 4,
        out_specs=[vmem_spec()] * 5,
        scratch_shapes=[
            pltpu.SMEM(lengths.shape, jnp.int32),
            pltpu.VMEM((1, micro, 5, groups, slots), F32),
            pltpu.VMEM(ctx_mask.shape, jnp.int32),
            pltpu.VMEM((n, 8, slots), F32),
            pltpu.VMEM((n, 8, 128), F32),
            pltpu.VMEM((n, 128), F32),
            pltpu.VMEM((WIDTH, head_mom.shape[1] // rows_n), F32),
            pltpu.VMEM((WIDTH, WIDTH), F32),
            pltpu.VMEM((rows_n, WIDTH // rows_n, WIDTH), F32),
            pltpu.VMEM((TILE, TILE), BF16),
            dma_sems(micro, n - 1),
            dma_sems(micro, n - 1),
            dma_sems(),
            dma_sems(2, rows_n - 1),
            dma_sems(3),
            dma_sems(2, n - 1),
        ],
        compiler_params=remote_params(1, 50),
        name="scatter_pixels",
        cost_estimate=busy(14),
    )(lengths, jnp.transpose(pixels, (0, 1, 3, 2, 4)), ctx_mask, head_mom)


def call_encode(received, seen, small_params, square_w):
    cap = received.shape[0] * received.shape[2] + 5 * SPAN
    return pl.pallas_call(
        encoder_kernel,
        out_shape=[shape(8, WIDTH), shape(8, 128), shape(8, cap), shape(8, cap), shape(1, dtype=jnp.int32)],
        in_specs=[vmem_spec()] * 4,
        out_specs=[vmem_spec()] * 4 + [smem_spec()],
        scratch_shapes=[
            pltpu.VMEM((8, 128), jnp.int32),
            pltpu.SMEM((8, 128), jnp.int32),
            pltpu.VMEM((3, WIDTH, SPAN), F32),
            pltpu.VMEM((WIDTH, WIDTH), BF16),
            pltpu.VMEM((WIDTH, 16), F32),
            pltpu.VMEM((WIDTH, SPAN), BF16),
            pltpu.VMEM((WIDTH, SPAN), BF16),
            dma_sems(),
        ],
        compiler_params=plain_params(),
        name="encode",
        cost_estimate=busy(10),
    )(received, seen, small_params, square_w)


def call_generate(n, latent, amount, head_w, tiles, share):
    height = WIDTH // n
    chunks = head_w.shape[1] // CHUNK
    return pl.pallas_call(
        functools.partial(theta_kernel, n),
        out_shape=[
            shape(WIDTH, WIDTH),
            shape(WIDTH, WIDTH, dtype=BF16),
            shape(8, WIDTH),
            shape(8, WIDTH),
            shape(8, WIDTH),
            shape(*tiles.shape),
            shape(*share.shape),
        ],
        in_specs=[vmem_spec()] * 2 + [any_spec()] + [vmem_spec()] * 2,
        out_specs=[vmem_spec()] * 7,
        scratch_shapes=[
            pltpu.VMEM((n, 8, WIDTH), F32),
            pltpu.VMEM((n, 8, 128), F32),
            pltpu.VMEM((chunks, WIDTH, CHUNK), F32),
            pltpu.VMEM((n, height, WIDTH), BF16),
            pltpu.VMEM((2, WIDTH, 128), F32),
            dma_sems(chunks),
            dma_sems(10, n - 1),
        ],
        compiler_params=remote_params(2),
        name="generate",
        cost_estimate=busy(17),
    )(latent, amount, head_w, tiles, share)


def call_siren(n, live_all, lengths, received, seen, gen, latent, small_params, square_w):
    cap = received.shape[0] * received.shape[2] + 5 * SPAN
    return pl.pallas_call(
        functools.partial(siren_kernel, live_all),
        out_shape=[shape(WIDTH, WIDTH), shape(8, WIDTH), shape(8, WIDTH)],
        in_specs=[smem_spec()] + [vmem_spec()] * 6,
        out_specs=[vmem_spec()] * 3,
        scratch_shapes=[
            pltpu.VMEM((8, cap), F32),
            pltpu.VMEM((8, 128), jnp.int32),
            pltpu.SMEM((8, 128), jnp.int32),
            pltpu.VMEM((WIDTH, WIDTH), BF16),
            pltpu.VMEM((WIDTH, SPAN), F32),
            pltpu.VMEM((WIDTH, SPAN), BF16),
            pltpu.VMEM((WIDTH, SPAN), BF16),
            pltpu.VMEM((WIDTH, SPAN), F32),
            pltpu.VMEM((WIDTH, SPAN), F32),
            pltpu.VMEM((WIDTH, SPAN), BF16),
            pltpu.VMEM((WIDTH, SPAN), BF16),
            pltpu.VMEM((WIDTH, SPAN), F32),
            pltpu.VMEM((WIDTH, SPAN), F32),
            pltpu.VMEM((WIDTH + 16, WIDTH), F32),
            pltpu.VMEM((WIDTH, 32), F32),
            pltpu.VMEM((WIDTH, 16), F32),
            pltpu.VMEM((8, SPAN), F32),
            dma_sems(),
        ],
        compiler_params=plain_params(),
        name="siren",
        cost_estimate=busy(16),
    )(lengths, received, seen, gen, latent, small_params, square_w)


def call_latent(n, groups_all, part, bias, theta, head_w, head_mom, z8, gram_part):
    height = WIDTH // n
    chunks = head_w.shape[1] // CHUNK
    slab = gram_part.shape[0] // n
    return pl.pallas_call(
        functools.partial(latent_kernel, n, groups_all),
        out_shape=[
            shape(8, WIDTH),
            shape(height + 2 + n, 8, WIDTH),
            shape(8, WIDTH),
        ],
        in_specs=[vmem_spec()] * 3 + [any_spec()] * 2 + [vmem_spec()] * 2,
        out_specs=[vmem_spec()] * 3,
        scratch_shapes=[
            pltpu.VMEM((WIDTH, WIDTH), F32),
            pltpu.VMEM((n, 8, WIDTH), F32),
            pltpu.VMEM((2, WIDTH, 128), F32),
            pltpu.VMEM((chunks, WIDTH, CHUNK), F32),
            pltpu.VMEM((chunks, WIDTH, CHUNK), F32),
            pltpu.VMEM((height, WIDTH, WIDTH), BF16),
            pltpu.VMEM((3, height, WIDTH, WIDTH), BF16),
            pltpu.VMEM((n, 8, WIDTH), F32),
            pltpu.VMEM((8, WIDTH), F32),
            pltpu.VMEM((height, 32, WIDTH), BF16),
            pltpu.VMEM((n, slab, WIDTH), F32),
            pltpu.VMEM((slab, WIDTH), F32),
            dma_sems(chunks),
            dma_sems(chunks),
            dma_sems(10, n - 1),
        ],
        compiler_params=remote_params(3),
        name="latent_grads",
        cost_estimate=busy(18),
    )(part, bias, theta, head_w, head_mom, z8, gram_part)


def call_back(counts, clist, stats, small_params, square_w, latent_grad, inverse, tall, narrow, regular):
    return pl.pallas_call(
        encoder_back_kernel,
        out_shape=[shape(2, 16, 8, WIDTH), shape(2, 16, 8, 128)],
        in_specs=[smem_spec()] + [vmem_spec()] * 9,
        out_specs=[vmem_spec()] * 2,
        scratch_shapes=[
            pltpu.VMEM((3, WIDTH, SPAN), F32),
            pltpu.VMEM((WIDTH, WIDTH), BF16),
            pltpu.VMEM((WIDTH + 16, WIDTH), BF16),
            pltpu.VMEM((WIDTH, SPAN), F32),
            pltpu.VMEM((WIDTH, SPAN), F32),
            pltpu.VMEM((WIDTH, SPAN), F32),
            pltpu.VMEM((WIDTH, SPAN), F32),
            pltpu.VMEM((WIDTH, SPAN), BF16),
            pltpu.VMEM((WIDTH, SPAN), BF16),
            pltpu.VMEM((WIDTH, SPAN), BF16),
            pltpu.VMEM((WIDTH, SPAN), BF16),
            pltpu.VMEM((WIDTH + 16, WIDTH), F32),
            pltpu.VMEM((WIDTH, 32), F32),
            pltpu.VMEM((WIDTH, SPAN), F32),
            pltpu.VMEM((16, WIDTH), F32),
        ],
        compiler_params=plain_params(),
        name="encode_back",
        cost_estimate=busy(16),
    )(counts, clist, stats, small_params, square_w, latent_grad, inverse, tall, narrow, regular)


def call_reduce(n, rows_n, grads, thin, own, far, cross, square_mom):
    chips = (rows_n // 2) * n
    return pl.pallas_call(
        functools.partial(reduce_kernel, n, rows_n),
        out_shape=[
            shape(*grads.shape),
            shape(*thin.shape),
            shape(own.shape[0], 8 * rows_n, WIDTH),
            shape(2, WIDTH, WIDTH),
        ],
        in_specs=[vmem_spec()] * 6,
        out_specs=[vmem_spec()] * 4,
        scratch_shapes=[
            pltpu.VMEM((chips, 8, WIDTH), F32),
            pltpu.VMEM((chips, 8, WIDTH), F32),
            pltpu.VMEM((chips, 8, WIDTH), F32),
            pltpu.VMEM((8, WIDTH), F32),
            pltpu.VMEM((chips, 8, 128), F32),
            pltpu.VMEM((chips, 8, 128), F32),
            pltpu.VMEM((chips, 8, 128), F32),
            pltpu.VMEM((8, 128), F32),
            pltpu.VMEM((32, 128), F32),
            pltpu.VMEM((n, 32, 128), F32),
            pltpu.VMEM((rows_n, 8, WIDTH), F32),
            pltpu.VMEM((n, 8, WIDTH), F32),
            pltpu.VMEM((WIDTH, WIDTH), F32),
            pltpu.VMEM((WIDTH, WIDTH), F32),
            pltpu.SMEM((1,), F32),
            dma_sems(4, n - 1),
            dma_sems(2, rows_n - 1),
            dma_sems(2, 6),
            dma_sems(8, chips - 1),
        ],
        compiler_params=remote_params(4, 16),
        name="reduce_grads",
        cost_estimate=busy(24),
    )(grads, thin, own, far, cross, square_mom)


def call_update(
    live_all, groups_all, head_mom, head_w, tall, move, sums, thin_sums, square_w, square_mom, small_params,
    small_mom, small_var,
):
    columns = head_w.shape[1]
    small_copy = shape(15, WIDTH, dtype=BF16)
    square_copy = shape(2, WIDTH, WIDTH, dtype=BF16)
    loss = shape(1, 128)
    others = [square_mom, square_w, square_copy, small_mom, small_var, small_params, small_copy, loss]
    return pl.pallas_call(
        functools.partial(update_kernel, live_all, groups_all),
        out_shape=[shape(WIDTH, columns), shape(WIDTH, columns), shape(WIDTH, columns, dtype=BF16)]
        + [shape(*one.shape, dtype=one.dtype) for one in others],
        in_specs=[vmem_spec()] * 11,
        out_specs=[any_spec()] * 3 + [vmem_spec()] * 8,
        scratch_shapes=[
            pltpu.VMEM((RING, WIDTH, CHUNK), F32),
            pltpu.VMEM((RING, WIDTH, CHUNK), F32),
            pltpu.VMEM((RING, WIDTH, CHUNK), BF16),
            pltpu.VMEM((WIDTH, 128), BF16),
            pltpu.VMEM((2 * WIDTH, WIDTH), BF16),
            dma_sems(3, RING),
        ],
        compiler_params=plain_params(30),
        name="update_all",
        cost_estimate=busy(12),
    )(
        head_mom, head_w, tall, move, sums, thin_sums, square_w, square_mom, small_params, small_mom, small_var
    )


def grouped(
    pixels, lengths, ctx_mask, head_w, head_mom, square_w, square_mom, small_params, small_mom, small_var
):
    micro, groups, slots = pixels.shape[1], pixels.shape[2], pixels.shape[4]
    n = lax.axis_size("ctx")
    rows_n = lax.axis_size("dp")
    live_all = rows_n * micro * (groups * slots * n * 5 // 8)
    groups_all = rows_n * micro * groups
    received, seen, tiles, share, gram_part = call_scatter(n, rows_n, lengths, pixels, ctx_mask, head_mom)
    latent, amount, clist, stats, counts = call_encode(received, seen, small_params, square_w)
    theta, gen, z8, inverse, regular, group_rows, group_seen = call_generate(
        n, latent, amount, head_w, tiles, share
    )
    part, bias, narrow = call_siren(
        n, live_all, lengths, group_rows, group_seen, gen, z8, small_params, square_w
    )
    latent_grad, own, cross = call_latent(
        n, groups_all, part, bias, theta, head_w, head_mom, z8, gram_part
    )
    far = lax.ppermute(own, "dp", [(r, (r + rows_n // 2) % rows_n) for r in range(rows_n)])
    grads, thin = call_back(
        counts, clist, stats, small_params, square_w, latent_grad, inverse, own, narrow, regular
    )
    sums, thin_sums, tall, move = call_reduce(n, rows_n, grads, thin, own, far, cross, square_mom)
    updated = call_update(
        live_all, groups_all, head_mom, head_w, tall, move, sums, thin_sums, square_w, square_mom, small_params,
        small_mom, small_var,
    )
    (
        head_moment,
        head_new,
        head_copy,
        square_moment,
        square_new,
        square_copy,
        small_moment,
        small_second,
        small_new,
        small_copy,
        loss,
    ) = updated
    return (
        head_moment,
        head_new,
        head_copy,
        square_moment,
        square_new,
        square_copy,
        small_moment,
        small_second,
        small_new,
        small_copy,
        loss[0, 0],
    )


def local(pixels, lengths, ctx_mask, head_w, *rest):
    n = lax.axis_size("ctx")
    fits = (
        pixels.shape[1] * pixels.shape[2] == n
        and n == 8
        and lax.axis_size("dp") == 4
        and pixels.shape[4] == 2048
        and head_w.shape == (WIDTH, 8192)
    )
    chosen = grouped if fits else general
    return chosen(pixels, lengths, ctx_mask, head_w, *rest)


def solution(mesh):
    placed = (
        P("dp", None, None, None, "ctx"),
        P("dp", None, None),
        P("dp", None, None, "ctx"),
        P(None, "ctx"),
        P(None, "ctx"),
        P(),
        P(),
        P(),
        P(),
        P(),
    )
    return jax.shard_map(
        local,
        mesh=mesh,
        in_specs=placed,
        out_specs=(
            P(None, "ctx"),
            P(None, "ctx"),
            P(None, "ctx"),
            P(),
            P(),
            P(),
            P(),
            P(),
            P(),
            P(),
            P(),
        ),
        check_vma=False,
    )
```

```python
import functools

import jax
import jax.numpy as jnp
from jax import lax
from jax.experimental import pallas as pl
from jax.experimental.pallas import tpu as pltpu
from jax.sharding import PartitionSpec as P

NS_STEPS = 5
STEP = 10


exact_arithmetic_mode = lax.Precision.HIGHEST
reg_weight = 0.5
momentum_rate = 0.95
head_rate = 0.003
square_rates = (0.3, 0.02)
adam_rate = 0.05
beta_first = 0.9
beta_second = 0.999
decay_rate = 0.01
first_coef = 3.4445
second_coef = -4.775
third_coef = 2.0315


def layer_norm(values, gain_row, bias_row):
    centered = values - jnp.mean(values, axis=-1, keepdims=True)
    variance = jnp.mean(centered * centered, axis=-1, keepdims=True)
    return centered * lax.rsqrt(variance + 1e-05) * gain_row + bias_row


def ns_update(current, gram_matrix):
    polynomial = second_coef * gram_matrix + third_coef * jnp.einsum(
        "kij,kjl->kil", gram_matrix, gram_matrix, precision=exact_arithmetic_mode
    )
    return first_coef * current + jnp.einsum(
        "kij,kjl->kil", polynomial, current, precision=exact_arithmetic_mode
    )


def orthogonal_local(matrices):
    norms = jnp.sqrt(jnp.sum(matrices * matrices, axis=(1, 2), keepdims=True))
    current = matrices / (norms + 1e-07)
    for sweep in range(NS_STEPS):
        gram_matrix = jnp.einsum("kij,klj->kil", current, current, precision=exact_arithmetic_mode)
        current = ns_update(current, gram_matrix)
    return current


def head_orthogonal(moment):
    current = moment[None]
    total = lax.psum(jnp.sum(moment * moment), "ctx")
    current = current / (jnp.sqrt(total) + 1e-07)
    for sweep in range(NS_STEPS):
        gram_matrix = lax.psum(
            jnp.dot(current[0], current[0].T, precision=exact_arithmetic_mode), "ctx"
        )
        current = ns_update(current, gram_matrix[None])
    return current[0]


def adam_update(params, grad, moment, second_moment):
    moment_new = beta_first * moment + (1.0 - beta_first) * grad
    second_new = beta_second * second_moment + (1.0 - beta_second) * grad * grad
    corrected = (
        moment_new
        / (1.0 - beta_first**STEP)
        / (jnp.sqrt(second_new / (1.0 - beta_second**STEP)) + 1e-08)
    )
    return (moment_new, second_new, params - adam_rate * (corrected + decay_rate * params))


def encoder_forward(features, context, small_params, second_low):
    first_pre = (
        jnp.einsum("gpc,cd->gpd", features, small_params[0:5], precision=exact_arithmetic_mode)
        + small_params[10]
    )
    first_act, gelu_first = jax.vjp(jax.nn.gelu, first_pre)
    normed, norm_back = jax.vjp(layer_norm, first_act, small_params[11], small_params[12])
    normed_low = normed.astype(jnp.bfloat16)
    second = (
        jnp.einsum("gpd,de->gpe", normed_low, second_low, preferred_element_type=jnp.float32)
        + small_params[13]
    )
    encoded, gelu_second = jax.vjp(jax.nn.gelu, second)
    summed = jnp.einsum("gp,gpe->ge", context, encoded, precision=exact_arithmetic_mode)
    return (
        summed,
        jnp.sum(context, axis=1),
        (first_pre, gelu_first, norm_back, normed_low, gelu_second),
    )


def general(
    pixels,
    lengths,
    ctx_mask,
    head_w,
    head_mom,
    square_w,
    square_mom,
    small_params,
    small_mom,
    small_var,
):
    micro_count = pixels.shape[1]
    groups = pixels.shape[2]
    slot_count = pixels.shape[4]
    model_width = square_w.shape[1]
    live_all = (
        lax.axis_size("dp") * micro_count * (groups * slot_count * lax.axis_size("ctx") * 5 // 8)
    )
    groups_all = lax.axis_size("dp") * micro_count * groups
    slot_ids = lax.axis_index("ctx") * slot_count + jnp.arange(slot_count, dtype=jnp.int32)
    head_low = head_w.astype(jnp.bfloat16)
    head_back = head_low.astype(jnp.float32)
    square_low = square_w.astype(jnp.bfloat16)
    bias_head = square_low[1].astype(jnp.float32)
    final_coefficient_reduced = small_params[7:10].astype(jnp.bfloat16)
    kept = []
    sum_list = []
    count_list = []
    for micro_index in range(micro_count):
        features = jnp.transpose(pixels[0, micro_index], (0, 2, 1))
        live_slot = slot_ids[None, :] < lengths[0, micro_index][:, None]
        context = jnp.where(live_slot & (ctx_mask[0, micro_index] == 1), 1.0, 0.0).astype(
            jnp.float32
        )
        query_mask = jnp.where(live_slot & (ctx_mask[0, micro_index] == 0), 1.0, 0.0).astype(
            jnp.float32
        )
        summed, counts, saved = encoder_forward(features, context, small_params, square_low[0])
        sum_list.append(summed)
        count_list.append(counts)
        kept.append((features, context, query_mask, saved))
    totals = [
        lax.psum((sum_list[index_micro], count_list[index_micro]), "ctx")
        for index_micro in range(micro_count)
    ]
    zeros_small = jnp.zeros((model_width,), jnp.float32)
    grad_first_w = jnp.zeros((5, model_width), jnp.float32)
    grad_coord_w = jnp.zeros((2, model_width), jnp.float32)
    grad_out_w = jnp.zeros((3, model_width), jnp.float32)
    grad_vectors = [zeros_small] * 5
    grad_square = jnp.zeros_like(square_w)
    latent_rows = []
    theta_rows = []
    squared = jnp.zeros((), jnp.float32)
    regular = jnp.zeros((), jnp.float32)
    for micro_index in range(micro_count):
        features, context, query_mask, saved = kept[micro_index]
        first_pre, gelu_first, norm_back, normed_low, gelu_second = saved
        summed, counts = totals[micro_index]
        divisor = counts[:, None] + 1.0
        latent_low = (summed / divisor).astype(jnp.bfloat16)
        latent_back = latent_low.astype(jnp.float32)
        generated = jnp.dot(latent_low, head_low, preferred_element_type=jnp.float32)
        gen_parts = generated.astype(jnp.bfloat16).reshape(groups, -1, model_width)
        gen_full = lax.all_gather(gen_parts, "ctx", axis=1, tiled=True)
        gen_bias = jnp.dot(latent_low, square_low[1], preferred_element_type=jnp.float32)
        coord_pre = (
            jnp.einsum(
                "gpc,cd->gpd",
                features[..., 3:5],
                small_params[5:7],
                precision=exact_arithmetic_mode,
            )
            + small_params[14]
        )
        siren_low = jnp.sin(30.0 * coord_pre).astype(jnp.bfloat16)
        siren_pre = (
            jnp.einsum("gpd,gde->gpe", siren_low, gen_full, preferred_element_type=jnp.float32)
            + gen_bias[:, None, :]
        )
        result_reduced_form = jnp.sin(30.0 * siren_pre).astype(jnp.bfloat16)
        estimated_colour_values = jnp.einsum(
            "kdg,cg->kcd",
            result_reduced_form,
            final_coefficient_reduced,
            preferred_element_type=jnp.float32,
        )
        errors = (
            estimated_colour_values - jnp.transpose(features[..., 0:3], (0, 2, 1))
        ) * query_mask[:, None, :]
        squared = squared + jnp.sum(errors * errors)
        regular = regular + jnp.sum(generated * generated)
        prediction_gradient = (2.0 / live_all * errors).astype(jnp.bfloat16)
        grad_out_w = grad_out_w + jnp.einsum(
            "dan,dnq->aq",
            prediction_gradient,
            result_reduced_form,
            preferred_element_type=jnp.float32,
        )
        grad_out = jnp.einsum(
            "xvw,vt->xwt",
            prediction_gradient,
            final_coefficient_reduced,
            preferred_element_type=jnp.float32,
        )
        grad_inner = (grad_out * 30.0 * jnp.cos(30.0 * siren_pre)).astype(jnp.bfloat16)
        gen_part = jnp.einsum(
            "gpd,gpe->gde", siren_low, grad_inner, preferred_element_type=jnp.float32
        )
        gen_grad = lax.psum_scatter(gen_part, "ctx", scatter_dimension=1, tiled=True).reshape(
            groups, -1
        )
        gen_grad = gen_grad + 2.0 * reg_weight / groups_all * generated
        bias_part = jnp.sum(grad_inner.astype(jnp.float32), axis=1)
        grad_siren = jnp.einsum(
            "gpe,gde->gpd", grad_inner, gen_full, preferred_element_type=jnp.float32
        )
        grad_coord = grad_siren * 30.0 * jnp.cos(30.0 * coord_pre)
        grad_coord_w = grad_coord_w + jnp.einsum(
            "gpc,gpd->cd", features[..., 3:5], grad_coord, precision=exact_arithmetic_mode
        )
        grad_vectors[4] = grad_vectors[4] + jnp.sum(grad_coord, axis=(0, 1))
        latent_rows.append(latent_back)
        theta_rows.append(gen_grad)
        latent_part = jnp.dot(gen_grad, head_back.T, precision=exact_arithmetic_mode)
        latent_part, bias_full = lax.psum((latent_part, bias_part), "ctx")
        grad_square = grad_square.at[1].add(
            jnp.dot(latent_back.T, bias_part, precision=exact_arithmetic_mode)
        )
        grad_latent = latent_part + jnp.dot(bias_full, bias_head.T, precision=exact_arithmetic_mode)
        grad_encoded = context[:, :, None] * (grad_latent / divisor)[:, None, :]
        (grad_second,) = gelu_second(grad_encoded)
        second_low = grad_second.astype(jnp.bfloat16)
        grad_square = grad_square.at[0].add(
            jnp.einsum("gpd,gpe->de", normed_low, second_low, preferred_element_type=jnp.float32)
        )
        grad_vectors[3] = grad_vectors[3] + jnp.sum(second_low.astype(jnp.float32), axis=(0, 1))
        grad_normed = jnp.einsum(
            "gpe,de->gpd", second_low, square_low[0], preferred_element_type=jnp.float32
        )
        grad_act, grad_gain, grad_beta = norm_back(grad_normed)
        (grad_first,) = gelu_first(grad_act)
        grad_first_w = grad_first_w + jnp.einsum(
            "gpc,gpd->cd", features, grad_first, precision=exact_arithmetic_mode
        )
        grad_vectors[0] = grad_vectors[0] + jnp.sum(grad_first, axis=(0, 1))
        grad_vectors[1] = grad_vectors[1] + grad_gain
        grad_vectors[2] = grad_vectors[2] + grad_beta
    grad_small = jnp.concatenate(
        [
            grad_first_w,
            grad_coord_w,
            grad_out_w,
            jnp.stack(
                [
                    grad_vectors[0],
                    grad_vectors[1],
                    grad_vectors[2],
                    grad_vectors[3],
                    grad_vectors[4],
                ]
            ),
        ],
        axis=0,
    )
    grad_small, grad_square, stat_sums = lax.psum(
        (grad_small, grad_square, jnp.stack([squared, regular])), ("dp", "ctx")
    )
    latent_stack = jnp.concatenate(latent_rows, axis=0)
    theta_stack = jnp.concatenate(theta_rows, axis=0)
    grad_head = lax.psum(
        jnp.dot(latent_stack.T, theta_stack, precision=exact_arithmetic_mode), "dp"
    )
    loss_value = stat_sums[0] / live_all + reg_weight * stat_sums[1] / groups_all
    head_moment = momentum_rate * head_mom + grad_head
    head_dir = head_orthogonal(head_moment)
    head_new = head_w - head_rate * (0.2 * model_width * head_dir + decay_rate * head_w)
    square_moment = momentum_rate * square_mom + grad_square
    rates = jnp.array(square_rates, jnp.float32)[:, None, None]
    square_new = square_w - rates * (
        0.2 * model_width**0.5 * orthogonal_local(square_moment) + decay_rate * square_w
    )
    small_moment, small_second, small_new = adam_update(
        small_params, grad_small, small_mom, small_var
    )
    return (
        head_moment,
        head_new,
        head_new.astype(jnp.bfloat16),
        square_moment,
        square_new,
        square_new.astype(jnp.bfloat16),
        small_moment,
        small_second,
        small_new,
        small_new.astype(jnp.bfloat16),
        loss_value,
    )


MESH = pl.DeviceIdType.MESH
F32 = jnp.float32
BF16 = jnp.bfloat16
WIDTH = 256
TILE = 256
MIB = 1024 * 1024
SPAN = 768
QUARTER = 64
HALF = 128
TURN = 30.0 / 6.283185307179586
GELU_ONE = 0.7978845608028654
GELU_CUBE = GELU_ONE * 0.044715
GELU_SCALE = GELU_CUBE ** (1.0 / 3.0)
GELU_SLOPE = GELU_ONE / GELU_SCALE
NORM_EPS = 1e-05 * (2.0 * GELU_SCALE) ** 2
SIN_TERMS = (4.442860272, -7.307432505, 3.594782484, -0.784372885)


def any_spec():
    return pl.BlockSpec(memory_space=pl.ANY)


def hbm_spec():
    return pl.BlockSpec(memory_space=pltpu.HBM)


def busy(micros):
    return pl.CostEstimate(flops=micros * 10**9, bytes_accessed=micros * 10**5, transcendentals=0)


def vmem_spec():
    return pl.BlockSpec(memory_space=pltpu.VMEM)


def smem_spec():
    return pl.BlockSpec(memory_space=pltpu.SMEM)


def turned(matrix):
    pad = jnp.zeros((matrix.shape[0], 128 - matrix.shape[1]), F32)
    return jnp.concatenate([matrix, pad], axis=1).T


def weave(order, first, second):
    for letter in order:
        next(first if letter == "A" else second, None)
    for rest in (first, second):
        for unused in rest:
            pass


def dot_nn(a, b):
    return lax.dot_general(a, b, (((1,), (0,)), ((), ())), preferred_element_type=F32)


def dot_nt(a, b):
    return lax.dot_general(a, b, (((1,), (1,)), ((), ())), preferred_element_type=F32)


def full_nn(a, b):
    return lax.dot_general(
        a, b, (((1,), (0,)), ((), ())), precision=lax.Precision.HIGHEST, preferred_element_type=F32
    )


def full_nt(a, b):
    return lax.dot_general(
        a, b, (((1,), (1,)), ((), ())), precision=lax.Precision.HIGHEST, preferred_element_type=F32
    )


def split3(v):
    high = v.astype(BF16).astype(F32)
    rest = v - high
    mid = rest.astype(BF16).astype(F32)
    return high, mid, rest - mid


def hail(peers):
    barrier = pltpu.get_barrier_semaphore()
    for peer in peers:
        pl.semaphore_signal(barrier, inc=1, device_id=peer, device_id_type=MESH)
    return len(peers)


def meet(count):
    pl.semaphore_wait(pltpu.get_barrier_semaphore(), count)


def greet(peers):
    meet(hail(peers))


def paired(place, d, n):
    partner, bit = 0, 1
    while bit < n:
        own = lax.rem(place // bit, 2)
        partner = partner + bit * (1 - own if (d // bit) % 2 else own)
        bit = 2 * bit
    return partner


def ring_peers(axis, n):
    me = lax.axis_index(axis)
    return [paired(me, d, n) for d in range(n - 1, 0, -1)]


def plan_all(axis, n, source, target, send_sem, recv_sem):
    return [
        pltpu.make_async_remote_copy(
            src_ref=source(peer),
            dst_ref=target,
            send_sem=send_sem.at[d],
            recv_sem=recv_sem.at[d],
            device_id={axis: peer},
            device_id_type=MESH,
        )
        for d, peer in enumerate(ring_peers(axis, n))
    ]


def send_all(*plan):
    copies = plan_all(*plan)
    for copy in copies:
        copy.start()
    return copies


def fenced(copies, before=None):
    @pl.when(lax.axis_index("ctx") >= 0)
    def run():
        if before is not None:
            before()
        for copy in copies:
            copy.start()

    return copies


def column(row, width):
    return jnp.broadcast_to(row, (width, row.shape[1])).T


def gelu_twice(y):
    return y + y * jnp.tanh(y * (GELU_SLOPE + y * y))


def gelu_both(y):
    square = y * y
    above = 1.0 + jnp.tanh(y * (GELU_SLOPE + square))
    value = y * above
    return value, above + (value * (2.0 - above)) * (3.0 * square + GELU_SLOPE)


def plain_twice(x):
    return x + x * jnp.tanh(x * (GELU_ONE + GELU_CUBE * (x * x)))


def plain_slope(x):
    square = GELU_CUBE * (x * x)
    above = 1.0 + jnp.tanh(x * (GELU_ONE + square))
    return above + (x * above) * (2.0 - above) * (3.0 * square + GELU_ONE)


def sine_pair(turns):
    frac = turns - jnp.round(turns)
    square = frac * frac
    s = SIN_TERMS[3] * square + SIN_TERMS[2]
    s = s * square + SIN_TERMS[1]
    s = (s * square + SIN_TERMS[0]) * frac
    cosine = 1.0 - s * s
    rest = 1.0 + cosine
    return s * (rest * lax.rsqrt(rest)), cosine


def triple_weights(block):
    high, mid, low = split3(block)
    rows = jnp.concatenate([high, mid, high, low, mid, high], axis=0)
    pad = jnp.zeros((128 - rows.shape[0], rows.shape[1]), F32)
    return jnp.concatenate([rows, pad], axis=0).T.astype(BF16)[:, 0:48]


def triple_from_list(rows):
    high, mid, low = split3(rows)
    return jnp.concatenate([high, high, mid, high, mid, low], axis=0).astype(BF16)


def three(matrix):
    high = matrix.astype(BF16)
    rest = matrix - high.astype(F32)
    mid = rest.astype(BF16)
    return high, mid, (rest - mid.astype(F32)).astype(BF16)


def six(left, right):
    rows = left[0].shape[0]
    first = dot_nn(jnp.concatenate(left, axis=0), right[0])
    second = dot_nn(jnp.concatenate(left[0:2], axis=0), right[1])
    third = dot_nn(left[0], right[2])
    return (first[0:rows] + second[0:rows] + third) + (
        first[rows : 2 * rows] + second[rows:] + first[2 * rows :]
    )


def few(left, right):
    rows = left[0].shape[0]
    first = dot_nn(jnp.concatenate(left[0:2], axis=0), right[0])
    return (first[0:rows] + dot_nn(left[0], right[1])) + first[rows:]


def gram_six(parts):
    high, mid, low = parts
    both = jnp.concatenate([high, mid], axis=1)
    cross = dot_nt(jnp.concatenate([high, high], axis=1), jnp.concatenate([mid, low], axis=1))
    return dot_nt(both, both) + (cross + cross.T)


def order_rows(row, per):
    return jnp.concatenate([row[:, k * TILE : (k + 1) * TILE] for k in range(per)], axis=0)


def bring_counts(seen_ref, cnt_v, cnt_s, sem):
    for s in range(seen_ref.shape[0]):
        cnt_v[s : s + 1, :] = seen_ref[s, 0:1, :].astype(jnp.int32)
    counts = pltpu.make_async_copy(cnt_v, cnt_s, sem)
    counts.start()
    return counts


def put(target, rows, extra, offset, start, amount):
    lane_ids = lax.broadcasted_iota(jnp.int32, (8, TILE), 1)
    shift = lax.rem(offset, TILE)
    base = pl.multiple_of(offset - shift, TILE)
    marks = [jnp.full((1, TILE), value, F32) for value in (0.0, 1.0, extra)]
    moved = pltpu.roll(jnp.concatenate([rows] + marks, axis=0), lax.rem(shift - start + TILE, TILE), 1)
    here = (lane_ids >= shift) & (lane_ids < shift + amount)
    there = lane_ids < shift + amount - TILE
    target[:, pl.ds(base, TILE)] += jnp.where(here, moved, 0.0)
    target[:, pl.ds(pl.multiple_of(base + TILE, TILE), TILE)] = jnp.where(there, moved, 0.0)


def clear_tail(target, amount):
    start = pl.multiple_of((amount // TILE + 1) * TILE, TILE)
    for step in range(4 * SPAN // TILE):
        target[:, pl.ds(start + step * TILE, TILE)] = jnp.zeros((8, TILE), F32)


def weight_block(weights, bias, place):
    rows = weights.shape[0]
    parts = []
    if place > 0:
        parts.append(jnp.zeros((place, WIDTH), F32))
    parts.append(weights)
    if place + rows < 6:
        parts.append(jnp.zeros((6 - place - rows, WIDTH), F32))
    parts.append(bias)
    parts.append(jnp.zeros((1, WIDTH), F32))
    return jnp.concatenate(parts, axis=0)


def scatter_kernel(
    n, rows_n, len_hbm, pix_hbm, mask_hbm, mom_ref, rx_ref, seen_ref, tiles_ref, share_ref, gram_ref,
    len_ref, pix_ref, mask_ref, stage, stage_n, told, buf, own, slab_rx, upper,
    send_sem, recv_sem, load_sem, slab_sem, own_sem, tell_sem,
):
    brought = [
        pltpu.make_async_copy(source, target, own_sem.at[j])
        for j, (source, target) in enumerate(((len_hbm, len_ref), (pix_hbm, pix_ref), (mask_hbm, mask_ref)))
    ]
    for copy in brought:
        copy.start()
    me = lax.axis_index("ctx")
    peers = ring_peers("ctx", n)
    r = lax.axis_index("dp")
    span = buf.shape[1]
    load = pltpu.make_async_copy(mom_ref.at[:, pl.ds(pl.multiple_of(r * span, span), span)], buf, load_sem)
    load.start()
    count = hail([{"ctx": peer} for peer in peers] + [{"dp": peer} for peer in ring_peers("dp", rows_n)])
    slots = pix_ref.shape[4]
    per = slots // TILE
    groups = mask_ref.shape[2]
    row_ids = lax.broadcasted_iota(jnp.int32, (TILE, TILE), 0)
    upper[...] = jnp.where(row_ids <= lax.broadcasted_iota(jnp.int32, (TILE, TILE), 1), 1.0, 0.0).astype(BF16)
    row_ids = row_ids.astype(F32)
    lane_ids = lax.broadcasted_iota(jnp.int32, (TILE, TILE), 1).astype(F32)
    place = (
        lax.broadcasted_iota(jnp.int32, (per, TILE), 0) * TILE
        + lax.broadcasted_iota(jnp.int32, (per, TILE), 1)
        + me * slots
    )
    pad = jnp.zeros((3, TILE), F32)
    ones = jnp.ones((16, TILE), BF16)
    blank = jnp.zeros((128 - 2 * per, TILE), BF16)
    wide_ids = lax.broadcasted_iota(jnp.int32, (per, 128), 1)
    told[...] = jnp.zeros_like(told)

    def arrange(b):
        def one(j, carry):
            g = b * groups + j
            mask = order_rows(mask_ref[0, b, pl.ds(j, 1), :], per)
            live = place < len_ref[0, b, j]
            context = jnp.where(live & (mask == 1), 1.0, 0.0)
            query = jnp.where(live & (mask == 0), 1.0, 0.0)
            both = jnp.concatenate([context, query], axis=0).astype(BF16)
            order = dot_nn(both, upper[...])
            before_c, before_q = order[0:per], order[per : 2 * per]
            live_c = before_c[:, TILE - 1 : TILE]
            target = jnp.where(
                context > 0.5, before_c, jnp.where(query > 0.5, live_c + before_q, 0.0)
            ) - 1.0
            amounts = dot_nt(ones, jnp.concatenate([both, blank], axis=0))[0:1]
            share_ref[g, 0:1, :] = amounts
            for t in range(per):
                place_t = pl.ds(lax.rem(g + t, n), 1)
                told[place_t, :] = jnp.where(wide_ids[0:1] == g, live_c[t : t + 1], told[place_t, :])
            for t in range(per):
                rows = jnp.concatenate(
                    [pix_ref[0, b, c, pl.ds(j, 1), t * TILE : (t + 1) * TILE] for c in range(5)]
                    + [pad], axis=0
                )
                high, mid, low = split3(rows)
                stack = jnp.concatenate([high, mid, low, jnp.zeros((8, TILE), F32)], axis=0).astype(BF16)
                if t % 2 == 0:
                    chosen = jnp.where(row_ids == target[t : t + 1], 1.0, 0.0).astype(BF16)
                    found = dot_nt(stack, chosen)
                else:
                    spot = column(target[t : t + 1], 128)
                    chosen = jnp.where(lane_ids == jnp.concatenate([spot, spot], axis=1), 1.0, 0.0).astype(BF16)
                    found = dot_nn(stack, chosen)
                found = found[0:8] + found[8:16] + found[16:24]
                tiles_ref[g, :, t * TILE : (t + 1) * TILE] = found
                stage[lax.rem(g + t, n), :, pl.ds(pl.multiple_of(g * TILE, TILE), TILE)] = found
            return carry

        lax.fori_loop(0, groups, one, 0)

    copies = []
    for copy in brought:
        copy.wait()
    for b in range(mask_ref.shape[1]):
        arrange(b)
        if b == 0:
            meet(count)
        lanes = pl.ds(b * groups * TILE, groups * TILE)
        copies += fenced(
            plan_all(
                "ctx",
                n,
                lambda peer: stage.at[peer, pl.ds(0, 5), lanes],
                rx_ref.at[me, pl.ds(0, 5), lanes],
                send_sem.at[b],
                recv_sem.at[b],
            )
        )
    for p in range(n):
        stage_n[p, 0:1, :] = told[p : p + 1, :]
    top = pl.ds(0, 1)
    copies += fenced(
        plan_all("ctx", n, lambda peer: stage_n.at[peer, top, :], seen_ref.at[me, top, :], tell_sem.at[0], tell_sem.at[1])
    )
    rx_ref[me, 0:5, :] = stage[me, 0:5, :]
    seen_ref[me, 0:1, :] = stage_n[me, 0:1, :]
    quarter = gram_ref.shape[0]
    same = jnp.zeros((WIDTH, WIDTH), F32)
    cross = jnp.zeros((WIDTH, WIDTH), F32)
    load.wait()
    for i in range(buf.shape[1] // WIDTH):
        high, mid, low = three(buf[:, i * WIDTH : (i + 1) * WIDTH])
        both = jnp.concatenate([high, mid], axis=1)
        same = same + dot_nt(both, both)
        cross = cross + dot_nt(jnp.concatenate([high, high], axis=1), jnp.concatenate([mid, low], axis=1))
    own[...] = same + (cross + cross.T)
    slabs = fenced(
        plan_all(
            "dp",
            rows_n,
            lambda peer: own.at[pl.ds(pl.multiple_of(peer * quarter, quarter), quarter), :],
            slab_rx.at[r],
            slab_sem.at[0],
            slab_sem.at[1],
        )
    )
    slab_rx[r] = own[pl.ds(pl.multiple_of(r * quarter, quarter), quarter), :]
    for copy in slabs:
        copy.wait()
    total = slab_rx[0]
    for s in range(1, rows_n):
        total = total + slab_rx[s]
    gram_ref[...] = total
    for copy in copies:
        copy.wait()


def encoder_kernel(
    rx_ref, seen_ref, small_ref, square_ref, z_ref, amount_ref, clist, stats_ref, count_ref, cnt_v, cnt_s, wide, second, zacc, low_a, low_b, sem
):
    sources = rx_ref.shape[0]
    per = rx_ref.shape[2] // TILE
    counts = bring_counts(seen_ref, cnt_v, cnt_s, sem)
    small = small_ref[...]
    first = triple_weights(weight_block(small[0:5] * GELU_SCALE, small[10:11] * GELU_SCALE, 0))
    wide[0] = column(small[11:12], SPAN)
    wide[1] = column(small[12:13], SPAN)
    wide[2] = column(small[13:14], SPAN)
    second[...] = square_ref[0].T.astype(BF16)
    zacc[...] = jnp.zeros_like(zacc)
    clist[:, 0:TILE] = jnp.zeros((8, TILE), F32)
    counts.wait()

    def place_tile(s, offset):
        for k in range(per):
            amount = cnt_s[s, k]
            put(clist, rx_ref[s, 0:5, k * TILE : (k + 1) * TILE], k + 1.0, offset, 0, amount)
            offset = offset + amount
        return offset

    num_c = lax.fori_loop(0, sources, place_tile, jnp.int32(0))
    clear_tail(clist, num_c)
    count_ref[0] = num_c
    ids = lax.broadcasted_iota(jnp.int32, (16, SPAN), 0).astype(F32) + 1.0

    def window(t):
        return clist[:, pl.ds(pl.multiple_of(t * SPAN, SPAN), SPAN)]

    def begin(t, low):
        pre = dot_nn(first, triple_from_list(window(t)))
        parts = []
        total = jnp.zeros((1, SPAN), F32)
        for c in range(0, WIDTH, HALF):
            parts.append(gelu_twice(pre[c : c + HALF]))
            total = total + jnp.sum(parts[-1], axis=0, keepdims=True)
            yield
        mean = total * (1.0 / WIDTH)
        total = jnp.zeros((1, SPAN), F32)
        for c in range(len(parts)):
            parts[c] = parts[c] - mean
            total = total + jnp.sum(parts[c] * parts[c], axis=0, keepdims=True)
        inverse = lax.rsqrt(total * (1.0 / WIDTH) + NORM_EPS)
        stats_ref[0:1, pl.ds(pl.multiple_of(t * SPAN, SPAN), SPAN)] = mean
        stats_ref[1:2, pl.ds(pl.multiple_of(t * SPAN, SPAN), SPAN)] = inverse
        yield
        for c in range(len(parts)):
            rows = slice(c * HALF, (c + 1) * HALF)
            low[rows, :] = (parts[c] * inverse * wide[0, rows, :] + wide[1, rows, :]).astype(BF16)
        yield

    def finish(t, low):
        pre = dot_nn(second[...], low[...])
        yield
        highs, rests = [], []
        for c in range(0, WIDTH, HALF):
            encoded = plain_twice(pre[c : c + HALF] + wide[2, c : c + HALF, :])
            highs.append(encoded.astype(BF16))
            rests.append((encoded - highs[-1].astype(F32)).astype(BF16))
            yield
        owner = jnp.where(ids == window(t)[7:8], 1.0, 0.0).astype(BF16)
        right = jnp.concatenate([jnp.concatenate(highs, axis=0), jnp.concatenate(rests, axis=0)], axis=1)
        zacc[...] += dot_nt(right, jnp.concatenate([owner, owner], axis=1))
        yield

    def pair(p, carry):
        weave("BAABABBABABA", begin(2 * p + 1, low_b), finish(2 * p, low_a))
        weave("BAABABBABABA", begin(2 * p + 2, low_a), finish(2 * p + 1, low_b))
        return carry

    spans = (num_c + SPAN - 1) // SPAN
    weave("", begin(0, low_a), iter(()))
    lax.fori_loop(0, spans // 2, pair, 0)

    @pl.when(lax.rem(spans, 2) == 1)
    def last():
        weave("", iter(()), finish(spans - 1, low_a))

    z_ref[...] = turned(zacc[...])[0:8] * 0.5
    total = seen_ref[0, 0:1, :]
    for s in range(1, sources):
        total = total + seen_ref[s, 0:1, :]
    amount_ref[...] = jnp.broadcast_to(total, (8, 128))


def theta_kernel(
    n, z_ref, amount_ref, head_ref, tiles_ref, share_ref, theta_ref, gen_ref, z8_ref, inv_ref, reg_ref,
    rx_ref, seen_ref, zall, nall, head, give, turn, load_sem, sems,
):
    me = lax.axis_index("ctx")
    peers = ring_peers("ctx", n)
    chunk = head.shape[2]
    per = chunk // WIDTH

    def load(k):
        return pltpu.make_async_copy(head_ref.at[:, pl.ds(k * chunk, chunk)], head.at[k], load_sem.at[k])

    for k in range(head.shape[0]):
        load(k).start()
    greet([{"ctx": peer} for peer in peers])
    top = pl.ds(0, 1)
    latents = send_all("ctx", n, lambda peer: z_ref, zall.at[me], sems.at[0], sems.at[1])
    latents += send_all(
        "ctx", n, lambda peer: amount_ref.at[top, :], nall.at[me, top, :], sems.at[6], sems.at[7]
    )
    pixels = send_all(
        "ctx",
        n,
        lambda peer: tiles_ref.at[peer, pl.ds(0, 5), :],
        rx_ref.at[me, pl.ds(0, 5), :],
        sems.at[2],
        sems.at[3],
    )
    pixels += send_all(
        "ctx", n, lambda peer: share_ref.at[peer, top, :], seen_ref.at[me, top, :], sems.at[8], sems.at[9]
    )
    zall[me] = z_ref[...]
    nall[me, 0:1, :] = amount_ref[0:1, :]
    rx_ref[me, 0:5, :] = tiles_ref[me, 0:5, :]
    seen_ref[me, 0:1, :] = share_ref[me, 0:1, :]
    for copy in latents:
        copy.wait()
    total = zall[0]
    amounts = nall[0, 0:1, :]
    for s in range(1, n):
        total = total + zall[s]
        amounts = amounts + nall[s, 0:1, :]
    lanes = lax.broadcasted_iota(jnp.int32, (8, 128), 1)
    rows = lax.broadcasted_iota(jnp.int32, (8, 128), 0)
    counts = jnp.sum(jnp.where(lanes == rows, amounts, 0.0), axis=1, keepdims=True) + 1.0
    latent = (total / counts).astype(BF16).astype(F32)
    z8_ref[...] = latent
    inv_ref[...] = jnp.broadcast_to(0.5 / counts, (8, WIDTH))
    left = jnp.concatenate([latent, jnp.zeros((8, WIDTH), F32)], axis=0).astype(BF16)
    regular = jnp.zeros((8, WIDTH), F32)
    for k in range(head.shape[0]):
        load(k).wait()
        part = dot_nn(left, head[k].astype(BF16))[0:8]
        for i in range(per):
            piece = part[:, i * WIDTH : (i + 1) * WIDTH]
            theta_ref[pl.ds((k * per + i) * 8, 8), :] = piece
            for half in range(2):
                turn[half, pl.ds((k * per + i) * 8, 8), :] = piece[:, half * 128 : half * 128 + 128]
            regular = regular + piece * piece
    reg_ref[...] = regular
    height = WIDTH // n
    for g in range(n):
        for half in range(2):
            give[g, :, half * 128 : half * 128 + 128] = turn[half, pl.ds(g, height, stride=8), :].astype(BF16)
    mine = pl.ds(pl.multiple_of(me * height, height), height)
    parts = fenced(
        plan_all("ctx", n, lambda peer: give.at[peer], gen_ref.at[mine, :], sems.at[4], sems.at[5])
    )
    gen_ref[mine, :] = give[me]
    for copy in pixels + parts:
        copy.wait()


def siren_kernel(
    live_all, len_ref, rx_ref, seen_ref, gen_ref, z_ref, small_ref, square_ref, out_ref, bias_ref, narrow_ref,
    q_ref, cnt_v, cnt_s, inner, shift, sa, sb, ca, cb, ma, mb, na, nb, acc_g, acc_c, acc_o, acc_e, sem,
):
    sin_in, cos_in, sin_mid, cos_mid = (sa, sb), (ca, cb), (ma, mb), (na, nb)
    me = lax.axis_index("ctx")
    per = rx_ref.shape[2] // TILE
    groups = len_ref.shape[2]
    length = len_ref[0, me // groups, lax.rem(me, groups)]
    counts = bring_counts(seen_ref, cnt_v, cnt_s, sem)
    small = small_ref[...]
    coord = triple_weights(weight_block(small[5:7] * TURN, small[14:15] * TURN, 3))
    latent = jnp.broadcast_to(z_ref[pl.ds(me, 1), :], (16, WIDTH)).astype(BF16)
    bias = dot_nn(latent, square_ref[1].astype(BF16))[0:1]
    inner[...] = gen_ref[...].astype(F32).T.astype(BF16)
    shift[...] = column(bias * TURN, SPAN)
    final = small[7:10].astype(BF16).astype(F32)
    final_rows = jnp.concatenate([final, jnp.zeros((13, WIDTH), F32)], axis=0).astype(BF16)
    large = final * 30.0
    high = large.astype(BF16).astype(F32)
    gap = jnp.zeros((5, WIDTH), F32)
    final_cols = jnp.concatenate([high, gap, large - high, jnp.zeros((117, WIDTH), F32)], axis=0).T.astype(BF16)[:, 0:16]
    for ref in (acc_g, acc_c, acc_o, acc_e):
        ref[...] = jnp.zeros_like(ref)
    scale = 2.0 / live_all
    ones = jnp.ones((16, SPAN), BF16)
    q_ref[:, 0:TILE] = jnp.zeros((8, TILE), F32)
    counts.wait()

    def place_tile(s, offset):
        for k in range(per):
            amount = cnt_s[s, per + k]
            put(q_ref, rx_ref[s, 0:5, k * TILE : (k + 1) * TILE], 0.0, offset, cnt_s[s, k], amount)
            offset = offset + amount
        return offset

    num_q = lax.fori_loop(0, (length + per * TILE - 1) // (per * TILE), place_tile, jnp.int32(0))
    clear_tail(q_ref, num_q)
    ids = lax.broadcasted_iota(jnp.int32, (8, SPAN), 0)

    def window(t):
        return q_ref[:, pl.ds(pl.multiple_of(t * SPAN, SPAN), SPAN)]

    def ahead(t, k):
        turns = dot_nn(coord, triple_from_list(window(t)))
        for c in range(0, WIDTH, WIDTH):
            s_in, c_in = sine_pair(turns[c : c + WIDTH])
            sin_in[k][c : c + WIDTH, :] = s_in.astype(BF16)
            cos_in[k][c : c + WIDTH, :] = c_in
            yield
        turns = dot_nn(inner[...], sin_in[k][...])
        yield
        for c in range(0, WIDTH, WIDTH):
            s_mid, c_mid = sine_pair(turns[c : c + WIDTH] * TURN + shift[c : c + WIDTH, :])
            sin_mid[k][c : c + WIDTH, :] = s_mid.astype(BF16)
            cos_mid[k][c : c + WIDTH, :] = c_mid
            yield

    def back_part(t, k):
        rows = window(t)
        pred = dot_nn(final_rows, sin_mid[k][...])[0:8]
        error = jnp.where(ids < 3, (pred - rows) * rows[6:7], 0.0)
        acc_e[...] += error * error
        slope = (error * scale).astype(BF16).astype(F32)
        slope = jnp.concatenate([slope, slope], axis=0).astype(BF16)
        yield
        acc_o[...] += dot_nt(sin_mid[k][...], slope)
        back = (cos_mid[k][...] * dot_nn(final_cols, slope)).astype(BF16)
        yield
        grads = dot_nn(gen_ref[...], back)
        yield
        outer = cos_in[k][...] * grads
        high = outer.astype(BF16)
        low = (outer - high.astype(F32)).astype(BF16)
        yield
        acc_g[...] += dot_nt(jnp.concatenate([sin_in[k][...], ones], axis=0), back)
        yield
        left = jnp.concatenate(split3(rows) + (jnp.zeros((8, SPAN), F32),), axis=0).astype(BF16)
        acc_c[...] += dot_nt(jnp.concatenate([high, low], axis=1), jnp.concatenate([left, left], axis=1))
        yield

    def pair(p, carry):
        weave("BABABABAABABAA", ahead(2 * p + 1, 1), back_part(2 * p, 0))
        weave("BABABABAABABAA", ahead(2 * p + 2, 0), back_part(2 * p + 1, 1))
        return carry

    spans = (num_q + SPAN - 1) // SPAN
    weave("", ahead(0, 0), iter(()))
    lax.fori_loop(0, spans // 2, pair, 0)

    @pl.when(lax.rem(spans, 2) == 1)
    def last():
        weave("", iter(()), back_part(spans - 1, 0))

    out_ref[...] = acc_g[0:WIDTH, :]
    bias_ref[...] = acc_g[WIDTH : WIDTH + 8, :]
    coords = turned(acc_c[...])
    coords = (coords[0:8] + coords[8:16] + coords[16:24]) * 30.0
    narrow_ref[0:2, :] = coords[3:5]
    narrow_ref[2:5, :] = turned(acc_o[...])[0:3]
    narrow_ref[5:6, :] = coords[6:7]
    narrow_ref[6:7, :] = jnp.broadcast_to(jnp.sum(acc_e[...]), (1, WIDTH))
    narrow_ref[7:8, :] = jnp.zeros((1, WIDTH), F32)


def latent_kernel(
    n, groups_all, part_ref, bias_ref, theta_ref, head_ref, mom_ref, z8_ref, gram_ref,
    dz_ref, tall_ref, cross_ref,
    rx, rxb, turn, head, mom, low_head, low_mom, rxz, dz_own, lefts, rxs, slab_sum, load_sem, mom_sem, sems,
):
    me = lax.axis_index("ctx")
    peers = ring_peers("ctx", n)
    chunk = head.shape[2]
    per = chunk // WIDTH
    height = WIDTH // n

    def load(k):
        return pltpu.make_async_copy(head_ref.at[:, pl.ds(k * chunk, chunk)], head.at[k], load_sem.at[k])

    def load_mom(k):
        return pltpu.make_async_copy(mom_ref.at[:, pl.ds(k * chunk, chunk)], mom.at[k], mom_sem.at[k])

    for k in range(head.shape[0]):
        load(k).start()
    for k in range(head.shape[0]):
        load_mom(k).start()
    greet([{"ctx": peer} for peer in peers])
    mine = pl.ds(pl.multiple_of(me * height, 8), height)
    parts = send_all(
        "ctx",
        n,
        lambda peer: part_ref.at[pl.ds(pl.multiple_of(peer * height, 8), height), :],
        rx.at[mine, :],
        sems.at[0],
        sems.at[1],
    )
    biases = send_all(
        "ctx", n, lambda peer: bias_ref.at[pl.ds(0, 1), :], rxb.at[me, pl.ds(0, 1), :], sems.at[6], sems.at[7]
    )
    slab = gram_ref.shape[0] // n
    grams = send_all(
        "ctx",
        n,
        lambda peer: gram_ref.at[pl.ds(pl.multiple_of(peer * slab, slab), slab), :],
        rxs.at[me],
        sems.at[4],
        sems.at[5],
    )
    rx[mine, :] = part_ref[mine, :]
    rxb[me, 0:1, :] = bias_ref[0:1, :]
    rxs[me] = gram_ref[pl.ds(pl.multiple_of(me * slab, slab), slab), :]

    def split_head(k, carry):
        load(k).wait()
        for i in range(per):
            low_head[k * per + i] = head[k, :, i * WIDTH : (i + 1) * WIDTH].astype(BF16)
        return carry

    lax.fori_loop(0, head.shape[0], split_head, 0)

    def split_mom(k, carry):
        load_mom(k).wait()
        for i in range(per):
            for j, part in enumerate(three(mom[k, :, i * WIDTH : (i + 1) * WIDTH].T)):
                low_mom[j, k * per + i] = part
        return carry

    lax.fori_loop(0, head.shape[0], split_mom, 0)

    def slab_total():
        for copy in grams:
            copy.wait()
        total = rxs[0]
        for s in range(1, n):
            total = total + rxs[s]
        slab_sum[...] = total
        tall_ref[height + 2 + me] = total

    slabs = fenced(
        plan_all("ctx", n, lambda peer: slab_sum, tall_ref.at[height + 2 + me], sems.at[8], sems.at[9]), slab_total
    )
    for copy in biases + parts:
        copy.wait()
    turn[0] = rx[:, 0:128]
    turn[1] = rx[:, 128:256]

    def across(i):
        return jnp.concatenate([turn[half, pl.ds(i, 8, stride=height), :] for half in range(2)], axis=1)

    blank = jnp.zeros((8, WIDTH), F32)
    for i in range(height):
        rows = across(i) + theta_ref[pl.ds(i * 8, 8), :] * (1.0 / groups_all)
        tall_ref[i] = rows
        lefts[i] = jnp.concatenate(split3(rows) + (blank,), axis=0).astype(BF16)
    tall_ref[height] = z8_ref[...]
    tall_ref[height + 1] = jnp.concatenate([rxb[s, 0:1, :] for s in range(n)], axis=0)
    totals = [jnp.zeros((32, WIDTH), F32)] * 2
    for i in range(height):
        totals[i % 2] = totals[i % 2] + dot_nt(lefts[i], low_head[i])
    total = totals[0] + totals[1]
    dz_own[...] = total[0:8] + total[8:16] + total[16:24]
    terms = fenced(plan_all("ctx", n, lambda peer: dz_own, rxz.at[me], sems.at[2], sems.at[3]))
    rxz[me] = dz_own[...]

    def mix(i, carry):
        totals = list(carry)
        for k in range(4):
            for j in range(3):
                totals[k % 2] = totals[k % 2] + dot_nn(lefts[4 * i + k], low_mom[j, 4 * i + k])
        return tuple(totals)

    empty = jnp.zeros((32, WIDTH), F32)
    totals = lax.fori_loop(0, height // 4, mix, (empty, empty))
    total = totals[0] + totals[1]
    cross_ref[...] = total[0:8] + total[8:16] + total[16:24]
    for copy in terms:
        copy.wait()
    total = rxz[0]
    for s in range(1, n):
        total = total + rxz[s]
    dz_ref[...] = total
    for copy in slabs:
        copy.wait()


def encoder_back_kernel(
    count_ref, c_ref, stats_ref, small_ref, square_ref, dz_ref, inv_ref, tall_ref, narrow_ref, reg_ref, out_ref, thin_ref,
    wide, second, spread, ua, ub, ka, kb, na, nb, ga, gb, acc_s, acc_f, acc_g, rows_out,
):
    unit, chain, normed, grad = (ua, ub), (ka, kb), (na, nb), (ga, gb)
    num_c = count_ref[0]
    small = small_ref[...]
    first = triple_weights(weight_block(small[0:5] * GELU_SCALE, small[10:11] * GELU_SCALE, 0))
    plain = square_ref[0].astype(BF16)
    low = plain.astype(F32)
    second[...] = low.T.astype(BF16)
    height = tall_ref.shape[0] - 10
    bias_back = full_nt(tall_ref[height + 1], square_ref[1].astype(BF16).astype(F32))
    latent_back = (dz_ref[...] + bias_back) * inv_ref[...]
    wide[0] = column(small[11:12], SPAN)
    wide[1] = column(small[12:13], SPAN)
    latent_cols = jnp.concatenate(split3(latent_back) + (jnp.zeros((104, WIDTH), F32),), axis=0).T.astype(BF16)[:, 0:32]
    wide[2] = column(small[13:14], SPAN)
    centre = split3(full_nn(jnp.broadcast_to(small[11:12], (8, WIDTH)), low) * (1.0 / WIDTH))
    rows = jnp.concatenate([part[0:1] for part in centre] + [jnp.zeros((13, WIDTH), F32)], axis=0)
    spread[...] = jnp.concatenate([plain, rows.astype(BF16)], axis=0)
    for ref in (acc_s, acc_f, acc_g):
        ref[...] = jnp.zeros_like(ref)
    ones = jnp.ones((16, SPAN), BF16)
    ids = lax.broadcasted_iota(jnp.int32, (8, SPAN), 0).astype(F32) + 1.0
    blank = jnp.zeros((8, SPAN), F32)

    def window(t):
        return c_ref[:, pl.ds(pl.multiple_of(t * SPAN, SPAN), SPAN)]

    def ahead(t, k):
        pre = dot_nn(first, triple_from_list(window(t)))
        stats = stats_ref[0:2, pl.ds(pl.multiple_of(t * SPAN, SPAN), SPAN)]
        mean, inverse = stats[0:1], stats[1:2]
        parts, slopes = [], []
        for c in range(0, WIDTH, QUARTER):
            value, slope = gelu_both(pre[c : c + QUARTER])
            parts.append((value - mean) * inverse)
            slopes.append(slope)
            yield
        scale = inverse * GELU_SCALE
        for c in range(len(parts)):
            rows = slice(c * QUARTER, (c + 1) * QUARTER)
            value = parts[c]
            unit[k][rows, :] = value
            normed[k][rows, :] = (value * wide[0, rows, :] + wide[1, rows, :]).astype(BF16)
            chain[k][rows, :] = slopes[c] * scale
        yield
        owner = jnp.where(ids == window(t)[7:8], 1.0, 0.0)
        owner = jnp.concatenate([owner, owner, owner, blank], axis=0).astype(BF16)
        pre = dot_nn(second[...], normed[k][...])
        outer = dot_nn(latent_cols, owner)
        yield
        for c in range(0, WIDTH, QUARTER):
            rows = slice(c, c + QUARTER)
            grad[k][rows, :] = (plain_slope(pre[rows] + wide[2, rows, :]) * outer[rows]).astype(BF16)
            yield

    def back_part(t, k):
        slopes = dot_nn(spread[...], grad[k][...])
        yield
        acc_s[...] += dot_nt(jnp.concatenate([normed[k][...], ones], axis=0), grad[k][...])
        yield
        means = jnp.sum(slopes[WIDTH : WIDTH + 8], axis=0, keepdims=True)
        total = jnp.zeros((1, SPAN), F32)
        parts = []
        for c in range(0, WIDTH, QUARTER):
            rows = slice(c, c + QUARTER)
            parts.append(slopes[rows] * wide[0, rows, :] - means)
            acc_g[rows, :] += slopes[rows] * unit[k][rows, :]
            total = total + jnp.sum(parts[-1] * unit[k][rows, :], axis=0, keepdims=True)
        mean = total * (1.0 / WIDTH)
        yield
        highs, rests = [], []
        for c in range(len(parts)):
            rows = slice(c * QUARTER, (c + 1) * QUARTER)
            outer = (parts[c] - unit[k][rows, :] * mean) * chain[k][rows, :]
            highs.append(outer.astype(BF16))
            rests.append((outer - highs[-1].astype(F32)).astype(BF16))
        yield
        left = jnp.concatenate(split3(window(t)) + (jnp.zeros((8, SPAN), F32),), axis=0).astype(BF16)
        right = jnp.concatenate([jnp.concatenate(highs, axis=0), jnp.concatenate(rests, axis=0)], axis=1)
        acc_f[...] += dot_nt(right, jnp.concatenate([left, left], axis=1))
        yield

    def pair(p, carry):
        weave("ABABAAAABABABAA", ahead(2 * p + 1, 1), back_part(2 * p, 0))
        weave("ABABAAAABABABAA", ahead(2 * p + 2, 0), back_part(2 * p + 1, 1))
        return carry

    spans = (num_c + SPAN - 1) // SPAN
    weave("", ahead(0, 0), iter(()))
    lax.fori_loop(0, spans // 2, pair, 0)

    @pl.when(lax.rem(spans, 2) == 1)
    def last():
        weave("", iter(()), back_part(spans - 1, 0))

    firsts = turned(acc_f[...])
    firsts = firsts[0:8] + firsts[8:16] + firsts[16:24]
    bias_grad = acc_s[WIDTH : WIDTH + 8]
    shift_grad = full_nt(bias_grad, low)
    gain_grad = full_nt(jnp.ones((8, SPAN), F32), acc_g[...])
    rows_out[0:5, :] = firsts[0:5]
    rows_out[5:10, :] = narrow_ref[0:5, :]
    rows_out[10:11, :] = firsts[6:7]
    rows_out[11:12, :] = gain_grad[0:1]
    rows_out[12:13, :] = shift_grad[0:1]
    rows_out[13:14, :] = bias_grad[0:1]
    rows_out[14:15, :] = narrow_ref[5:6, :]
    lane = lax.broadcasted_iota(jnp.int32, (1, WIDTH), 1)
    regular = jnp.broadcast_to(jnp.sum(reg_ref[...]), (1, WIDTH))
    rows_out[15:16, :] = jnp.where(lane == 0, narrow_ref[6:7, :], jnp.where(lane == 1, regular, 0.0))
    for q in range(32):
        out_ref[q // 16, q % 16] = acc_s[8 * q : 8 * q + 8, :]
        lanes = slice((q % 2) * 128, (q % 2) * 128 + 128)
        thin_ref[q // 16, q % 16, 0:1, :] = rows_out[q // 2 : q // 2 + 1, lanes]


def newton(gram, sharp):
    ids = lax.broadcasted_iota(jnp.int32, (WIDTH, WIDTH), 0) == lax.broadcasted_iota(jnp.int32, (WIDTH, WIDTH), 1)
    scale = 1.0 / (jnp.sqrt(jnp.sum(jnp.where(ids, gram, 0.0))) + 1e-07)
    sides = (slice(0, WIDTH // 2), slice(WIDTH // 2, WIDTH))
    state = [gram[side] * (scale * scale) for side in sides]
    unit = [jnp.where(ids[side], first_coef, 0.0) for side in sides]

    def joined(halves):
        return [jnp.concatenate(pair, axis=0) for pair in zip(*halves)]

    product = None
    for k in range(NS_STEPS):
        times = six if k < sharp else few
        parts = [three(one) for one in state]
        whole = joined(parts)
        square = [few(part, whole) for part in parts]
        yield None
        poly = [unit[j] + second_coef * state[j] + third_coef * square[j] for j in range(2)]
        left = [three(one) for one in poly]
        if k + 1 < NS_STEPS:
            half = [times(one, whole) for one in left]
            yield None
        if k == 0:
            product = poly
        else:
            right = joined([three(one) for one in product])
            product = [times(one, right) for one in left]
        if k + 1 < NS_STEPS:
            yield None
            outer = joined(left)
            state = [times(three(one), outer) for one in half]
            yield None
    yield jnp.concatenate([one * scale for one in product], axis=0)


def drain(chain):
    result = None
    for result in chain:
        pass
    return result


def newton_begin(gram, state_ref, product_ref):
    ids = lax.broadcasted_iota(jnp.int32, (WIDTH, WIDTH), 0) == lax.broadcasted_iota(jnp.int32, (WIDTH, WIDTH), 1)
    scale = 1.0 / (jnp.sqrt(jnp.sum(jnp.where(ids, gram, 0.0))) + 1e-07)
    state_ref[...] = gram * (scale * scale)
    product_ref[...] = jnp.where(ids, 1.0, 0.0)
    return scale


def newton_step(state_ref, product_ref):
    ids = lax.broadcasted_iota(jnp.int32, (WIDTH, WIDTH), 0) == lax.broadcasted_iota(jnp.int32, (WIDTH, WIDTH), 1)
    sides = (slice(0, WIDTH // 2), slice(WIDTH // 2, WIDTH))
    state = [state_ref[side, :] for side in sides]
    parts = [three(one) for one in state]
    whole = [jnp.concatenate(pair, axis=0) for pair in zip(*parts)]
    square = [few(part, whole) for part in parts]
    left = [
        three(jnp.where(ids[side], first_coef, 0.0) + second_coef * state[j] + third_coef * square[j])
        for j, side in enumerate(sides)
    ]
    half = [six(one, whole) for one in left]
    right = three(product_ref[...])
    for one, side in zip(left, sides):
        product_ref[side, :] = six(one, right)
    outer = [jnp.concatenate(pair, axis=0) for pair in zip(*left)]
    for one, side in zip(half, sides):
        state_ref[side, :] = six(three(one), outer)


def square_rows(sum_ref):
    return jnp.concatenate([sum_ref[q // 16, q % 16] for q in range(32)], axis=0)


def small_rows(sum_ref):
    halves = [sum_ref[q // 16, q % 16, 0:1, :] for q in range(32)]
    return jnp.concatenate(
        [jnp.concatenate([halves[2 * k], halves[2 * k + 1]], axis=1) for k in range(16)], axis=0
    )


def reduce_kernel(
    n, rows_n, grad_ref, thin_ref, own_ref, far_ref, cross_ref, smom_ref,
    sum_ref, thin_sum, tall_ref, move_ref,
    rxh, half_sum, rxq, fin, rxh_thin, half_thin, rxq_thin, fin_thin, mixed, rxm, rxc, rxx, state, product, scales, sems, dsems, csems, qsems,
):
    me = lax.axis_index("ctx")
    r = lax.axis_index("dp")
    chips = (rows_n // 2) * n
    par = lax.rem(r, 2)
    chip = (r // 2) * n + me
    far = lax.rem(r + rows_n // 2, rows_n)
    near = r + 1 - 2 * par
    diag = lax.rem(near + rows_n // 2, rows_n)
    places_here = [pl.ds(pl.multiple_of(place * 8, 8), 8) for place in (r, far)]
    far_first = sorted(range(1, chips), key=lambda d: (-(d % n // 2), -d))
    others = [paired(chip, d, chips) for d in far_first]
    places = [{"dp": 2 * (other // n) + par, "ctx": lax.rem(other, n)} for other in others]
    count = hail(places + [{"dp": near}, {"dp": diag}])
    for i in range(own_ref.shape[0]):
        for rows, ref in zip(places_here, (own_ref, far_ref)):
            tall_ref[i, rows, :] = ref[i]
    height = own_ref.shape[0] - 10

    def near_copy(source, target, j):
        return pltpu.make_async_remote_copy(
            src_ref=source,
            dst_ref=target,
            send_sem=csems.at[0, j],
            recv_sem=csems.at[1, j],
            device_id={"dp": near},
            device_id_type=MESH,
        )

    def chip_copies(source, target, k):
        return [
            copy for pair in zip(*(chip_plan(*plan, k + 2 * j) for j, plan in enumerate(zip(source, target)))) for copy in pair
        ]

    def chip_plan(source, target, k):
        return [
            pltpu.make_async_remote_copy(
                src_ref=source(other),
                dst_ref=target,
                send_sem=qsems.at[2 * k, d],
                recv_sem=qsems.at[2 * k + 1, d],
                device_id=place,
                device_id_type=MESH,
            )
            for d, (other, place) in enumerate(zip(others, places))
        ]

    top = pl.ds(0, 1)
    halves = [
        near_copy(grad_ref.at[1 - par], rxh, 0),
        near_copy(thin_ref.at[1 - par, :, top, :], rxh_thin.at[:, top, :], 4),
    ]
    crosses = plan_all("ctx", n, lambda peer: cross_ref, rxx.at[me], sems.at[0], sems.at[1])
    terms = plan_all("ctx", n, lambda peer: mixed, rxm.at[me], sems.at[2], sems.at[3])
    blocks = [
        near_copy(tall_ref.at[:, rows, :], tall_ref.at[:, rows, :], j + 1) for j, rows in enumerate(places_here)
    ]
    fenced(halves + blocks + crosses, lambda: meet(count))
    rxx[me] = cross_ref[...]

    def first_sum():
        for copy in halves:
            copy.wait()
        half_sum[...] = grad_ref[par] + rxh[...]
        half_thin[:, 0:1, :] = thin_ref[par, :, 0:1, :] + rxh_thin[:, 0:1, :]
        rxq[chip] = half_sum[chip]
        rxq_thin[chip, 0:1, :] = half_thin[chip, 0:1, :]

    scattered = fenced(
        chip_copies(
            (lambda other: half_sum.at[other], lambda other: half_thin.at[other, top, :]),
            (rxq.at[chip], rxq_thin.at[chip, top, :]),
            0,
        ),
        first_sum,
    )
    for copy in blocks:
        copy.wait()
    inners = [jnp.zeros((96, 96), F32)] * 2
    for i in range(height):
        stack = jnp.concatenate(split3(tall_ref[i]), axis=0).astype(BF16)
        inners[i % 2] = inners[i % 2] + dot_nt(stack, stack)
    inner = inners[0] + inners[1]
    inner = inner[0:32] + inner[32:64] + inner[64:96]
    inner = inner[:, 0:32] + inner[:, 32:64] + inner[:, 64:96]
    mixed[...] = jnp.concatenate([inner, jnp.zeros((32, 96), F32)], axis=1)
    rxm[me] = mixed[...]
    fenced(terms)
    latents = tall_ref[height]
    bias_moment = momentum_rate * smom_ref[1] + full_nn(latents.T, tall_ref[height + 1])
    scales[0] = newton_begin(gram_six(three(bias_moment)), state, product)

    def share():
        for copy in crosses:
            copy.wait()
        total = rxx[0]
        for s in range(1, n):
            total = total + rxx[s]
        rxc[r] = total

    def second_sum():
        for copy in scattered:
            copy.wait()
        total = rxq[0]
        thin = rxq_thin[0, 0:1, :]
        for s in range(1, chips):
            total = total + rxq[s]
            thin = thin + rxq_thin[s, 0:1, :]
        fin[...] = total
        fin_thin[0:1, :] = thin
        sum_ref[par, chip] = total
        thin_sum[par, chip, 0:1, :] = thin

    def change_chain():
        move_ref[1] = product[...] * scales[0]
        for copy in terms:
            copy.wait()
        total = rxm[0]
        for s in range(1, n):
            total = total + rxm[s]
        inner = total[:, 0:32]
        for copy in shared:
            copy.wait()
        latents = tall_ref[height]
        cross = jnp.concatenate([rxc[s] for s in range(rows_n)], axis=0)
        weight = momentum_rate * cross + 0.5 * full_nn(inner, latents)
        half = full_nn(latents.T, weight)
        slabs = [tall_ref[height + 2 + t, 8 * s : 8 * s + 8, :] for s in range(rows_n) for t in range(n)]
        gram = (momentum_rate * momentum_rate) * jnp.concatenate(slabs, axis=0) + (half + half.T)
        scales[0] = newton_begin(gram, state, product)

    def all_here():
        for copy in gathered:
            copy.wait()

    shared = plan_all("dp", rows_n, lambda peer: rxc.at[r], rxc.at[r], dsems.at[0], dsems.at[1])
    gathered = chip_copies(
        (lambda other: fin, lambda other: fin_thin.at[top, :]),
        (sum_ref.at[par, chip], thin_sum.at[par, chip, top, :]),
        1,
    )
    last = [
        near_copy(sum_ref.at[par], sum_ref.at[par], 3),
        near_copy(thin_sum.at[par, :, top, :], thin_sum.at[par, :, top, :], 5),
    ]
    events = ((1, share, shared), (3, second_sum, gathered), (5, change_chain, []), (8, all_here, last))

    def iterate(i, carry):
        for place, before, copies in events:

            @pl.when(i == place)
            def run():
                before()
                for copy in copies:
                    copy.start()

        newton_step(state, product)
        return carry

    lax.fori_loop(0, 2 * NS_STEPS, iterate, 0)
    move_ref[0] = product[...] * scales[0]
    for copy in last:
        copy.wait()


def update_kernel(
    live_all, groups_all, mom_ref, head_ref, tall_ref, move_ref, sum_ref, thin_ref, square_ref, smom_ref,
    small_ref, mmom_ref, mvar_ref,
    mom_out, head_out, copy_out, smom_out, square_out, scopy_out, mmom_out, mvar_out, small_out, mcopy_out,
    loss_out, mom, head, low_copy, left, wide, store_sem,
):
    ring, unused, chunk = mom.shape
    chunks = mom_ref.shape[1] // chunk
    per = chunk // WIDTH

    def stores(k):
        lanes = pl.ds(k * chunk, chunk)
        return [
            pltpu.make_async_copy(source.at[k % ring], target.at[:, lanes], store_sem.at[j, k % ring])
            for j, (source, target) in enumerate(((mom, mom_out), (head, head_out), (low_copy, copy_out)))
        ]

    height = tall_ref.shape[0] - 10
    latents = tall_ref[height]
    rows = jnp.concatenate([latents] * 3 + [jnp.zeros((32, WIDTH), F32)], axis=0)
    left[...] = rows.T.astype(BF16)
    ids = lax.broadcasted_iota(jnp.int32, (WIDTH, WIDTH), 0) == lax.broadcasted_iota(jnp.int32, (WIDTH, WIDTH), 1)
    move = move_ref[0] * (-head_rate * 0.2 * WIDTH)
    centre = jnp.sum(jnp.where(ids, move, 0.0)) * (1.0 / WIDTH)
    wide[...] = jnp.concatenate(three(jnp.where(ids, move - centre, move))[0:2], axis=0)
    narrow = small_rows(thin_ref)
    stats = narrow[15:16]
    lane = lax.broadcasted_iota(jnp.int32, (1, WIDTH), 1)
    weight = jnp.where(lane == 0, 1.0 / live_all, jnp.where(lane == 1, reg_weight / groups_all, 0.0))
    loss_out[...] = jnp.broadcast_to(jnp.sum(stats * weight), loss_out.shape)
    moment, second, new = adam_update(small_ref[...], narrow[0:15], mmom_ref[...], mvar_ref[...])
    mmom_out[...] = moment
    mvar_out[...] = second
    small_out[...] = new
    mcopy_out[...] = new.astype(BF16)
    keep = 1.0 - head_rate * decay_rate

    grads = [square_rows(sum_ref), full_nn(latents.T, tall_ref[height + 1])]
    moments = [momentum_rate * smom_ref[k] + grads[k] for k in range(2)]
    side = newton(gram_six(three(moments[0])), NS_STEPS)
    for k in range(chunks):
        slot = k % ring
        if k >= ring:
            for copy in stores(k - ring):
                copy.wait()

        def begin_tile(i):
            lanes = slice(i * WIDTH, (i + 1) * WIDTH)
            wide_lanes = slice(k * chunk + i * WIDTH, k * chunk + (i + 1) * WIDTH)
            high, mid, low = three(tall_ref[k * per + i])
            right = jnp.concatenate([high, mid, low, jnp.zeros_like(high)], axis=0)
            moment = momentum_rate * mom_ref[:, wide_lanes] + dot_nn(left[...], right)
            mom[slot, :, lanes] = moment
            high = moment.astype(BF16)
            mid = (moment - high.astype(F32)).astype(BF16)
            return keep * head_ref[:, wide_lanes] + centre * moment, high, mid

        def finish_tile(i):
            lanes = slice(i * WIDTH, (i + 1) * WIDTH)
            base, high, mid = ready[i]
            first = dot_nn(wide[...], high)
            new = (first[0:WIDTH] + dot_nn(wide[0:WIDTH, :], mid)) + (first[WIDTH:] + base)
            head[slot, :, lanes] = new
            low_copy[slot, :, lanes] = new.astype(BF16)

        ready = [begin_tile(0), begin_tile(1)]
        for i in range(per):
            if i + 2 < per:
                ready.append(begin_tile(i + 2))
            finish_tile(i)
            if i < 3:
                next(side, None) if k * 3 + i < 17 else None
        for copy in stores(k):
            copy.start()
    for k, move in enumerate((drain(side), move_ref[1])):
        smom_out[k] = moments[k]
        old = square_ref[k]
        change = 0.2 * WIDTH**0.5 * six(three(move), three(moments[k])) + decay_rate * old
        new = old - square_rates[k] * change
        square_out[k] = new
        scopy_out[k] = new.astype(BF16)
    for k in range(chunks - ring, chunks):
        for copy in stores(k):
            copy.wait()


def shape(*dims, dtype=F32):
    return jax.ShapeDtypeStruct(dims, dtype)


def dma_sems(*dims):
    return pltpu.SemaphoreType.DMA(dims)


def remote_params(ident, room=50):
    return pltpu.CompilerParams(collective_id=ident, has_side_effects=True, vmem_limit_bytes=room * MIB)


def plain_params(room=16):
    return pltpu.CompilerParams(vmem_limit_bytes=room * MIB)


CHUNK = 1024
RING = 4


def call_scatter(n, rows_n, lengths, pixels, ctx_mask, head_mom):
    micro, groups, slots = pixels.shape[1], pixels.shape[2], pixels.shape[4]
    return pl.pallas_call(
        functools.partial(scatter_kernel, n, rows_n),
        out_shape=[
            shape(n, 8, slots),
            shape(n, 8, 128),
            shape(n, 8, slots),
            shape(n, 8, 128),
            shape(WIDTH // rows_n, WIDTH),
        ],
        in_specs=[hbm_spec()] * 4,
        out_specs=[vmem_spec()] * 5,
        scratch_shapes=[
            pltpu.SMEM(lengths.shape, jnp.int32),
            pltpu.VMEM((1, micro, 5, groups, slots), F32),
            pltpu.VMEM(ctx_mask.shape, jnp.int32),
            pltpu.VMEM((n, 8, slots), F32),
            pltpu.VMEM((n, 8, 128), F32),
            pltpu.VMEM((n, 128), F32),
            pltpu.VMEM((WIDTH, head_mom.shape[1] // rows_n), F32),
            pltpu.VMEM((WIDTH, WIDTH), F32),
            pltpu.VMEM((rows_n, WIDTH // rows_n, WIDTH), F32),
            pltpu.VMEM((TILE, TILE), BF16),
            dma_sems(micro, n - 1),
            dma_sems(micro, n - 1),
            dma_sems(),
            dma_sems(2, rows_n - 1),
            dma_sems(3),
            dma_sems(2, n - 1),
        ],
        compiler_params=remote_params(1, 50),
        name="scatter_pixels",
        cost_estimate=busy(14),
    )(lengths, jnp.transpose(pixels, (0, 1, 3, 2, 4)), ctx_mask, head_mom)


def call_encode(received, seen, small_params, square_w):
    cap = received.shape[0] * received.shape[2] + 5 * SPAN
    return pl.pallas_call(
        encoder_kernel,
        out_shape=[shape(8, WIDTH), shape(8, 128), shape(8, cap), shape(8, cap), shape(1, dtype=jnp.int32)],
        in_specs=[vmem_spec()] * 4,
        out_specs=[vmem_spec()] * 4 + [smem_spec()],
        scratch_shapes=[
            pltpu.VMEM((8, 128), jnp.int32),
            pltpu.SMEM((8, 128), jnp.int32),
            pltpu.VMEM((3, WIDTH, SPAN), F32),
            pltpu.VMEM((WIDTH, WIDTH), BF16),
            pltpu.VMEM((WIDTH, 16), F32),
            pltpu.VMEM((WIDTH, SPAN), BF16),
            pltpu.VMEM((WIDTH, SPAN), BF16),
            dma_sems(),
        ],
        compiler_params=plain_params(),
        name="encode",
        cost_estimate=busy(10),
    )(received, seen, small_params, square_w)


def call_generate(n, latent, amount, head_w, tiles, share):
    height = WIDTH // n
    chunks = head_w.shape[1] // CHUNK
    return pl.pallas_call(
        functools.partial(theta_kernel, n),
        out_shape=[
            shape(WIDTH, WIDTH),
            shape(WIDTH, WIDTH, dtype=BF16),
            shape(8, WIDTH),
            shape(8, WIDTH),
            shape(8, WIDTH),
            shape(*tiles.shape),
            shape(*share.shape),
        ],
        in_specs=[vmem_spec()] * 2 + [any_spec()] + [vmem_spec()] * 2,
        out_specs=[vmem_spec()] * 7,
        scratch_shapes=[
            pltpu.VMEM((n, 8, WIDTH), F32),
            pltpu.VMEM((n, 8, 128), F32),
            pltpu.VMEM((chunks, WIDTH, CHUNK), F32),
            pltpu.VMEM((n, height, WIDTH), BF16),
            pltpu.VMEM((2, WIDTH, 128), F32),
            dma_sems(chunks),
            dma_sems(10, n - 1),
        ],
        compiler_params=remote_params(2),
        name="generate",
        cost_estimate=busy(17),
    )(latent, amount, head_w, tiles, share)


def call_siren(n, live_all, lengths, received, seen, gen, latent, small_params, square_w):
    cap = received.shape[0] * received.shape[2] + 5 * SPAN
    return pl.pallas_call(
        functools.partial(siren_kernel, live_all),
        out_shape=[shape(WIDTH, WIDTH), shape(8, WIDTH), shape(8, WIDTH)],
        in_specs=[smem_spec()] + [vmem_spec()] * 6,
        out_specs=[vmem_spec()] * 3,
        scratch_shapes=[
            pltpu.VMEM((8, cap), F32),
            pltpu.VMEM((8, 128), jnp.int32),
            pltpu.SMEM((8, 128), jnp.int32),
            pltpu.VMEM((WIDTH, WIDTH), BF16),
            pltpu.VMEM((WIDTH, SPAN), F32),
            pltpu.VMEM((WIDTH, SPAN), BF16),
            pltpu.VMEM((WIDTH, SPAN), BF16),
            pltpu.VMEM((WIDTH, SPAN), F32),
            pltpu.VMEM((WIDTH, SPAN), F32),
            pltpu.VMEM((WIDTH, SPAN), BF16),
            pltpu.VMEM((WIDTH, SPAN), BF16),
            pltpu.VMEM((WIDTH, SPAN), F32),
            pltpu.VMEM((WIDTH, SPAN), F32),
            pltpu.VMEM((WIDTH + 16, WIDTH), F32),
            pltpu.VMEM((WIDTH, 32), F32),
            pltpu.VMEM((WIDTH, 16), F32),
            pltpu.VMEM((8, SPAN), F32),
            dma_sems(),
        ],
        compiler_params=plain_params(),
        name="siren",
        cost_estimate=busy(16),
    )(lengths, received, seen, gen, latent, small_params, square_w)


def call_latent(n, groups_all, part, bias, theta, head_w, head_mom, z8, gram_part):
    height = WIDTH // n
    chunks = head_w.shape[1] // CHUNK
    slab = gram_part.shape[0] // n
    return pl.pallas_call(
        functools.partial(latent_kernel, n, groups_all),
        out_shape=[
            shape(8, WIDTH),
            shape(height + 2 + n, 8, WIDTH),
            shape(8, WIDTH),
        ],
        in_specs=[vmem_spec()] * 3 + [any_spec()] * 2 + [vmem_spec()] * 2,
        out_specs=[vmem_spec()] * 3,
        scratch_shapes=[
            pltpu.VMEM((WIDTH, WIDTH), F32),
            pltpu.VMEM((n, 8, WIDTH), F32),
            pltpu.VMEM((2, WIDTH, 128), F32),
            pltpu.VMEM((chunks, WIDTH, CHUNK), F32),
            pltpu.VMEM((chunks, WIDTH, CHUNK), F32),
            pltpu.VMEM((height, WIDTH, WIDTH), BF16),
            pltpu.VMEM((3, height, WIDTH, WIDTH), BF16),
            pltpu.VMEM((n, 8, WIDTH), F32),
            pltpu.VMEM((8, WIDTH), F32),
            pltpu.VMEM((height, 32, WIDTH), BF16),
            pltpu.VMEM((n, slab, WIDTH), F32),
            pltpu.VMEM((slab, WIDTH), F32),
            dma_sems(chunks),
            dma_sems(chunks),
            dma_sems(10, n - 1),
        ],
        compiler_params=remote_params(3),
        name="latent_grads",
        cost_estimate=busy(18),
    )(part, bias, theta, head_w, head_mom, z8, gram_part)


def call_back(counts, clist, stats, small_params, square_w, latent_grad, inverse, tall, narrow, regular):
    return pl.pallas_call(
        encoder_back_kernel,
        out_shape=[shape(2, 16, 8, WIDTH), shape(2, 16, 8, 128)],
        in_specs=[smem_spec()] + [vmem_spec()] * 9,
        out_specs=[vmem_spec()] * 2,
        scratch_shapes=[
            pltpu.VMEM((3, WIDTH, SPAN), F32),
            pltpu.VMEM((WIDTH, WIDTH), BF16),
            pltpu.VMEM((WIDTH + 16, WIDTH), BF16),
            pltpu.VMEM((WIDTH, SPAN), F32),
            pltpu.VMEM((WIDTH, SPAN), F32),
            pltpu.VMEM((WIDTH, SPAN), F32),
            pltpu.VMEM((WIDTH, SPAN), F32),
            pltpu.VMEM((WIDTH, SPAN), BF16),
            pltpu.VMEM((WIDTH, SPAN), BF16),
            pltpu.VMEM((WIDTH, SPAN), BF16),
            pltpu.VMEM((WIDTH, SPAN), BF16),
            pltpu.VMEM((WIDTH + 16, WIDTH), F32),
            pltpu.VMEM((WIDTH, 32), F32),
            pltpu.VMEM((WIDTH, SPAN), F32),
            pltpu.VMEM((16, WIDTH), F32),
        ],
        compiler_params=plain_params(),
        name="encode_back",
        cost_estimate=busy(16),
    )(counts, clist, stats, small_params, square_w, latent_grad, inverse, tall, narrow, regular)


def call_reduce(n, rows_n, grads, thin, own, far, cross, square_mom):
    chips = (rows_n // 2) * n
    return pl.pallas_call(
        functools.partial(reduce_kernel, n, rows_n),
        out_shape=[
            shape(*grads.shape),
            shape(*thin.shape),
            shape(own.shape[0], 8 * rows_n, WIDTH),
            shape(2, WIDTH, WIDTH),
        ],
        in_specs=[vmem_spec()] * 6,
        out_specs=[vmem_spec()] * 4,
        scratch_shapes=[
            pltpu.VMEM((chips, 8, WIDTH), F32),
            pltpu.VMEM((chips, 8, WIDTH), F32),
            pltpu.VMEM((chips, 8, WIDTH), F32),
            pltpu.VMEM((8, WIDTH), F32),
            pltpu.VMEM((chips, 8, 128), F32),
            pltpu.VMEM((chips, 8, 128), F32),
            pltpu.VMEM((chips, 8, 128), F32),
            pltpu.VMEM((8, 128), F32),
            pltpu.VMEM((32, 128), F32),
            pltpu.VMEM((n, 32, 128), F32),
            pltpu.VMEM((rows_n, 8, WIDTH), F32),
            pltpu.VMEM((n, 8, WIDTH), F32),
            pltpu.VMEM((WIDTH, WIDTH), F32),
            pltpu.VMEM((WIDTH, WIDTH), F32),
            pltpu.SMEM((1,), F32),
            dma_sems(4, n - 1),
            dma_sems(2, rows_n - 1),
            dma_sems(2, 6),
            dma_sems(8, chips - 1),
        ],
        compiler_params=remote_params(4, 16),
        name="reduce_grads",
        cost_estimate=busy(24),
    )(grads, thin, own, far, cross, square_mom)


def call_update(
    live_all, groups_all, head_mom, head_w, tall, move, sums, thin_sums, square_w, square_mom, small_params,
    small_mom, small_var,
):
    columns = head_w.shape[1]
    small_copy = shape(15, WIDTH, dtype=BF16)
    square_copy = shape(2, WIDTH, WIDTH, dtype=BF16)
    loss = shape(1, 128)
    others = [square_mom, square_w, square_copy, small_mom, small_var, small_params, small_copy, loss]
    return pl.pallas_call(
        functools.partial(update_kernel, live_all, groups_all),
        out_shape=[shape(WIDTH, columns), shape(WIDTH, columns), shape(WIDTH, columns, dtype=BF16)]
        + [shape(*one.shape, dtype=one.dtype) for one in others],
        in_specs=[vmem_spec()] * 11,
        out_specs=[any_spec()] * 3 + [vmem_spec()] * 8,
        scratch_shapes=[
            pltpu.VMEM((RING, WIDTH, CHUNK), F32),
            pltpu.VMEM((RING, WIDTH, CHUNK), F32),
            pltpu.VMEM((RING, WIDTH, CHUNK), BF16),
            pltpu.VMEM((WIDTH, 128), BF16),
            pltpu.VMEM((2 * WIDTH, WIDTH), BF16),
            dma_sems(3, RING),
        ],
        compiler_params=plain_params(30),
        name="update_all",
        cost_estimate=busy(12),
    )(
        head_mom, head_w, tall, move, sums, thin_sums, square_w, square_mom, small_params, small_mom, small_var
    )


def grouped(
    pixels, lengths, ctx_mask, head_w, head_mom, square_w, square_mom, small_params, small_mom, small_var
):
    micro, groups, slots = pixels.shape[1], pixels.shape[2], pixels.shape[4]
    n = lax.axis_size("ctx")
    rows_n = lax.axis_size("dp")
    live_all = rows_n * micro * (groups * slots * n * 5 // 8)
    groups_all = rows_n * micro * groups
    received, seen, tiles, share, gram_part = call_scatter(n, rows_n, lengths, pixels, ctx_mask, head_mom)
    latent, amount, clist, stats, counts = call_encode(received, seen, small_params, square_w)
    theta, gen, z8, inverse, regular, group_rows, group_seen = call_generate(
        n, latent, amount, head_w, tiles, share
    )
    part, bias, narrow = call_siren(
        n, live_all, lengths, group_rows, group_seen, gen, z8, small_params, square_w
    )
    latent_grad, own, cross = call_latent(
        n, groups_all, part, bias, theta, head_w, head_mom, z8, gram_part
    )
    far = lax.ppermute(own, "dp", [(r, (r + rows_n // 2) % rows_n) for r in range(rows_n)])
    grads, thin = call_back(
        counts, clist, stats, small_params, square_w, latent_grad, inverse, own, narrow, regular
    )
    sums, thin_sums, tall, move = call_reduce(n, rows_n, grads, thin, own, far, cross, square_mom)
    updated = call_update(
        live_all, groups_all, head_mom, head_w, tall, move, sums, thin_sums, square_w, square_mom, small_params,
        small_mom, small_var,
    )
    (
        head_moment,
        head_new,
        head_copy,
        square_moment,
        square_new,
        square_copy,
        small_moment,
        small_second,
        small_new,
        small_copy,
        loss,
    ) = updated
    return (
        head_moment,
        head_new,
        head_copy,
        square_moment,
        square_new,
        square_copy,
        small_moment,
        small_second,
        small_new,
        small_copy,
        loss[0, 0],
    )


def local(pixels, lengths, ctx_mask, head_w, *rest):
    n = lax.axis_size("ctx")
    fits = (
        pixels.shape[1] * pixels.shape[2] == n
        and n == 8
        and lax.axis_size("dp") == 4
        and pixels.shape[4] == 2048
        and head_w.shape == (WIDTH, 8192)
    )
    chosen = grouped if fits else general
    return chosen(pixels, lengths, ctx_mask, head_w, *rest)


def solution(mesh):
    placed = (
        P("dp", None, None, None, "ctx"),
        P("dp", None, None),
        P("dp", None, None, "ctx"),
        P(None, "ctx"),
        P(None, "ctx"),
        P(),
        P(),
        P(),
        P(),
        P(),
    )
    return jax.shard_map(
        local,
        mesh=mesh,
        in_specs=placed,
        out_specs=(
            P(None, "ctx"),
            P(None, "ctx"),
            P(None, "ctx"),
            P(),
            P(),
            P(),
            P(),
            P(),
            P(),
            P(),
            P(),
        ),
        check_vma=False,
    )
```
